32 devices in a mesh: grp: 2 (over y), dp: 4 (over z), mp: 2 (over x), sub: 2 (over core).
Axes of the slice: x: 2, y: 2, z: 4, core: 2. Of those that a mesh axis runs over, the one named last changes fastest.
Arguments:
- tokens: bfloat16 [4096, 16384], P(('grp', 'dp', 'sub'), 'mp'), parts along dimension 0
- cotangent: bfloat16 [4096, 16384], P(('grp', 'dp', 'sub'), 'mp'), parts along dimension 0, may hold values from -6 to 6
- rms_norm_gain: bfloat16 [16384], P('mp'), may hold values from 0.5 to 1.5
- gate_codes: bfloat16 [128, 128, 256], P('mp', ('dp', 'sub')), may hold values from -6 to 6
- gate_block_scale: bfloat16 [128, 2], P('mp'), may hold values from 0.0039978027 to 0.015991211
- up_codes: bfloat16 [128, 128, 256], P('mp', ('dp', 'sub')), may hold values from -6 to 6
- up_block_scale: bfloat16 [128, 2], P('mp'), may hold values from 0.0039978027 to 0.015991211
- down_codes: bfloat16 [256, 128, 128], P(('dp', 'sub'), 'mp'), may hold values from -6 to 6
- down_block_scale: bfloat16 [2, 128], P(None, 'mp'), may hold values from 0.014953613 to 0.059814453
- up_adapter_in: bfloat16 [32768, 128], P(('grp', 'mp')), parts along dimension 0, may hold values from -0.046875 to 0.046875
- up_adapter_out: bfloat16 [256, 256], P('grp', 'mp'), parts along dimension 0, may hold values from -0.5 to 0.5
- down_adapter_in: bfloat16 [512, 128], P(('grp', 'mp')), parts along dimension 0, may hold values from -0.375 to 0.375
- down_adapter_out: bfloat16 [256, 16384], P('grp', 'mp'), parts along dimension 0, may hold values from -0.5 to 0.5
- sequence_length_list: int32 [16, 2], P(('grp', 'dp', 'sub')), parts along dimension 0, may hold values from 32 to 128, as said below
- slot_sequence_index: int32 [4096], P(('grp', 'dp', 'sub')), parts along dimension 0, may hold values from 0 to 2, as said below
Outputs:
- up_in_gradient: bfloat16 [32768, 128], P(('grp', 'mp')), parts along dimension 0
- up_out_gradient: bfloat16 [256, 256], P('grp', 'mp'), parts along dimension 0
- down_in_gradient: bfloat16 [512, 128], P(('grp', 'mp')), parts along dimension 0
- down_out_gradient: bfloat16 [256, 16384], P('grp', 'mp'), parts along dimension 0
The draws below stay inside these ranges and needn't reach their ends.
There are 2 independent parts, one for each index of `grp`. The reference program is written for one: setup_inputs(seed, part) draws one part's arguments, and reference() takes and returns one part's arrays. A program takes and returns all parts, laid end to end along the dimension named above; an argument that names none is the same for every part. Nothing has to cross between parts.
Inputs may be any that keep to these rules, and one draw needn't show every extreme that they name: `sequence_length_list`: row d holds, in order, the lengths of the 2 sequences packed from the first token slot of data device d on; the rest of its 256 slots are padding. At least one row fills all slots. `slot_sequence_index`: within each data device's 256 slots, the number of the sequence that holds the slot as given by sequence_length_list, and 2 for padding slots; some device has padding.
All inputs are finite; a program needn't handle non-finite values.
Results may differ from the reference program's by a relative error of at most 0.0091.
Values may be sent and summed in bfloat16 or wider, within the bound.
No kernel may reach another device: no remote copies, remote signals or barrier semaphores. Data moves between devices by JAX's collectives and lax.ppermute only.
A program may use at most 128 MiB of HBM per device.

```python
import math
import jax
import jax.numpy as jnp
from jax import lax

MODEL_WIDTH = 16384
ADAPTER_RANK = 128
QB = 128
TOK_DEV = 256
SEQ_DEV = 2
LMAX = 128
LMIN = 32
N_DATA = 8
TOKENS = 2048
FEED_UNITS = 256


def packing(key):
    lengths = jax.random.randint(jax.random.fold_in(key, 11), (N_DATA, SEQ_DEV), LMIN, LMAX + 1)
    filled = jax.random.randint(jax.random.fold_in(key, 12), (), 0, N_DATA)
    rows = jnp.arange(N_DATA, dtype=jnp.int32)[:, None]
    cols = jnp.arange(SEQ_DEV, dtype=jnp.int32)[None, :]
    lengths = jnp.where(rows == filled, LMAX, lengths)
    shorter = (filled + 1) % N_DATA
    lengths = jnp.where((rows == shorter) & (cols == 0) & (rows != filled), LMIN, lengths).astype(jnp.int32)
    ends = jnp.cumsum(lengths, axis=1)
    places = jnp.arange(TOK_DEV, dtype=jnp.int32)
    owners = jnp.sum((places[None, :, None] >= ends[:, None, :]).astype(jnp.int32), axis=-1)
    return (lengths, owners.reshape(-1).astype(jnp.int32))


def draw_sequence_length_list(key, part):
    lengths, owners = packing(key)
    return lengths


def draw_slot_sequence_index(key, part):
    lengths, owners = packing(key)
    return owners


def draw_tokens(key, part):
    key = jax.random.fold_in(key, 21)
    column = jnp.arange(MODEL_WIDTH, dtype=jnp.float32)[None, :] / MODEL_WIDTH
    rough = jax.random.uniform(jax.random.fold_in(key, 1), (1, MODEL_WIDTH), jnp.float32, 0.6, 1.4)
    base = jnp.clip(jax.random.normal(jax.random.fold_in(key, 2), (TOKENS, MODEL_WIDTH), jnp.float32), -4.0, 4.0)
    rising = jnp.exp(jnp.log(3.0) * column) / 1.7
    return (base * rising * rough).astype(jnp.bfloat16)


def block_levels(rng, shape, shards, low, high):
    level = 1.0
    for position, parts in shards:
        heights = jax.random.uniform(jax.random.fold_in(jax.random.fold_in(rng, 6), position), (parts,), jnp.float32, low / len(shards), high / len(shards))
        level = level * jnp.repeat(jnp.exp(heights), shape[position] // parts).reshape((-1,) + (1,) * (len(shape) - 1 - position))
    return level


def gaussian(rng, extent, scale, limit, split=(), kind=jnp.bfloat16):
    array = scale * jax.random.normal(rng, extent, jnp.float32)
    if split:
        array = array * block_levels(rng, extent, split, -0.22, 0.18)
    return jnp.clip(array, -limit, limit).astype(kind)


def setup_inputs(seed: int = 0, part: int = 0) -> dict:
    seeds = jax.random.split(jax.random.key(seed), 16)
    part_keys = jax.random.split(jax.random.fold_in(seeds[15], part), 16)
    tokens = draw_tokens(jax.random.fold_in(jax.random.fold_in(seeds[15], part), 71), part)
    cotangent = gaussian(part_keys[1], (TOKENS, MODEL_WIDTH), 1.0, 6.0, ((0, 8), (1, 2)))
    rms_norm_gain = jnp.clip(1.0 + 0.1 * jax.random.normal(seeds[2], (MODEL_WIDTH,), jnp.float32), 0.5, 1.5).astype(jnp.bfloat16)
    gate_codes = gaussian(seeds[3], (MODEL_WIDTH // QB, QB, FEED_UNITS), 1.0, 6.0, ((0, 2), (1, 8)))
    gate_block_scale = jnp.clip(jnp.exp(math.log(0.015991211) - 1.3862944 * jax.random.uniform(seeds[4], (MODEL_WIDTH // QB, FEED_UNITS // QB), jnp.float32) ** block_levels(seeds[4], (MODEL_WIDTH // QB, FEED_UNITS // QB), ((0, 2),), -0.2, 0.2)), 0.0039978027, 0.015991211).astype(jnp.bfloat16)
    up_codes = gaussian(seeds[5], (MODEL_WIDTH // QB, QB, FEED_UNITS), 1.0, 6.0, ((0, 2), (1, 8)))
    up_block_scale = jnp.clip(jnp.exp(math.log(0.015991211) - 1.3862944 * jax.random.uniform(seeds[6], (MODEL_WIDTH // QB, FEED_UNITS // QB), jnp.float32) ** block_levels(seeds[6], (MODEL_WIDTH // QB, FEED_UNITS // QB), ((0, 2),), -0.2, 0.2)), 0.0039978027, 0.015991211).astype(jnp.bfloat16)
    down_codes = gaussian(seeds[7], (FEED_UNITS, MODEL_WIDTH // QB, QB), 1.0, 6.0, ((0, 8), (1, 2)))
    down_block_scale = jnp.clip(jnp.exp(math.log(0.059814453) - 1.3862944 * jax.random.uniform(seeds[8], (FEED_UNITS // QB, MODEL_WIDTH // QB), jnp.float32) ** block_levels(seeds[8], (FEED_UNITS // QB, MODEL_WIDTH // QB), ((1, 2),), -0.2, 0.2)), 0.014953613, 0.059814453).astype(jnp.bfloat16)
    up_adapter_in = gaussian(part_keys[9], (MODEL_WIDTH, ADAPTER_RANK), MODEL_WIDTH ** -0.5, 0.046875, ((0, 2),))
    up_adapter_out = gaussian(part_keys[10], (ADAPTER_RANK, FEED_UNITS), ADAPTER_RANK ** -0.5, 0.5, ((1, 2),))
    down_adapter_in = gaussian(part_keys[11], (FEED_UNITS, ADAPTER_RANK), FEED_UNITS ** -0.5, 0.375, ((0, 2),))
    down_adapter_out = gaussian(part_keys[12], (ADAPTER_RANK, MODEL_WIDTH), ADAPTER_RANK ** -0.5, 0.5, ((1, 2),))
    sequence_length_list = draw_sequence_length_list(jax.random.fold_in(jax.random.fold_in(seeds[15], part), 71), part)
    slot_sequence_index = draw_slot_sequence_index(jax.random.fold_in(jax.random.fold_in(seeds[15], part), 71), part)
    return {"tokens": tokens, "cotangent": cotangent, "rms_norm_gain": rms_norm_gain, "gate_codes": gate_codes, "gate_block_scale": gate_block_scale, "up_codes": up_codes, "up_block_scale": up_block_scale, "down_codes": down_codes, "down_block_scale": down_block_scale, "up_adapter_in": up_adapter_in, "up_adapter_out": up_adapter_out, "down_adapter_in": down_adapter_in, "down_adapter_out": down_adapter_out, "sequence_length_list": sequence_length_list, "slot_sequence_index": slot_sequence_index}


ADAPTER_SCALE = 2.0
EPS = 1e-05

def dequant_rows(quant, scale):
    width = quant.shape[1]
    wide = jnp.repeat(scale.astype(jnp.float32), width, axis=1)[:, None, :]
    return (quant.astype(jnp.float32) * wide).astype(jnp.bfloat16).reshape(-1, quant.shape[2])

def dequant_cols(quant, scale):
    width = quant.shape[2]
    wide = jnp.repeat(scale.astype(jnp.float32), width, axis=0)[:, :, None]
    return (quant.astype(jnp.float32) * wide).astype(jnp.bfloat16).reshape(quant.shape[0], -1)

def contract_dims(left, right, left_dim, right_dim):
    return lax.dot_general(left, right, (((left_dim,), (right_dim,)), ((), ())), preferred_element_type=jnp.float32)

def reference(tokens, cotangent, rms_norm_gain, gate_codes, gate_block_scale, up_codes, up_block_scale, down_codes, down_block_scale, up_adapter_in, up_adapter_out, down_adapter_in, down_adapter_out, sequence_length_list, slot_sequence_index):
    squares = lax.optimization_barrier(jnp.mean(jnp.square(tokens.astype(jnp.float32)), axis=-1, keepdims=True))
    inv_rms = lax.rsqrt(squares + EPS)
    normed_input = (tokens.astype(jnp.float32) * inv_rms * rms_norm_gain.astype(jnp.float32)).astype(jnp.bfloat16)
    w_gate = dequant_rows(gate_codes, gate_block_scale)
    up_weight = dequant_rows(up_codes, up_block_scale)
    gate = jnp.dot(normed_input, w_gate, preferred_element_type=jnp.float32)
    up_adapter_rank = jnp.dot(normed_input, up_adapter_in, preferred_element_type=jnp.float32).astype(jnp.bfloat16)
    up_projected = jnp.dot(normed_input, up_weight, preferred_element_type=jnp.float32) + ADAPTER_SCALE * jnp.dot(up_adapter_rank, up_adapter_out, preferred_element_type=jnp.float32)
    silu_gate = jax.nn.silu(gate)
    hidden_units = (silu_gate * up_projected).astype(jnp.bfloat16)
    ratios = LMAX / sequence_length_list.astype(jnp.float32)
    slots = slot_sequence_index.reshape(N_DATA, TOK_DEV)
    match = slots[:, :, None] == jnp.arange(SEQ_DEV, dtype=jnp.int32)[None, None, :]
    token_weight = lax.optimization_barrier(jnp.sum(jnp.where(match, ratios[:, None, :], jnp.float32(0.0)), axis=-1)).reshape(-1)
    token_weight = token_weight * jnp.float32(1.0 / math.sqrt(TOKENS))
    output_gradient = (cotangent.astype(jnp.float32) * token_weight[:, None]).astype(jnp.bfloat16)
    output_adapter_rank = contract_dims(output_gradient, down_adapter_out, 1, 1).astype(jnp.bfloat16)
    down_weight = dequant_cols(down_codes, down_block_scale)
    hidden_gradient = contract_dims(output_gradient, down_weight, 1, 1) + ADAPTER_SCALE * contract_dims(output_adapter_rank, down_adapter_in, 1, 1)
    up_gradient = (hidden_gradient * silu_gate).astype(jnp.bfloat16)
    hidden_adapter_rank = jnp.dot(hidden_units, down_adapter_in, preferred_element_type=jnp.float32).astype(jnp.bfloat16)
    up_adapter_rank_gradient = contract_dims(up_gradient, up_adapter_out, 1, 1).astype(jnp.bfloat16)
    up_in_gradient = (ADAPTER_SCALE * contract_dims(normed_input, up_adapter_rank_gradient, 0, 0)).astype(jnp.bfloat16)
    up_out_gradient = (ADAPTER_SCALE * contract_dims(up_adapter_rank, up_gradient, 0, 0)).astype(jnp.bfloat16)
    down_in_gradient = (ADAPTER_SCALE * contract_dims(hidden_units, output_adapter_rank, 0, 0)).astype(jnp.bfloat16)
    down_out_gradient = (ADAPTER_SCALE * contract_dims(hidden_adapter_rank, output_gradient, 0, 0)).astype(jnp.bfloat16)
    return (up_in_gradient, up_out_gradient, down_in_gradient, down_out_gradient)
```

```python
import math

import jax
import jax.numpy as jnp
from jax import lax
from jax.experimental import pallas as pl
from jax.experimental.pallas import tpu as pltpu
from jax.sharding import PartitionSpec as P

ADAPTER_SCALE = 2.0
EPS = 1e-05
ROW_TILE = 16
CHUNKS = 4
VMEM_LIMIT = 48 * 1024 * 1024

F32 = jnp.float32
BF16 = jnp.bfloat16


def contract_dims(left, right, left_dim, right_dim):
    return lax.dot_general(
        left, right, (((left_dim,), (right_dim,)), ((), ())), preferred_element_type=F32
    )


def vmem_specs(count):
    return [pl.BlockSpec(memory_space=pltpu.VMEM)] * count


def swap(x, axis):
    return lax.ppermute(x, axis, [(0, 1), (1, 0)])


def others(x, axis):
    n = lax.axis_size(axis)
    return [lax.ppermute(x, axis, [(i, (i + k) % n) for i in range(n)]) for k in range(1, n)]


def ring_order(n):
    return [0] + list(range(1, n, 2)) + [i for i in reversed(range(2, n)) if i % 2 == 0]


def gather_line(own):
    n = lax.axis_size("dp")
    order = ring_order(n)
    ring = [(order[i], order[(i + 1) % n]) for i in range(n)]
    half = own.shape[0] // 2
    moving = lax.dynamic_slice_in_dim(own, lax.axis_index("grp") * half, half, 0)
    steps = []
    for _ in range(n - 1):
        moving = lax.ppermute(moving, "dp", ring)
        steps.append((moving, swap(moving, "grp")))
    return own, steps


def gather_chip(own):
    mine, steps = gather_line(own)
    flat = [mine] + [part for step in steps for part in step]
    return flat + [swap(part, "sub") for part in flat]


def line_sum(x, axis):
    n = lax.axis_size(axis)
    place = lax.axis_index(axis)
    half = n // 2

    def add(left, right):
        return (left.astype(F32) + right.astype(F32)).astype(BF16)

    for s in range(half - 1):
        x = add(x, lax.ppermute(x, axis, [(s, s + 1), (n - 1 - s, n - 2 - s)]))
    x = add(x, lax.ppermute(x, axis, [(half - 1, half), (half, half - 1)]))
    for s in reversed(range(half - 1)):
        got = lax.ppermute(x, axis, [(s + 1, s), (n - 2 - s, n - 1 - s)])
        x = jnp.where((place == s) | (place == n - 1 - s), got, x)
    return x


def place_shards(meta, bufs, store):
    steps = (len(bufs) // 2 - 1) // 2
    grp, sub = meta[steps + 1], meta[steps + 2]
    half = bufs[1].shape[0]
    per_core = 1 + 2 * steps
    for core in range(2):
        core_id = sub if core == 0 else 1 - sub
        own = bufs[core * per_core]

        @pl.loop(0, 2 * half)
        def _(b, own=own, core_id=core_id):
            store(b, meta[0] * 2 + core_id, own[b])

        for k in range(steps):
            shard = meta[k + 1] * 2 + core_id
            for which in range(2):
                buf = bufs[core * per_core + 1 + 2 * k + which]
                first = (grp if which == 0 else 1 - grp) * half

                @pl.loop(0, half)
                def _(b, buf=buf, first=first, shard=shard):
                    store(first + b, shard, buf[b])


def front_kernel(meta, scale, x_ref, *refs):
    bufs, (out_ref, send_ref, weight) = refs[:-3], refs[-3:]
    rows = bufs[0].shape[1]
    block, units = weight.shape[1], weight.shape[2]
    groups = scale.shape[1]
    wide = units // groups

    def store(b, shard, codes):
        at = pl.ds(pl.multiple_of(shard * rows, ROW_TILE), rows)
        for g in range(groups):
            cols = slice(g * wide, (g + 1) * wide)
            weight[b, at, cols] = (codes[:, cols].astype(F32) * scale[b, g]).astype(BF16)

    place_shards(meta, bufs, store)
    total = jnp.dot(
        x_ref[...], weight[...].reshape(-1, units), preferred_element_type=F32
    )
    out_ref[...] = total
    send_ref[...] = total.astype(BF16)


def back_kernel(meta, scale, x_ref, *refs):
    bufs, (out_ref, send_ref, weight) = refs[:-3], refs[-3:]
    rows, block = bufs[0].shape[1], bufs[0].shape[2]
    per_group = weight.shape[0] // scale.shape[0]

    def store(b, shard, codes):
        first = pl.multiple_of(shard * rows, ROW_TILE)
        at = pl.ds(first, rows)
        factor = scale[first // per_group, b]
        weight[at, pl.ds(pl.multiple_of(b * block, block), block)] = (
            codes.astype(F32) * factor
        ).astype(BF16)

    place_shards(meta, bufs, store)
    total = contract_dims(x_ref[...], weight[...], 1, 1)
    out_ref[...] = total
    send_ref[...] = total.astype(BF16)


def weight_product(kernel, meta, scale, x, bufs, weight_shape, units, name):
    rows = x.shape[0]
    return pl.pallas_call(
        kernel,
        out_shape=(
            jax.ShapeDtypeStruct((rows, units), F32),
            jax.ShapeDtypeStruct((rows, units), BF16),
        ),
        in_specs=[pl.BlockSpec(memory_space=pltpu.SMEM)] * 2 + vmem_specs(1 + len(bufs)),
        out_specs=tuple(vmem_specs(2)),
        scratch_shapes=[pltpu.VMEM(weight_shape, BF16)],
        compiler_params=pltpu.CompilerParams(vmem_limit_bytes=VMEM_LIMIT),
        cost_estimate=pl.CostEstimate(
            flops=2 * rows * x.shape[1] * units,
            bytes_accessed=2 * x.size + 2 * x.shape[1] * units,
            transcendentals=0,
        ),
        name=name,
    )(meta, scale, x, *bufs)


def hidden_kernel(
    count, place, gate_ref, up_ref, low_up_ref, up_out_ref, down_in_ref, low_out_ref, grad_ref, *refs
):
    gate_more, up_more = refs[:count], refs[count : 2 * count]
    silu_ref, keep_ref, send_ref, down_in_grad_ref = refs[2 * count :]
    gate, up = gate_ref[...], up_ref[...]
    for ref in gate_more:
        gate = gate + ref[...].astype(F32)
    for ref in up_more:
        up = up + ref[...].astype(F32)
    up = up + ADAPTER_SCALE * jnp.dot(low_up_ref[...], up_out_ref[...], preferred_element_type=F32)
    silu = gate * jax.nn.sigmoid(gate)
    silu_ref[...] = silu
    hidden_wide = silu * up
    hidden = hidden_wide.astype(BF16)
    low_hidden = jnp.dot(hidden, down_in_ref[...], preferred_element_type=F32)
    low_hidden = (ADAPTER_SCALE * low_hidden.T).astype(BF16)
    sub, mp = place[0], place[1]
    half = grad_ref.shape[1] // 2
    for which, out_ref in ((sub, keep_ref), (1 - sub, send_ref)):
        cols = pl.ds(pl.multiple_of(which * half, half), half)
        out_ref[...] = jnp.dot(low_hidden, grad_ref[:, cols], preferred_element_type=F32).astype(BF16)
    own = down_in_grad_ref.shape[0]
    full = ADAPTER_SCALE * jnp.dot(
        hidden_wide.astype(BF16).astype(F32).T.astype(BF16), low_out_ref[...], preferred_element_type=F32
    )
    for i in range(full.shape[0] // own):

        @pl.when(mp == i)
        def _(i=i):
            down_in_grad_ref[...] = full[i * own : (i + 1) * own].astype(BF16)


def gradient_kernel(
    count, place, back_ref, silu_ref, low_out_ref, down_in_ref, up_out_ref, low_up_ref, x_t_ref, *refs
):
    back_more = refs[:count]
    keep_ref, send_ref, up_out_grad_ref = refs[count:]
    back = back_ref[...]
    for ref in back_more:
        back = back + ref[...].astype(F32)
    back = back + ADAPTER_SCALE * contract_dims(low_out_ref[...], down_in_ref[...], 1, 1)
    up_grad = (back * silu_ref[...]).astype(BF16)
    low = (ADAPTER_SCALE * contract_dims(up_grad, up_out_ref[...], 1, 1)).astype(BF16)
    sub, mp = place[0], place[1]
    half = x_t_ref.shape[0] // 2
    for which, out_ref in ((sub, keep_ref), (1 - sub, send_ref)):
        at = pl.ds(pl.multiple_of(which * half, half), half)
        out_ref[...] = jnp.dot(x_t_ref[at, :], low, preferred_element_type=F32).astype(BF16)
    own = up_out_grad_ref.shape[1]
    low_up_t = low_up_ref[...].astype(F32).T.astype(BF16)
    full = ADAPTER_SCALE * jnp.dot(low_up_t, up_grad, preferred_element_type=F32)
    for i in range(full.shape[1] // own):

        @pl.when(mp == i)
        def _(i=i):
            up_out_grad_ref[...] = full[:, i * own : (i + 1) * own].astype(BF16)


def small_call(kernel, name, place, args, out_shape):
    flops = 4 * 256 * 8192 * 128
    return pl.pallas_call(
        kernel,
        out_shape=out_shape,
        in_specs=[pl.BlockSpec(memory_space=pltpu.SMEM)] + vmem_specs(len(args)),
        out_specs=tuple(vmem_specs(len(out_shape))),
        compiler_params=pltpu.CompilerParams(vmem_limit_bytes=VMEM_LIMIT),
        cost_estimate=pl.CostEstimate(flops=flops, bytes_accessed=6 * 2**20, transcendentals=0),
        name=name,
    )(place, *args)


def token_weights(sequence_length_list, slot_sequence_index, rows):
    seq_count = sequence_length_list.shape[1]
    longest = rows // seq_count
    total = rows * lax.axis_size("dp") * lax.axis_size("sub")
    ratios = longest / sequence_length_list[0].astype(F32)
    match = slot_sequence_index[:, None] == jnp.arange(seq_count, dtype=jnp.int32)[None, :]
    weight = jnp.sum(jnp.where(match, ratios[None, :], F32(0.0)), axis=-1)
    return weight * F32(1.0 / math.sqrt(total))


def summed_halves(keep, send, axis, extra=None):
    mine = keep.astype(F32) + swap(send, "sub").astype(F32)
    mine = mine.astype(BF16)
    pieces = [line_sum(p, "dp") for p in jnp.split(mine, CHUNKS, axis=axis)]
    theirs = [swap(p, "sub") for p in pieces]
    first = lax.axis_index("sub") == 0
    low = [jnp.where(first, a, b) for a, b in zip(pieces, theirs)]
    high = [jnp.where(first, b, a) for a, b in zip(pieces, theirs)]
    return jnp.concatenate(low + high, axis=axis)


def fast_body(
    tokens,
    cotangent,
    rms_norm_gain,
    gate_codes,
    gate_block_scale,
    up_codes,
    up_block_scale,
    down_codes,
    down_block_scale,
    up_adapter_in,
    up_adapter_out,
    down_adapter_in,
    down_adapter_out,
    sequence_length_list,
    slot_sequence_index,
):
    rows, local_width = tokens.shape
    blocks, _, units = gate_codes.shape
    block = local_width // blocks
    total_width = local_width * lax.axis_size("mp")
    line = lax.axis_size("dp")
    sub, mp, grp, dp = (lax.axis_index(a) for a in ("sub", "mp", "grp", "dp"))

    order = ring_order(line)
    sources = [[order[(order.index(d) - k) % line] for k in range(line)] for d in range(line)]
    meta = jnp.concatenate(
        [jnp.array(sources, jnp.int32)[dp], jnp.stack([grp, sub]).astype(jnp.int32)]
    )
    place = jnp.stack([sub, mp]).astype(jnp.int32)

    gate_bufs = gather_chip(gate_codes)
    up_bufs = gather_chip(up_codes)
    down_bufs = gather_chip(jnp.swapaxes(down_codes, 0, 1))

    own_squares = jnp.sum(jnp.square(tokens.astype(F32)), axis=-1)
    squares = sum(others(own_squares, "mp"), own_squares) / total_width
    inv_rms = lax.rsqrt(squares + EPS)[:, None]
    normed = (tokens.astype(F32) * inv_rms * rms_norm_gain.astype(F32)[None, :]).astype(BF16)
    weight = token_weights(sequence_length_list, slot_sequence_index, rows)
    out_grad = (cotangent.astype(F32) * weight[:, None]).astype(BF16)
    low_up = jnp.dot(normed, up_adapter_in, preferred_element_type=F32)
    low_out = contract_dims(out_grad, down_adapter_out, 1, 1)
    low_up = sum(others(low_up, "mp"), low_up).astype(BF16)
    low_out = sum(others(low_out, "mp"), low_out).astype(BF16)
    up_out = lax.all_gather(up_adapter_out, "mp", axis=1, tiled=True)
    down_in = lax.all_gather(down_adapter_in, "mp", axis=0, tiled=True)
    normed_t = normed.T

    gate, gate_send = weight_product(
        front_kernel, meta, gate_block_scale.astype(F32), normed, gate_bufs,
        (blocks, block, units), units, "gate_product",
    )
    gate_more = others(gate_send, "mp")
    up, up_send = weight_product(
        front_kernel, meta, up_block_scale.astype(F32), normed, up_bufs,
        (blocks, block, units), units, "up_product",
    )
    up_more = others(up_send, "mp")
    count = len(up_more)

    own_units = up_adapter_out.shape[1]
    rank = up_adapter_out.shape[0]
    half = local_width // 2
    silu, down_keep, down_send, down_in_term = small_call(
        lambda *refs: hidden_kernel(count, *refs),
        "hidden_units",
        place,
        [gate, up, low_up, up_out, down_in, low_out, out_grad, *gate_more, *up_more],
        (
            jax.ShapeDtypeStruct((rows, units), F32),
            jax.ShapeDtypeStruct((rank, half), BF16),
            jax.ShapeDtypeStruct((rank, half), BF16),
            jax.ShapeDtypeStruct((own_units, rank), BF16),
        ),
    )
    down_out_gradient = summed_halves(down_keep, down_send, 1)

    back, back_send = weight_product(
        back_kernel, meta, down_block_scale.astype(F32), out_grad, down_bufs,
        (units, local_width), units, "hidden_gradient",
    )
    up_keep, up_send_grad, up_out_term = small_call(
        lambda *refs: gradient_kernel(count, *refs),
        "up_gradient",
        place,
        [back, silu, low_out, down_in, up_out, low_up, normed_t, *others(back_send, "mp")],
        (
            jax.ShapeDtypeStruct((half, rank), BF16),
            jax.ShapeDtypeStruct((half, rank), BF16),
            jax.ShapeDtypeStruct((rank, own_units), BF16),
        ),
    )
    up_in_gradient = summed_halves(up_keep, up_send_grad, 0)

    small = jnp.stack([up_out_term, down_in_term])
    small = (small.astype(F32) + swap(small, "sub").astype(F32)).astype(BF16)
    small = line_sum(small, "dp")
    return up_in_gradient, small[0], small[1], down_out_gradient


def general_body(
    tokens,
    cotangent,
    rms_norm_gain,
    gate_codes,
    gate_block_scale,
    up_codes,
    up_block_scale,
    down_codes,
    down_block_scale,
    up_adapter_in,
    up_adapter_out,
    down_adapter_in,
    down_adapter_out,
    sequence_length_list,
    slot_sequence_index,
):
    rows = tokens.shape[0]
    local_width = tokens.shape[1]
    block = gate_block_scale.shape[0] and local_width // gate_codes.shape[0]
    blocks_here = gate_codes.shape[0]
    total_width = local_width * lax.axis_size("mp")
    own_squares = jnp.sum(jnp.square(tokens.astype(jnp.float32)), axis=-1, keepdims=True)
    squares = lax.psum(own_squares, "mp") / total_width
    inv_rms = lax.rsqrt(squares + EPS)
    local_normed_input = (
        tokens.astype(jnp.float32) * inv_rms * rms_norm_gain.astype(jnp.float32)[None, :]
    ).astype(jnp.bfloat16)
    seq_count = sequence_length_list.shape[1]
    longest = rows // seq_count
    total = rows * lax.axis_size("dp") * lax.axis_size("sub")
    ratios = longest / sequence_length_list[0].astype(jnp.float32)
    match = slot_sequence_index[:, None] == jnp.arange(seq_count, dtype=jnp.int32)[None, :]
    token_weight = jnp.sum(jnp.where(match, ratios[None, :], jnp.float32(0.0)), axis=-1)
    token_weight = token_weight * jnp.float32(1.0 / math.sqrt(total))
    local_output = (cotangent.astype(jnp.float32) * token_weight[:, None]).astype(jnp.bfloat16)
    partial_up = jnp.dot(local_normed_input, up_adapter_in, preferred_element_type=jnp.float32)
    partial_output = contract_dims(local_output, down_adapter_out, 1, 1)
    up_adapter_rank, output_adapter_rank = lax.psum((partial_up, partial_output), "mp")
    up_adapter_rank = up_adapter_rank.astype(jnp.bfloat16)
    output_adapter_rank = output_adapter_rank.astype(jnp.bfloat16)
    normed_blocks = local_normed_input.reshape(rows, blocks_here, block)
    out_blocks = local_output.reshape(rows, blocks_here, block)
    wide_gate = jnp.repeat(gate_block_scale.astype(jnp.float32), block, axis=1)[:, None, :]
    wide_up = jnp.repeat(up_block_scale.astype(jnp.float32), block, axis=1)[:, None, :]
    wide_down = jnp.repeat(down_block_scale.astype(jnp.float32), block, axis=0)
    dims_front = (((1, 2), (0, 1)), ((), ()))
    dims_back = (((1, 2), (1, 2)), ((), ()))
    quant_g = lax.all_gather(gate_codes, ("dp", "sub"), axis=1, tiled=True)
    quant_u = lax.all_gather(up_codes, ("dp", "sub"), axis=1, tiled=True)
    weight_g = (quant_g.astype(jnp.float32) * wide_gate).astype(jnp.bfloat16)
    weight_u = (quant_u.astype(jnp.float32) * wide_up).astype(jnp.bfloat16)
    gate_next = lax.dot_general(
        normed_blocks, weight_g, dims_front, preferred_element_type=jnp.float32
    )
    up_next = lax.dot_general(
        normed_blocks, weight_u, dims_front, preferred_element_type=jnp.float32
    )
    gate, base_up_projected = (
        lax.psum_scatter(gate_next, "mp", scatter_dimension=1, tiled=True),
        lax.psum_scatter(up_next, "mp", scatter_dimension=1, tiled=True),
    )
    up_projected = base_up_projected + ADAPTER_SCALE * jnp.dot(
        up_adapter_rank, up_adapter_out, preferred_element_type=jnp.float32
    )
    silu_gate = jax.nn.silu(gate)
    hidden_units = (silu_gate * up_projected).astype(jnp.bfloat16)
    partial_hidden = jnp.dot(hidden_units, down_adapter_in, preferred_element_type=jnp.float32)
    hidden_adapter_rank = lax.psum(partial_hidden, "mp").astype(jnp.bfloat16)
    weight_d = (
        lax.all_gather(down_codes, ("dp", "sub"), axis=0, tiled=True).astype(jnp.float32)
        * wide_down[:, :, None]
    ).astype(jnp.bfloat16)
    back_part = lax.dot_general(out_blocks, weight_d, dims_back, preferred_element_type=jnp.float32)
    base_backward = lax.psum_scatter(back_part, "mp", scatter_dimension=1, tiled=True)
    hidden_gradient = base_backward + ADAPTER_SCALE * contract_dims(
        output_adapter_rank, down_adapter_in, 1, 1
    )
    up_gradient = (hidden_gradient * silu_gate).astype(jnp.bfloat16)
    partial_gradient = contract_dims(up_gradient, up_adapter_out, 1, 1)
    up_adapter_rank_gradient = lax.psum(partial_gradient, "mp").astype(jnp.bfloat16)
    up_in_term = ADAPTER_SCALE * contract_dims(local_normed_input, up_adapter_rank_gradient, 0, 0)
    up_out_term = ADAPTER_SCALE * contract_dims(up_adapter_rank, up_gradient, 0, 0)
    down_in_term = ADAPTER_SCALE * contract_dims(hidden_units, output_adapter_rank, 0, 0)
    down_out_term = ADAPTER_SCALE * contract_dims(hidden_adapter_rank, local_output, 0, 0)
    sum_up_a, sum_up_b, sum_down_a, sum_down_b = lax.psum(
        (up_in_term, up_out_term, down_in_term, down_out_term), ("dp", "sub")
    )
    return (
        sum_up_a.astype(jnp.bfloat16),
        sum_up_b.astype(jnp.bfloat16),
        sum_down_a.astype(jnp.bfloat16),
        sum_down_b.astype(jnp.bfloat16),
    )


def body(tokens, cotangent, rms_norm_gain, gate_codes, *rest):
    whole_tiles = gate_codes.shape[1] % ROW_TILE == 0
    form = fast_body if whole_tiles else general_body
    return form(tokens, cotangent, rms_norm_gain, gate_codes, *rest)


def solution(mesh):
    placed = (
        P(("grp", "dp", "sub"), "mp"),
        P(("grp", "dp", "sub"), "mp"),
        P("mp"),
        P("mp", ("dp", "sub"), None),
        P("mp", None),
        P("mp", ("dp", "sub"), None),
        P("mp", None),
        P(("dp", "sub"), "mp", None),
        P(None, "mp"),
        P(("grp", "mp"), None),
        P("grp", "mp"),
        P(("grp", "mp"), None),
        P("grp", "mp"),
        P(("grp", "dp", "sub"), None),
        P(("grp", "dp", "sub")),
    )
    return jax.shard_map(
        body,
        mesh=mesh,
        in_specs=placed,
        out_specs=(P(("grp", "mp"), None), P("grp", "mp"), P(("grp", "mp"), None), P("grp", "mp")),
        check_vma=False,
    )
```

```python
import math

import jax
import jax.numpy as jnp
from jax import lax
from jax.experimental import pallas as pl
from jax.experimental.pallas import tpu as pltpu
from jax.sharding import PartitionSpec as P

ADAPTER_SCALE = 2.0
EPS = 1e-05
ROW_TILE = 16
LANES = 128
MIB = 1024 * 1024

F32 = jnp.float32
BF16 = jnp.bfloat16


def contract_dims(left, right, left_dim, right_dim):
    return lax.dot_general(
        left, right, (((left_dim,), (right_dim,)), ((), ())), preferred_element_type=F32
    )


def dot(left, right):
    return jnp.dot(left, right, preferred_element_type=F32)


def ring_at(pos, n):
    if isinstance(pos, int):
        return 0 if pos == 0 else (2 * pos - 1 if 2 * pos <= n else 2 * (n - pos))
    return jnp.where(pos == 0, 0, jnp.where(2 * pos <= n, 2 * pos - 1, 2 * (n - pos)))


def ring_position():
    n = lax.axis_size("dp")
    place = lax.axis_index("dp")
    odd = lax.rem(place, 2) == 1
    return jnp.where(place == 0, 0, jnp.where(odd, (place + 1) // 2, n - place // 2))


def ring_step(x):
    n = lax.axis_size("dp")
    return lax.ppermute(x, "dp", [(ring_at(i, n), ring_at((i + 1) % n, n)) for i in range(n)])


def swap(x, axis):
    return lax.ppermute(x, axis, [(0, 1), (1, 0)])


def others(x, axis):
    n = lax.axis_size(axis)
    return [lax.ppermute(x, axis, [(i, (i + k) % n) for i in range(n)]) for k in range(1, n)]


def after(x, *done):
    return lax.optimization_barrier((x, *done))[0]


def add(*terms):
    return sum(t.astype(F32) for t in terms).astype(BF16)


def ring_sum(parts):
    total = parts[0]
    for part in parts[1:]:
        total = add(ring_step(total), part)
    return total


def ring_gather(block):
    blocks = [block]
    for _ in range(lax.axis_size("dp") - 1):
        blocks.append(ring_step(blocks[-1]))
    return blocks, [swap(b, "sub") for b in blocks]


def call(kernel, name, args, out_shape, scratch=(), specs=None, limit=24, flops=0, out_specs=None):
    vmem = pl.BlockSpec(memory_space=pltpu.VMEM)
    moved = sum(a.size * a.dtype.itemsize for a in args) + sum(
        math.prod(s.shape) * s.dtype.itemsize for s in out_shape
    )
    return pl.pallas_call(
        kernel,
        out_shape=tuple(out_shape),
        in_specs=specs or [vmem] * len(args),
        out_specs=out_specs or tuple([vmem] * len(out_shape)),
        scratch_shapes=list(scratch),
        compiler_params=pltpu.CompilerParams(vmem_limit_bytes=limit * MIB),
        cost_estimate=pl.CostEstimate(flops=flops, bytes_accessed=moved, transcendentals=0),
        name=name,
    )(*args)


def shape(dims, dtype=BF16):
    return jax.ShapeDtypeStruct(tuple(dims), dtype)


def halves_call(kernel, name, place, wide, narrow, adapter, adapter_rows):
    rows, width = wide.shape
    step = width // 8
    per = width // 2 // step
    rank = adapter.shape[1] if adapter_rows else adapter.shape[0]

    def at(j, place):
        return jnp.where(j < per, (1 - place[0]) * per + j, place[0] * per + j - per)

    adapter_spec = (
        pl.BlockSpec((step, rank), lambda j, place: (at(j, place), 0))
        if adapter_rows
        else pl.BlockSpec((rank, step), lambda j, place: (0, at(j, place)))
    )
    narrow_specs = [
        pl.BlockSpec((rows, 1), lambda j, place: (0, 0))
        if n.shape[0] == rows
        else pl.BlockSpec((1, step), lambda j, place: (0, at(j, place)))
        for n in narrow
    ]
    return pl.pallas_call(
        kernel,
        out_shape=(shape((rows, width // 2)), shape((rows, width // 2)), shape((rows, rank), F32)),
        grid_spec=pltpu.PrefetchScalarGridSpec(
            num_scalar_prefetch=1,
            grid=(2 * per,),
            in_specs=[pl.BlockSpec((rows, step), lambda j, place: (0, at(j, place)))]
            + narrow_specs
            + [adapter_spec],
            out_specs=(
                pl.BlockSpec((rows, step), lambda j, place: (0, jnp.minimum(j, per - 1))),
                pl.BlockSpec((rows, step), lambda j, place: (0, jnp.maximum(j - per, 0))),
                pl.BlockSpec((rows, rank), lambda j, place: (0, 0)),
            ),
        ),
        compiler_params=pltpu.CompilerParams(vmem_limit_bytes=16 * MIB),
        cost_estimate=pl.CostEstimate(
            flops=2 * rows * width * rank, bytes_accessed=4 * wide.size, transcendentals=0
        ),
        name=name,
    )(place, wide, *narrow, adapter)


def store_half(value, send_ref, own_ref):
    j = pl.program_id(0)
    first = j < pl.num_programs(0) // 2

    @pl.when(first)
    def _():
        send_ref[...] = value

    @pl.when(jnp.logical_not(first))
    def _():
        own_ref[...] = value


def accumulate(ref, term):
    j = pl.program_id(0)

    @pl.when(j == 0)
    def _():
        ref[...] = term

    @pl.when(j > 0)
    def _():
        ref[...] += term


def token_kernel(place, tokens, inv_rms, gain, adapter, send_ref, own_ref, low_ref):
    value = tokens[...].astype(F32) * inv_rms[...] * gain[...].astype(F32)
    value = value.astype(BF16)
    store_half(value, send_ref, own_ref)
    accumulate(low_ref, dot(value, adapter[...]))


def cotangent_kernel(place, cotangent, weight, adapter, send_ref, own_ref, low_ref):
    value = (cotangent[...].astype(F32) * weight[...]).astype(BF16)
    store_half(value, send_ref, own_ref)
    accumulate(low_ref, contract_dims(value, adapter[...], 1, 1))


def transpose_kernel(own, got, out_ref):
    rows, step = own.shape[0], out_ref.shape[0]
    for i, ref in enumerate((own, got)):
        out_ref[:, i * rows : (i + 1) * rows] = ref[...].astype(F32).T.astype(BF16)


def widen(scale, wide):
    table = scale[...].astype(F32)
    for g in range(scale.shape[1]):
        wide[g] = jnp.broadcast_to(table[:, g : g + 1], wide.shape[1:])


def place_shards(codes, got, moved, store):
    n = lax.axis_size("dp")
    sub, grp, place = (lax.axis_index(a) for a in ("sub", "grp", "dp"))
    pos = ring_position()
    blocks = got.shape[0]
    quarter = blocks // 2

    @pl.loop(0, blocks, unroll=4)
    def _(b):
        store(b, place * 2 + sub, codes[sub * blocks + b])
        store(b, place * 2 + 1 - sub, got[b])

    for k in range(n - 1):
        there = ring_at(lax.rem(pos - k - 1 + n, n), n)
        for which in range(2):
            piece = moved[2 * k + which]
            start = (grp if which == 0 else 1 - grp) * quarter

            @pl.loop(0, quarter, unroll=4)
            def _(b, piece=piece, start=start, there=there):
                store(start + b, there * 2 + sub, piece[b])
                store(start + b, there * 2 + 1 - sub, piece[quarter + b])


def front_kernel(own, got, scale, codes, codes_got, *refs):
    moved, (mine_ref, theirs_ref, wide, weight) = refs[:-4], refs[-4:]
    blocks, rows, units = codes_got.shape
    first = lax.axis_index("sub") * blocks
    widen(scale, wide)

    def store(b, shard, piece):
        at = pl.ds(pl.multiple_of(shard * rows, ROW_TILE), rows)
        for g in range(units // LANES):
            cols = slice(g * LANES, (g + 1) * LANES)
            factor = wide[g * wide.shape[0] * LANES // units, pl.ds(first + b, 1), :]
            weight[b, at, cols] = (piece[:, cols].astype(F32) * factor).astype(BF16)

    place_shards(codes, codes_got, moved, store)
    matrix = weight[...].reshape(-1, units)
    mine_ref[...] = dot(own[...], matrix)
    theirs_ref[...] = dot(got[...], matrix).astype(BF16)


def back_kernel(own, got, scale, codes, codes_got, *refs):
    moved, (mine_ref, theirs_ref, wide, weight) = refs[:-4], refs[-4:]
    blocks, rows, block = codes_got.shape
    first = lax.axis_index("sub") * blocks
    per_group = weight.shape[0] // wide.shape[0]
    widen(scale, wide)

    def store(b, shard, piece):
        at = pl.multiple_of(shard * rows, ROW_TILE)
        factor = wide[at // per_group, pl.ds(first + b, 1), :]
        cols = pl.ds(pl.multiple_of(b * block, block), block)
        weight[pl.ds(at, rows), cols] = (piece.astype(F32) * factor).astype(BF16)

    place_shards(codes, codes_got, moved, store)
    matrix = weight[...]
    mine_ref[...] = contract_dims(own[...], matrix, 1, 1)
    theirs_ref[...] = contract_dims(got[...], matrix, 1, 1).astype(BF16)


def place_own(scratch, own, more, axis):
    n = len(more) + 1
    size = own.shape[axis]
    for k, ref in enumerate((own, *more)):
        at = pl.ds(pl.multiple_of(lax.rem(lax.axis_index("mp") + n - k, n) * size, size), size)
        if axis == 0:
            scratch[at, :] = ref[...]
        else:
            scratch[:, at] = ref[...]


def own_units(full, ref, axis):
    size = ref.shape[axis]
    for i in range(full.shape[axis] // size):

        @pl.when(lax.axis_index("mp") == i)
        def _(i=i):
            ref[...] = lax.slice_in_dim(full, i * size, (i + 1) * size, axis=axis).astype(BF16)


def hidden_kernel(more, gate, up, low_up, low_out, up_out, down_in, *refs):
    gate_more, up_more = refs[:more], refs[more : 2 * more]
    up_out_more, down_in_more = refs[2 * more : 3 * more], refs[3 * more : 4 * more]
    silu_ref, low_ref, down_in_term, up_out_all, down_in_all = refs[4 * more :]
    place_own(up_out_all, up_out, up_out_more, 1)
    place_own(down_in_all, down_in, down_in_more, 0)
    gate_sum, up_sum = gate[...], up[...]
    for ref in gate_more:
        gate_sum = gate_sum + ref[...].astype(F32)
    for ref in up_more:
        up_sum = up_sum + ref[...].astype(F32)
    up_sum = up_sum + ADAPTER_SCALE * dot(low_up[...], up_out_all[...])
    silu = gate_sum * jax.nn.sigmoid(gate_sum)
    silu_ref[...] = silu
    hidden = (silu * up_sum).astype(BF16)
    low_ref[...] = (ADAPTER_SCALE * dot(hidden, down_in_all[...])).astype(BF16)
    hidden_t = hidden.astype(F32).T.astype(BF16)
    own_units(ADAPTER_SCALE * dot(hidden_t, low_out[...]), down_in_term, 0)


def up_grad_kernel(more, back, silu, low_up, low_out, up_out, down_in, *refs):
    back_more, up_out_more, down_in_more = (refs[i * more : (i + 1) * more] for i in range(3))
    low_ref, up_out_term, up_out_all, down_in_all = refs[3 * more :]
    place_own(up_out_all, up_out, up_out_more, 1)
    place_own(down_in_all, down_in, down_in_more, 0)
    total = back[...]
    for ref in back_more:
        total = total + ref[...].astype(F32)
    total = total + ADAPTER_SCALE * contract_dims(low_out[...], down_in_all[...], 1, 1)
    up_grad = (total * silu[...]).astype(BF16)
    low_ref[...] = (ADAPTER_SCALE * contract_dims(up_grad, up_out_all[...], 1, 1)).astype(BF16)
    low_up_t = low_up[...].astype(F32).T.astype(BF16)
    own_units(ADAPTER_SCALE * dot(low_up_t, up_grad), up_out_term, 1)


def down_out_kernel(low, low_got, grad, grad_got, *out_refs):
    n = len(out_refs)
    pos = ring_position()
    low_t = jnp.concatenate([low[...], low_got[...]], axis=0).astype(F32).T.astype(BF16)
    rows = low.shape[0]
    for k, ref in enumerate(out_refs):
        size = ref.shape[1]
        at = pl.ds(pl.multiple_of(lax.rem(pos - 1 - k + 2 * n, n) * size, size), size)
        ref[...] = (
            dot(low_t[:, :rows], grad[:, at]) + dot(low_t[:, rows:], grad_got[:, at])
        ).astype(BF16)


def up_in_kernel(low, low_got, normed_t, up_out_term, down_in_term, *out_refs):
    n = len(out_refs)
    pos = ring_position()
    size = normed_t.shape[0] // n
    extra = out_refs[0].shape[0] - size
    both = jnp.concatenate([low[...], low_got[...]], axis=0)
    for k, ref in enumerate(out_refs):
        block = lax.rem(pos - 1 - k + 2 * n, n)
        at = pl.ds(pl.multiple_of(block * size, size), size)
        ref[pl.ds(0, size), :] = dot(normed_t[at, :], both).astype(BF16)
        per = up_out_term.shape[0] // extra
        index = pl.ds(pl.multiple_of(lax.rem(block, per) * extra, extra), extra)

        @pl.when(block < per)
        def _(ref=ref, index=index):
            ref[pl.ds(size, extra), :] = up_out_term[index, :]

        @pl.when(block >= per)
        def _(ref=ref, index=index):
            ref[pl.ds(size, extra), :] = down_in_term[index, :]


def copy_all(copies):
    for c in copies:
        c.start()
    for c in copies:
        c.wait()


def down_out_place_kernel(n, *refs):
    pieces, out_ref, sems = refs[: 2 * n], refs[2 * n], refs[2 * n + 1]
    pos, sub = ring_position(), lax.axis_index("sub")
    copies = []
    for i, piece in enumerate(pieces):
        half = sub if i < n else 1 - sub
        block = lax.rem(pos - i % n + n, n)
        size = piece.shape[1]
        at = pl.ds(pl.multiple_of((half * n + block) * size, size), size)
        copies.append(pltpu.make_async_copy(piece, out_ref.at[:, at], sems.at[i]))
    copy_all(copies)


def up_in_place_kernel(n, *refs):
    pieces = refs[: 2 * n]
    out_ref, up_out_ref, down_in_ref, small, sems = refs[2 * n :]
    pos, sub = ring_position(), lax.axis_index("sub")
    size = out_ref.shape[0] // (2 * n)
    extra = pieces[0].shape[0] - size
    copies = []
    for i, piece in enumerate(pieces):
        half = sub if i < n else 1 - sub
        block = lax.rem(pos - i % n + n, n)
        at = pl.ds(pl.multiple_of((half * n + block) * size, size), size)
        copies.append(
            pltpu.make_async_copy(piece.at[pl.ds(0, size), :], out_ref.at[at, :], sems.at[2 * i])
        )
        at = pl.ds(pl.multiple_of(block * extra, extra), extra)
        copies.append(
            pltpu.make_async_copy(
                piece.at[pl.ds(size, extra), :], small.at[i // n, at, :], sems.at[2 * i + 1]
            )
        )
    copy_all(copies)
    total = (small[0].astype(F32) + small[1].astype(F32)).astype(BF16)
    rows = up_out_ref.shape[0]
    up_out_ref[...] = total[:rows]
    down_in_ref[...] = total[rows:]


def token_weights(sequence_length_list, slot_sequence_index, rows):
    seq_count = sequence_length_list.shape[1]
    longest = rows // seq_count
    total = rows * lax.axis_size("dp") * lax.axis_size("sub")
    ratios = longest / sequence_length_list[0].astype(F32)
    match = slot_sequence_index[:, None] == jnp.arange(seq_count, dtype=jnp.int32)[None, :]
    weight = jnp.sum(jnp.where(match, ratios[None, :], F32(0.0)), axis=-1)
    return weight * F32(1.0 / math.sqrt(total))


class Shards:
    def __init__(self, codes):
        sub, grp = lax.axis_index("sub"), lax.axis_index("grp")
        half = codes.shape[0] // 2
        quarter = half // 2
        self.codes = codes
        self.got = swap(lax.dynamic_slice_in_dim(codes, (1 - sub) * half, half, 0), "sub")
        own = lax.dynamic_slice_in_dim(codes, sub * half + grp * quarter, quarter, 0)
        got = lax.dynamic_slice_in_dim(self.got, grp * quarter, quarter, 0)
        self.moving = jnp.concatenate([own, got], axis=0)
        self.moved = []

    def step(self, *done):
        self.moving = ring_step(after(self.moving, *done) if done else self.moving)
        self.moved += [self.moving, swap(self.moving, "grp")]
        return self.moving

    def args(self):
        return [self.codes, self.got, *self.moved]


def fast_body(
    tokens,
    cotangent,
    rms_norm_gain,
    gate_codes,
    gate_block_scale,
    up_codes,
    up_block_scale,
    down_codes,
    down_block_scale,
    up_adapter_in,
    up_adapter_out,
    down_adapter_in,
    down_adapter_out,
    sequence_length_list,
    slot_sequence_index,
):
    rows, local_width = tokens.shape
    blocks, _, units = gate_codes.shape
    block = local_width // blocks
    half = local_width // 2
    rank = up_adapter_in.shape[1]
    total_width = local_width * lax.axis_size("mp")
    n = lax.axis_size("dp")
    more = lax.axis_size("mp") - 1
    place = lax.axis_index("sub").astype(jnp.int32).reshape(1)

    gate_shards = Shards(gate_codes)
    up_shards = Shards(up_codes)
    down_shards = Shards(jnp.swapaxes(down_codes, 0, 1))
    order = [gate_shards, up_shards] * 2 + [down_shards, gate_shards, up_shards]
    if n != 4:
        order = [gate_shards, up_shards] * (n - 1)
    order += [down_shards] * (n - 1 - order.count(down_shards))
    arrived = []
    for shards in order:
        arrived.append(shards.step(*arrived[-2:-1]))

    weight = token_weights(sequence_length_list, slot_sequence_index, rows)
    grad_send, grad, low_out = halves_call(
        cotangent_kernel, "cotangent", place, cotangent, [weight[:, None]], down_adapter_out, False
    )
    grad_got = swap(grad_send, "sub")
    own_squares = jnp.sum(jnp.square(tokens.astype(F32)), axis=-1)
    squares = sum(others(own_squares, "mp"), own_squares) / total_width
    inv_rms = lax.rsqrt(squares + EPS)[:, None]
    normed_send, normed, low_up = halves_call(
        token_kernel, "tokens", place, tokens, [inv_rms, rms_norm_gain[None, :]], up_adapter_in, True
    )
    normed_got = swap(normed_send, "sub")
    low_up = sum(others(low_up, "mp"), low_up).astype(BF16)
    low_out = sum(others(low_out, "mp"), low_out).astype(BF16)
    up_out_more = others(up_adapter_out, "mp")
    down_in_more = others(down_adapter_in, "mp")
    (normed_t,) = call(
        transpose_kernel, "transpose", [normed, normed_got], [shape((half, 2 * rows))], limit=32
    )

    def product(kernel, name, own, got, scale, shards, weight_shape):
        groups = scale.shape[1]
        mine, theirs = call(
            kernel,
            name,
            [own, got, scale, *shards.args()],
            [shape((rows, units), F32), shape((rows, units))],
            scratch=[pltpu.VMEM((groups, blocks, LANES), F32), pltpu.VMEM(weight_shape, BF16)],
            flops=4 * rows * half * units,
        )
        mine = mine + swap(theirs, "sub").astype(F32)
        return mine, others(mine.astype(BF16), "mp")

    front = (blocks // 2, block, units)
    gate, gate_more = product(
        front_kernel, "gate", normed, normed_got, gate_block_scale, gate_shards, front
    )
    up, up_more = product(front_kernel, "up", normed, normed_got, up_block_scale, up_shards, front)
    small_scratch = [
        pltpu.VMEM((rank, units), BF16),
        pltpu.VMEM((units, rank), BF16),
    ]
    adapters = [low_up, low_out, up_adapter_out, down_adapter_in]
    silu, low_hidden, down_in_term = call(
        lambda *refs: hidden_kernel(more, *refs),
        "hidden",
        [gate, up, *adapters, *gate_more, *up_more, *up_out_more, *down_in_more],
        [shape((rows, units), F32), shape((rows, rank)), shape(down_adapter_in.shape)],
        scratch=small_scratch,
        limit=8,
    )
    down_out_parts = call(
        down_out_kernel,
        "down_out",
        [low_hidden, swap(low_hidden, "sub"), grad, grad_got],
        [shape((rank, half // n))] * n,
        flops=4 * rows * half * rank,
    )
    down_out_blocks = ring_gather(ring_sum(down_out_parts))

    back, back_more = product(
        back_kernel, "back", grad, grad_got, down_block_scale.T, down_shards, (units, half)
    )
    low_grad, up_out_term = call(
        lambda *refs: up_grad_kernel(more, *refs),
        "up_grad",
        [back, silu, *adapters, *back_more, *up_out_more, *down_in_more],
        [shape((rows, rank)), shape(up_adapter_out.shape)],
        scratch=small_scratch,
        limit=8,
    )
    extra = 2 * rank // n
    up_in_parts = call(
        up_in_kernel,
        "up_in",
        [low_grad, swap(low_grad, "sub"), normed_t, up_out_term, down_in_term],
        [shape((half // n + extra, rank))] * n,
        flops=4 * rows * half * rank,
    )
    up_in_blocks = ring_gather(ring_sum(up_in_parts))

    anywhere = pl.BlockSpec(memory_space=pl.ANY)
    vmem = pl.BlockSpec(memory_space=pltpu.VMEM)
    (down_out_gradient,) = call(
        lambda *refs: down_out_place_kernel(n, *refs),
        "down_out_place",
        [*down_out_blocks[0], *down_out_blocks[1]],
        [shape((rank, local_width))],
        scratch=[pltpu.SemaphoreType.DMA((2 * n,))],
        specs=[anywhere] * (2 * n),
        out_specs=(anywhere,),
        limit=4,
    )
    up_in_gradient, up_out_gradient, down_in_gradient = call(
        lambda *refs: up_in_place_kernel(n, *refs),
        "up_in_place",
        [*up_in_blocks[0], *up_in_blocks[1]],
        [shape((local_width, rank)), shape(up_adapter_out.shape), shape(down_adapter_in.shape)],
        scratch=[pltpu.VMEM((2, 2 * rank, rank), BF16), pltpu.SemaphoreType.DMA((4 * n,))],
        specs=[anywhere] * (2 * n),
        out_specs=(anywhere, vmem, vmem),
        limit=4,
    )
    return up_in_gradient, up_out_gradient, down_in_gradient, down_out_gradient


def general_body(
    tokens,
    cotangent,
    rms_norm_gain,
    gate_codes,
    gate_block_scale,
    up_codes,
    up_block_scale,
    down_codes,
    down_block_scale,
    up_adapter_in,
    up_adapter_out,
    down_adapter_in,
    down_adapter_out,
    sequence_length_list,
    slot_sequence_index,
):
    rows = tokens.shape[0]
    local_width = tokens.shape[1]
    block = gate_block_scale.shape[0] and local_width // gate_codes.shape[0]
    blocks_here = gate_codes.shape[0]
    total_width = local_width * lax.axis_size("mp")
    own_squares = jnp.sum(jnp.square(tokens.astype(jnp.float32)), axis=-1, keepdims=True)
    squares = lax.psum(own_squares, "mp") / total_width
    inv_rms = lax.rsqrt(squares + EPS)
    local_normed_input = (
        tokens.astype(jnp.float32) * inv_rms * rms_norm_gain.astype(jnp.float32)[None, :]
    ).astype(jnp.bfloat16)
    seq_count = sequence_length_list.shape[1]
    longest = rows // seq_count
    total = rows * lax.axis_size("dp") * lax.axis_size("sub")
    ratios = longest / sequence_length_list[0].astype(jnp.float32)
    match = slot_sequence_index[:, None] == jnp.arange(seq_count, dtype=jnp.int32)[None, :]
    token_weight = jnp.sum(jnp.where(match, ratios[None, :], jnp.float32(0.0)), axis=-1)
    token_weight = token_weight * jnp.float32(1.0 / math.sqrt(total))
    local_output = (cotangent.astype(jnp.float32) * token_weight[:, None]).astype(jnp.bfloat16)
    partial_up = jnp.dot(local_normed_input, up_adapter_in, preferred_element_type=jnp.float32)
    partial_output = contract_dims(local_output, down_adapter_out, 1, 1)
    up_adapter_rank, output_adapter_rank = lax.psum((partial_up, partial_output), "mp")
    up_adapter_rank = up_adapter_rank.astype(jnp.bfloat16)
    output_adapter_rank = output_adapter_rank.astype(jnp.bfloat16)
    normed_blocks = local_normed_input.reshape(rows, blocks_here, block)
    out_blocks = local_output.reshape(rows, blocks_here, block)
    wide_gate = jnp.repeat(gate_block_scale.astype(jnp.float32), block, axis=1)[:, None, :]
    wide_up = jnp.repeat(up_block_scale.astype(jnp.float32), block, axis=1)[:, None, :]
    wide_down = jnp.repeat(down_block_scale.astype(jnp.float32), block, axis=0)
    dims_front = (((1, 2), (0, 1)), ((), ()))
    dims_back = (((1, 2), (1, 2)), ((), ()))
    quant_g = lax.all_gather(gate_codes, ("dp", "sub"), axis=1, tiled=True)
    quant_u = lax.all_gather(up_codes, ("dp", "sub"), axis=1, tiled=True)
    weight_g = (quant_g.astype(jnp.float32) * wide_gate).astype(jnp.bfloat16)
    weight_u = (quant_u.astype(jnp.float32) * wide_up).astype(jnp.bfloat16)
    gate_next = lax.dot_general(
        normed_blocks, weight_g, dims_front, preferred_element_type=jnp.float32
    )
    up_next = lax.dot_general(
        normed_blocks, weight_u, dims_front, preferred_element_type=jnp.float32
    )
    gate, base_up_projected = (
        lax.psum_scatter(gate_next, "mp", scatter_dimension=1, tiled=True),
        lax.psum_scatter(up_next, "mp", scatter_dimension=1, tiled=True),
    )
    up_projected = base_up_projected + ADAPTER_SCALE * jnp.dot(
        up_adapter_rank, up_adapter_out, preferred_element_type=jnp.float32
    )
    silu_gate = jax.nn.silu(gate)
    hidden_units = (silu_gate * up_projected).astype(jnp.bfloat16)
    partial_hidden = jnp.dot(hidden_units, down_adapter_in, preferred_element_type=jnp.float32)
    hidden_adapter_rank = lax.psum(partial_hidden, "mp").astype(jnp.bfloat16)
    weight_d = (
        lax.all_gather(down_codes, ("dp", "sub"), axis=0, tiled=True).astype(jnp.float32)
        * wide_down[:, :, None]
    ).astype(jnp.bfloat16)
    back_part = lax.dot_general(out_blocks, weight_d, dims_back, preferred_element_type=jnp.float32)
    base_backward = lax.psum_scatter(back_part, "mp", scatter_dimension=1, tiled=True)
    hidden_gradient = base_backward + ADAPTER_SCALE * contract_dims(
        output_adapter_rank, down_adapter_in, 1, 1
    )
    up_gradient = (hidden_gradient * silu_gate).astype(jnp.bfloat16)
    partial_gradient = contract_dims(up_gradient, up_adapter_out, 1, 1)
    up_adapter_rank_gradient = lax.psum(partial_gradient, "mp").astype(jnp.bfloat16)
    up_in_term = ADAPTER_SCALE * contract_dims(local_normed_input, up_adapter_rank_gradient, 0, 0)
    up_out_term = ADAPTER_SCALE * contract_dims(up_adapter_rank, up_gradient, 0, 0)
    down_in_term = ADAPTER_SCALE * contract_dims(hidden_units, output_adapter_rank, 0, 0)
    down_out_term = ADAPTER_SCALE * contract_dims(hidden_adapter_rank, local_output, 0, 0)
    sum_up_a, sum_up_b, sum_down_a, sum_down_b = lax.psum(
        (up_in_term, up_out_term, down_in_term, down_out_term), ("dp", "sub")
    )
    return (
        sum_up_a.astype(jnp.bfloat16),
        sum_up_b.astype(jnp.bfloat16),
        sum_down_a.astype(jnp.bfloat16),
        sum_down_b.astype(jnp.bfloat16),
    )


def body(tokens, cotangent, rms_norm_gain, gate_codes, *rest):
    whole_tiles = gate_codes.shape[1] % ROW_TILE == 0
    form = fast_body if whole_tiles else general_body
    return form(tokens, cotangent, rms_norm_gain, gate_codes, *rest)


def solution(mesh):
    placed = (
        P(("grp", "dp", "sub"), "mp"),
        P(("grp", "dp", "sub"), "mp"),
        P("mp"),
        P("mp", ("dp", "sub"), None),
        P("mp", None),
        P("mp", ("dp", "sub"), None),
        P("mp", None),
        P(("dp", "sub"), "mp", None),
        P(None, "mp"),
        P(("grp", "mp"), None),
        P("grp", "mp"),
        P(("grp", "mp"), None),
        P("grp", "mp"),
        P(("grp", "dp", "sub"), None),
        P(("grp", "dp", "sub")),
    )
    return jax.shard_map(
        body,
        mesh=mesh,
        in_specs=placed,
        out_specs=(P(("grp", "mp"), None), P("grp", "mp"), P(("grp", "mp"), None), P("grp", "mp")),
        check_vma=False,
    )
```

```python
import math

import jax
import jax.numpy as jnp
from jax import lax
from jax.experimental import pallas as pl
from jax.experimental.pallas import tpu as pltpu
from jax.sharding import PartitionSpec as P

ADAPTER_SCALE = 2.0
EPS = 1e-05
ROW_TILE = 16
LANES = 128
PIECES = 4
MIB = 1024 * 1024

F32 = jnp.float32
BF16 = jnp.bfloat16


def contract_dims(left, right, left_dim, right_dim):
    return lax.dot_general(
        left, right, (((left_dim,), (right_dim,)), ((), ())), preferred_element_type=F32
    )


def dot(left, right):
    return jnp.dot(left, right, preferred_element_type=F32)


def ring_at(pos, n):
    if isinstance(pos, int):
        return 0 if pos == 0 else (2 * pos - 1 if 2 * pos <= n else 2 * (n - pos))
    return jnp.where(pos == 0, 0, jnp.where(2 * pos <= n, 2 * pos - 1, 2 * (n - pos)))


def ring_position():
    n = lax.axis_size("dp")
    place = lax.axis_index("dp")
    odd = lax.rem(place, 2) == 1
    return jnp.where(place == 0, 0, jnp.where(odd, (place + 1) // 2, n - place // 2))


def ring_step(x):
    n = lax.axis_size("dp")
    return lax.ppermute(x, "dp", [(ring_at(i, n), ring_at((i + 1) % n, n)) for i in range(n)])


def swap(x, axis):
    return lax.ppermute(x, axis, [(0, 1), (1, 0)])


def others(x, axis):
    n = lax.axis_size(axis)
    return [lax.ppermute(x, axis, [(i, (i + k) % n) for i in range(n)]) for k in range(1, n)]


def after(x, *done):
    return lax.optimization_barrier((x, *done))[0]


def add(*terms):
    return sum(t.astype(F32) for t in terms).astype(BF16)


def line_sums(parts):
    n = lax.axis_size("dp")
    place = lax.axis_index("dp")
    middle = n // 2
    entered, sums = [], []
    for x in parts:
        if len(entered) > 1:
            x = after(x, entered[-2])
        for s in range(middle - 1):
            x = add(x, lax.ppermute(x, "dp", [(s, s + 1), (n - 1 - s, n - 2 - s)]))
            if s == 0:
                entered.append(x)
        x = add(x, lax.ppermute(x, "dp", [(middle - 1, middle), (middle, middle - 1)]))
        for s in reversed(range(middle - 1)):
            got = lax.ppermute(x, "dp", [(s + 1, s), (n - 2 - s, n - 1 - s)])
            x = jnp.where((place == s) | (place == n - 1 - s), got, x)
        sums.append(x)
    return sums, [swap(x, "sub") for x in sums]


def call(kernel, name, args, out_shape, scratch=(), specs=None, limit=24, flops=0, out_specs=None):
    vmem = pl.BlockSpec(memory_space=pltpu.VMEM)
    moved = sum(a.size * a.dtype.itemsize for a in args) + sum(
        math.prod(s.shape) * s.dtype.itemsize for s in out_shape
    )
    return pl.pallas_call(
        kernel,
        out_shape=tuple(out_shape),
        in_specs=specs or [vmem] * len(args),
        out_specs=out_specs or tuple([vmem] * len(out_shape)),
        scratch_shapes=list(scratch),
        compiler_params=pltpu.CompilerParams(vmem_limit_bytes=limit * MIB),
        cost_estimate=pl.CostEstimate(flops=flops, bytes_accessed=moved, transcendentals=0),
        name=name,
    )(*args)


def shape(dims, dtype=BF16):
    return jax.ShapeDtypeStruct(tuple(dims), dtype)


def halves_call(kernel, name, place, wide, adapter, adapter_rows, rest, rest_specs, outs):
    rows, width = wide[0].shape
    per = 2
    step = width // (2 * per)
    rank = adapter.shape[1] if adapter_rows else adapter.shape[0]

    def at(j, place):
        return jnp.where(j < per, (1 - place[0]) * per + j, place[0] * per + j - per)

    adapter_spec = (
        pl.BlockSpec((step, rank), lambda j, place: (at(j, place), 0))
        if adapter_rows
        else pl.BlockSpec((rank, step), lambda j, place: (0, at(j, place)))
    )
    specs = [pl.BlockSpec((rows, step), lambda j, place: (0, at(j, place)))] * len(wide)
    whole = pl.BlockSpec(memory_space=pltpu.VMEM)
    for kind in rest_specs:
        specs.append(
            pl.BlockSpec((1, step), lambda j, place: (0, at(j, place)))
            if kind == "features"
            else (pl.BlockSpec(memory_space=pltpu.SMEM) if kind == "scalars" else whole)
        )
    return pl.pallas_call(
        kernel,
        out_shape=(shape((rows, width // 2)),) * 2 + tuple(shape((rows, c), F32) for c in outs),
        grid_spec=pltpu.PrefetchScalarGridSpec(
            num_scalar_prefetch=1,
            grid=(2 * per,),
            in_specs=specs + [adapter_spec],
            out_specs=(
                pl.BlockSpec((rows, step), lambda j, place: (0, jnp.minimum(j, per - 1))),
                pl.BlockSpec((rows, step), lambda j, place: (0, jnp.maximum(j - per, 0))),
            )
            + tuple(pl.BlockSpec((rows, c), lambda j, place: (0, 0)) for c in outs),
            scratch_shapes=[pltpu.VMEM((rows, LANES), F32)],
        ),
        compiler_params=pltpu.CompilerParams(vmem_limit_bytes=60 * MIB),
        cost_estimate=pl.CostEstimate(
            flops=2 * rows * width * rank, bytes_accessed=8 * rows * width, transcendentals=0
        ),
        name=name,
    )(place, *wide, *rest, adapter)


def store_half(value, send_ref, own_ref):
    j = pl.program_id(0)
    first = j < pl.num_programs(0) // 2

    @pl.when(first)
    def _():
        send_ref[...] = value

    @pl.when(jnp.logical_not(first))
    def _():
        own_ref[...] = value


def accumulate(ref, term, cols=slice(None)):
    j = pl.program_id(0)

    @pl.when(j == 0)
    def _():
        ref[:, cols] = term

    @pl.when(j > 0)
    def _():
        ref[:, cols] += term


def cotangent_kernel(
    total, place, cotangent, tokens, lengths, slots, adapter, send_ref, own_ref, low_ref, square_ref, row
):
    rows = cotangent.shape[0]
    count = lengths.shape[1]

    @pl.when(pl.program_id(0) == 0)
    def _():
        index = jnp.broadcast_to(slots[...], (LANES, rows))
        weight = jnp.zeros((LANES, rows), F32)
        for s in range(count):
            length = jnp.full((LANES, rows), lengths[0, s], jnp.int32).astype(F32)
            weight = weight + jnp.where(index == s, (rows // count) / length, 0.0)
        row[...] = (weight * F32(1.0 / math.sqrt(total))).T

    value = (cotangent[...].astype(F32) * row[:, :1]).astype(BF16)
    store_half(value, send_ref, own_ref)
    accumulate(low_ref, contract_dims(value, adapter[...], 1, 1))
    squares = jnp.zeros((rows, LANES), F32)
    for i in range(tokens.shape[1] // LANES):
        squares = squares + jnp.square(tokens[:, i * LANES : (i + 1) * LANES].astype(F32))
    squares = jnp.broadcast_to(jnp.sum(squares, axis=1, keepdims=True), (rows, LANES))
    accumulate(square_ref, squares)


def token_kernel(total_width, place, tokens, gain, low_out, squares, *refs):
    squares_more, (adapter, send_ref, own_ref, low_ref, row) = refs[:-5], refs[-5:]
    rank = adapter.shape[1]

    @pl.when(pl.program_id(0) == 0)
    def _():
        total = squares[...]
        for ref in squares_more:
            total = total + ref[...]
        row[...] = lax.rsqrt(total / total_width + EPS)
        low_ref[:, rank:] = low_out[...]

    value = tokens[...].astype(F32) * row[:, :1] * gain[...].astype(F32)
    value = value.astype(BF16)
    store_half(value, send_ref, own_ref)
    accumulate(low_ref, dot(value, adapter[...]), slice(0, rank))


def transpose_kernel(own, got, out_ref):
    rows, step = own.shape[0], out_ref.shape[0]
    for i, ref in enumerate((own, got)):
        out_ref[:, i * rows : (i + 1) * rows] = ref[...].astype(F32).T.astype(BF16)


def widen(scale, wide):
    for g in range(scale.shape[0]):
        row = scale[g : g + 1, :].astype(F32)
        wide[g] = jnp.broadcast_to(row, (LANES, row.shape[1])).T


def place_shards(codes, got, moved, store):
    n = lax.axis_size("dp")
    sub, grp, place = (lax.axis_index(a) for a in ("sub", "grp", "dp"))
    pos = ring_position()
    blocks = got.shape[0]
    quarter = blocks // 2

    @pl.loop(0, blocks, unroll=4)
    def _(b):
        store(b, place * 2 + sub, codes[sub * blocks + b])
        store(b, place * 2 + 1 - sub, got[b])

    for k in range(n - 1):
        there = ring_at(lax.rem(pos - k - 1 + n, n), n)
        for which in range(2):
            piece = moved[2 * k + which]
            start = (grp if which == 0 else 1 - grp) * quarter

            @pl.loop(0, quarter, unroll=4)
            def _(b, piece=piece, start=start, there=there):
                store(start + b, there * 2 + sub, piece[b])
                store(start + b, there * 2 + 1 - sub, piece[quarter + b])


def front_kernel(own, got, scale, codes, codes_got, *refs):
    moved, (mine_ref, theirs_ref, wide, weight) = refs[:-4], refs[-4:]
    blocks, rows, units = codes_got.shape
    first = lax.axis_index("sub") * blocks
    widen(scale, wide)

    def store(b, shard, piece):
        at = pl.ds(pl.multiple_of(shard * rows, ROW_TILE), rows)
        for g in range(units // LANES):
            cols = slice(g * LANES, (g + 1) * LANES)
            factor = wide[g * wide.shape[0] * LANES // units, pl.ds(first + b, 1), :]
            weight[b, at, cols] = (piece[:, cols].astype(F32) * factor).astype(BF16)

    place_shards(codes, codes_got, moved, store)
    matrix = weight[...].reshape(-1, units)
    mine_ref[...] = dot(own[...], matrix)
    theirs_ref[...] = dot(got[...], matrix).astype(BF16)


def back_kernel(own, got, scale, codes, codes_got, *refs):
    moved, (mine_ref, theirs_ref, wide, weight) = refs[:-4], refs[-4:]
    blocks, rows, block = codes_got.shape
    first = lax.axis_index("sub") * blocks
    per_group = weight.shape[0] // wide.shape[0]
    widen(scale, wide)

    def store(b, shard, piece):
        at = pl.multiple_of(shard * rows, ROW_TILE)
        factor = wide[at // per_group, pl.ds(first + b, 1), :]
        cols = pl.ds(pl.multiple_of(b * block, block), block)
        weight[pl.ds(at, rows), cols] = (piece.astype(F32) * factor).astype(BF16)

    place_shards(codes, codes_got, moved, store)
    matrix = weight[...]
    mine_ref[...] = contract_dims(own[...], matrix, 1, 1)
    theirs_ref[...] = contract_dims(got[...], matrix, 1, 1).astype(BF16)


def place_own(scratch, own, more, axis):
    n = len(more) + 1
    size = own.shape[axis]
    for k, ref in enumerate((own, *more)):
        at = pl.ds(pl.multiple_of(lax.rem(lax.axis_index("mp") + n - k, n) * size, size), size)
        if axis == 0:
            scratch[at, :] = ref[...]
        else:
            scratch[:, at] = ref[...]


def own_units(full, ref, axis):
    size = ref.shape[axis]
    for i in range(full.shape[axis] // size):

        @pl.when(lax.axis_index("mp") == i)
        def _(i=i):
            ref[...] = lax.slice_in_dim(full, i * size, (i + 1) * size, axis=axis).astype(BF16)


def low_sums(low, low_more):
    total = low[...]
    for ref in low_more:
        total = total + ref[...]
    half = total.shape[1] // 2
    return total[:, :half].astype(BF16), total[:, half:].astype(BF16)


def gather_adapters(adapters, adapters_more, up_out_all, down_in_all):
    rank = up_out_all.shape[0]
    place_own(up_out_all, adapters.at[:rank], [r.at[:rank] for r in adapters_more], 1)
    place_own(down_in_all, adapters.at[rank:], [r.at[rank:] for r in adapters_more], 0)


def hidden_kernel(more, gate, up, low, adapters, *refs):
    gate_more, up_more, low_more, adapters_more = (refs[i * more : (i + 1) * more] for i in range(4))
    silu_ref, low_ref, down_in_term, up_out_all, down_in_all = refs[4 * more :]
    gather_adapters(adapters, adapters_more, up_out_all, down_in_all)
    low_up, low_out = low_sums(low, low_more)
    gate_sum, up_sum = gate[...], up[...]
    for ref in gate_more:
        gate_sum = gate_sum + ref[...].astype(F32)
    for ref in up_more:
        up_sum = up_sum + ref[...].astype(F32)
    up_sum = up_sum + ADAPTER_SCALE * dot(low_up, up_out_all[...])
    silu = gate_sum * jax.nn.sigmoid(gate_sum)
    silu_ref[...] = silu
    hidden = (silu * up_sum).astype(BF16)
    low_ref[...] = (ADAPTER_SCALE * dot(hidden, down_in_all[...])).astype(BF16)
    hidden_t = hidden.astype(F32).T.astype(BF16)
    own_units(ADAPTER_SCALE * dot(hidden_t, low_out), down_in_term, 0)


def up_grad_kernel(more, back, silu, low, adapters, *refs):
    back_more, low_more, adapters_more = (refs[i * more : (i + 1) * more] for i in range(3))
    low_ref, up_out_term, up_out_all, down_in_all = refs[3 * more :]
    gather_adapters(adapters, adapters_more, up_out_all, down_in_all)
    low_up, low_out = low_sums(low, low_more)
    total = back[...]
    for ref in back_more:
        total = total + ref[...].astype(F32)
    total = total + ADAPTER_SCALE * contract_dims(low_out, down_in_all[...], 1, 1)
    up_grad = (total * silu[...]).astype(BF16)
    low_ref[...] = (ADAPTER_SCALE * contract_dims(up_grad, up_out_all[...], 1, 1)).astype(BF16)
    low_up_t = low_up.astype(F32).T.astype(BF16)
    own_units(ADAPTER_SCALE * dot(low_up_t, up_grad), up_out_term, 1)


def down_out_kernel(low, low_got, grad, grad_got, *out_refs):
    low_t = jnp.concatenate([low[...], low_got[...]], axis=0).astype(F32).T.astype(BF16)
    rows = low.shape[0]
    for k, ref in enumerate(out_refs):
        size = ref.shape[1]
        at = slice(k * size, (k + 1) * size)
        ref[...] = (
            dot(low_t[:, :rows], grad[:, at]) + dot(low_t[:, rows:], grad_got[:, at])
        ).astype(BF16)


def up_in_kernel(low, low_got, normed_t, up_out_term, down_in_term, *out_refs):
    n = len(out_refs)
    size = normed_t.shape[0] // n
    extra = out_refs[0].shape[0] - size
    both = jnp.concatenate([low[...], low_got[...]], axis=0)
    small = jnp.concatenate([up_out_term[...], down_in_term[...]], axis=0)
    for k, ref in enumerate(out_refs):
        ref[:size, :] = dot(normed_t[k * size : (k + 1) * size, :], both).astype(BF16)
        ref[size:, :] = small[k * extra : (k + 1) * extra, :]


def copy_all(copies):
    for c in copies:
        c.start()
    for c in copies:
        c.wait()


def down_out_place_kernel(n, *refs):
    pieces, out_ref, sems = refs[: 2 * n], refs[2 * n], refs[2 * n + 1]
    sub = lax.axis_index("sub")
    copies = []
    for i, piece in enumerate(pieces):
        half = sub if i < n else 1 - sub
        size = piece.shape[1]
        at = pl.ds(pl.multiple_of((half * n + i % n) * size, size), size)
        copies.append(pltpu.make_async_copy(piece, out_ref.at[:, at], sems.at[i]))
    copy_all(copies)


def up_in_place_kernel(n, *refs):
    pieces = refs[: 2 * n]
    out_ref, up_out_ref, down_in_ref, small, sems = refs[2 * n :]
    sub = lax.axis_index("sub")
    size = out_ref.shape[0] // (2 * n)
    extra = pieces[0].shape[0] - size
    copies = []
    for i, piece in enumerate(pieces):
        half = sub if i < n else 1 - sub
        k = i % n
        at = pl.ds(pl.multiple_of((half * n + k) * size, size), size)
        copies.append(
            pltpu.make_async_copy(piece.at[pl.ds(0, size), :], out_ref.at[at, :], sems.at[2 * i])
        )
        copies.append(
            pltpu.make_async_copy(
                piece.at[pl.ds(size, extra), :],
                small.at[i // n, pl.ds(k * extra, extra), :],
                sems.at[2 * i + 1],
            )
        )
    copy_all(copies)
    total = (small[0].astype(F32) + small[1].astype(F32)).astype(BF16)
    rows = up_out_ref.shape[0]
    up_out_ref[...] = total[:rows]
    down_in_ref[...] = total[rows:]


class Shards:
    def __init__(self, codes):
        sub, grp = lax.axis_index("sub"), lax.axis_index("grp")
        half = codes.shape[0] // 2
        quarter = half // 2
        self.codes = codes
        self.got = swap(lax.dynamic_slice_in_dim(codes, (1 - sub) * half, half, 0), "sub")
        own = lax.dynamic_slice_in_dim(codes, sub * half + grp * quarter, quarter, 0)
        got = lax.dynamic_slice_in_dim(self.got, grp * quarter, quarter, 0)
        self.moving = jnp.concatenate([own, got], axis=0)
        self.moved = []

    def step(self, *done):
        self.moving = ring_step(after(self.moving, *done) if done else self.moving)
        self.moved += [self.moving, swap(self.moving, "grp")]
        return self.moved[-2:]

    def args(self):
        return [self.codes, self.got, *self.moved]


def fast_body(
    tokens,
    cotangent,
    rms_norm_gain,
    gate_codes,
    gate_block_scale,
    up_codes,
    up_block_scale,
    down_codes,
    down_block_scale,
    up_adapter_in,
    up_adapter_out,
    down_adapter_in,
    down_adapter_out,
    sequence_length_list,
    slot_sequence_index,
):
    rows, local_width = tokens.shape
    blocks, _, units = gate_codes.shape
    block = local_width // blocks
    half = local_width // 2
    rank = up_adapter_in.shape[1]
    total_width = local_width * lax.axis_size("mp")
    n = lax.axis_size("dp")
    more = lax.axis_size("mp") - 1
    place = lax.axis_index("sub").astype(jnp.int32).reshape(1)

    gate_shards = Shards(gate_codes)
    up_shards = Shards(up_codes)
    down_shards = Shards(jnp.swapaxes(after(down_codes, up_shards.moving), 0, 1))
    arrived = []
    for shards in [gate_shards, up_shards] * (n - 1) + [down_shards] * (n - 1):
        done = [ring for ring, _ in arrived[-2:-1]] + [crossed for _, crossed in arrived[-4:-3]]
        arrived.append(shards.step(*done))

    adapters = jnp.concatenate([up_adapter_out, down_adapter_in], axis=0)
    adapters_more = others(after(adapters, arrived[0][0]), "mp")
    tokens_then, cotangent_then, _ = lax.optimization_barrier((tokens, cotangent, arrived[0][0]))
    grad_send, grad, low_out, squares = halves_call(
        lambda *refs: cotangent_kernel(rows * n * lax.axis_size("sub"), *refs),
        "cotangent",
        place,
        [cotangent_then, tokens_then],
        down_adapter_out,
        False,
        [sequence_length_list, slot_sequence_index[None, :]],
        ["scalars", "whole"],
        [rank, LANES],
    )
    grad_got = swap(grad_send, "sub")
    squares_more = others(squares, "mp")
    tokens_then = after(tokens, arrived[2][0])
    normed_send, normed, low = halves_call(
        lambda *refs: token_kernel(total_width, *refs),
        "tokens",
        place,
        [tokens_then],
        up_adapter_in,
        True,
        [rms_norm_gain[None, :], low_out, squares, *squares_more],
        ["features"] + ["whole"] * (2 + more),
        [2 * rank],
    )
    normed_got = swap(normed_send, "sub")
    low_more = others(low, "mp")

    def product(kernel, name, own, got, scale, shards, weight_shape):
        groups = scale.shape[0]
        mine, theirs = call(
            kernel,
            name,
            [own, got, scale, *shards.args()],
            [shape((rows, units), F32), shape((rows, units))],
            scratch=[pltpu.VMEM((groups, blocks, LANES), F32), pltpu.VMEM(weight_shape, BF16)],
            flops=4 * rows * half * units,
        )
        mine = mine + swap(theirs, "sub").astype(F32)
        return mine, others(mine.astype(BF16), "mp")

    front = (blocks // 2, block, units)
    gate, gate_more = product(
        front_kernel, "gate", normed, normed_got, gate_block_scale.T, gate_shards, front
    )
    up, up_more = product(front_kernel, "up", normed, normed_got, up_block_scale.T, up_shards, front)
    small_scratch = [
        pltpu.VMEM((rank, units), BF16),
        pltpu.VMEM((units, rank), BF16),
    ]
    silu, low_hidden, down_in_term = call(
        lambda *refs: hidden_kernel(more, *refs),
        "hidden",
        [gate, up, low, adapters, *gate_more, *up_more, *low_more, *adapters_more],
        [shape((rows, units), F32), shape((rows, rank)), shape(down_adapter_in.shape)],
        scratch=small_scratch,
        limit=8,
    )
    down_out_parts = call(
        down_out_kernel,
        "down_out",
        [low_hidden, swap(low_hidden, "sub"), grad, grad_got],
        [shape((rank, half // PIECES))] * PIECES,
        flops=4 * rows * half * rank,
    )
    (normed_t,) = call(
        transpose_kernel,
        "transpose",
        [normed, after(normed_got, low_hidden)],
        [shape((half, 2 * rows))],
        limit=32,
    )

    back, back_more = product(
        back_kernel, "back", grad, grad_got, down_block_scale, down_shards, (units, half)
    )
    low_grad, up_out_term = call(
        lambda *refs: up_grad_kernel(more, *refs),
        "up_grad",
        [back, silu, low, adapters, *back_more, *low_more, *adapters_more],
        [shape((rows, rank)), shape(up_adapter_out.shape)],
        scratch=small_scratch,
        limit=8,
    )
    extra = 2 * rank // PIECES
    up_in_parts = call(
        up_in_kernel,
        "up_in",
        [low_grad, swap(low_grad, "sub"), normed_t, up_out_term, down_in_term],
        [shape((half // PIECES + extra, rank))] * PIECES,
        flops=4 * rows * half * rank,
    )
    sums, sums_got = line_sums([*down_out_parts, *up_in_parts])

    anywhere = pl.BlockSpec(memory_space=pl.ANY)
    vmem = pl.BlockSpec(memory_space=pltpu.VMEM)
    (down_out_gradient,) = call(
        lambda *refs: down_out_place_kernel(PIECES, *refs),
        "down_out_place",
        [*sums[:PIECES], *sums_got[:PIECES]],
        [shape((rank, local_width))],
        scratch=[pltpu.SemaphoreType.DMA((2 * PIECES,))],
        specs=[anywhere] * (2 * PIECES),
        out_specs=(anywhere,),
        limit=4,
    )
    up_in_gradient, up_out_gradient, down_in_gradient = call(
        lambda *refs: up_in_place_kernel(PIECES, *refs),
        "up_in_place",
        [*sums[PIECES:], *sums_got[PIECES:]],
        [shape((local_width, rank)), shape(up_adapter_out.shape), shape(down_adapter_in.shape)],
        scratch=[pltpu.VMEM((2, 2 * rank, rank), BF16), pltpu.SemaphoreType.DMA((4 * PIECES,))],
        specs=[anywhere] * (2 * PIECES),
        out_specs=(anywhere, vmem, vmem),
        limit=4,
    )
    return up_in_gradient, up_out_gradient, down_in_gradient, down_out_gradient


def general_body(
    tokens,
    cotangent,
    rms_norm_gain,
    gate_codes,
    gate_block_scale,
    up_codes,
    up_block_scale,
    down_codes,
    down_block_scale,
    up_adapter_in,
    up_adapter_out,
    down_adapter_in,
    down_adapter_out,
    sequence_length_list,
    slot_sequence_index,
):
    rows = tokens.shape[0]
    local_width = tokens.shape[1]
    block = gate_block_scale.shape[0] and local_width // gate_codes.shape[0]
    blocks_here = gate_codes.shape[0]
    total_width = local_width * lax.axis_size("mp")
    own_squares = jnp.sum(jnp.square(tokens.astype(jnp.float32)), axis=-1, keepdims=True)
    squares = lax.psum(own_squares, "mp") / total_width
    inv_rms = lax.rsqrt(squares + EPS)
    local_normed_input = (
        tokens.astype(jnp.float32) * inv_rms * rms_norm_gain.astype(jnp.float32)[None, :]
    ).astype(jnp.bfloat16)
    seq_count = sequence_length_list.shape[1]
    longest = rows // seq_count
    total = rows * lax.axis_size("dp") * lax.axis_size("sub")
    ratios = longest / sequence_length_list[0].astype(jnp.float32)
    match = slot_sequence_index[:, None] == jnp.arange(seq_count, dtype=jnp.int32)[None, :]
    token_weight = jnp.sum(jnp.where(match, ratios[None, :], jnp.float32(0.0)), axis=-1)
    token_weight = token_weight * jnp.float32(1.0 / math.sqrt(total))
    local_output = (cotangent.astype(jnp.float32) * token_weight[:, None]).astype(jnp.bfloat16)
    partial_up = jnp.dot(local_normed_input, up_adapter_in, preferred_element_type=jnp.float32)
    partial_output = contract_dims(local_output, down_adapter_out, 1, 1)
    up_adapter_rank, output_adapter_rank = lax.psum((partial_up, partial_output), "mp")
    up_adapter_rank = up_adapter_rank.astype(jnp.bfloat16)
    output_adapter_rank = output_adapter_rank.astype(jnp.bfloat16)
    normed_blocks = local_normed_input.reshape(rows, blocks_here, block)
    out_blocks = local_output.reshape(rows, blocks_here, block)
    wide_gate = jnp.repeat(gate_block_scale.astype(jnp.float32), block, axis=1)[:, None, :]
    wide_up = jnp.repeat(up_block_scale.astype(jnp.float32), block, axis=1)[:, None, :]
    wide_down = jnp.repeat(down_block_scale.astype(jnp.float32), block, axis=0)
    dims_front = (((1, 2), (0, 1)), ((), ()))
    dims_back = (((1, 2), (1, 2)), ((), ()))
    quant_g = lax.all_gather(gate_codes, ("dp", "sub"), axis=1, tiled=True)
    quant_u = lax.all_gather(up_codes, ("dp", "sub"), axis=1, tiled=True)
    weight_g = (quant_g.astype(jnp.float32) * wide_gate).astype(jnp.bfloat16)
    weight_u = (quant_u.astype(jnp.float32) * wide_up).astype(jnp.bfloat16)
    gate_next = lax.dot_general(
        normed_blocks, weight_g, dims_front, preferred_element_type=jnp.float32
    )
    up_next = lax.dot_general(
        normed_blocks, weight_u, dims_front, preferred_element_type=jnp.float32
    )
    gate, base_up_projected = (
        lax.psum_scatter(gate_next, "mp", scatter_dimension=1, tiled=True),
        lax.psum_scatter(up_next, "mp", scatter_dimension=1, tiled=True),
    )
    up_projected = base_up_projected + ADAPTER_SCALE * jnp.dot(
        up_adapter_rank, up_adapter_out, preferred_element_type=jnp.float32
    )
    silu_gate = jax.nn.silu(gate)
    hidden_units = (silu_gate * up_projected).astype(jnp.bfloat16)
    partial_hidden = jnp.dot(hidden_units, down_adapter_in, preferred_element_type=jnp.float32)
    hidden_adapter_rank = lax.psum(partial_hidden, "mp").astype(jnp.bfloat16)
    weight_d = (
        lax.all_gather(down_codes, ("dp", "sub"), axis=0, tiled=True).astype(jnp.float32)
        * wide_down[:, :, None]
    ).astype(jnp.bfloat16)
    back_part = lax.dot_general(out_blocks, weight_d, dims_back, preferred_element_type=jnp.float32)
    base_backward = lax.psum_scatter(back_part, "mp", scatter_dimension=1, tiled=True)
    hidden_gradient = base_backward + ADAPTER_SCALE * contract_dims(
        output_adapter_rank, down_adapter_in, 1, 1
    )
    up_gradient = (hidden_gradient * silu_gate).astype(jnp.bfloat16)
    partial_gradient = contract_dims(up_gradient, up_adapter_out, 1, 1)
    up_adapter_rank_gradient = lax.psum(partial_gradient, "mp").astype(jnp.bfloat16)
    up_in_term = ADAPTER_SCALE * contract_dims(local_normed_input, up_adapter_rank_gradient, 0, 0)
    up_out_term = ADAPTER_SCALE * contract_dims(up_adapter_rank, up_gradient, 0, 0)
    down_in_term = ADAPTER_SCALE * contract_dims(hidden_units, output_adapter_rank, 0, 0)
    down_out_term = ADAPTER_SCALE * contract_dims(hidden_adapter_rank, local_output, 0, 0)
    sum_up_a, sum_up_b, sum_down_a, sum_down_b = lax.psum(
        (up_in_term, up_out_term, down_in_term, down_out_term), ("dp", "sub")
    )
    return (
        sum_up_a.astype(jnp.bfloat16),
        sum_up_b.astype(jnp.bfloat16),
        sum_down_a.astype(jnp.bfloat16),
        sum_down_b.astype(jnp.bfloat16),
    )


def body(tokens, cotangent, rms_norm_gain, gate_codes, *rest):
    whole_tiles = gate_codes.shape[1] % ROW_TILE == 0
    form = fast_body if whole_tiles else general_body
    return form(tokens, cotangent, rms_norm_gain, gate_codes, *rest)


def solution(mesh):
    placed = (
        P(("grp", "dp", "sub"), "mp"),
        P(("grp", "dp", "sub"), "mp"),
        P("mp"),
        P("mp", ("dp", "sub"), None),
        P("mp", None),
        P("mp", ("dp", "sub"), None),
        P("mp", None),
        P(("dp", "sub"), "mp", None),
        P(None, "mp"),
        P(("grp", "mp"), None),
        P("grp", "mp"),
        P(("grp", "mp"), None),
        P("grp", "mp"),
        P(("grp", "dp", "sub"), None),
        P(("grp", "dp", "sub")),
    )
    return jax.shard_map(
        body,
        mesh=mesh,
        in_specs=placed,
        out_specs=(P(("grp", "mp"), None), P("grp", "mp"), P(("grp", "mp"), None), P("grp", "mp")),
        check_vma=False,
    )
```

```python
import math

import jax
import jax.numpy as jnp
from jax import lax
from jax.experimental import pallas as pl
from jax.experimental.pallas import tpu as pltpu
from jax.sharding import PartitionSpec as P

ADAPTER_SCALE = 2.0
EPS = 1e-05
ROW_TILE = 16
LANES = 128
MIB = 1024 * 1024

F32 = jnp.float32
BF16 = jnp.bfloat16


def contract_dims(left, right, left_dim, right_dim):
    return lax.dot_general(
        left, right, (((left_dim,), (right_dim,)), ((), ())), preferred_element_type=F32
    )


def dot(left, right):
    return jnp.dot(left, right, preferred_element_type=F32)


def ring_at(pos, n):
    if isinstance(pos, int):
        return 0 if pos == 0 else (2 * pos - 1 if 2 * pos <= n else 2 * (n - pos))
    return jnp.where(pos == 0, 0, jnp.where(2 * pos <= n, 2 * pos - 1, 2 * (n - pos)))


def ring_position():
    n = lax.axis_size("dp")
    place = lax.axis_index("dp")
    odd = lax.rem(place, 2) == 1
    return jnp.where(place == 0, 0, jnp.where(odd, (place + 1) // 2, n - place // 2))


def ring_step(x):
    n = lax.axis_size("dp")
    return lax.ppermute(x, "dp", [(ring_at(i, n), ring_at((i + 1) % n, n)) for i in range(n)])


def swap(x, axis):
    return lax.ppermute(x, axis, [(0, 1), (1, 0)])


def others(x, axis):
    n = lax.axis_size(axis)
    return [lax.ppermute(x, axis, [(i, (i + k) % n) for i in range(n)]) for k in range(1, n)]


def after(x, *done):
    return lax.optimization_barrier((x, *done))[0]


def add(*terms):
    return sum(t.astype(F32) for t in terms).astype(BF16)


def ring_sum(parts, seen=None):
    total = parts[0]
    for part in parts[1:]:
        total = ring_step(total)
        if seen is not None:
            seen.append(total)
        total = add(total, part)
    return total


def ring_gather(block):
    blocks = [block]
    for _ in range(lax.axis_size("dp") - 1):
        blocks.append(ring_step(blocks[-1]))
    return blocks, [swap(b, "sub") for b in blocks]


def call(kernel, name, args, out_shape, scratch=(), specs=None, limit=24, flops=0, out_specs=None):
    vmem = pl.BlockSpec(memory_space=pltpu.VMEM)
    moved = sum(a.size * a.dtype.itemsize for a in args) + sum(
        math.prod(s.shape) * s.dtype.itemsize for s in out_shape
    )
    return pl.pallas_call(
        kernel,
        out_shape=tuple(out_shape),
        in_specs=specs or [vmem] * len(args),
        out_specs=out_specs or tuple([vmem] * len(out_shape)),
        scratch_shapes=list(scratch),
        compiler_params=pltpu.CompilerParams(vmem_limit_bytes=limit * MIB),
        cost_estimate=pl.CostEstimate(flops=flops, bytes_accessed=moved, transcendentals=0),
        name=name,
    )(*args)


def shape(dims, dtype=BF16):
    return jax.ShapeDtypeStruct(tuple(dims), dtype)


def scaled_halves(wide, low_ref, cols, scaled, product, send_ref, own_ref):
    half = send_ref.shape[1]
    step = half // 4
    sub = lax.axis_index("sub")
    low_ref[:, cols] = jnp.zeros((wide.shape[0], LANES), F32)
    for which, out_ref in ((1 - sub, send_ref), (sub, own_ref)):

        @pl.loop(0, half // step)
        def _(j, which=which, out_ref=out_ref):
            first = pl.multiple_of(which * half + j * step, step)
            parts = []
            for i in range(step // LANES):
                tile = pl.ds(pl.multiple_of(first + i * LANES, LANES), LANES)
                parts.append(scaled(wide[:, tile].astype(F32), tile).astype(BF16))
            value = jnp.concatenate(parts, axis=1)
            out_ref[:, pl.ds(pl.multiple_of(j * step, step), step)] = value
            low_ref[:, cols] += product(value, pl.ds(first, step))


def cotangent_kernel(
    total, cotangent, tokens, lengths, slots, adapter, send_ref, own_ref, low_ref, square_ref
):
    rows, width = cotangent.shape
    index = jnp.broadcast_to(slots[...], (LANES, rows))
    weight = jnp.zeros((LANES, rows), F32)
    for s in range(lengths.shape[1]):
        length = jnp.full((LANES, rows), lengths[0, s], jnp.int32).astype(F32)
        weight = weight + jnp.where(index == s, (rows // lengths.shape[1]) / length, 0.0)
    row = (weight * F32(1.0 / math.sqrt(total))).T

    square_ref[...] = jnp.zeros_like(square_ref)

    @pl.loop(0, width // (8 * LANES))
    def _(j):
        squares = square_ref[...]
        for i in range(8):
            tile = pl.ds(pl.multiple_of((j * 8 + i) * LANES, LANES), LANES)
            squares = squares + jnp.square(tokens[:, tile].astype(F32))
        square_ref[...] = squares

    square_ref[...] = jnp.broadcast_to(
        jnp.sum(square_ref[...], axis=1, keepdims=True), square_ref.shape
    )
    scaled_halves(
        cotangent,
        low_ref,
        slice(None),
        lambda tile, cols: tile * row,
        lambda value, cols: contract_dims(value, adapter[:, cols], 1, 1),
        send_ref,
        own_ref,
    )


def token_kernel(total_width, tokens, gain, adapter, low_out, squares, *refs):
    squares_more, (send_ref, own_ref, low_ref) = refs[:-3], refs[-3:]
    rank = adapter.shape[1]
    total = squares[...]
    for ref in squares_more:
        total = total + ref[...]
    row = lax.rsqrt(total / total_width + EPS)
    low_ref[:, rank:] = low_out[...]
    scaled_halves(
        tokens,
        low_ref,
        slice(0, rank),
        lambda tile, cols: tile * row * gain[:, cols].astype(F32),
        lambda value, cols: dot(value, adapter[cols, :]),
        send_ref,
        own_ref,
    )


def transpose_kernel(own, got, out_ref):
    rows, step = own.shape[0], out_ref.shape[0]
    for i, ref in enumerate((own, got)):
        out_ref[:, i * rows : (i + 1) * rows] = ref[...].astype(F32).T.astype(BF16)


def widen(scale, wide):
    for g in range(scale.shape[0]):
        row = scale[g : g + 1, :].astype(F32)
        wide[g] = jnp.broadcast_to(row, (LANES, row.shape[1])).T


def place_shards(codes, got, first_got, moved, store):
    n = lax.axis_size("dp")
    sub, grp, place = (lax.axis_index(a) for a in ("sub", "grp", "dp"))
    pos = ring_position()
    blocks = codes.shape[0] // 2
    quarter = blocks // 2

    @pl.loop(0, blocks, unroll=4)
    def _(b):
        store(b, place * 2 + sub, codes[sub * blocks + b])
        store(b, place * 2 + 1 - sub, got[first_got + b])

    for k in range(n - 1):
        there = ring_at(lax.rem(pos - k - 1 + n, n), n)
        for which in range(2):
            piece = moved[2 * k + which]
            start = (grp if which == 0 else 1 - grp) * quarter

            @pl.loop(0, quarter, unroll=4)
            def _(b, piece=piece, start=start, there=there):
                store(start + b, there * 2 + sub, piece[b])
                store(start + b, there * 2 + 1 - sub, piece[quarter + b])


def front_kernel(first_got, own, got, scale, codes, codes_got, *refs):
    moved, (mine_ref, theirs_ref, wide, weight) = refs[:-4], refs[-4:]
    blocks, rows, units = codes.shape
    first = lax.axis_index("sub") * (blocks // 2)
    widen(scale, wide)

    def store(b, shard, piece):
        at = pl.ds(pl.multiple_of(shard * rows, ROW_TILE), rows)
        for g in range(units // LANES):
            cols = slice(g * LANES, (g + 1) * LANES)
            factor = wide[g * wide.shape[0] * LANES // units, pl.ds(first + b, 1), :]
            weight[b, at, cols] = (piece[:, cols].astype(F32) * factor).astype(BF16)

    place_shards(codes, codes_got, first_got, moved, store)
    matrix = weight[...].reshape(-1, units)
    mine_ref[...] = dot(own[...], matrix)
    theirs_ref[...] = dot(got[...], matrix).astype(BF16)


def back_kernel(first_got, own, got, scale, codes, codes_got, *refs):
    moved, (mine_ref, theirs_ref, wide, weight) = refs[:-4], refs[-4:]
    blocks, rows, block = codes.shape
    first = lax.axis_index("sub") * (blocks // 2)
    per_group = weight.shape[0] // wide.shape[0]
    widen(scale, wide)

    def store(b, shard, piece):
        at = pl.multiple_of(shard * rows, ROW_TILE)
        factor = wide[at // per_group, pl.ds(first + b, 1), :]
        cols = pl.ds(pl.multiple_of(b * block, block), block)
        weight[pl.ds(at, rows), cols] = (piece.astype(F32) * factor).astype(BF16)

    place_shards(codes, codes_got, first_got, moved, store)
    matrix = weight[...]
    mine_ref[...] = contract_dims(own[...], matrix, 1, 1)
    theirs_ref[...] = contract_dims(got[...], matrix, 1, 1).astype(BF16)


def place_own(scratch, own, more, axis):
    n = len(more) + 1
    size = own.shape[axis]
    for k, ref in enumerate((own, *more)):
        at = pl.ds(pl.multiple_of(lax.rem(lax.axis_index("mp") + n - k, n) * size, size), size)
        if axis == 0:
            scratch[at, :] = ref[...]
        else:
            scratch[:, at] = ref[...]


def own_units(full, ref, axis):
    size = ref.shape[axis]
    for i in range(full.shape[axis] // size):

        @pl.when(lax.axis_index("mp") == i)
        def _(i=i):
            ref[...] = lax.slice_in_dim(full, i * size, (i + 1) * size, axis=axis).astype(BF16)


def low_sums(low, low_more):
    total = low[...]
    for ref in low_more:
        total = total + ref[...]
    half = total.shape[1] // 2
    return total[:, :half].astype(BF16), total[:, half:].astype(BF16)


def gather_adapters(adapters, adapters_more, up_out_all, down_in_all):
    rank = up_out_all.shape[0]
    place_own(up_out_all, adapters.at[:rank], [r.at[:rank] for r in adapters_more], 1)
    place_own(down_in_all, adapters.at[rank:], [r.at[rank:] for r in adapters_more], 0)


def hidden_kernel(more, gate, up, low, adapters, *refs):
    gate_more, up_more, low_more, adapters_more = (refs[i * more : (i + 1) * more] for i in range(4))
    silu_ref, low_ref, down_in_term, up_out_all, down_in_all = refs[4 * more :]
    gather_adapters(adapters, adapters_more, up_out_all, down_in_all)
    low_up, low_out = low_sums(low, low_more)
    gate_sum, up_sum = gate[...], up[...]
    for ref in gate_more:
        gate_sum = gate_sum + ref[...].astype(F32)
    for ref in up_more:
        up_sum = up_sum + ref[...].astype(F32)
    up_sum = up_sum + ADAPTER_SCALE * dot(low_up, up_out_all[...])
    silu = gate_sum * jax.nn.sigmoid(gate_sum)
    silu_ref[...] = silu
    hidden = (silu * up_sum).astype(BF16)
    low_ref[...] = (ADAPTER_SCALE * dot(hidden, down_in_all[...])).astype(BF16)
    hidden_t = hidden.astype(F32).T.astype(BF16)
    own_units(ADAPTER_SCALE * dot(hidden_t, low_out), down_in_term, 0)


def up_grad_kernel(more, back, silu, low, adapters, *refs):
    back_more, low_more, adapters_more = (refs[i * more : (i + 1) * more] for i in range(3))
    low_ref, up_out_term, up_out_all, down_in_all = refs[3 * more :]
    gather_adapters(adapters, adapters_more, up_out_all, down_in_all)
    low_up, low_out = low_sums(low, low_more)
    total = back[...]
    for ref in back_more:
        total = total + ref[...].astype(F32)
    total = total + ADAPTER_SCALE * contract_dims(low_out, down_in_all[...], 1, 1)
    up_grad = (total * silu[...]).astype(BF16)
    low_ref[...] = (ADAPTER_SCALE * contract_dims(up_grad, up_out_all[...], 1, 1)).astype(BF16)
    low_up_t = low_up.astype(F32).T.astype(BF16)
    own_units(ADAPTER_SCALE * dot(low_up_t, up_grad), up_out_term, 1)


def down_out_kernel(low, low_got, grad, grad_got, *out_refs):
    n = len(out_refs)
    pos = ring_position()
    low_t = jnp.concatenate([low[...], low_got[...]], axis=0).astype(F32).T.astype(BF16)
    rows = low.shape[0]
    for k, ref in enumerate(out_refs):
        size = ref.shape[1]
        at = pl.ds(pl.multiple_of(lax.rem(pos - 1 - k + 2 * n, n) * size, size), size)
        ref[...] = (
            dot(low_t[:, :rows], grad[:, at]) + dot(low_t[:, rows:], grad_got[:, at])
        ).astype(BF16)


def up_in_kernel(low, low_got, normed_t, up_out_term, down_in_term, *out_refs):
    n = len(out_refs)
    pos = ring_position()
    size = normed_t.shape[0] // n
    extra = out_refs[0].shape[0] - size
    both = jnp.concatenate([low[...], low_got[...]], axis=0)
    for k, ref in enumerate(out_refs):
        block = lax.rem(pos - 1 - k + 2 * n, n)
        at = pl.ds(pl.multiple_of(block * size, size), size)
        ref[pl.ds(0, size), :] = dot(normed_t[at, :], both).astype(BF16)
        per = up_out_term.shape[0] // extra
        index = pl.ds(pl.multiple_of(lax.rem(block, per) * extra, extra), extra)

        @pl.when(block < per)
        def _(ref=ref, index=index):
            ref[pl.ds(size, extra), :] = up_out_term[index, :]

        @pl.when(block >= per)
        def _(ref=ref, index=index):
            ref[pl.ds(size, extra), :] = down_in_term[index, :]


def copy_all(copies):
    for c in copies:
        c.start()
    for c in copies:
        c.wait()


def down_out_place_kernel(n, *refs):
    pieces, out_ref, sems = refs[: 2 * n], refs[2 * n], refs[2 * n + 1]
    pos, sub = ring_position(), lax.axis_index("sub")
    copies = []
    for i, piece in enumerate(pieces):
        half = sub if i < n else 1 - sub
        block = lax.rem(pos - i % n + n, n)
        size = piece.shape[1]
        at = pl.ds(pl.multiple_of((half * n + block) * size, size), size)
        copies.append(pltpu.make_async_copy(piece, out_ref.at[:, at], sems.at[i]))
    copy_all(copies)


def up_in_place_kernel(n, *refs):
    pieces = refs[: 2 * n]
    out_ref, up_out_ref, down_in_ref, small, sems = refs[2 * n :]
    pos, sub = ring_position(), lax.axis_index("sub")
    size = out_ref.shape[0] // (2 * n)
    extra = pieces[0].shape[0] - size
    copies = []
    for i, piece in enumerate(pieces):
        half = sub if i < n else 1 - sub
        block = lax.rem(pos - i % n + n, n)
        at = pl.ds(pl.multiple_of((half * n + block) * size, size), size)
        copies.append(
            pltpu.make_async_copy(piece.at[pl.ds(0, size), :], out_ref.at[at, :], sems.at[2 * i])
        )
        at = pl.ds(pl.multiple_of(block * extra, extra), extra)
        copies.append(
            pltpu.make_async_copy(
                piece.at[pl.ds(size, extra), :], small.at[i // n, at, :], sems.at[2 * i + 1]
            )
        )
    copy_all(copies)
    total = (small[0].astype(F32) + small[1].astype(F32)).astype(BF16)
    rows = up_out_ref.shape[0]
    up_out_ref[...] = total[:rows]
    down_in_ref[...] = total[rows:]


def half_kernel(*refs):
    sources, out_ref, sems = refs[:-2], refs[-2], refs[-1]
    other = 1 - lax.axis_index("sub")
    half = sources[0].shape[0] // 2
    copy_all(
        [
            pltpu.make_async_copy(
                ref.at[pl.ds(other * half, half)], out_ref.at[pl.ds(i * half, half)], sems.at[i]
            )
            for i, ref in enumerate(sources)
        ]
    )


def quarter_kernel(*refs):
    count = (len(refs) - 2) // 2
    sources, got, out_refs, sems = refs[:count], refs[count], refs[count + 1 : -1], refs[-1]
    sub, grp = lax.axis_index("sub"), lax.axis_index("grp")
    half = sources[0].shape[0] // 2
    quarter = half // 2
    copies = []
    for i, (ref, out_ref) in enumerate(zip(sources, out_refs)):
        own = ref.at[pl.ds(sub * half + grp * quarter, quarter)]
        theirs = got.at[pl.ds(i * half + grp * quarter, quarter)]
        for k, source in enumerate((own, theirs)):
            copies.append(
                pltpu.make_async_copy(
                    source, out_ref.at[pl.ds(k * quarter, quarter)], sems.at[2 * i + k]
                )
            )
    copy_all(copies)


def start_shards(codes):
    blocks, rows, units = codes[0].shape
    count = len(codes)
    anywhere = pl.BlockSpec(memory_space=pl.ANY)
    (send,) = call(
        half_kernel,
        "halves",
        codes,
        [shape((count * blocks // 2, rows, units))],
        scratch=[pltpu.SemaphoreType.DMA((count,))],
        specs=[anywhere] * count,
        out_specs=(anywhere,),
        limit=4,
    )
    got = swap(send, "sub")
    moving = call(
        quarter_kernel,
        "quarters",
        [*codes, got],
        [shape((blocks // 2, rows, units))] * count,
        scratch=[pltpu.SemaphoreType.DMA((2 * count,))],
        specs=[anywhere] * (count + 1),
        out_specs=(anywhere,) * count,
        limit=4,
    )
    return list(moving), got


def fast_body(
    tokens,
    cotangent,
    rms_norm_gain,
    gate_codes,
    gate_block_scale,
    up_codes,
    up_block_scale,
    down_codes,
    down_block_scale,
    up_adapter_in,
    up_adapter_out,
    down_adapter_in,
    down_adapter_out,
    sequence_length_list,
    slot_sequence_index,
):
    rows, local_width = tokens.shape
    blocks, _, units = gate_codes.shape
    block = local_width // blocks
    half = local_width // 2
    rank = up_adapter_in.shape[1]
    total_width = local_width * lax.axis_size("mp")
    n = lax.axis_size("dp")
    more = lax.axis_size("mp") - 1

    (gate_moving, up_moving), front_got = start_shards([gate_codes, up_codes])
    ring, crossed = [], []

    def step(moving, *done):
        k = len(ring)
        waits = ring[k - 2 : k - 1] if k > 1 else []
        waits += ring[k - 3 : k - 2] if k > 2 else []
        waits += crossed[k - 4 : k - 3] if k > 3 else []
        ring.append(ring_step(after(moving, *waits, *done) if waits else moving))
        crossed.append(swap(ring[-1], "grp"))
        return ring[-1]

    step(gate_moving)
    step(up_moving)

    adapters = jnp.concatenate([up_adapter_out, down_adapter_in], axis=0)
    adapters_more = others(after(adapters, ring[1]), "mp")
    tokens_then, cotangent_then, down_then, _ = lax.optimization_barrier(
        (tokens, cotangent, down_codes, ring[1])
    )
    vmem = pl.BlockSpec(memory_space=pltpu.VMEM)
    smem = pl.BlockSpec(memory_space=pltpu.SMEM)
    grad_send, grad, low_out, squares = call(
        lambda *refs: cotangent_kernel(rows * n * lax.axis_size("sub"), *refs),
        "cotangent",
        [cotangent_then, tokens_then, sequence_length_list, slot_sequence_index[None, :], down_adapter_out],
        [shape((rows, half))] * 2 + [shape((rows, rank), F32), shape((rows, LANES), F32)],
        specs=[vmem, vmem, smem, vmem, vmem],
        flops=2 * rows * local_width * rank,
    )
    step(ring[0])
    squares_more = others(squares, "mp")
    down_turned = jnp.swapaxes(down_then, 0, 1)
    (down_moving,), down_got = start_shards([down_turned])
    step(ring[1])
    grad_got = swap(grad_send, "sub")
    step(ring[2], grad, down_moving)
    step(ring[3])
    normed_send, normed, low = call(
        lambda *refs: token_kernel(total_width, *refs),
        "tokens",
        [after(tokens, ring[3]), rms_norm_gain[None, :], up_adapter_in, low_out, squares, *squares_more],
        [shape((rows, half))] * 2 + [shape((rows, 2 * rank), F32)],
        flops=2 * rows * local_width * rank,
    )
    normed_got = swap(normed_send, "sub")
    low_more = others(low, "mp")
    step(down_moving, normed)
    step(ring[6], grad_got, *adapters_more)

    def product(kernel, name, own, got, scale, codes, codes_got, first_got, steps, weight_shape):
        groups = scale.shape[0]
        mine, theirs = call(
            lambda *refs: kernel(first_got, *refs),
            name,
            [own, got, scale, codes, codes_got, *[x for k in steps for x in (ring[k], crossed[k])]],
            [shape((rows, units), F32), shape((rows, units))],
            scratch=[pltpu.VMEM((groups, blocks, LANES), F32), pltpu.VMEM(weight_shape, BF16)],
            flops=4 * rows * half * units,
        )
        total = mine + swap(theirs, "sub").astype(F32)
        return total, others(total.astype(BF16), "mp"), mine

    front = (blocks // 2, block, units)
    half_blocks = blocks // 2
    gate, gate_more, gate_mine = product(
        front_kernel, "gate", normed, normed_got, gate_block_scale.T, gate_codes, front_got, 0,
        range(0, 2 * (n - 1), 2), front,
    )
    up, up_more, up_mine = product(
        front_kernel, "up", normed, normed_got, up_block_scale.T, up_codes, front_got, half_blocks,
        range(1, 2 * (n - 1), 2), front,
    )
    step(ring[7], gate_mine, up_mine)
    small_scratch = [
        pltpu.VMEM((rank, units), BF16),
        pltpu.VMEM((units, rank), BF16),
    ]
    silu, low_hidden, down_in_term = call(
        lambda *refs: hidden_kernel(more, *refs),
        "hidden",
        [gate, up, low, adapters, *gate_more, *up_more, *low_more, *adapters_more],
        [shape((rows, units), F32), shape((rows, rank)), shape(down_adapter_in.shape)],
        scratch=small_scratch,
        limit=8,
    )
    down_out_parts = call(
        down_out_kernel,
        "down_out",
        [low_hidden, swap(low_hidden, "sub"), grad, grad_got],
        [shape((rank, half // n))] * n,
        flops=4 * rows * half * rank,
    )
    seen = []
    down_out_blocks = ring_gather(ring_sum(down_out_parts, seen))
    (normed_t,) = call(
        transpose_kernel,
        "transpose",
        [normed, after(normed_got, low_hidden)],
        [shape((half, 2 * rows))],
        limit=32,
    )

    back, back_more, _ = product(
        back_kernel, "back", after(grad, down_out_parts[0]), grad_got, down_block_scale, down_turned, down_got, 0,
        range(2 * (n - 1), 3 * (n - 1)), (units, half),
    )
    low_grad, up_out_term = call(
        lambda *refs: up_grad_kernel(more, *refs),
        "up_grad",
        [after(back, seen[0]), silu, low, adapters, *back_more, *low_more, *adapters_more],
        [shape((rows, rank)), shape(up_adapter_out.shape)],
        scratch=small_scratch,
        limit=8,
    )
    extra = 2 * rank // n
    up_in_parts = call(
        up_in_kernel,
        "up_in",
        [low_grad, swap(low_grad, "sub"), normed_t, up_out_term, down_in_term],
        [shape((half // n + extra, rank))] * n,
        flops=4 * rows * half * rank,
    )
    up_in_blocks = ring_gather(ring_sum(up_in_parts))

    anywhere = pl.BlockSpec(memory_space=pl.ANY)
    (down_out_gradient,) = call(
        lambda *refs: down_out_place_kernel(n, *refs),
        "down_out_place",
        [*down_out_blocks[0], *down_out_blocks[1]],
        [shape((rank, local_width))],
        scratch=[pltpu.SemaphoreType.DMA((2 * n,))],
        specs=[anywhere] * (2 * n),
        out_specs=(anywhere,),
        limit=4,
    )
    up_in_gradient, up_out_gradient, down_in_gradient = call(
        lambda *refs: up_in_place_kernel(n, *refs),
        "up_in_place",
        [*up_in_blocks[0], *up_in_blocks[1]],
        [shape((local_width, rank)), shape(up_adapter_out.shape), shape(down_adapter_in.shape)],
        scratch=[pltpu.VMEM((2, 2 * rank, rank), BF16), pltpu.SemaphoreType.DMA((4 * n,))],
        specs=[anywhere] * (2 * n),
        out_specs=(anywhere, vmem, vmem),
        limit=4,
    )
    return up_in_gradient, up_out_gradient, down_in_gradient, down_out_gradient


def general_body(
    tokens,
    cotangent,
    rms_norm_gain,
    gate_codes,
    gate_block_scale,
    up_codes,
    up_block_scale,
    down_codes,
    down_block_scale,
    up_adapter_in,
    up_adapter_out,
    down_adapter_in,
    down_adapter_out,
    sequence_length_list,
    slot_sequence_index,
):
    rows = tokens.shape[0]
    local_width = tokens.shape[1]
    block = gate_block_scale.shape[0] and local_width // gate_codes.shape[0]
    blocks_here = gate_codes.shape[0]
    total_width = local_width * lax.axis_size("mp")
    own_squares = jnp.sum(jnp.square(tokens.astype(jnp.float32)), axis=-1, keepdims=True)
    squares = lax.psum(own_squares, "mp") / total_width
    inv_rms = lax.rsqrt(squares + EPS)
    local_normed_input = (
        tokens.astype(jnp.float32) * inv_rms * rms_norm_gain.astype(jnp.float32)[None, :]
    ).astype(jnp.bfloat16)
    seq_count = sequence_length_list.shape[1]
    longest = rows // seq_count
    total = rows * lax.axis_size("dp") * lax.axis_size("sub")
    ratios = longest / sequence_length_list[0].astype(jnp.float32)
    match = slot_sequence_index[:, None] == jnp.arange(seq_count, dtype=jnp.int32)[None, :]
    token_weight = jnp.sum(jnp.where(match, ratios[None, :], jnp.float32(0.0)), axis=-1)
    token_weight = token_weight * jnp.float32(1.0 / math.sqrt(total))
    local_output = (cotangent.astype(jnp.float32) * token_weight[:, None]).astype(jnp.bfloat16)
    partial_up = jnp.dot(local_normed_input, up_adapter_in, preferred_element_type=jnp.float32)
    partial_output = contract_dims(local_output, down_adapter_out, 1, 1)
    up_adapter_rank, output_adapter_rank = lax.psum((partial_up, partial_output), "mp")
    up_adapter_rank = up_adapter_rank.astype(jnp.bfloat16)
    output_adapter_rank = output_adapter_rank.astype(jnp.bfloat16)
    normed_blocks = local_normed_input.reshape(rows, blocks_here, block)
    out_blocks = local_output.reshape(rows, blocks_here, block)
    wide_gate = jnp.repeat(gate_block_scale.astype(jnp.float32), block, axis=1)[:, None, :]
    wide_up = jnp.repeat(up_block_scale.astype(jnp.float32), block, axis=1)[:, None, :]
    wide_down = jnp.repeat(down_block_scale.astype(jnp.float32), block, axis=0)
    dims_front = (((1, 2), (0, 1)), ((), ()))
    dims_back = (((1, 2), (1, 2)), ((), ()))
    quant_g = lax.all_gather(gate_codes, ("dp", "sub"), axis=1, tiled=True)
    quant_u = lax.all_gather(up_codes, ("dp", "sub"), axis=1, tiled=True)
    weight_g = (quant_g.astype(jnp.float32) * wide_gate).astype(jnp.bfloat16)
    weight_u = (quant_u.astype(jnp.float32) * wide_up).astype(jnp.bfloat16)
    gate_next = lax.dot_general(
        normed_blocks, weight_g, dims_front, preferred_element_type=jnp.float32
    )
    up_next = lax.dot_general(
        normed_blocks, weight_u, dims_front, preferred_element_type=jnp.float32
    )
    gate, base_up_projected = (
        lax.psum_scatter(gate_next, "mp", scatter_dimension=1, tiled=True),
        lax.psum_scatter(up_next, "mp", scatter_dimension=1, tiled=True),
    )
    up_projected = base_up_projected + ADAPTER_SCALE * jnp.dot(
        up_adapter_rank, up_adapter_out, preferred_element_type=jnp.float32
    )
    silu_gate = jax.nn.silu(gate)
    hidden_units = (silu_gate * up_projected).astype(jnp.bfloat16)
    partial_hidden = jnp.dot(hidden_units, down_adapter_in, preferred_element_type=jnp.float32)
    hidden_adapter_rank = lax.psum(partial_hidden, "mp").astype(jnp.bfloat16)
    weight_d = (
        lax.all_gather(down_codes, ("dp", "sub"), axis=0, tiled=True).astype(jnp.float32)
        * wide_down[:, :, None]
    ).astype(jnp.bfloat16)
    back_part = lax.dot_general(out_blocks, weight_d, dims_back, preferred_element_type=jnp.float32)
    base_backward = lax.psum_scatter(back_part, "mp", scatter_dimension=1, tiled=True)
    hidden_gradient = base_backward + ADAPTER_SCALE * contract_dims(
        output_adapter_rank, down_adapter_in, 1, 1
    )
    up_gradient = (hidden_gradient * silu_gate).astype(jnp.bfloat16)
    partial_gradient = contract_dims(up_gradient, up_adapter_out, 1, 1)
    up_adapter_rank_gradient = lax.psum(partial_gradient, "mp").astype(jnp.bfloat16)
    up_in_term = ADAPTER_SCALE * contract_dims(local_normed_input, up_adapter_rank_gradient, 0, 0)
    up_out_term = ADAPTER_SCALE * contract_dims(up_adapter_rank, up_gradient, 0, 0)
    down_in_term = ADAPTER_SCALE * contract_dims(hidden_units, output_adapter_rank, 0, 0)
    down_out_term = ADAPTER_SCALE * contract_dims(hidden_adapter_rank, local_output, 0, 0)
    sum_up_a, sum_up_b, sum_down_a, sum_down_b = lax.psum(
        (up_in_term, up_out_term, down_in_term, down_out_term), ("dp", "sub")
    )
    return (
        sum_up_a.astype(jnp.bfloat16),
        sum_up_b.astype(jnp.bfloat16),
        sum_down_a.astype(jnp.bfloat16),
        sum_down_b.astype(jnp.bfloat16),
    )


def body(tokens, cotangent, rms_norm_gain, gate_codes, *rest):
    whole_tiles = gate_codes.shape[1] % ROW_TILE == 0
    form = fast_body if whole_tiles else general_body
    return form(tokens, cotangent, rms_norm_gain, gate_codes, *rest)


def solution(mesh):
    placed = (
        P(("grp", "dp", "sub"), "mp"),
        P(("grp", "dp", "sub"), "mp"),
        P("mp"),
        P("mp", ("dp", "sub"), None),
        P("mp", None),
        P("mp", ("dp", "sub"), None),
        P("mp", None),
        P(("dp", "sub"), "mp", None),
        P(None, "mp"),
        P(("grp", "mp"), None),
        P("grp", "mp"),
        P(("grp", "mp"), None),
        P("grp", "mp"),
        P(("grp", "dp", "sub"), None),
        P(("grp", "dp", "sub")),
    )
    return jax.shard_map(
        body,
        mesh=mesh,
        in_specs=placed,
        out_specs=(P(("grp", "mp"), None), P("grp", "mp"), P(("grp", "mp"), None), P("grp", "mp")),
        check_vma=False,
    )
```

```python
import math

import jax
import jax.numpy as jnp
from jax import lax
from jax.experimental import pallas as pl
from jax.experimental.pallas import tpu as pltpu
from jax.sharding import PartitionSpec as P

ADAPTER_SCALE = 2.0
EPS = 1e-05
ROW_TILE = 16
LANES = 128
MIB = 1024 * 1024

F32 = jnp.float32
BF16 = jnp.bfloat16


def contract_dims(left, right, left_dim, right_dim):
    return lax.dot_general(
        left, right, (((left_dim,), (right_dim,)), ((), ())), preferred_element_type=F32
    )


def dot(left, right):
    return jnp.dot(left, right, preferred_element_type=F32)


def ring_at(pos, n):
    if isinstance(pos, int):
        return 0 if pos == 0 else (2 * pos - 1 if 2 * pos <= n else 2 * (n - pos))
    return jnp.where(pos == 0, 0, jnp.where(2 * pos <= n, 2 * pos - 1, 2 * (n - pos)))


def ring_position():
    n = lax.axis_size("dp")
    place = lax.axis_index("dp")
    odd = lax.rem(place, 2) == 1
    return jnp.where(place == 0, 0, jnp.where(odd, (place + 1) // 2, n - place // 2))


def ring_step(x):
    n = lax.axis_size("dp")
    return lax.ppermute(x, "dp", [(ring_at(i, n), ring_at((i + 1) % n, n)) for i in range(n)])


def swap(x, axis):
    return lax.ppermute(x, axis, [(0, 1), (1, 0)])


def others(x, axis):
    n = lax.axis_size(axis)
    return [lax.ppermute(x, axis, [(i, (i + k) % n) for i in range(n)]) for k in range(1, n)]


def after(x, *done):
    return lax.optimization_barrier((x, *done))[0]


def add(*terms):
    return sum(t.astype(F32) for t in terms).astype(BF16)


def ring_all(parts, seen, gates=()):
    n = lax.axis_size("dp")

    def step(x):
        k = len(seen)
        seen.append(ring_step(after(x, gates[k]) if k < len(gates) else x))
        return seen[-1]

    total = parts[0]
    for part in parts[1:]:
        total = add(step(total), part)
    blocks = [total]
    for _ in range(n - 1):
        blocks.append(step(blocks[-1]))
    return blocks, [swap(b, "sub") for b in blocks]


def call(kernel, name, args, out_shape, scratch=(), specs=None, limit=24, flops=0, out_specs=None):
    vmem = pl.BlockSpec(memory_space=pltpu.VMEM)
    moved = sum(a.size * a.dtype.itemsize for a in args) + sum(
        math.prod(s.shape) * s.dtype.itemsize for s in out_shape
    )
    return pl.pallas_call(
        kernel,
        out_shape=tuple(out_shape),
        in_specs=specs or [vmem] * len(args),
        out_specs=out_specs or tuple([vmem] * len(out_shape)),
        scratch_shapes=list(scratch),
        compiler_params=pltpu.CompilerParams(vmem_limit_bytes=limit * MIB),
        cost_estimate=pl.CostEstimate(flops=flops, bytes_accessed=moved, transcendentals=0),
        name=name,
    )(*args)


def shape(dims, dtype=BF16):
    return jax.ShapeDtypeStruct(tuple(dims), dtype)


def scaled_halves(wide, low_ref, cols, scaled, product, send_ref, own_ref):
    half = send_ref.shape[1]
    step = half // 4
    sub = lax.axis_index("sub")
    low_ref[:, cols] = jnp.zeros((wide.shape[0], LANES), F32)
    for which, out_ref in ((1 - sub, send_ref), (sub, own_ref)):

        @pl.loop(0, half // step)
        def _(j, which=which, out_ref=out_ref):
            first = pl.multiple_of(which * half + j * step, step)
            parts = []
            for i in range(step // LANES):
                tile = pl.ds(pl.multiple_of(first + i * LANES, LANES), LANES)
                parts.append(scaled(wide[:, tile].astype(F32), tile).astype(BF16))
            value = jnp.concatenate(parts, axis=1)
            out_ref[:, pl.ds(pl.multiple_of(j * step, step), step)] = value
            low_ref[:, cols] += product(value, pl.ds(first, step))


def cotangent_kernel(
    total, cotangent, tokens, lengths, slots, adapter, send_ref, own_ref, low_ref, square_ref
):
    rows, width = cotangent.shape
    index = jnp.broadcast_to(slots[...], (LANES, rows))
    weight = jnp.zeros((LANES, rows), F32)
    for s in range(lengths.shape[1]):
        length = jnp.full((LANES, rows), lengths[0, s], jnp.int32).astype(F32)
        weight = weight + jnp.where(index == s, (rows // lengths.shape[1]) / length, 0.0)
    row = (weight * F32(1.0 / math.sqrt(total))).T

    square_ref[...] = jnp.zeros_like(square_ref)

    @pl.loop(0, width // (8 * LANES))
    def _(j):
        squares = square_ref[...]
        for i in range(8):
            tile = pl.ds(pl.multiple_of((j * 8 + i) * LANES, LANES), LANES)
            squares = squares + jnp.square(tokens[:, tile].astype(F32))
        square_ref[...] = squares

    square_ref[...] = jnp.broadcast_to(
        jnp.sum(square_ref[...], axis=1, keepdims=True), square_ref.shape
    )
    scaled_halves(
        cotangent,
        low_ref,
        slice(None),
        lambda tile, cols: tile * row,
        lambda value, cols: contract_dims(value, adapter[:, cols], 1, 1),
        send_ref,
        own_ref,
    )


def token_kernel(total_width, tokens, gain, adapter, low_out, squares, *refs):
    squares_more, (send_ref, own_ref, low_ref) = refs[:-3], refs[-3:]
    rank = adapter.shape[1]
    total = squares[...]
    for ref in squares_more:
        total = total + ref[...]
    row = lax.rsqrt(total / total_width + EPS)
    low_ref[:, rank:] = low_out[...]
    scaled_halves(
        tokens,
        low_ref,
        slice(0, rank),
        lambda tile, cols: tile * row * gain[:, cols].astype(F32),
        lambda value, cols: dot(value, adapter[cols, :]),
        send_ref,
        own_ref,
    )


def transpose_kernel(own, got, out_ref):
    rows, step = own.shape[0], out_ref.shape[0]
    for i, ref in enumerate((own, got)):
        out_ref[:, i * rows : (i + 1) * rows] = ref[...].astype(F32).T.astype(BF16)


def widen(scale, wide):
    for g in range(scale.shape[0]):
        row = scale[g : g + 1, :].astype(F32)
        wide[g] = jnp.broadcast_to(row, (LANES, row.shape[1])).T


def place_shards(codes, got, first_got, moved, store):
    n = lax.axis_size("dp")
    sub, grp, place = (lax.axis_index(a) for a in ("sub", "grp", "dp"))
    pos = ring_position()
    blocks = codes.shape[0] // 2
    quarter = blocks // 2

    @pl.loop(0, blocks, unroll=4)
    def _(b):
        store(b, place * 2 + sub, codes[sub * blocks + b])
        store(b, place * 2 + 1 - sub, got[first_got + b])

    for k in range(n - 1):
        there = ring_at(lax.rem(pos - k - 1 + n, n), n)
        for which in range(2):
            piece = moved[2 * k + which]
            start = (grp if which == 0 else 1 - grp) * quarter

            @pl.loop(0, quarter, unroll=4)
            def _(b, piece=piece, start=start, there=there):
                store(start + b, there * 2 + sub, piece[b])
                store(start + b, there * 2 + 1 - sub, piece[quarter + b])


def front_kernel(first_got, own, got, scale, codes, codes_got, *refs):
    moved, (mine_ref, theirs_ref, wide, weight) = refs[:-4], refs[-4:]
    blocks, rows, units = codes.shape
    first = lax.axis_index("sub") * (blocks // 2)
    widen(scale, wide)

    def store(b, shard, piece):
        at = pl.ds(pl.multiple_of(shard * rows, ROW_TILE), rows)
        for g in range(units // LANES):
            cols = slice(g * LANES, (g + 1) * LANES)
            factor = wide[g * wide.shape[0] * LANES // units, pl.ds(first + b, 1), :]
            weight[b, at, cols] = (piece[:, cols].astype(F32) * factor).astype(BF16)

    place_shards(codes, codes_got, first_got, moved, store)
    matrix = weight[...].reshape(-1, units)
    mine_ref[...] = dot(own[...], matrix)
    theirs_ref[...] = dot(got[...], matrix).astype(BF16)


def back_kernel(first_got, own, got, scale, codes, codes_got, *refs):
    moved, (mine_ref, theirs_ref, wide, weight) = refs[:-4], refs[-4:]
    blocks, rows, block = codes.shape
    first = lax.axis_index("sub") * (blocks // 2)
    per_group = weight.shape[0] // wide.shape[0]
    widen(scale, wide)

    def store(b, shard, piece):
        at = pl.multiple_of(shard * rows, ROW_TILE)
        factor = wide[at // per_group, pl.ds(first + b, 1), :]
        cols = pl.ds(pl.multiple_of(b * block, block), block)
        weight[pl.ds(at, rows), cols] = (piece.astype(F32) * factor).astype(BF16)

    place_shards(codes, codes_got, first_got, moved, store)
    matrix = weight[...]
    mine_ref[...] = contract_dims(own[...], matrix, 1, 1)
    theirs_ref[...] = contract_dims(got[...], matrix, 1, 1).astype(BF16)


def place_own(scratch, own, more, axis):
    n = len(more) + 1
    size = own.shape[axis]
    for k, ref in enumerate((own, *more)):
        at = pl.ds(pl.multiple_of(lax.rem(lax.axis_index("mp") + n - k, n) * size, size), size)
        if axis == 0:
            scratch[at, :] = ref[...]
        else:
            scratch[:, at] = ref[...]


def own_units(full, ref, axis):
    size = ref.shape[axis]
    for i in range(full.shape[axis] // size):

        @pl.when(lax.axis_index("mp") == i)
        def _(i=i):
            ref[...] = lax.slice_in_dim(full, i * size, (i + 1) * size, axis=axis).astype(BF16)


def low_sums(low, low_more):
    total = low[...]
    for ref in low_more:
        total = total + ref[...]
    half = total.shape[1] // 2
    return total[:, :half].astype(BF16), total[:, half:].astype(BF16)


def gather_adapters(adapters, adapters_more, up_out_all, down_in_all):
    rank = up_out_all.shape[0]
    place_own(up_out_all, adapters.at[:rank], [r.at[:rank] for r in adapters_more], 1)
    place_own(down_in_all, adapters.at[rank:], [r.at[rank:] for r in adapters_more], 0)


def hidden_kernel(more, gate, up, low, adapters, *refs):
    gate_more, up_more, low_more, adapters_more = (refs[i * more : (i + 1) * more] for i in range(4))
    silu_ref, low_ref, down_in_term, up_out_all, down_in_all = refs[4 * more :]
    gather_adapters(adapters, adapters_more, up_out_all, down_in_all)
    low_up, low_out = low_sums(low, low_more)
    gate_sum, up_sum = gate[...], up[...]
    for ref in gate_more:
        gate_sum = gate_sum + ref[...].astype(F32)
    for ref in up_more:
        up_sum = up_sum + ref[...].astype(F32)
    up_sum = up_sum + ADAPTER_SCALE * dot(low_up, up_out_all[...])
    silu = gate_sum * jax.nn.sigmoid(gate_sum)
    silu_ref[...] = silu
    hidden = (silu * up_sum).astype(BF16)
    low_ref[...] = (ADAPTER_SCALE * dot(hidden, down_in_all[...])).astype(BF16)
    hidden_t = hidden.astype(F32).T.astype(BF16)
    own_units(ADAPTER_SCALE * dot(hidden_t, low_out), down_in_term, 0)


def up_grad_kernel(more, back, silu, low, adapters, *refs):
    back_more, low_more, adapters_more = (refs[i * more : (i + 1) * more] for i in range(3))
    low_ref, up_out_term, up_out_all, down_in_all = refs[3 * more :]
    gather_adapters(adapters, adapters_more, up_out_all, down_in_all)
    low_up, low_out = low_sums(low, low_more)
    total = back[...]
    for ref in back_more:
        total = total + ref[...].astype(F32)
    total = total + ADAPTER_SCALE * contract_dims(low_out, down_in_all[...], 1, 1)
    up_grad = (total * silu[...]).astype(BF16)
    low_ref[...] = (ADAPTER_SCALE * contract_dims(up_grad, up_out_all[...], 1, 1)).astype(BF16)
    low_up_t = low_up.astype(F32).T.astype(BF16)
    own_units(ADAPTER_SCALE * dot(low_up_t, up_grad), up_out_term, 1)


def down_out_kernel(low, low_got, grad, grad_got, *out_refs):
    n = len(out_refs)
    pos = ring_position()
    low_t = jnp.concatenate([low[...], low_got[...]], axis=0).astype(F32).T.astype(BF16)
    rows = low.shape[0]
    for k, ref in enumerate(out_refs):
        size = ref.shape[1]
        at = pl.ds(pl.multiple_of(lax.rem(pos - 1 - k + 2 * n, n) * size, size), size)
        ref[...] = (
            dot(low_t[:, :rows], grad[:, at]) + dot(low_t[:, rows:], grad_got[:, at])
        ).astype(BF16)


def up_in_kernel(low, low_got, normed_t, up_out_term, down_in_term, *out_refs):
    n = len(out_refs)
    pos = ring_position()
    size = normed_t.shape[0] // n
    extra = out_refs[0].shape[0] - size
    both = jnp.concatenate([low[...], low_got[...]], axis=0)
    for k, ref in enumerate(out_refs):
        block = lax.rem(pos - 1 - k + 2 * n, n)
        at = pl.ds(pl.multiple_of(block * size, size), size)
        ref[pl.ds(0, size), :] = dot(normed_t[at, :], both).astype(BF16)
        per = up_out_term.shape[0] // extra
        index = pl.ds(pl.multiple_of(lax.rem(block, per) * extra, extra), extra)

        @pl.when(block < per)
        def _(ref=ref, index=index):
            ref[pl.ds(size, extra), :] = up_out_term[index, :]

        @pl.when(block >= per)
        def _(ref=ref, index=index):
            ref[pl.ds(size, extra), :] = down_in_term[index, :]


def copy_all(copies):
    for c in copies:
        c.start()
    for c in copies:
        c.wait()


def down_out_place_kernel(n, *refs):
    pieces, out_ref, sems = refs[: 2 * n], refs[2 * n], refs[2 * n + 1]
    pos, sub = ring_position(), lax.axis_index("sub")
    copies = []
    for i, piece in enumerate(pieces):
        half = sub if i < n else 1 - sub
        block = lax.rem(pos - i % n + n, n)
        size = piece.shape[1]
        at = pl.ds(pl.multiple_of((half * n + block) * size, size), size)
        copies.append(pltpu.make_async_copy(piece, out_ref.at[:, at], sems.at[i]))
    copy_all(copies)


def up_in_place_kernel(n, *refs):
    pieces = refs[: 2 * n]
    out_ref, up_out_ref, down_in_ref, small, sems = refs[2 * n :]
    pos, sub = ring_position(), lax.axis_index("sub")
    size = out_ref.shape[0] // (2 * n)
    extra = pieces[0].shape[0] - size
    copies = []
    for i, piece in enumerate(pieces):
        half = sub if i < n else 1 - sub
        block = lax.rem(pos - i % n + n, n)
        at = pl.ds(pl.multiple_of((half * n + block) * size, size), size)
        copies.append(
            pltpu.make_async_copy(piece.at[pl.ds(0, size), :], out_ref.at[at, :], sems.at[2 * i])
        )
        at = pl.ds(pl.multiple_of(block * extra, extra), extra)
        copies.append(
            pltpu.make_async_copy(
                piece.at[pl.ds(size, extra), :], small.at[i // n, at, :], sems.at[2 * i + 1]
            )
        )
    copy_all(copies)
    total = (small[0].astype(F32) + small[1].astype(F32)).astype(BF16)
    rows = up_out_ref.shape[0]
    up_out_ref[...] = total[:rows]
    down_in_ref[...] = total[rows:]


def half_kernel(*refs):
    sources, out_ref, sems = refs[:-2], refs[-2], refs[-1]
    other = 1 - lax.axis_index("sub")
    half = sources[0].shape[0] // 2
    copy_all(
        [
            pltpu.make_async_copy(
                ref.at[pl.ds(other * half, half)], out_ref.at[pl.ds(i * half, half)], sems.at[i]
            )
            for i, ref in enumerate(sources)
        ]
    )


def quarter_kernel(*refs):
    count = (len(refs) - 2) // 2
    sources, got, out_refs, sems = refs[:count], refs[count], refs[count + 1 : -1], refs[-1]
    sub, grp = lax.axis_index("sub"), lax.axis_index("grp")
    half = sources[0].shape[0] // 2
    quarter = half // 2
    copies = []
    for i, (ref, out_ref) in enumerate(zip(sources, out_refs)):
        own = ref.at[pl.ds(sub * half + grp * quarter, quarter)]
        theirs = got.at[pl.ds(i * half + grp * quarter, quarter)]
        for k, source in enumerate((own, theirs)):
            copies.append(
                pltpu.make_async_copy(
                    source, out_ref.at[pl.ds(k * quarter, quarter)], sems.at[2 * i + k]
                )
            )
    copy_all(copies)


def start_shards(codes):
    blocks, rows, units = codes[0].shape
    count = len(codes)
    anywhere = pl.BlockSpec(memory_space=pl.ANY)
    (send,) = call(
        half_kernel,
        "halves",
        codes,
        [shape((count * blocks // 2, rows, units))],
        scratch=[pltpu.SemaphoreType.DMA((count,))],
        specs=[anywhere] * count,
        out_specs=(anywhere,),
        limit=60,
    )
    got = swap(send, "sub")
    moving = call(
        quarter_kernel,
        "quarters",
        [*codes, got],
        [shape((blocks // 2, rows, units))] * count,
        scratch=[pltpu.SemaphoreType.DMA((2 * count,))],
        specs=[anywhere] * (count + 1),
        out_specs=(anywhere,) * count,
        limit=60,
    )
    return list(moving), got


def fast_body(
    tokens,
    cotangent,
    rms_norm_gain,
    gate_codes,
    gate_block_scale,
    up_codes,
    up_block_scale,
    down_codes,
    down_block_scale,
    up_adapter_in,
    up_adapter_out,
    down_adapter_in,
    down_adapter_out,
    sequence_length_list,
    slot_sequence_index,
):
    rows, local_width = tokens.shape
    blocks, _, units = gate_codes.shape
    block = local_width // blocks
    half = local_width // 2
    rank = up_adapter_in.shape[1]
    total_width = local_width * lax.axis_size("mp")
    n = lax.axis_size("dp")
    more = lax.axis_size("mp") - 1

    (gate_moving, up_moving), front_got = start_shards([gate_codes, up_codes])
    ring, crossed = [], []

    def step(moving, *done):
        ring.append(ring_step(after(moving, *done) if done else moving))
        crossed.append(swap(ring[-1], "grp"))

    step(gate_moving)
    step(up_moving)

    vmem = pl.BlockSpec(memory_space=pltpu.VMEM)
    smem = pl.BlockSpec(memory_space=pltpu.SMEM)
    lengths = after(sequence_length_list, gate_moving, up_moving)
    grad_send, grad, low_out, squares = call(
        lambda *refs: cotangent_kernel(rows * n * lax.axis_size("sub"), *refs),
        "cotangent",
        [cotangent, tokens, lengths, slot_sequence_index[None, :], down_adapter_out],
        [shape((rows, half))] * 2 + [shape((rows, rank), F32), shape((rows, LANES), F32)],
        specs=[vmem, vmem, smem, vmem, vmem],
        flops=2 * rows * local_width * rank,
    )
    squares_more = others(squares, "mp")
    step(ring[0], ring[1], grad)
    step(ring[1], ring[0], grad)
    normed_send, normed, low = call(
        lambda *refs: token_kernel(total_width, *refs),
        "tokens",
        [tokens, rms_norm_gain[None, :], up_adapter_in, low_out, after(squares, *ring[:2]), *squares_more],
        [shape((rows, half))] * 2 + [shape((rows, 2 * rank), F32)],
        flops=2 * rows * local_width * rank,
    )
    grad_got = swap(grad_send, "sub")
    normed_got = swap(normed_send, "sub")
    low_more = others(low, "mp")
    step(ring[2], ring[3], normed, *crossed[:2])
    step(ring[3], ring[2], normed, *crossed[:2])
    down_turned = jnp.swapaxes(after(down_codes, *ring[2:4]), 0, 1)
    (down_moving,), down_got = start_shards([down_turned])
    adapters = jnp.concatenate([up_adapter_out, down_adapter_in], axis=0)
    adapters_more = others(after(adapters, *ring[2:4]), "mp")
    step(down_moving, *ring[4:6], *crossed[2:4], grad_got, normed_got, *low_more, *adapters_more)
    step(ring[6])

    def product(kernel, name, own, got, scale, codes, codes_got, first_got, steps, weight_shape):
        groups = scale.shape[0]
        mine, theirs = call(
            lambda *refs: kernel(first_got, *refs),
            name,
            [own, got, scale, codes, codes_got, *[x for k in steps for x in (ring[k], crossed[k])]],
            [shape((rows, units), F32), shape((rows, units))],
            scratch=[pltpu.VMEM((groups, blocks, LANES), F32), pltpu.VMEM(weight_shape, BF16)],
            flops=4 * rows * half * units,
        )
        total = mine + swap(theirs, "sub").astype(F32)
        return total, others(total.astype(BF16), "mp"), mine

    front = (blocks // 2, block, units)
    half_blocks = blocks // 2
    gate, gate_more, gate_mine = product(
        front_kernel, "gate", normed, normed_got, gate_block_scale.T, gate_codes, front_got, 0,
        range(0, 2 * (n - 1), 2), front,
    )
    up, up_more, up_mine = product(
        front_kernel, "up", normed, normed_got, up_block_scale.T, up_codes, front_got, half_blocks,
        range(1, 2 * (n - 1), 2), front,
    )
    step(ring[7], gate_mine, up_mine, crossed[6])
    small_scratch = [
        pltpu.VMEM((rank, units), BF16),
        pltpu.VMEM((units, rank), BF16),
    ]
    silu, low_hidden, down_in_term = call(
        lambda *refs: hidden_kernel(more, *refs),
        "hidden",
        [gate, up, low, adapters, *gate_more, *up_more, *low_more, *adapters_more],
        [shape((rows, units), F32), shape((rows, rank)), shape(down_adapter_in.shape)],
        scratch=small_scratch,
        limit=8,
    )
    down_out_parts = call(
        down_out_kernel,
        "down_out",
        [low_hidden, swap(low_hidden, "sub"), grad, grad_got],
        [shape((rank, half // n))] * n,
        flops=4 * rows * half * rank,
    )
    seen = []
    down_out_blocks = ring_all(down_out_parts, seen)
    (normed_t,) = call(
        transpose_kernel,
        "transpose",
        [normed, after(normed_got, low_hidden)],
        [shape((half, 2 * rows))],
        limit=32,
    )

    back, back_more, _ = product(
        back_kernel, "back", after(grad, seen[0]), grad_got, down_block_scale, down_turned, down_got, 0,
        range(2 * (n - 1), 3 * (n - 1)), (units, half),
    )
    low_grad, up_out_term = call(
        lambda *refs: up_grad_kernel(more, *refs),
        "up_grad",
        [back, silu, low, adapters, *back_more, *low_more, *adapters_more],
        [shape((rows, rank)), shape(up_adapter_out.shape)],
        scratch=small_scratch,
        limit=8,
    )
    extra = 2 * rank // n
    up_in_parts = call(
        up_in_kernel,
        "up_in",
        [after(low_grad, seen[1]), swap(low_grad, "sub"), normed_t, up_out_term, down_in_term],
        [shape((half // n + extra, rank))] * n,
        flops=4 * rows * half * rank,
    )
    up_in_blocks = ring_all(up_in_parts, [], seen[1:])

    anywhere = pl.BlockSpec(memory_space=pl.ANY)
    (down_out_gradient,) = call(
        lambda *refs: down_out_place_kernel(n, *refs),
        "down_out_place",
        [*down_out_blocks[0], *down_out_blocks[1]],
        [shape((rank, local_width))],
        scratch=[pltpu.SemaphoreType.DMA((2 * n,))],
        specs=[anywhere] * (2 * n),
        out_specs=(anywhere,),
        limit=4,
    )
    up_in_gradient, up_out_gradient, down_in_gradient = call(
        lambda *refs: up_in_place_kernel(n, *refs),
        "up_in_place",
        [*up_in_blocks[0], *up_in_blocks[1]],
        [shape((local_width, rank)), shape(up_adapter_out.shape), shape(down_adapter_in.shape)],
        scratch=[pltpu.VMEM((2, 2 * rank, rank), BF16), pltpu.SemaphoreType.DMA((4 * n,))],
        specs=[anywhere] * (2 * n),
        out_specs=(anywhere, vmem, vmem),
        limit=4,
    )
    return up_in_gradient, up_out_gradient, down_in_gradient, down_out_gradient


def general_body(
    tokens,
    cotangent,
    rms_norm_gain,
    gate_codes,
    gate_block_scale,
    up_codes,
    up_block_scale,
    down_codes,
    down_block_scale,
    up_adapter_in,
    up_adapter_out,
    down_adapter_in,
    down_adapter_out,
    sequence_length_list,
    slot_sequence_index,
):
    rows = tokens.shape[0]
    local_width = tokens.shape[1]
    block = gate_block_scale.shape[0] and local_width // gate_codes.shape[0]
    blocks_here = gate_codes.shape[0]
    total_width = local_width * lax.axis_size("mp")
    own_squares = jnp.sum(jnp.square(tokens.astype(jnp.float32)), axis=-1, keepdims=True)
    squares = lax.psum(own_squares, "mp") / total_width
    inv_rms = lax.rsqrt(squares + EPS)
    local_normed_input = (
        tokens.astype(jnp.float32) * inv_rms * rms_norm_gain.astype(jnp.float32)[None, :]
    ).astype(jnp.bfloat16)
    seq_count = sequence_length_list.shape[1]
    longest = rows // seq_count
    total = rows * lax.axis_size("dp") * lax.axis_size("sub")
    ratios = longest / sequence_length_list[0].astype(jnp.float32)
    match = slot_sequence_index[:, None] == jnp.arange(seq_count, dtype=jnp.int32)[None, :]
    token_weight = jnp.sum(jnp.where(match, ratios[None, :], jnp.float32(0.0)), axis=-1)
    token_weight = token_weight * jnp.float32(1.0 / math.sqrt(total))
    local_output = (cotangent.astype(jnp.float32) * token_weight[:, None]).astype(jnp.bfloat16)
    partial_up = jnp.dot(local_normed_input, up_adapter_in, preferred_element_type=jnp.float32)
    partial_output = contract_dims(local_output, down_adapter_out, 1, 1)
    up_adapter_rank, output_adapter_rank = lax.psum((partial_up, partial_output), "mp")
    up_adapter_rank = up_adapter_rank.astype(jnp.bfloat16)
    output_adapter_rank = output_adapter_rank.astype(jnp.bfloat16)
    normed_blocks = local_normed_input.reshape(rows, blocks_here, block)
    out_blocks = local_output.reshape(rows, blocks_here, block)
    wide_gate = jnp.repeat(gate_block_scale.astype(jnp.float32), block, axis=1)[:, None, :]
    wide_up = jnp.repeat(up_block_scale.astype(jnp.float32), block, axis=1)[:, None, :]
    wide_down = jnp.repeat(down_block_scale.astype(jnp.float32), block, axis=0)
    dims_front = (((1, 2), (0, 1)), ((), ()))
    dims_back = (((1, 2), (1, 2)), ((), ()))
    quant_g = lax.all_gather(gate_codes, ("dp", "sub"), axis=1, tiled=True)
    quant_u = lax.all_gather(up_codes, ("dp", "sub"), axis=1, tiled=True)
    weight_g = (quant_g.astype(jnp.float32) * wide_gate).astype(jnp.bfloat16)
    weight_u = (quant_u.astype(jnp.float32) * wide_up).astype(jnp.bfloat16)
    gate_next = lax.dot_general(
        normed_blocks, weight_g, dims_front, preferred_element_type=jnp.float32
    )
    up_next = lax.dot_general(
        normed_blocks, weight_u, dims_front, preferred_element_type=jnp.float32
    )
    gate, base_up_projected = (
        lax.psum_scatter(gate_next, "mp", scatter_dimension=1, tiled=True),
        lax.psum_scatter(up_next, "mp", scatter_dimension=1, tiled=True),
    )
    up_projected = base_up_projected + ADAPTER_SCALE * jnp.dot(
        up_adapter_rank, up_adapter_out, preferred_element_type=jnp.float32
    )
    silu_gate = jax.nn.silu(gate)
    hidden_units = (silu_gate * up_projected).astype(jnp.bfloat16)
    partial_hidden = jnp.dot(hidden_units, down_adapter_in, preferred_element_type=jnp.float32)
    hidden_adapter_rank = lax.psum(partial_hidden, "mp").astype(jnp.bfloat16)
    weight_d = (
        lax.all_gather(down_codes, ("dp", "sub"), axis=0, tiled=True).astype(jnp.float32)
        * wide_down[:, :, None]
    ).astype(jnp.bfloat16)
    back_part = lax.dot_general(out_blocks, weight_d, dims_back, preferred_element_type=jnp.float32)
    base_backward = lax.psum_scatter(back_part, "mp", scatter_dimension=1, tiled=True)
    hidden_gradient = base_backward + ADAPTER_SCALE * contract_dims(
        output_adapter_rank, down_adapter_in, 1, 1
    )
    up_gradient = (hidden_gradient * silu_gate).astype(jnp.bfloat16)
    partial_gradient = contract_dims(up_gradient, up_adapter_out, 1, 1)
    up_adapter_rank_gradient = lax.psum(partial_gradient, "mp").astype(jnp.bfloat16)
    up_in_term = ADAPTER_SCALE * contract_dims(local_normed_input, up_adapter_rank_gradient, 0, 0)
    up_out_term = ADAPTER_SCALE * contract_dims(up_adapter_rank, up_gradient, 0, 0)
    down_in_term = ADAPTER_SCALE * contract_dims(hidden_units, output_adapter_rank, 0, 0)
    down_out_term = ADAPTER_SCALE * contract_dims(hidden_adapter_rank, local_output, 0, 0)
    sum_up_a, sum_up_b, sum_down_a, sum_down_b = lax.psum(
        (up_in_term, up_out_term, down_in_term, down_out_term), ("dp", "sub")
    )
    return (
        sum_up_a.astype(jnp.bfloat16),
        sum_up_b.astype(jnp.bfloat16),
        sum_down_a.astype(jnp.bfloat16),
        sum_down_b.astype(jnp.bfloat16),
    )


def body(tokens, cotangent, rms_norm_gain, gate_codes, *rest):
    whole_tiles = gate_codes.shape[1] % ROW_TILE == 0
    form = fast_body if whole_tiles else general_body
    return form(tokens, cotangent, rms_norm_gain, gate_codes, *rest)


def solution(mesh):
    placed = (
        P(("grp", "dp", "sub"), "mp"),
        P(("grp", "dp", "sub"), "mp"),
        P("mp"),
        P("mp", ("dp", "sub"), None),
        P("mp", None),
        P("mp", ("dp", "sub"), None),
        P("mp", None),
        P(("dp", "sub"), "mp", None),
        P(None, "mp"),
        P(("grp", "mp"), None),
        P("grp", "mp"),
        P(("grp", "mp"), None),
        P("grp", "mp"),
        P(("grp", "dp", "sub"), None),
        P(("grp", "dp", "sub")),
    )
    return jax.shard_map(
        body,
        mesh=mesh,
        in_specs=placed,
        out_specs=(P(("grp", "mp"), None), P("grp", "mp"), P(("grp", "mp"), None), P("grp", "mp")),
        check_vma=False,
    )
```

```python
import math

import jax
import jax.numpy as jnp
from jax import lax
from jax.experimental import pallas as pl
from jax.experimental.pallas import tpu as pltpu
from jax.sharding import PartitionSpec as P

ADAPTER_SCALE = 2.0
EPS = 1e-05
ROW_TILE = 16
LANES = 128
MIB = 1024 * 1024

F32 = jnp.float32
BF16 = jnp.bfloat16


def contract_dims(left, right, left_dim, right_dim):
    return lax.dot_general(
        left, right, (((left_dim,), (right_dim,)), ((), ())), preferred_element_type=F32
    )


def dot(left, right):
    return jnp.dot(left, right, preferred_element_type=F32)


def ring_at(pos, n):
    if isinstance(pos, int):
        return 0 if pos == 0 else (2 * pos - 1 if 2 * pos <= n else 2 * (n - pos))
    return jnp.where(pos == 0, 0, jnp.where(2 * pos <= n, 2 * pos - 1, 2 * (n - pos)))


def ring_position():
    n = lax.axis_size("dp")
    place = lax.axis_index("dp")
    odd = lax.rem(place, 2) == 1
    return jnp.where(place == 0, 0, jnp.where(odd, (place + 1) // 2, n - place // 2))


def ring_step(x):
    n = lax.axis_size("dp")
    return lax.ppermute(x, "dp", [(ring_at(i, n), ring_at((i + 1) % n, n)) for i in range(n)])


def swap(x, axis):
    return lax.ppermute(x, axis, [(0, 1), (1, 0)])


def others(x, axis):
    n = lax.axis_size(axis)
    return [lax.ppermute(x, axis, [(i, (i + k) % n) for i in range(n)]) for k in range(1, n)]


def after(x, *done):
    return lax.optimization_barrier((x, *done))[0]


def add(*terms):
    return sum(t.astype(F32) for t in terms).astype(BF16)


def ring_all(parts, seen, gates=()):
    n = lax.axis_size("dp")

    def step(x):
        k = len(seen)
        seen.append(ring_step(after(x, gates[k]) if k < len(gates) else x))
        return seen[-1]

    total = parts[0]
    for part in parts[1:]:
        total = add(step(total), part)
    blocks = [total]
    for _ in range(n - 1):
        blocks.append(step(blocks[-1]))
    return blocks, [swap(b, "sub") for b in blocks]


def call(kernel, name, args, out_shape, scratch=(), specs=None, limit=24, flops=0, out_specs=None):
    vmem = pl.BlockSpec(memory_space=pltpu.VMEM)
    moved = sum(a.size * a.dtype.itemsize for a in args) + sum(
        math.prod(s.shape) * s.dtype.itemsize for s in out_shape
    )
    return pl.pallas_call(
        kernel,
        out_shape=tuple(out_shape),
        in_specs=specs or [vmem] * len(args),
        out_specs=out_specs or tuple([vmem] * len(out_shape)),
        scratch_shapes=list(scratch),
        compiler_params=pltpu.CompilerParams(vmem_limit_bytes=limit * MIB),
        cost_estimate=pl.CostEstimate(flops=flops, bytes_accessed=moved, transcendentals=0),
        name=name,
    )(*args)


def shape(dims, dtype=BF16):
    return jax.ShapeDtypeStruct(tuple(dims), dtype)


def scaled_halves(wide, low_ref, cols, scaled, product, send_ref, own_ref):
    half = send_ref.shape[1]
    step = half // 4
    sub = lax.axis_index("sub")
    low_ref[:, cols] = jnp.zeros((wide.shape[0], LANES), F32)
    for which, out_ref in ((1 - sub, send_ref), (sub, own_ref)):

        @pl.loop(0, half // step)
        def _(j, which=which, out_ref=out_ref):
            first = pl.multiple_of(which * half + j * step, step)
            parts = []
            for i in range(step // LANES):
                tile = pl.ds(pl.multiple_of(first + i * LANES, LANES), LANES)
                parts.append(scaled(wide[:, tile].astype(F32), tile).astype(BF16))
            value = jnp.concatenate(parts, axis=1)
            out_ref[:, pl.ds(pl.multiple_of(j * step, step), step)] = value
            low_ref[:, cols] += product(value, pl.ds(first, step))


def cotangent_kernel(
    total, cotangent, tokens, lengths, slots, adapter, send_ref, own_ref, low_ref, square_ref
):
    rows, width = cotangent.shape
    index = jnp.broadcast_to(slots[...], (LANES, rows))
    weight = jnp.zeros((LANES, rows), F32)
    for s in range(lengths.shape[1]):
        length = jnp.full((LANES, rows), lengths[0, s], jnp.int32).astype(F32)
        weight = weight + jnp.where(index == s, (rows // lengths.shape[1]) / length, 0.0)
    row = (weight * F32(1.0 / math.sqrt(total))).T

    square_ref[...] = jnp.zeros_like(square_ref)

    @pl.loop(0, width // (8 * LANES))
    def _(j):
        squares = square_ref[...]
        for i in range(8):
            tile = pl.ds(pl.multiple_of((j * 8 + i) * LANES, LANES), LANES)
            squares = squares + jnp.square(tokens[:, tile].astype(F32))
        square_ref[...] = squares

    square_ref[...] = jnp.broadcast_to(
        jnp.sum(square_ref[...], axis=1, keepdims=True), square_ref.shape
    )
    scaled_halves(
        cotangent,
        low_ref,
        slice(None),
        lambda tile, cols: tile * row,
        lambda value, cols: contract_dims(value, adapter[:, cols], 1, 1),
        send_ref,
        own_ref,
    )


def token_kernel(total_width, tokens, gain, adapter, low_out, squares, *refs):
    squares_more, (send_ref, own_ref, low_ref) = refs[:-3], refs[-3:]
    rank = adapter.shape[1]
    total = squares[...]
    for ref in squares_more:
        total = total + ref[...]
    row = lax.rsqrt(total / total_width + EPS)
    low_ref[:, rank:] = low_out[...]
    scaled_halves(
        tokens,
        low_ref,
        slice(0, rank),
        lambda tile, cols: tile * row * gain[:, cols].astype(F32),
        lambda value, cols: dot(value, adapter[cols, :]),
        send_ref,
        own_ref,
    )


def transpose_kernel(own, got, out_ref):
    rows, step = own.shape[0], out_ref.shape[0]
    for i, ref in enumerate((own, got)):
        out_ref[:, i * rows : (i + 1) * rows] = ref[...].astype(F32).T.astype(BF16)


def widen(scale, wide):
    for g in range(scale.shape[0]):
        row = scale[g : g + 1, :].astype(F32)
        wide[g] = jnp.broadcast_to(row, (LANES, row.shape[1])).T


def place_shards(codes, got, first_got, moved, store):
    n = lax.axis_size("dp")
    sub, grp, place = (lax.axis_index(a) for a in ("sub", "grp", "dp"))
    pos = ring_position()
    blocks = codes.shape[0] // 2
    quarter = blocks // 2

    @pl.loop(0, blocks, unroll=4)
    def _(b):
        store(b, place * 2 + sub, codes[sub * blocks + b])
        store(b, place * 2 + 1 - sub, got[first_got + b])

    for k in range(n - 1):
        there = ring_at(lax.rem(pos - k - 1 + n, n), n)
        for which in range(2):
            piece = moved[2 * k + which]
            start = (grp if which == 0 else 1 - grp) * quarter

            @pl.loop(0, quarter, unroll=4)
            def _(b, piece=piece, start=start, there=there):
                store(start + b, there * 2 + sub, piece[b])
                store(start + b, there * 2 + 1 - sub, piece[quarter + b])


def front_kernel(first_got, own, got, scale, codes, codes_got, *refs):
    moved, (mine_ref, theirs_ref, wide, weight) = refs[:-4], refs[-4:]
    blocks, rows, units = codes.shape
    first = lax.axis_index("sub") * (blocks // 2)
    widen(scale, wide)

    def store(b, shard, piece):
        at = pl.ds(pl.multiple_of(shard * rows, ROW_TILE), rows)
        for g in range(units // LANES):
            cols = slice(g * LANES, (g + 1) * LANES)
            factor = wide[g * wide.shape[0] * LANES // units, pl.ds(first + b, 1), :]
            weight[b, at, cols] = (piece[:, cols].astype(F32) * factor).astype(BF16)

    place_shards(codes, codes_got, first_got, moved, store)
    matrix = weight[...].reshape(-1, units)
    mine_ref[...] = dot(own[...], matrix)
    theirs_ref[...] = dot(got[...], matrix).astype(BF16)


def back_kernel(first_got, own, got, scale, codes, codes_got, *refs):
    moved, (mine_ref, theirs_ref, wide, weight) = refs[:-4], refs[-4:]
    blocks, rows, block = codes.shape
    first = lax.axis_index("sub") * (blocks // 2)
    per_group = weight.shape[0] // wide.shape[0]
    widen(scale, wide)

    def store(b, shard, piece):
        at = pl.multiple_of(shard * rows, ROW_TILE)
        factor = wide[at // per_group, pl.ds(first + b, 1), :]
        cols = pl.ds(pl.multiple_of(b * block, block), block)
        weight[pl.ds(at, rows), cols] = (piece.astype(F32) * factor).astype(BF16)

    place_shards(codes, codes_got, first_got, moved, store)
    matrix = weight[...]
    mine_ref[...] = contract_dims(own[...], matrix, 1, 1)
    theirs_ref[...] = contract_dims(got[...], matrix, 1, 1).astype(BF16)


def place_own(scratch, own, more, axis):
    n = len(more) + 1
    size = own.shape[axis]
    for k, ref in enumerate((own, *more)):
        at = pl.ds(pl.multiple_of(lax.rem(lax.axis_index("mp") + n - k, n) * size, size), size)
        if axis == 0:
            scratch[at, :] = ref[...]
        else:
            scratch[:, at] = ref[...]


def own_units(full, ref, axis):
    size = ref.shape[axis]
    for i in range(full.shape[axis] // size):

        @pl.when(lax.axis_index("mp") == i)
        def _(i=i):
            ref[...] = lax.slice_in_dim(full, i * size, (i + 1) * size, axis=axis).astype(BF16)


def low_sums(low, low_more):
    total = low[...]
    for ref in low_more:
        total = total + ref[...]
    half = total.shape[1] // 2
    return total[:, :half].astype(BF16), total[:, half:].astype(BF16)


def gather_adapters(adapters, adapters_more, up_out_all, down_in_all):
    rank = up_out_all.shape[0]
    place_own(up_out_all, adapters.at[:rank], [r.at[:rank] for r in adapters_more], 1)
    place_own(down_in_all, adapters.at[rank:], [r.at[rank:] for r in adapters_more], 0)


def hidden_kernel(more, gate, up, low, adapters, *refs):
    gate_more, up_more, low_more, adapters_more = (refs[i * more : (i + 1) * more] for i in range(4))
    silu_ref, low_ref, down_in_term, up_out_all, down_in_all = refs[4 * more :]
    gather_adapters(adapters, adapters_more, up_out_all, down_in_all)
    low_up, low_out = low_sums(low, low_more)
    gate_sum, up_sum = gate[...], up[...]
    for ref in gate_more:
        gate_sum = gate_sum + ref[...].astype(F32)
    for ref in up_more:
        up_sum = up_sum + ref[...].astype(F32)
    up_sum = up_sum + ADAPTER_SCALE * dot(low_up, up_out_all[...])
    silu = gate_sum * jax.nn.sigmoid(gate_sum)
    silu_ref[...] = silu
    hidden = (silu * up_sum).astype(BF16)
    low_ref[...] = (ADAPTER_SCALE * dot(hidden, down_in_all[...])).astype(BF16)
    hidden_t = hidden.astype(F32).T.astype(BF16)
    own_units(ADAPTER_SCALE * dot(hidden_t, low_out), down_in_term, 0)


def up_grad_kernel(more, back, silu, low, adapters, *refs):
    back_more, low_more, adapters_more = (refs[i * more : (i + 1) * more] for i in range(3))
    low_ref, up_out_term, up_out_all, down_in_all = refs[3 * more :]
    gather_adapters(adapters, adapters_more, up_out_all, down_in_all)
    low_up, low_out = low_sums(low, low_more)
    total = back[...]
    for ref in back_more:
        total = total + ref[...].astype(F32)
    total = total + ADAPTER_SCALE * contract_dims(low_out, down_in_all[...], 1, 1)
    up_grad = (total * silu[...]).astype(BF16)
    low_ref[...] = (ADAPTER_SCALE * contract_dims(up_grad, up_out_all[...], 1, 1)).astype(BF16)
    low_up_t = low_up.astype(F32).T.astype(BF16)
    own_units(ADAPTER_SCALE * dot(low_up_t, up_grad), up_out_term, 1)


def down_out_kernel(low, low_got, grad, grad_got, *out_refs):
    n = len(out_refs)
    pos = ring_position()
    low_t = jnp.concatenate([low[...], low_got[...]], axis=0).astype(F32).T.astype(BF16)
    rows = low.shape[0]
    for k, ref in enumerate(out_refs):
        size = ref.shape[1]
        at = pl.ds(pl.multiple_of(lax.rem(pos - 1 - k + 2 * n, n) * size, size), size)
        ref[...] = (
            dot(low_t[:, :rows], grad[:, at]) + dot(low_t[:, rows:], grad_got[:, at])
        ).astype(BF16)


def up_in_kernel(low, low_got, normed_t, up_out_term, down_in_term, *out_refs):
    n = len(out_refs)
    pos = ring_position()
    size = normed_t.shape[0] // n
    extra = out_refs[0].shape[0] - size
    both = jnp.concatenate([low[...], low_got[...]], axis=0)
    for k, ref in enumerate(out_refs):
        block = lax.rem(pos - 1 - k + 2 * n, n)
        at = pl.ds(pl.multiple_of(block * size, size), size)
        ref[pl.ds(0, size), :] = dot(normed_t[at, :], both).astype(BF16)
        per = up_out_term.shape[0] // extra
        index = pl.ds(pl.multiple_of(lax.rem(block, per) * extra, extra), extra)

        @pl.when(block < per)
        def _(ref=ref, index=index):
            ref[pl.ds(size, extra), :] = up_out_term[index, :]

        @pl.when(block >= per)
        def _(ref=ref, index=index):
            ref[pl.ds(size, extra), :] = down_in_term[index, :]


def copy_all(copies):
    for c in copies:
        c.start()
    for c in copies:
        c.wait()


def down_out_place_kernel(n, *refs):
    pieces, out_ref, sems = refs[: 2 * n], refs[2 * n], refs[2 * n + 1]
    pos, sub = ring_position(), lax.axis_index("sub")
    copies = []
    for i, piece in enumerate(pieces):
        half = sub if i < n else 1 - sub
        block = lax.rem(pos - i % n + n, n)
        size = piece.shape[1]
        at = pl.ds(pl.multiple_of((half * n + block) * size, size), size)
        copies.append(pltpu.make_async_copy(piece, out_ref.at[:, at], sems.at[i]))
    copy_all(copies)


def up_in_place_kernel(n, *refs):
    pieces = refs[: 2 * n]
    out_ref, up_out_ref, down_in_ref, small, sems = refs[2 * n :]
    pos, sub = ring_position(), lax.axis_index("sub")
    size = out_ref.shape[0] // (2 * n)
    extra = pieces[0].shape[0] - size
    copies = []
    for i, piece in enumerate(pieces):
        half = sub if i < n else 1 - sub
        block = lax.rem(pos - i % n + n, n)
        at = pl.ds(pl.multiple_of((half * n + block) * size, size), size)
        copies.append(
            pltpu.make_async_copy(piece.at[pl.ds(0, size), :], out_ref.at[at, :], sems.at[2 * i])
        )
        at = pl.ds(pl.multiple_of(block * extra, extra), extra)
        copies.append(
            pltpu.make_async_copy(
                piece.at[pl.ds(size, extra), :], small.at[i // n, at, :], sems.at[2 * i + 1]
            )
        )
    copy_all(copies)
    total = (small[0].astype(F32) + small[1].astype(F32)).astype(BF16)
    rows = up_out_ref.shape[0]
    up_out_ref[...] = total[:rows]
    down_in_ref[...] = total[rows:]


def half_kernel(*refs):
    sources, out_ref, sems = refs[:-2], refs[-2], refs[-1]
    other = 1 - lax.axis_index("sub")
    half = sources[0].shape[0] // 2
    copy_all(
        [
            pltpu.make_async_copy(
                ref.at[pl.ds(other * half, half)], out_ref.at[pl.ds(i * half, half)], sems.at[i]
            )
            for i, ref in enumerate(sources)
        ]
    )


def quarter_kernel(*refs):
    count = (len(refs) - 2) // 2
    sources, got, out_refs, sems = refs[:count], refs[count], refs[count + 1 : -1], refs[-1]
    sub, grp = lax.axis_index("sub"), lax.axis_index("grp")
    half = sources[0].shape[0] // 2
    quarter = half // 2
    copies = []
    for i, (ref, out_ref) in enumerate(zip(sources, out_refs)):
        own = ref.at[pl.ds(sub * half + grp * quarter, quarter)]
        theirs = got.at[pl.ds(i * half + grp * quarter, quarter)]
        for k, source in enumerate((own, theirs)):
            copies.append(
                pltpu.make_async_copy(
                    source, out_ref.at[pl.ds(k * quarter, quarter)], sems.at[2 * i + k]
                )
            )
    copy_all(copies)


def start_shards(codes):
    blocks, rows, units = codes[0].shape
    count = len(codes)
    anywhere = pl.BlockSpec(memory_space=pl.ANY)
    (send,) = call(
        half_kernel,
        "halves",
        codes,
        [shape((count * blocks // 2, rows, units))],
        scratch=[pltpu.SemaphoreType.DMA((count,))],
        specs=[anywhere] * count,
        out_specs=(anywhere,),
        limit=4,
    )
    got = swap(send, "sub")
    moving = call(
        quarter_kernel,
        "quarters",
        [*codes, got],
        [shape((blocks // 2, rows, units))] * count,
        scratch=[pltpu.SemaphoreType.DMA((2 * count,))],
        specs=[anywhere] * (count + 1),
        out_specs=(anywhere,) * count,
        limit=4,
    )
    return list(moving), got


def fast_body(
    tokens,
    cotangent,
    rms_norm_gain,
    gate_codes,
    gate_block_scale,
    up_codes,
    up_block_scale,
    down_codes,
    down_block_scale,
    up_adapter_in,
    up_adapter_out,
    down_adapter_in,
    down_adapter_out,
    sequence_length_list,
    slot_sequence_index,
):
    rows, local_width = tokens.shape
    blocks, _, units = gate_codes.shape
    block = local_width // blocks
    half = local_width // 2
    rank = up_adapter_in.shape[1]
    total_width = local_width * lax.axis_size("mp")
    n = lax.axis_size("dp")
    more = lax.axis_size("mp") - 1

    (gate_moving, up_moving), front_got = start_shards([gate_codes, up_codes])
    ring, crossed = [], []

    def step(moving, *done):
        ring.append(ring_step(after(moving, *done) if done else moving))
        crossed.append(swap(ring[-1], "grp"))

    step(gate_moving)
    step(up_moving)

    vmem = pl.BlockSpec(memory_space=pltpu.VMEM)
    smem = pl.BlockSpec(memory_space=pltpu.SMEM)
    lengths = after(sequence_length_list, gate_moving, up_moving)
    grad_send, grad, low_out, squares = call(
        lambda *refs: cotangent_kernel(rows * n * lax.axis_size("sub"), *refs),
        "cotangent",
        [cotangent, tokens, lengths, slot_sequence_index[None, :], down_adapter_out],
        [shape((rows, half))] * 2 + [shape((rows, rank), F32), shape((rows, LANES), F32)],
        specs=[vmem, vmem, smem, vmem, vmem],
        flops=2 * rows * local_width * rank,
    )
    squares_more = others(squares, "mp")
    step(ring[0], ring[1], grad)
    step(ring[1], ring[0], grad)
    normed_send, normed, low = call(
        lambda *refs: token_kernel(total_width, *refs),
        "tokens",
        [tokens, rms_norm_gain[None, :], up_adapter_in, low_out, after(squares, *ring[:2]), *squares_more],
        [shape((rows, half))] * 2 + [shape((rows, 2 * rank), F32)],
        flops=2 * rows * local_width * rank,
    )
    grad_got = swap(grad_send, "sub")
    normed_got = swap(normed_send, "sub")
    low_more = others(low, "mp")
    step(ring[2], ring[3], normed, *crossed[:2])
    step(ring[3], ring[2], normed, *crossed[:2])
    down_turned = jnp.swapaxes(after(down_codes, *ring[2:4]), 0, 1)
    (down_moving,), down_got = start_shards([down_turned])
    adapters = jnp.concatenate([up_adapter_out, down_adapter_in], axis=0)
    adapters_more = others(after(adapters, *ring[2:4]), "mp")
    step(down_moving, *ring[4:6], *crossed[2:4], grad_got, normed_got, *low_more, *adapters_more)
    step(ring[6])

    def product(kernel, name, own, got, scale, codes, codes_got, first_got, steps, weight_shape):
        groups = scale.shape[0]
        mine, theirs = call(
            lambda *refs: kernel(first_got, *refs),
            name,
            [own, got, scale, codes, codes_got, *[x for k in steps for x in (ring[k], crossed[k])]],
            [shape((rows, units), F32), shape((rows, units))],
            scratch=[pltpu.VMEM((groups, blocks, LANES), F32), pltpu.VMEM(weight_shape, BF16)],
            flops=4 * rows * half * units,
        )
        total = mine + swap(theirs, "sub").astype(F32)
        return total, others(total.astype(BF16), "mp"), mine

    front = (blocks // 2, block, units)
    half_blocks = blocks // 2
    gate, gate_more, gate_mine = product(
        front_kernel, "gate", normed, normed_got, gate_block_scale.T, gate_codes, front_got, 0,
        range(0, 2 * (n - 1), 2), front,
    )
    up, up_more, up_mine = product(
        front_kernel, "up", normed, normed_got, up_block_scale.T, up_codes, front_got, half_blocks,
        range(1, 2 * (n - 1), 2), front,
    )
    step(ring[7], gate_mine, up_mine, crossed[6])
    small_scratch = [
        pltpu.VMEM((rank, units), BF16),
        pltpu.VMEM((units, rank), BF16),
    ]
    silu, low_hidden, down_in_term = call(
        lambda *refs: hidden_kernel(more, *refs),
        "hidden",
        [gate, up, low, adapters, *gate_more, *up_more, *low_more, *adapters_more],
        [shape((rows, units), F32), shape((rows, rank)), shape(down_adapter_in.shape)],
        scratch=small_scratch,
        limit=8,
    )
    down_out_parts = call(
        down_out_kernel,
        "down_out",
        [low_hidden, swap(low_hidden, "sub"), grad, grad_got],
        [shape((rank, half // n))] * n,
        flops=4 * rows * half * rank,
    )
    seen = []
    down_out_blocks = ring_all(down_out_parts, seen)
    (normed_t,) = call(
        transpose_kernel,
        "transpose",
        [normed, after(normed_got, low_hidden)],
        [shape((half, 2 * rows))],
        limit=32,
    )

    back, back_more, _ = product(
        back_kernel, "back", after(grad, seen[0]), grad_got, down_block_scale, down_turned, down_got, 0,
        range(2 * (n - 1), 3 * (n - 1)), (units, half),
    )
    low_grad, up_out_term = call(
        lambda *refs: up_grad_kernel(more, *refs),
        "up_grad",
        [back, silu, low, adapters, *back_more, *low_more, *adapters_more],
        [shape((rows, rank)), shape(up_adapter_out.shape)],
        scratch=small_scratch,
        limit=8,
    )
    extra = 2 * rank // n
    up_in_parts = call(
        up_in_kernel,
        "up_in",
        [after(low_grad, seen[2]), swap(low_grad, "sub"), normed_t, up_out_term, down_in_term],
        [shape((half // n + extra, rank))] * n,
        flops=4 * rows * half * rank,
    )
    up_in_blocks = ring_all(up_in_parts, [])

    anywhere = pl.BlockSpec(memory_space=pl.ANY)
    (down_out_gradient,) = call(
        lambda *refs: down_out_place_kernel(n, *refs),
        "down_out_place",
        [*down_out_blocks[0], *down_out_blocks[1]],
        [shape((rank, local_width))],
        scratch=[pltpu.SemaphoreType.DMA((2 * n,))],
        specs=[anywhere] * (2 * n),
        out_specs=(anywhere,),
        limit=4,
    )
    up_in_gradient, up_out_gradient, down_in_gradient = call(
        lambda *refs: up_in_place_kernel(n, *refs),
        "up_in_place",
        [*up_in_blocks[0], *up_in_blocks[1]],
        [shape((local_width, rank)), shape(up_adapter_out.shape), shape(down_adapter_in.shape)],
        scratch=[pltpu.VMEM((2, 2 * rank, rank), BF16), pltpu.SemaphoreType.DMA((4 * n,))],
        specs=[anywhere] * (2 * n),
        out_specs=(anywhere, vmem, vmem),
        limit=4,
    )
    return up_in_gradient, up_out_gradient, down_in_gradient, down_out_gradient


def general_body(
    tokens,
    cotangent,
    rms_norm_gain,
    gate_codes,
    gate_block_scale,
    up_codes,
    up_block_scale,
    down_codes,
    down_block_scale,
    up_adapter_in,
    up_adapter_out,
    down_adapter_in,
    down_adapter_out,
    sequence_length_list,
    slot_sequence_index,
):
    rows = tokens.shape[0]
    local_width = tokens.shape[1]
    block = gate_block_scale.shape[0] and local_width // gate_codes.shape[0]
    blocks_here = gate_codes.shape[0]
    total_width = local_width * lax.axis_size("mp")
    own_squares = jnp.sum(jnp.square(tokens.astype(jnp.float32)), axis=-1, keepdims=True)
    squares = lax.psum(own_squares, "mp") / total_width
    inv_rms = lax.rsqrt(squares + EPS)
    local_normed_input = (
        tokens.astype(jnp.float32) * inv_rms * rms_norm_gain.astype(jnp.float32)[None, :]
    ).astype(jnp.bfloat16)
    seq_count = sequence_length_list.shape[1]
    longest = rows // seq_count
    total = rows * lax.axis_size("dp") * lax.axis_size("sub")
    ratios = longest / sequence_length_list[0].astype(jnp.float32)
    match = slot_sequence_index[:, None] == jnp.arange(seq_count, dtype=jnp.int32)[None, :]
    token_weight = jnp.sum(jnp.where(match, ratios[None, :], jnp.float32(0.0)), axis=-1)
    token_weight = token_weight * jnp.float32(1.0 / math.sqrt(total))
    local_output = (cotangent.astype(jnp.float32) * token_weight[:, None]).astype(jnp.bfloat16)
    partial_up = jnp.dot(local_normed_input, up_adapter_in, preferred_element_type=jnp.float32)
    partial_output = contract_dims(local_output, down_adapter_out, 1, 1)
    up_adapter_rank, output_adapter_rank = lax.psum((partial_up, partial_output), "mp")
    up_adapter_rank = up_adapter_rank.astype(jnp.bfloat16)
    output_adapter_rank = output_adapter_rank.astype(jnp.bfloat16)
    normed_blocks = local_normed_input.reshape(rows, blocks_here, block)
    out_blocks = local_output.reshape(rows, blocks_here, block)
    wide_gate = jnp.repeat(gate_block_scale.astype(jnp.float32), block, axis=1)[:, None, :]
    wide_up = jnp.repeat(up_block_scale.astype(jnp.float32), block, axis=1)[:, None, :]
    wide_down = jnp.repeat(down_block_scale.astype(jnp.float32), block, axis=0)
    dims_front = (((1, 2), (0, 1)), ((), ()))
    dims_back = (((1, 2), (1, 2)), ((), ()))
    quant_g = lax.all_gather(gate_codes, ("dp", "sub"), axis=1, tiled=True)
    quant_u = lax.all_gather(up_codes, ("dp", "sub"), axis=1, tiled=True)
    weight_g = (quant_g.astype(jnp.float32) * wide_gate).astype(jnp.bfloat16)
    weight_u = (quant_u.astype(jnp.float32) * wide_up).astype(jnp.bfloat16)
    gate_next = lax.dot_general(
        normed_blocks, weight_g, dims_front, preferred_element_type=jnp.float32
    )
    up_next = lax.dot_general(
        normed_blocks, weight_u, dims_front, preferred_element_type=jnp.float32
    )
    gate, base_up_projected = (
        lax.psum_scatter(gate_next, "mp", scatter_dimension=1, tiled=True),
        lax.psum_scatter(up_next, "mp", scatter_dimension=1, tiled=True),
    )
    up_projected = base_up_projected + ADAPTER_SCALE * jnp.dot(
        up_adapter_rank, up_adapter_out, preferred_element_type=jnp.float32
    )
    silu_gate = jax.nn.silu(gate)
    hidden_units = (silu_gate * up_projected).astype(jnp.bfloat16)
    partial_hidden = jnp.dot(hidden_units, down_adapter_in, preferred_element_type=jnp.float32)
    hidden_adapter_rank = lax.psum(partial_hidden, "mp").astype(jnp.bfloat16)
    weight_d = (
        lax.all_gather(down_codes, ("dp", "sub"), axis=0, tiled=True).astype(jnp.float32)
        * wide_down[:, :, None]
    ).astype(jnp.bfloat16)
    back_part = lax.dot_general(out_blocks, weight_d, dims_back, preferred_element_type=jnp.float32)
    base_backward = lax.psum_scatter(back_part, "mp", scatter_dimension=1, tiled=True)
    hidden_gradient = base_backward + ADAPTER_SCALE * contract_dims(
        output_adapter_rank, down_adapter_in, 1, 1
    )
    up_gradient = (hidden_gradient * silu_gate).astype(jnp.bfloat16)
    partial_gradient = contract_dims(up_gradient, up_adapter_out, 1, 1)
    up_adapter_rank_gradient = lax.psum(partial_gradient, "mp").astype(jnp.bfloat16)
    up_in_term = ADAPTER_SCALE * contract_dims(local_normed_input, up_adapter_rank_gradient, 0, 0)
    up_out_term = ADAPTER_SCALE * contract_dims(up_adapter_rank, up_gradient, 0, 0)
    down_in_term = ADAPTER_SCALE * contract_dims(hidden_units, output_adapter_rank, 0, 0)
    down_out_term = ADAPTER_SCALE * contract_dims(hidden_adapter_rank, local_output, 0, 0)
    sum_up_a, sum_up_b, sum_down_a, sum_down_b = lax.psum(
        (up_in_term, up_out_term, down_in_term, down_out_term), ("dp", "sub")
    )
    return (
        sum_up_a.astype(jnp.bfloat16),
        sum_up_b.astype(jnp.bfloat16),
        sum_down_a.astype(jnp.bfloat16),
        sum_down_b.astype(jnp.bfloat16),
    )


def body(tokens, cotangent, rms_norm_gain, gate_codes, *rest):
    whole_tiles = gate_codes.shape[1] % ROW_TILE == 0
    form = fast_body if whole_tiles else general_body
    return form(tokens, cotangent, rms_norm_gain, gate_codes, *rest)


def solution(mesh):
    placed = (
        P(("grp", "dp", "sub"), "mp"),
        P(("grp", "dp", "sub"), "mp"),
        P("mp"),
        P("mp", ("dp", "sub"), None),
        P("mp", None),
        P("mp", ("dp", "sub"), None),
        P("mp", None),
        P(("dp", "sub"), "mp", None),
        P(None, "mp"),
        P(("grp", "mp"), None),
        P("grp", "mp"),
        P(("grp", "mp"), None),
        P("grp", "mp"),
        P(("grp", "dp", "sub"), None),
        P(("grp", "dp", "sub")),
    )
    return jax.shard_map(
        body,
        mesh=mesh,
        in_specs=placed,
        out_specs=(P(("grp", "mp"), None), P("grp", "mp"), P(("grp", "mp"), None), P("grp", "mp")),
        check_vma=False,
    )
```

```python
import math

import jax
import jax.numpy as jnp
from jax import lax
from jax.experimental import pallas as pl
from jax.experimental.pallas import tpu as pltpu
from jax.sharding import PartitionSpec as P

ADAPTER_SCALE = 2.0
EPS = 1e-05
ROW_TILE = 16
LANES = 128
STREAMS = 2
MIB = 1024 * 1024

F32 = jnp.float32
BF16 = jnp.bfloat16


def contract_dims(left, right, left_dim, right_dim):
    return lax.dot_general(
        left, right, (((left_dim,), (right_dim,)), ((), ())), preferred_element_type=F32
    )


def dot(left, right):
    return jnp.dot(left, right, preferred_element_type=F32)


def ring_at(pos, n):
    if isinstance(pos, int):
        return 0 if pos == 0 else (2 * pos - 1 if 2 * pos <= n else 2 * (n - pos))
    return jnp.where(pos == 0, 0, jnp.where(2 * pos <= n, 2 * pos - 1, 2 * (n - pos)))


def ring_position():
    n = lax.axis_size("dp")
    place = lax.axis_index("dp")
    odd = lax.rem(place, 2) == 1
    return jnp.where(place == 0, 0, jnp.where(odd, (place + 1) // 2, n - place // 2))


def ring_step(x):
    n = lax.axis_size("dp")
    return lax.ppermute(x, "dp", [(ring_at(i, n), ring_at((i + 1) % n, n)) for i in range(n)])


def swap(x, axis):
    return lax.ppermute(x, axis, [(0, 1), (1, 0)])


def others(x, axis):
    n = lax.axis_size(axis)
    return [lax.ppermute(x, axis, [(i, (i + k) % n) for i in range(n)]) for k in range(1, n)]


def after(x, *done):
    return lax.optimization_barrier((x, *done))[0]


def add(*terms):
    return sum(t.astype(F32) for t in terms).astype(BF16)


def ring_all(parts, streams):
    n = lax.axis_size("dp")
    seen = []
    totals = list(parts[:streams])
    for k in range(1, n):
        seen.append([ring_step(t) for t in totals])
        totals = [add(t, p) for t, p in zip(seen[-1], parts[k * streams : (k + 1) * streams])]
    blocks = list(totals)
    for _ in range(n - 1):
        totals = [ring_step(t) for t in totals]
        seen.append(totals)
        blocks += totals
    return blocks + [swap(b, "sub") for b in blocks], seen


def call(kernel, name, args, out_shape, scratch=(), specs=None, limit=24, flops=0, out_specs=None):
    vmem = pl.BlockSpec(memory_space=pltpu.VMEM)
    moved = sum(a.size * a.dtype.itemsize for a in args) + sum(
        math.prod(s.shape) * s.dtype.itemsize for s in out_shape
    )
    return pl.pallas_call(
        kernel,
        out_shape=tuple(out_shape),
        in_specs=specs or [vmem] * len(args),
        out_specs=out_specs or tuple([vmem] * len(out_shape)),
        scratch_shapes=list(scratch),
        compiler_params=pltpu.CompilerParams(vmem_limit_bytes=limit * MIB),
        cost_estimate=pl.CostEstimate(flops=0, bytes_accessed=0, transcendentals=0),
        name=name,
    )(*args)


def shape(dims, dtype=BF16):
    return jax.ShapeDtypeStruct(tuple(dims), dtype)


def scaled_halves(wide, low_ref, cols, scaled, product, send_ref, own_ref, arrive=None):
    half = send_ref.shape[1]
    step = half // 4
    sub = lax.axis_index("sub")
    low_ref[:, cols] = jnp.zeros((wide.shape[0], LANES), F32)
    for n, (which, out_ref) in enumerate(((1 - sub, send_ref), (sub, own_ref))):

        @pl.loop(0, half // step)
        def _(j, n=n, which=which, out_ref=out_ref):
            first = pl.multiple_of(which * half + j * step, step)
            if arrive is not None:
                arrive(n * (half // step) + j, first, step)
            parts = []
            for i in range(step // LANES):
                tile = pl.ds(pl.multiple_of(first + i * LANES, LANES), LANES)
                parts.append(scaled(wide[:, tile].astype(F32), tile).astype(BF16))
            value = jnp.concatenate(parts, axis=1)
            out_ref[:, pl.ds(pl.multiple_of(j * step, step), step)] = value
            low_ref[:, cols] += product(value, pl.ds(first, step))


def column_copy(source, buffer, sems):
    def copy(k, first, step):
        at = pl.ds(first, step)
        return pltpu.make_async_copy(source.at[:, at], buffer.at[:, at], sems.at[k])

    return copy


def square_kernel(tokens, square_ref, buffer, sems):
    width = tokens.shape[1]
    step = width // sems.shape[0]
    copy = column_copy(tokens, buffer, sems)
    for k in range(width // step):
        copy(k, k * step, step).start()
    squares = jnp.zeros(square_ref.shape, F32)
    for k in range(width // step):
        copy(k, k * step, step).wait()
        for i in range(step // LANES):
            at = k * step + i * LANES
            squares = squares + jnp.square(buffer[:, at : at + LANES].astype(F32))
    square_ref[...] = jnp.broadcast_to(jnp.sum(squares, axis=1, keepdims=True), square_ref.shape)


def cotangent_kernel(
    total, cotangent, lengths, slots, adapter, send_ref, own_ref, low_ref, buffer, sems
):
    rows, width = cotangent.shape
    half = width // 2
    step = half // 4
    copy = column_copy(cotangent, buffer, sems)
    sub = lax.axis_index("sub")
    for k in range(8):
        which = 1 - sub if k < 4 else sub
        copy(k, pl.multiple_of(which * half + k % 4 * step, step), step).start()
    index = jnp.broadcast_to(slots[...], (LANES, rows))
    weight = jnp.zeros((LANES, rows), F32)
    for s in range(lengths.shape[1]):
        length = jnp.full((LANES, rows), lengths[0, s], jnp.int32).astype(F32)
        weight = weight + jnp.where(index == s, (rows // lengths.shape[1]) / length, 0.0)
    row = (weight * F32(1.0 / math.sqrt(total))).T
    scaled_halves(
        buffer,
        low_ref,
        slice(None),
        lambda tile, cols: tile * row,
        lambda value, cols: contract_dims(value, adapter[:, cols], 1, 1),
        send_ref,
        own_ref,
        lambda k, first, step: copy(k, first, step).wait(),
    )


def token_kernel(total_width, tokens, gain, adapter, low_out, squares, *refs):
    squares_more, (send_ref, own_ref, low_ref) = refs[:-3], refs[-3:]
    rank = adapter.shape[1]
    total = squares[...]
    for ref in squares_more:
        total = total + ref[...]
    row = lax.rsqrt(total / total_width + EPS)
    low_ref[:, rank:] = low_out[...]
    scaled_halves(
        tokens,
        low_ref,
        slice(0, rank),
        lambda tile, cols: tile * row * gain[:, cols].astype(F32),
        lambda value, cols: dot(value, adapter[cols, :]),
        send_ref,
        own_ref,
    )


def transpose_kernel(own, got, out_ref):
    rows, step = own.shape[0], out_ref.shape[0]
    for i, ref in enumerate((own, got)):
        out_ref[:, i * rows : (i + 1) * rows] = ref[...].astype(F32).T.astype(BF16)


def widen(scale, wide):
    for g in range(scale.shape[0]):
        row = scale[g : g + 1, :].astype(F32)
        wide[g] = jnp.broadcast_to(row, (LANES, row.shape[1])).T


def place_shards(codes, got, first_got, moved, store):
    n = lax.axis_size("dp")
    sub, grp, place = (lax.axis_index(a) for a in ("sub", "grp", "dp"))
    pos = ring_position()
    blocks = codes.shape[0] // 2
    quarter = blocks // 2

    @pl.loop(0, blocks, unroll=4)
    def _(b):
        store(b, place * 2 + sub, codes[sub * blocks + b])
        store(b, place * 2 + 1 - sub, got[first_got + b])

    streams = len(moved) // (2 * (n - 1))
    size = quarter // streams
    for k in range(n - 1):
        there = ring_at(lax.rem(pos - k - 1 + n, n), n)
        for i in range(2 * streams):
            piece = moved[2 * streams * k + i]
            start = (grp if i % 2 == 0 else 1 - grp) * quarter + i // 2 * size

            @pl.loop(0, size, unroll=4)
            def _(b, piece=piece, start=start, there=there):
                store(start + b, there * 2 + sub, piece[b])
                store(start + b, there * 2 + 1 - sub, piece[size + b])


def front_kernel(first_got, own, got, scale, codes, codes_got, *refs):
    moved, (mine_ref, theirs_ref, wide, weight) = refs[:-4], refs[-4:]
    blocks, rows, units = codes.shape
    first = lax.axis_index("sub") * (blocks // 2)
    widen(scale, wide)

    def store(b, shard, piece):
        at = pl.ds(pl.multiple_of(shard * rows, ROW_TILE), rows)
        for g in range(units // LANES):
            cols = slice(g * LANES, (g + 1) * LANES)
            factor = wide[g * wide.shape[0] * LANES // units, pl.ds(first + b, 1), :]
            weight[b, at, cols] = (piece[:, cols].astype(F32) * factor).astype(BF16)

    place_shards(codes, codes_got, first_got, moved, store)
    matrix = weight[...].reshape(-1, units)
    mine_ref[...] = dot(own[...], matrix)
    theirs_ref[...] = dot(got[...], matrix).astype(BF16)


def back_kernel(first_got, own, got, scale, codes, codes_got, *refs):
    moved, (mine_ref, theirs_ref, wide, weight) = refs[:-4], refs[-4:]
    blocks, rows, block = codes.shape
    first = lax.axis_index("sub") * (blocks // 2)
    per_group = weight.shape[0] // wide.shape[0]
    widen(scale, wide)

    def store(b, shard, piece):
        at = pl.multiple_of(shard * rows, ROW_TILE)
        factor = wide[at // per_group, pl.ds(first + b, 1), :]
        cols = pl.ds(pl.multiple_of(b * block, block), block)
        weight[pl.ds(at, rows), cols] = (piece.astype(F32) * factor).astype(BF16)

    place_shards(codes, codes_got, first_got, moved, store)
    matrix = weight[...]
    mine_ref[...] = contract_dims(own[...], matrix, 1, 1)
    theirs_ref[...] = contract_dims(got[...], matrix, 1, 1).astype(BF16)


def place_own(scratch, own, more, axis):
    n = len(more) + 1
    size = own.shape[axis]
    for k, ref in enumerate((own, *more)):
        at = pl.ds(pl.multiple_of(lax.rem(lax.axis_index("mp") + n - k, n) * size, size), size)
        if axis == 0:
            scratch[at, :] = ref[...]
        else:
            scratch[:, at] = ref[...]


def own_units(full, ref, axis):
    size = ref.shape[axis]
    for i in range(full.shape[axis] // size):

        @pl.when(lax.axis_index("mp") == i)
        def _(i=i):
            ref[...] = lax.slice_in_dim(full, i * size, (i + 1) * size, axis=axis).astype(BF16)


def low_sums(low, low_more):
    total = low[...]
    for ref in low_more:
        total = total + ref[...]
    half = total.shape[1] // 2
    return total[:, :half].astype(BF16), total[:, half:].astype(BF16)


def gather_adapters(adapters, adapters_more, up_out_all, down_in_all):
    rank = up_out_all.shape[0]
    place_own(up_out_all, adapters.at[:rank], [r.at[:rank] for r in adapters_more], 1)
    place_own(down_in_all, adapters.at[rank:], [r.at[rank:] for r in adapters_more], 0)


def hidden_kernel(more, gate, up, low, adapters, *refs):
    gate_more, up_more, low_more, adapters_more = (refs[i * more : (i + 1) * more] for i in range(4))
    silu_ref, low_ref, down_in_term, up_out_all, down_in_all = refs[4 * more :]
    gather_adapters(adapters, adapters_more, up_out_all, down_in_all)
    low_up, low_out = low_sums(low, low_more)
    gate_sum, up_sum = gate[...], up[...]
    for ref in gate_more:
        gate_sum = gate_sum + ref[...].astype(F32)
    for ref in up_more:
        up_sum = up_sum + ref[...].astype(F32)
    up_sum = up_sum + ADAPTER_SCALE * dot(low_up, up_out_all[...])
    silu = gate_sum * jax.nn.sigmoid(gate_sum)
    silu_ref[...] = silu
    hidden = (silu * up_sum).astype(BF16)
    low_ref[...] = (ADAPTER_SCALE * dot(hidden, down_in_all[...])).astype(BF16)
    hidden_t = hidden.astype(F32).T.astype(BF16)
    own_units(ADAPTER_SCALE * dot(hidden_t, low_out), down_in_term, 0)


def up_grad_kernel(more, back, silu, low, adapters, *refs):
    back_more, low_more, adapters_more = (refs[i * more : (i + 1) * more] for i in range(3))
    low_ref, up_out_term, up_out_all, down_in_all = refs[3 * more :]
    gather_adapters(adapters, adapters_more, up_out_all, down_in_all)
    low_up, low_out = low_sums(low, low_more)
    total = back[...]
    for ref in back_more:
        total = total + ref[...].astype(F32)
    total = total + ADAPTER_SCALE * contract_dims(low_out, down_in_all[...], 1, 1)
    up_grad = (total * silu[...]).astype(BF16)
    low_ref[...] = (ADAPTER_SCALE * contract_dims(up_grad, up_out_all[...], 1, 1)).astype(BF16)
    low_up_t = low_up.astype(F32).T.astype(BF16)
    own_units(ADAPTER_SCALE * dot(low_up_t, up_grad), up_out_term, 1)


def down_out_kernel(n, low, low_got, grad, grad_got, *out_refs):
    pos = ring_position()
    streams = len(out_refs) // n
    low_t = jnp.concatenate([low[...], low_got[...]], axis=0).astype(F32).T.astype(BF16)
    rows = low.shape[0]
    for k, ref in enumerate(out_refs):
        size = ref.shape[1]
        block = lax.rem(pos - 1 - k // streams + 2 * n, n) * streams + k % streams
        at = pl.ds(pl.multiple_of(block * size, size), size)
        ref[...] = (
            dot(low_t[:, :rows], grad[:, at]) + dot(low_t[:, rows:], grad_got[:, at])
        ).astype(BF16)


def up_in_kernel(n, low, low_got, normed_t, up_out_term, down_in_term, *out_refs):
    pos = ring_position()
    streams = len(out_refs) // n
    size = normed_t.shape[0] // len(out_refs)
    extra = out_refs[0].shape[0] - size
    both = jnp.concatenate([low[...], low_got[...]], axis=0)
    for k, ref in enumerate(out_refs):
        block = lax.rem(pos - 1 - k // streams + 2 * n, n) * streams + k % streams
        at = pl.ds(pl.multiple_of(block * size, size), size)
        ref[pl.ds(0, size), :] = dot(normed_t[at, :], both).astype(BF16)
        per = up_out_term.shape[0] // extra
        index = pl.ds(pl.multiple_of(lax.rem(block, per) * extra, extra), extra)

        @pl.when(block < per)
        def _(ref=ref, index=index):
            ref[pl.ds(size, extra), :] = up_out_term[index, :]

        @pl.when(block >= per)
        def _(ref=ref, index=index):
            ref[pl.ds(size, extra), :] = down_in_term[index, :]


def copy_all(copies):
    for c in copies:
        c.start()
    for c in copies:
        c.wait()


def down_out_place_kernel(n, *refs):
    pieces, (out_ref, sems) = refs[:-2], refs[-2:]
    pos, sub = ring_position(), lax.axis_index("sub")
    per_core = len(pieces) // 2
    streams = per_core // n
    copies = []
    for i, piece in enumerate(pieces):
        half = sub if i < per_core else 1 - sub
        block = lax.rem(pos - i % per_core // streams + n, n) * streams + i % streams
        size = piece.shape[1]
        at = pl.ds(pl.multiple_of((half * per_core + block) * size, size), size)
        copies.append(pltpu.make_async_copy(piece, out_ref.at[:, at], sems.at[i]))
    copy_all(copies)


def up_in_place_kernel(n, *refs):
    pieces, (out_ref, up_out_ref, down_in_ref, small, sems) = refs[:-5], refs[-5:]
    pos, sub = ring_position(), lax.axis_index("sub")
    per_core = len(pieces) // 2
    streams = per_core // n
    size = out_ref.shape[0] // len(pieces)
    extra = pieces[0].shape[0] - size
    copies = []
    for i, piece in enumerate(pieces):
        half = sub if i < per_core else 1 - sub
        block = lax.rem(pos - i % per_core // streams + n, n) * streams + i % streams
        at = pl.ds(pl.multiple_of((half * per_core + block) * size, size), size)
        copies.append(
            pltpu.make_async_copy(piece.at[pl.ds(0, size), :], out_ref.at[at, :], sems.at[2 * i])
        )
        at = pl.ds(pl.multiple_of(block * extra, extra), extra)
        copies.append(
            pltpu.make_async_copy(
                piece.at[pl.ds(size, extra), :], small.at[i // per_core, at, :], sems.at[2 * i + 1]
            )
        )
    copy_all(copies)
    total = (small[0].astype(F32) + small[1].astype(F32)).astype(BF16)
    rows = up_out_ref.shape[0]
    up_out_ref[...] = total[:rows]
    down_in_ref[...] = total[rows:]


def half_kernel(*refs):
    sources, out_ref, sems = refs[:-2], refs[-2], refs[-1]
    other = 1 - lax.axis_index("sub")
    half = sources[0].shape[0] // 2
    copy_all(
        [
            pltpu.make_async_copy(
                ref.at[pl.ds(other * half, half)], out_ref.at[pl.ds(i * half, half)], sems.at[i]
            )
            for i, ref in enumerate(sources)
        ]
    )


def quarter_kernel(count, *refs):
    sources, got, out_refs, sems = refs[:count], refs[count], refs[count + 1 : -1], refs[-1]
    streams = len(out_refs) // count
    sub, grp = lax.axis_index("sub"), lax.axis_index("grp")
    half = sources[0].shape[0] // 2
    quarter = half // 2
    copies = []
    size = quarter // streams
    for i, out_ref in enumerate(out_refs):
        first = grp * quarter + i % streams * size
        own = sources[i // streams].at[pl.ds(sub * half + first, size)]
        theirs = got.at[pl.ds(i // streams * half + first, size)]
        for k, source in enumerate((own, theirs)):
            copies.append(
                pltpu.make_async_copy(source, out_ref.at[pl.ds(k * size, size)], sems.at[2 * i + k])
            )
    copy_all(copies)


def start_shards(codes, streams):
    blocks, rows, units = codes[0].shape
    count = len(codes)
    anywhere = pl.BlockSpec(memory_space=pl.ANY)
    (send,) = call(
        half_kernel,
        "halves",
        codes,
        [shape((count * blocks // 2, rows, units))],
        scratch=[pltpu.SemaphoreType.DMA((count,))],
        specs=[anywhere] * count,
        out_specs=(anywhere,),
        limit=4,
    )
    got = swap(send, "sub")
    moving = call(
        lambda *refs: quarter_kernel(count, *refs),
        "quarters",
        [*codes, got],
        [shape((blocks // 2 // streams, rows, units))] * (count * streams),
        scratch=[pltpu.SemaphoreType.DMA((2 * count * streams,))],
        specs=[anywhere] * (count + 1),
        out_specs=(anywhere,) * (count * streams),
        limit=4,
    )
    return list(moving), got


def fast_body(
    tokens,
    cotangent,
    rms_norm_gain,
    gate_codes,
    gate_block_scale,
    up_codes,
    up_block_scale,
    down_codes,
    down_block_scale,
    up_adapter_in,
    up_adapter_out,
    down_adapter_in,
    down_adapter_out,
    sequence_length_list,
    slot_sequence_index,
):
    rows, local_width = tokens.shape
    blocks, _, units = gate_codes.shape
    block = local_width // blocks
    half = local_width // 2
    rank = up_adapter_in.shape[1]
    total_width = local_width * lax.axis_size("mp")
    n = lax.axis_size("dp")
    more = lax.axis_size("mp") - 1

    (gate_moving, up_moving), front_got = start_shards([gate_codes, up_codes], 1)
    ring, crossed = [], []

    def step(moving, *done):
        ring.append(ring_step(after(moving, *done) if done else moving))
        crossed.append(swap(ring[-1], "grp"))

    step(gate_moving)
    step(up_moving)

    vmem = pl.BlockSpec(memory_space=pltpu.VMEM)
    smem = pl.BlockSpec(memory_space=pltpu.SMEM)
    hbm = pl.BlockSpec(memory_space=pltpu.HBM)
    buffers = [pltpu.VMEM((rows, local_width), BF16), pltpu.SemaphoreType.DMA((8,))]
    (squares,) = call(
        square_kernel, "squares", [tokens], [shape((rows, LANES), F32)],
        scratch=buffers, specs=[hbm], limit=16,
    )
    squares_more = others(squares, "mp")
    lengths = after(sequence_length_list, gate_moving, up_moving, squares)
    grad_send, grad, low_out = call(
        lambda *refs: cotangent_kernel(rows * n * lax.axis_size("sub"), *refs),
        "cotangent",
        [cotangent, lengths, slot_sequence_index[None, :], down_adapter_out],
        [shape((rows, half))] * 2 + [shape((rows, rank), F32)],
        scratch=buffers,
        specs=[hbm, smem, vmem, vmem],
    )
    step(ring[0], ring[1], grad)
    step(ring[1], ring[0], grad)
    normed_send, normed, low = call(
        lambda *refs: token_kernel(total_width, *refs),
        "tokens",
        [tokens, rms_norm_gain[None, :], up_adapter_in, low_out, squares, *squares_more],
        [shape((rows, half))] * 2 + [shape((rows, 2 * rank), F32)],
    )
    grad_got = swap(grad_send, "sub")
    normed_got = swap(normed_send, "sub")
    low_more = others(low, "mp")
    down_turned = jnp.swapaxes(after(down_codes, *ring[:2]), 0, 1)
    down_moving, down_got = start_shards([down_turned], STREAMS)
    step(ring[2], ring[3], normed, *down_moving, *crossed[:2])
    step(ring[3], ring[2], normed, *down_moving, *crossed[:2])
    adapters = jnp.concatenate([up_adapter_out, down_adapter_in], axis=0)
    adapters_more = others(after(adapters, *ring[2:4]), "mp")
    pinned = [*ring[4:6], *crossed[2:4], grad_got, normed_got, *low_more, *adapters_more]
    for moving in down_moving:
        step(moving, *pinned)
    for moving in ring[-STREAMS:]:
        step(moving)

    def product(kernel, name, own, got, scale, codes, codes_got, first_got, steps, weight_shape):
        groups = scale.shape[0]
        mine, theirs = call(
            lambda *refs: kernel(first_got, *refs),
            name,
            [own, got, scale, codes, codes_got, *[x for k in steps for x in (ring[k], crossed[k])]],
            [shape((rows, units), F32), shape((rows, units))],
            scratch=[pltpu.VMEM((groups, blocks, LANES), F32), pltpu.VMEM(weight_shape, BF16)],
            flops=4 * rows * half * units,
        )
        total = mine + swap(theirs, "sub").astype(F32)
        return total, others(total.astype(BF16), "mp"), mine

    front = (blocks // 2, block, units)
    half_blocks = blocks // 2
    gate, gate_more, gate_mine = product(
        front_kernel, "gate", normed, normed_got, gate_block_scale.T, gate_codes, front_got, 0,
        range(0, 2 * (n - 1), 2), front,
    )
    up, up_more, up_mine = product(
        front_kernel, "up", normed, normed_got, up_block_scale.T, up_codes, front_got, half_blocks,
        range(1, 2 * (n - 1), 2), front,
    )
    for _ in range(n - 3):
        for moving, other in zip(ring[-STREAMS:], crossed[-2 * STREAMS : -STREAMS]):
            step(moving, gate_mine, up_mine, other)
    small_scratch = [
        pltpu.VMEM((rank, units), BF16),
        pltpu.VMEM((units, rank), BF16),
    ]
    silu, low_hidden, down_in_term = call(
        lambda *refs: hidden_kernel(more, *refs),
        "hidden",
        [gate, up, low, adapters, *gate_more, *up_more, *low_more, *adapters_more],
        [shape((rows, units), F32), shape((rows, rank)), shape(down_adapter_in.shape)],
        scratch=small_scratch,
        limit=8,
    )
    pieces = STREAMS * n
    down_out_parts = call(
        lambda *refs: down_out_kernel(n, *refs),
        "down_out",
        [low_hidden, swap(low_hidden, "sub"), grad, grad_got],
        [shape((rank, half // pieces))] * pieces,
        flops=4 * rows * half * rank,
    )
    down_out_blocks, seen = ring_all(down_out_parts, STREAMS)
    (normed_t,) = call(
        transpose_kernel,
        "transpose",
        [normed, after(normed_got, low_hidden)],
        [shape((half, 2 * rows))],
        limit=32,
    )

    back, back_more, _ = product(
        back_kernel, "back", after(grad, *seen[0]), grad_got, down_block_scale, down_turned, down_got, 0,
        range(2 * (n - 1), (2 + STREAMS) * (n - 1)), (units, half),
    )
    low_grad, up_out_term = call(
        lambda *refs: up_grad_kernel(more, *refs),
        "up_grad",
        [back, silu, low, adapters, *back_more, *low_more, *adapters_more],
        [shape((rows, rank)), shape(up_adapter_out.shape)],
        scratch=small_scratch,
        limit=8,
    )
    extra = 2 * rank // pieces
    up_in_parts = call(
        lambda *refs: up_in_kernel(n, *refs),
        "up_in",
        [after(low_grad, *seen[3]), swap(low_grad, "sub"), normed_t, up_out_term, down_in_term],
        [shape((half // pieces + extra, rank))] * pieces,
        flops=4 * rows * half * rank,
    )
    up_in_blocks, _ = ring_all(up_in_parts, STREAMS)

    anywhere = pl.BlockSpec(memory_space=pl.ANY)
    (down_out_gradient,) = call(
        lambda *refs: down_out_place_kernel(n, *refs),
        "down_out_place",
        down_out_blocks,
        [shape((rank, local_width))],
        scratch=[pltpu.SemaphoreType.DMA((2 * pieces,))],
        specs=[anywhere] * (2 * pieces),
        out_specs=(anywhere,),
        limit=4,
    )
    up_in_gradient, up_out_gradient, down_in_gradient = call(
        lambda *refs: up_in_place_kernel(n, *refs),
        "up_in_place",
        up_in_blocks,
        [shape((local_width, rank)), shape(up_adapter_out.shape), shape(down_adapter_in.shape)],
        scratch=[pltpu.VMEM((2, 2 * rank, rank), BF16), pltpu.SemaphoreType.DMA((4 * pieces,))],
        specs=[anywhere] * (2 * pieces),
        out_specs=(anywhere, vmem, vmem),
        limit=4,
    )
    return up_in_gradient, up_out_gradient, down_in_gradient, down_out_gradient


def general_body(
    tokens,
    cotangent,
    rms_norm_gain,
    gate_codes,
    gate_block_scale,
    up_codes,
    up_block_scale,
    down_codes,
    down_block_scale,
    up_adapter_in,
    up_adapter_out,
    down_adapter_in,
    down_adapter_out,
    sequence_length_list,
    slot_sequence_index,
):
    rows = tokens.shape[0]
    local_width = tokens.shape[1]
    block = gate_block_scale.shape[0] and local_width // gate_codes.shape[0]
    blocks_here = gate_codes.shape[0]
    total_width = local_width * lax.axis_size("mp")
    own_squares = jnp.sum(jnp.square(tokens.astype(jnp.float32)), axis=-1, keepdims=True)
    squares = lax.psum(own_squares, "mp") / total_width
    inv_rms = lax.rsqrt(squares + EPS)
    local_normed_input = (
        tokens.astype(jnp.float32) * inv_rms * rms_norm_gain.astype(jnp.float32)[None, :]
    ).astype(jnp.bfloat16)
    seq_count = sequence_length_list.shape[1]
    longest = rows // seq_count
    total = rows * lax.axis_size("dp") * lax.axis_size("sub")
    ratios = longest / sequence_length_list[0].astype(jnp.float32)
    match = slot_sequence_index[:, None] == jnp.arange(seq_count, dtype=jnp.int32)[None, :]
    token_weight = jnp.sum(jnp.where(match, ratios[None, :], jnp.float32(0.0)), axis=-1)
    token_weight = token_weight * jnp.float32(1.0 / math.sqrt(total))
    local_output = (cotangent.astype(jnp.float32) * token_weight[:, None]).astype(jnp.bfloat16)
    partial_up = jnp.dot(local_normed_input, up_adapter_in, preferred_element_type=jnp.float32)
    partial_output = contract_dims(local_output, down_adapter_out, 1, 1)
    up_adapter_rank, output_adapter_rank = lax.psum((partial_up, partial_output), "mp")
    up_adapter_rank = up_adapter_rank.astype(jnp.bfloat16)
    output_adapter_rank = output_adapter_rank.astype(jnp.bfloat16)
    normed_blocks = local_normed_input.reshape(rows, blocks_here, block)
    out_blocks = local_output.reshape(rows, blocks_here, block)
    wide_gate = jnp.repeat(gate_block_scale.astype(jnp.float32), block, axis=1)[:, None, :]
    wide_up = jnp.repeat(up_block_scale.astype(jnp.float32), block, axis=1)[:, None, :]
    wide_down = jnp.repeat(down_block_scale.astype(jnp.float32), block, axis=0)
    dims_front = (((1, 2), (0, 1)), ((), ()))
    dims_back = (((1, 2), (1, 2)), ((), ()))
    quant_g = lax.all_gather(gate_codes, ("dp", "sub"), axis=1, tiled=True)
    quant_u = lax.all_gather(up_codes, ("dp", "sub"), axis=1, tiled=True)
    weight_g = (quant_g.astype(jnp.float32) * wide_gate).astype(jnp.bfloat16)
    weight_u = (quant_u.astype(jnp.float32) * wide_up).astype(jnp.bfloat16)
    gate_next = lax.dot_general(
        normed_blocks, weight_g, dims_front, preferred_element_type=jnp.float32
    )
    up_next = lax.dot_general(
        normed_blocks, weight_u, dims_front, preferred_element_type=jnp.float32
    )
    gate, base_up_projected = (
        lax.psum_scatter(gate_next, "mp", scatter_dimension=1, tiled=True),
        lax.psum_scatter(up_next, "mp", scatter_dimension=1, tiled=True),
    )
    up_projected = base_up_projected + ADAPTER_SCALE * jnp.dot(
        up_adapter_rank, up_adapter_out, preferred_element_type=jnp.float32
    )
    silu_gate = jax.nn.silu(gate)
    hidden_units = (silu_gate * up_projected).astype(jnp.bfloat16)
    partial_hidden = jnp.dot(hidden_units, down_adapter_in, preferred_element_type=jnp.float32)
    hidden_adapter_rank = lax.psum(partial_hidden, "mp").astype(jnp.bfloat16)
    weight_d = (
        lax.all_gather(down_codes, ("dp", "sub"), axis=0, tiled=True).astype(jnp.float32)
        * wide_down[:, :, None]
    ).astype(jnp.bfloat16)
    back_part = lax.dot_general(out_blocks, weight_d, dims_back, preferred_element_type=jnp.float32)
    base_backward = lax.psum_scatter(back_part, "mp", scatter_dimension=1, tiled=True)
    hidden_gradient = base_backward + ADAPTER_SCALE * contract_dims(
        output_adapter_rank, down_adapter_in, 1, 1
    )
    up_gradient = (hidden_gradient * silu_gate).astype(jnp.bfloat16)
    partial_gradient = contract_dims(up_gradient, up_adapter_out, 1, 1)
    up_adapter_rank_gradient = lax.psum(partial_gradient, "mp").astype(jnp.bfloat16)
    up_in_term = ADAPTER_SCALE * contract_dims(local_normed_input, up_adapter_rank_gradient, 0, 0)
    up_out_term = ADAPTER_SCALE * contract_dims(up_adapter_rank, up_gradient, 0, 0)
    down_in_term = ADAPTER_SCALE * contract_dims(hidden_units, output_adapter_rank, 0, 0)
    down_out_term = ADAPTER_SCALE * contract_dims(hidden_adapter_rank, local_output, 0, 0)
    sum_up_a, sum_up_b, sum_down_a, sum_down_b = lax.psum(
        (up_in_term, up_out_term, down_in_term, down_out_term), ("dp", "sub")
    )
    return (
        sum_up_a.astype(jnp.bfloat16),
        sum_up_b.astype(jnp.bfloat16),
        sum_down_a.astype(jnp.bfloat16),
        sum_down_b.astype(jnp.bfloat16),
    )


def body(tokens, cotangent, rms_norm_gain, gate_codes, *rest):
    whole_tiles = gate_codes.shape[1] % ROW_TILE == 0
    form = fast_body if whole_tiles else general_body
    return form(tokens, cotangent, rms_norm_gain, gate_codes, *rest)


def solution(mesh):
    placed = (
        P(("grp", "dp", "sub"), "mp"),
        P(("grp", "dp", "sub"), "mp"),
        P("mp"),
        P("mp", ("dp", "sub"), None),
        P("mp", None),
        P("mp", ("dp", "sub"), None),
        P("mp", None),
        P(("dp", "sub"), "mp", None),
        P(None, "mp"),
        P(("grp", "mp"), None),
        P("grp", "mp"),
        P(("grp", "mp"), None),
        P("grp", "mp"),
        P(("grp", "dp", "sub"), None),
        P(("grp", "dp", "sub")),
    )
    return jax.shard_map(
        body,
        mesh=mesh,
        in_specs=placed,
        out_specs=(P(("grp", "mp"), None), P("grp", "mp"), P(("grp", "mp"), None), P("grp", "mp")),
        check_vma=False,
    )
```

```python
import math

import jax
import jax.numpy as jnp
from jax import lax
from jax.experimental import pallas as pl
from jax.experimental.pallas import tpu as pltpu
from jax.sharding import PartitionSpec as P

ADAPTER_SCALE = 2.0
EPS = 1e-05
ROW_TILE = 16
LANES = 128
STREAMS = 2
MIB = 1024 * 1024

F32 = jnp.float32
BF16 = jnp.bfloat16


def contract_dims(left, right, left_dim, right_dim):
    return lax.dot_general(
        left, right, (((left_dim,), (right_dim,)), ((), ())), preferred_element_type=F32
    )


def dot(left, right):
    return jnp.dot(left, right, preferred_element_type=F32)


def ring_at(pos, n):
    if isinstance(pos, int):
        return 0 if pos == 0 else (2 * pos - 1 if 2 * pos <= n else 2 * (n - pos))
    return jnp.where(pos == 0, 0, jnp.where(2 * pos <= n, 2 * pos - 1, 2 * (n - pos)))


def ring_position():
    n = lax.axis_size("dp")
    place = lax.axis_index("dp")
    odd = lax.rem(place, 2) == 1
    return jnp.where(place == 0, 0, jnp.where(odd, (place + 1) // 2, n - place // 2))


def ring_step(x):
    n = lax.axis_size("dp")
    return lax.ppermute(x, "dp", [(ring_at(i, n), ring_at((i + 1) % n, n)) for i in range(n)])


def swap(x, axis):
    return lax.ppermute(x, axis, [(0, 1), (1, 0)])


def others(x, axis):
    n = lax.axis_size(axis)
    return [lax.ppermute(x, axis, [(i, (i + k) % n) for i in range(n)]) for k in range(1, n)]


def after(x, *done):
    return lax.optimization_barrier((x, *done))[0]


def call(kernel, name, args, out_shape, scratch=(), specs=None, limit=24, flops=0, out_specs=None):
    vmem = pl.BlockSpec(memory_space=pltpu.VMEM)
    moved = sum(a.size * a.dtype.itemsize for a in args) + sum(
        math.prod(s.shape) * s.dtype.itemsize for s in out_shape
    )
    return pl.pallas_call(
        kernel,
        out_shape=tuple(out_shape),
        in_specs=specs or [vmem] * len(args),
        out_specs=out_specs or tuple([vmem] * len(out_shape)),
        scratch_shapes=list(scratch),
        compiler_params=pltpu.CompilerParams(vmem_limit_bytes=limit * MIB),
        cost_estimate=pl.CostEstimate(flops=0, bytes_accessed=0, transcendentals=0),
        name=name,
    )(*args)


def shape(dims, dtype=BF16):
    return jax.ShapeDtypeStruct(tuple(dims), dtype)


def add_kernel(left, right, out_ref):
    out_ref[...] = (left[...].astype(F32) + right[...].astype(F32)).astype(BF16)


def add(left, right):
    return call(add_kernel, "add", [left, right], [shape(left.shape)], limit=4)[0]


def ring_all(parts, streams):
    n = lax.axis_size("dp")
    seen = []
    totals = list(parts[:streams])
    for k in range(1, n):
        seen.append([ring_step(t) for t in totals])
        totals = [add(t, p) for t, p in zip(seen[-1], parts[k * streams : (k + 1) * streams])]
    blocks = list(totals)
    for _ in range(n - 1):
        totals = [ring_step(t) for t in totals]
        seen.append(totals)
        blocks += totals
    return blocks + [swap(b, "sub") for b in blocks], seen


def scaled_halves(wide, low_ref, cols, scaled, product, send_ref, own_ref, arrive=None):
    half = send_ref.shape[1]
    step = half // 4
    sub = lax.axis_index("sub")
    low_ref[:, cols] = jnp.zeros((wide.shape[0], LANES), F32)
    for n, (which, out_ref) in enumerate(((1 - sub, send_ref), (sub, own_ref))):

        @pl.loop(0, half // step)
        def _(j, n=n, which=which, out_ref=out_ref):
            first = pl.multiple_of(which * half + j * step, step)
            if arrive is not None:
                arrive(n * (half // step) + j, first, step)
            parts = []
            for i in range(step // LANES):
                tile = pl.ds(pl.multiple_of(first + i * LANES, LANES), LANES)
                parts.append(scaled(wide[:, tile].astype(F32), tile).astype(BF16))
            value = jnp.concatenate(parts, axis=1)
            out_ref[:, pl.ds(pl.multiple_of(j * step, step), step)] = value
            low_ref[:, cols] += product(value, pl.ds(first, step))


def column_copy(source, buffer, sems):
    def copy(k, first, step):
        at = pl.ds(first, step)
        return pltpu.make_async_copy(source.at[:, at], buffer.at[:, at], sems.at[k])

    return copy


def square_kernel(tokens, lengths, square_ref, buffer, sems):
    width = tokens.shape[1]
    step = width // sems.shape[0]
    copy = column_copy(tokens, buffer, sems)
    for k in range(width // step):
        copy(k, k * step, step).start()
    squares = jnp.zeros(square_ref.shape, F32)
    for k in range(width // step):
        copy(k, k * step, step).wait()
        for i in range(step // LANES):
            at = k * step + i * LANES
            squares = squares + jnp.square(buffer[:, at : at + LANES].astype(F32))
    square_ref[...] = jnp.broadcast_to(jnp.sum(squares, axis=1, keepdims=True), square_ref.shape)


def cotangent_kernel(
    total, cotangent, lengths, slots, adapter, send_ref, own_ref, low_ref, buffer, sems
):
    rows, width = cotangent.shape
    half = width // 2
    step = half // 4
    copy = column_copy(cotangent, buffer, sems)
    sub = lax.axis_index("sub")
    for k in range(8):
        which = 1 - sub if k < 4 else sub
        copy(k, pl.multiple_of(which * half + k % 4 * step, step), step).start()
    index = jnp.broadcast_to(slots[...], (LANES, rows))
    weight = jnp.zeros((LANES, rows), F32)
    for s in range(lengths.shape[1]):
        length = jnp.full((LANES, rows), lengths[0, s], jnp.int32).astype(F32)
        weight = weight + jnp.where(index == s, (rows // lengths.shape[1]) / length, 0.0)
    row = (weight * F32(1.0 / math.sqrt(total))).T
    scaled_halves(
        buffer,
        low_ref,
        slice(None),
        lambda tile, cols: tile * row,
        lambda value, cols: contract_dims(value, adapter[:, cols], 1, 1),
        send_ref,
        own_ref,
        lambda k, first, step: copy(k, first, step).wait(),
    )


def token_kernel(total_width, tokens, gain, adapter, low_out, squares, *refs):
    squares_more, (send_ref, own_ref, low_ref) = refs[:-3], refs[-3:]
    rank = adapter.shape[1]
    total = squares[...]
    for ref in squares_more:
        total = total + ref[...]
    row = lax.rsqrt(total / total_width + EPS)
    low_ref[:, rank:] = low_out[...]
    scaled_halves(
        tokens,
        low_ref,
        slice(0, rank),
        lambda tile, cols: tile * row * gain[:, cols].astype(F32),
        lambda value, cols: dot(value, adapter[cols, :]),
        send_ref,
        own_ref,
    )


def transpose_kernel(own, got, out_ref):
    rows, step = own.shape[0], out_ref.shape[0]
    for i, ref in enumerate((own, got)):
        out_ref[:, i * rows : (i + 1) * rows] = ref[...].astype(F32).T.astype(BF16)


def widen(scale, wide):
    for g in range(scale.shape[0]):
        row = scale[g : g + 1, :].astype(F32)
        wide[g] = jnp.broadcast_to(row, (LANES, row.shape[1])).T


def place_shards(codes, got, first_got, moved, store):
    n = lax.axis_size("dp")
    sub, grp, place = (lax.axis_index(a) for a in ("sub", "grp", "dp"))
    pos = ring_position()
    blocks = codes.shape[0] // 2
    quarter = blocks // 2

    @pl.loop(0, blocks, unroll=4)
    def _(b):
        store(b, place * 2 + sub, codes[sub * blocks + b])
        store(b, place * 2 + 1 - sub, got[first_got + b])

    streams = len(moved) // (2 * (n - 1))
    size = quarter // streams
    for k in range(n - 1):
        there = ring_at(lax.rem(pos - k - 1 + n, n), n)
        for i in range(2 * streams):
            piece = moved[2 * streams * k + i]
            start = (grp if i % 2 == 0 else 1 - grp) * quarter + i // 2 * size

            @pl.loop(0, size, unroll=4)
            def _(b, piece=piece, start=start, there=there):
                store(start + b, there * 2 + sub, piece[b])
                store(start + b, there * 2 + 1 - sub, piece[size + b])


def front_kernel(first_got, own, got, scale, codes, codes_got, *refs):
    moved, (mine_ref, theirs_ref, wide, weight) = refs[:-4], refs[-4:]
    blocks, rows, units = codes.shape
    first = lax.axis_index("sub") * (blocks // 2)
    widen(scale, wide)

    def store(b, shard, piece):
        at = pl.ds(pl.multiple_of(shard * rows, ROW_TILE), rows)
        for g in range(units // LANES):
            cols = slice(g * LANES, (g + 1) * LANES)
            factor = wide[g * wide.shape[0] * LANES // units, pl.ds(first + b, 1), :]
            weight[b, at, cols] = (piece[:, cols].astype(F32) * factor).astype(BF16)

    place_shards(codes, codes_got, first_got, moved, store)
    matrix = weight[...].reshape(-1, units)
    mine_ref[...] = dot(own[...], matrix)
    theirs_ref[...] = dot(got[...], matrix).astype(BF16)


def back_kernel(first_got, own, got, scale, codes, codes_got, *refs):
    moved, (mine_ref, theirs_ref, wide, weight) = refs[:-4], refs[-4:]
    blocks, rows, block = codes.shape
    first = lax.axis_index("sub") * (blocks // 2)
    per_group = weight.shape[0] // wide.shape[0]
    widen(scale, wide)

    def store(b, shard, piece):
        at = pl.multiple_of(shard * rows, ROW_TILE)
        factor = wide[at // per_group, pl.ds(first + b, 1), :]
        cols = pl.ds(pl.multiple_of(b * block, block), block)
        weight[pl.ds(at, rows), cols] = (piece.astype(F32) * factor).astype(BF16)

    place_shards(codes, codes_got, first_got, moved, store)
    matrix = weight[...]
    mine_ref[...] = contract_dims(own[...], matrix, 1, 1)
    theirs_ref[...] = contract_dims(got[...], matrix, 1, 1).astype(BF16)


def place_own(scratch, own, more, axis):
    n = len(more) + 1
    size = own.shape[axis]
    for k, ref in enumerate((own, *more)):
        at = pl.ds(pl.multiple_of(lax.rem(lax.axis_index("mp") + n - k, n) * size, size), size)
        if axis == 0:
            scratch[at, :] = ref[...]
        else:
            scratch[:, at] = ref[...]


def own_units(full, ref, axis):
    size = ref.shape[axis]
    for i in range(full.shape[axis] // size):

        @pl.when(lax.axis_index("mp") == i)
        def _(i=i):
            ref[...] = lax.slice_in_dim(full, i * size, (i + 1) * size, axis=axis).astype(BF16)


def low_sums(low, low_more):
    total = low[...]
    for ref in low_more:
        total = total + ref[...]
    half = total.shape[1] // 2
    return total[:, :half].astype(BF16), total[:, half:].astype(BF16)


def gather_adapters(adapters, adapters_more, up_out_all, down_in_all):
    rank = up_out_all.shape[0]
    place_own(up_out_all, adapters.at[:rank], [r.at[:rank] for r in adapters_more], 1)
    place_own(down_in_all, adapters.at[rank:], [r.at[rank:] for r in adapters_more], 0)


def hidden_kernel(more, gate, up, low, adapters, *refs):
    gate_more, up_more, low_more, adapters_more = (refs[i * more : (i + 1) * more] for i in range(4))
    silu_ref, low_ref, down_in_term, up_out_all, down_in_all = refs[4 * more :]
    gather_adapters(adapters, adapters_more, up_out_all, down_in_all)
    low_up, low_out = low_sums(low, low_more)
    gate_sum, up_sum = gate[...], up[...]
    for ref in gate_more:
        gate_sum = gate_sum + ref[...].astype(F32)
    for ref in up_more:
        up_sum = up_sum + ref[...].astype(F32)
    up_sum = up_sum + ADAPTER_SCALE * dot(low_up, up_out_all[...])
    silu = gate_sum * jax.nn.sigmoid(gate_sum)
    silu_ref[...] = silu
    hidden = (silu * up_sum).astype(BF16)
    low_ref[...] = (ADAPTER_SCALE * dot(hidden, down_in_all[...])).astype(BF16)
    hidden_t = hidden.astype(F32).T.astype(BF16)
    own_units(ADAPTER_SCALE * dot(hidden_t, low_out), down_in_term, 0)


def up_grad_kernel(more, back, silu, low, adapters, *refs):
    back_more, low_more, adapters_more = (refs[i * more : (i + 1) * more] for i in range(3))
    low_ref, up_out_term, up_out_all, down_in_all = refs[3 * more :]
    gather_adapters(adapters, adapters_more, up_out_all, down_in_all)
    low_up, low_out = low_sums(low, low_more)
    total = back[...]
    for ref in back_more:
        total = total + ref[...].astype(F32)
    total = total + ADAPTER_SCALE * contract_dims(low_out, down_in_all[...], 1, 1)
    up_grad = (total * silu[...]).astype(BF16)
    low_ref[...] = (ADAPTER_SCALE * contract_dims(up_grad, up_out_all[...], 1, 1)).astype(BF16)
    low_up_t = low_up.astype(F32).T.astype(BF16)
    own_units(ADAPTER_SCALE * dot(low_up_t, up_grad), up_out_term, 1)


def down_out_kernel(n, low, low_got, grad, grad_got, *out_refs):
    pos = ring_position()
    streams = len(out_refs) // n
    low_t = jnp.concatenate([low[...], low_got[...]], axis=0).astype(F32).T.astype(BF16)
    rows = low.shape[0]
    for k, ref in enumerate(out_refs):
        size = ref.shape[1]
        block = lax.rem(pos - 1 - k // streams + 2 * n, n) * streams + k % streams
        at = pl.ds(pl.multiple_of(block * size, size), size)
        ref[...] = (
            dot(low_t[:, :rows], grad[:, at]) + dot(low_t[:, rows:], grad_got[:, at])
        ).astype(BF16)


def up_in_kernel(n, low, low_got, normed_t, up_out_term, down_in_term, *out_refs):
    pos = ring_position()
    streams = len(out_refs) // n
    size = normed_t.shape[0] // len(out_refs)
    extra = out_refs[0].shape[0] - size
    both = jnp.concatenate([low[...], low_got[...]], axis=0)
    for k, ref in enumerate(out_refs):
        block = lax.rem(pos - 1 - k // streams + 2 * n, n) * streams + k % streams
        at = pl.ds(pl.multiple_of(block * size, size), size)
        ref[pl.ds(0, size), :] = dot(normed_t[at, :], both).astype(BF16)
        per = up_out_term.shape[0] // extra
        index = pl.ds(pl.multiple_of(lax.rem(block, per) * extra, extra), extra)

        @pl.when(block < per)
        def _(ref=ref, index=index):
            ref[pl.ds(size, extra), :] = up_out_term[index, :]

        @pl.when(block >= per)
        def _(ref=ref, index=index):
            ref[pl.ds(size, extra), :] = down_in_term[index, :]


def copy_all(copies):
    for c in copies:
        c.start()
    for c in copies:
        c.wait()


def down_out_place_kernel(n, *refs):
    pieces, (out_ref, sems) = refs[:-2], refs[-2:]
    pos, sub = ring_position(), lax.axis_index("sub")
    per_core = len(pieces) // 2
    streams = per_core // n
    copies = []
    for i, piece in enumerate(pieces):
        half = sub if i < per_core else 1 - sub
        block = lax.rem(pos - i % per_core // streams + n, n) * streams + i % streams
        size = piece.shape[1]
        at = pl.ds(pl.multiple_of((half * per_core + block) * size, size), size)
        copies.append(pltpu.make_async_copy(piece, out_ref.at[:, at], sems.at[i]))
    copy_all(copies)


def up_in_place_kernel(n, *refs):
    pieces, (out_ref, up_out_ref, down_in_ref, small, sems) = refs[:-5], refs[-5:]
    pos, sub = ring_position(), lax.axis_index("sub")
    per_core = len(pieces) // 2
    streams = per_core // n
    size = out_ref.shape[0] // len(pieces)
    extra = pieces[0].shape[0] - size
    copies = []
    for i, piece in enumerate(pieces):
        half = sub if i < per_core else 1 - sub
        block = lax.rem(pos - i % per_core // streams + n, n) * streams + i % streams
        at = pl.ds(pl.multiple_of((half * per_core + block) * size, size), size)
        copies.append(
            pltpu.make_async_copy(piece.at[pl.ds(0, size), :], out_ref.at[at, :], sems.at[2 * i])
        )
        at = pl.ds(pl.multiple_of(block * extra, extra), extra)
        copies.append(
            pltpu.make_async_copy(
                piece.at[pl.ds(size, extra), :], small.at[i // per_core, at, :], sems.at[2 * i + 1]
            )
        )
    copy_all(copies)
    total = (small[0].astype(F32) + small[1].astype(F32)).astype(BF16)
    rows = up_out_ref.shape[0]
    up_out_ref[...] = total[:rows]
    down_in_ref[...] = total[rows:]


def half_kernel(*refs):
    sources, out_ref, sems = refs[:-2], refs[-2], refs[-1]
    other = 1 - lax.axis_index("sub")
    half = sources[0].shape[0] // 2
    copy_all(
        [
            pltpu.make_async_copy(
                ref.at[pl.ds(other * half, half)], out_ref.at[pl.ds(i * half, half)], sems.at[i]
            )
            for i, ref in enumerate(sources)
        ]
    )


def quarter_kernel(count, *refs):
    sources, got, out_refs, sems = refs[:count], refs[count], refs[count + 1 : -1], refs[-1]
    streams = len(out_refs) // count
    sub, grp = lax.axis_index("sub"), lax.axis_index("grp")
    half = sources[0].shape[0] // 2
    quarter = half // 2
    copies = []
    size = quarter // streams
    for i, out_ref in enumerate(out_refs):
        first = grp * quarter + i % streams * size
        own = sources[i // streams].at[pl.ds(sub * half + first, size)]
        theirs = got.at[pl.ds(i // streams * half + first, size)]
        for k, source in enumerate((own, theirs)):
            copies.append(
                pltpu.make_async_copy(source, out_ref.at[pl.ds(k * size, size)], sems.at[2 * i + k])
            )
    copy_all(copies)


def start_shards(codes, streams):
    blocks, rows, units = codes[0].shape
    count = len(codes)
    anywhere = pl.BlockSpec(memory_space=pl.ANY)
    (send,) = call(
        half_kernel,
        "halves",
        codes,
        [shape((count * blocks // 2, rows, units))],
        scratch=[pltpu.SemaphoreType.DMA((count,))],
        specs=[anywhere] * count,
        out_specs=(anywhere,),
        limit=4,
    )
    got = swap(send, "sub")
    moving = call(
        lambda *refs: quarter_kernel(count, *refs),
        "quarters",
        [*codes, got],
        [shape((blocks // 2 // streams, rows, units))] * (count * streams),
        scratch=[pltpu.SemaphoreType.DMA((2 * count * streams,))],
        specs=[anywhere] * (count + 1),
        out_specs=(anywhere,) * (count * streams),
        limit=4,
    )
    return list(moving), got


def fast_body(
    tokens,
    cotangent,
    rms_norm_gain,
    gate_codes,
    gate_block_scale,
    up_codes,
    up_block_scale,
    down_codes,
    down_block_scale,
    up_adapter_in,
    up_adapter_out,
    down_adapter_in,
    down_adapter_out,
    sequence_length_list,
    slot_sequence_index,
):
    rows, local_width = tokens.shape
    blocks, _, units = gate_codes.shape
    block = local_width // blocks
    half = local_width // 2
    rank = up_adapter_in.shape[1]
    total_width = local_width * lax.axis_size("mp")
    n = lax.axis_size("dp")
    more = lax.axis_size("mp") - 1

    (gate_moving, up_moving), front_got = start_shards([gate_codes, up_codes], 1)
    ring, crossed = [], []

    def step(moving, *done):
        ring.append(ring_step(after(moving, *done) if done else moving))
        if len(ring) > 2:
            crossed.append(swap(ring[-1], "grp"))

    step(gate_moving)
    step(up_moving)

    vmem = pl.BlockSpec(memory_space=pltpu.VMEM)
    smem = pl.BlockSpec(memory_space=pltpu.SMEM)
    hbm = pl.BlockSpec(memory_space=pltpu.HBM)
    buffers = [pltpu.VMEM((rows, local_width), BF16), pltpu.SemaphoreType.DMA((8,))]
    lengths = after(sequence_length_list, gate_moving, up_moving)
    (squares,) = call(
        square_kernel, "squares", [tokens, lengths], [shape((rows, LANES), F32)],
        scratch=buffers, specs=[hbm, smem], limit=16,
    )
    squares_more = others(squares, "mp")
    grad_send, grad, low_out = call(
        lambda *refs: cotangent_kernel(rows * n * lax.axis_size("sub"), *refs),
        "cotangent",
        [cotangent, after(lengths, squares), slot_sequence_index[None, :], down_adapter_out],
        [shape((rows, half))] * 2 + [shape((rows, rank), F32)],
        scratch=buffers,
        specs=[hbm, smem, vmem, vmem],
    )
    crossed += [swap(after(r, grad), "grp") for r in ring]
    step(ring[0], ring[1], grad)
    step(ring[1], ring[0], grad)
    normed_send, normed, low = call(
        lambda *refs: token_kernel(total_width, *refs),
        "tokens",
        [tokens, rms_norm_gain[None, :], up_adapter_in, low_out, after(squares, *ring[2:4], *crossed[:2]), *squares_more],
        [shape((rows, half))] * 2 + [shape((rows, 2 * rank), F32)],
    )
    grad_got = swap(grad_send, "sub")
    normed_got = swap(normed_send, "sub")
    low_more = others(low, "mp")
    down_turned = jnp.swapaxes(after(down_codes, *ring[2:4]), 0, 1)
    down_moving, down_got = start_shards([down_turned], STREAMS)
    step(ring[2], ring[3], *crossed[:2])
    step(ring[3], ring[2], *crossed[:2])
    adapters = jnp.concatenate([up_adapter_out, down_adapter_in], axis=0)
    adapters_more = others(after(adapters, *ring[2:4]), "mp")
    pinned = [*ring[4:6], *crossed[2:4], grad_got, normed_got, *low_more, *adapters_more]
    for moving in down_moving:
        step(moving, *pinned)
    for moving in ring[-STREAMS:]:
        step(moving)

    def product(kernel, name, own, got, scale, codes, codes_got, first_got, steps, weight_shape):
        groups = scale.shape[0]
        mine, theirs = call(
            lambda *refs: kernel(first_got, *refs),
            name,
            [own, got, scale, codes, codes_got, *[x for k in steps for x in (ring[k], crossed[k])]],
            [shape((rows, units), F32), shape((rows, units))],
            scratch=[pltpu.VMEM((groups, blocks, LANES), F32), pltpu.VMEM(weight_shape, BF16)],
            flops=4 * rows * half * units,
        )
        total = mine + swap(theirs, "sub").astype(F32)
        return total, others(total.astype(BF16), "mp"), mine

    front = (blocks // 2, block, units)
    first_down = ring[2 * (n - 1) : 2 * (n - 1) + STREAMS]
    half_blocks = blocks // 2
    gate, gate_more, gate_mine = product(
        front_kernel, "gate", normed, normed_got, after(gate_block_scale.T, *first_down), gate_codes, front_got, 0,
        range(0, 2 * (n - 1), 2), front,
    )
    up, up_more, up_mine = product(
        front_kernel, "up", normed, normed_got, after(up_block_scale.T, *first_down), up_codes, front_got, half_blocks,
        range(1, 2 * (n - 1), 2), front,
    )
    for _ in range(n - 3):
        for moving, other in zip(ring[-STREAMS:], crossed[-2 * STREAMS : -STREAMS]):
            step(moving, gate_mine, up_mine, other)
    small_scratch = [
        pltpu.VMEM((rank, units), BF16),
        pltpu.VMEM((units, rank), BF16),
    ]
    silu, low_hidden, down_in_term = call(
        lambda *refs: hidden_kernel(more, *refs),
        "hidden",
        [gate, up, low, after(adapters, *ring[-2 * STREAMS : -STREAMS]), *gate_more, *up_more, *low_more, *adapters_more],
        [shape((rows, units), F32), shape((rows, rank)), shape(down_adapter_in.shape)],
        scratch=small_scratch,
        limit=8,
    )
    pieces = STREAMS * n
    down_out_parts = call(
        lambda *refs: down_out_kernel(n, *refs),
        "down_out",
        [low_hidden, swap(low_hidden, "sub"), grad, grad_got],
        [shape((rank, half // pieces))] * pieces,
        flops=4 * rows * half * rank,
    )
    down_out_blocks, seen = ring_all(down_out_parts, STREAMS)
    (normed_t,) = call(
        transpose_kernel,
        "transpose",
        [normed, after(normed_got, low_hidden)],
        [shape((half, 2 * rows))],
        limit=32,
    )

    back, back_more, _ = product(
        back_kernel, "back", after(grad, *seen[0]), grad_got, down_block_scale, down_turned, down_got, 0,
        range(2 * (n - 1), (2 + STREAMS) * (n - 1)), (units, half),
    )
    low_grad, up_out_term = call(
        lambda *refs: up_grad_kernel(more, *refs),
        "up_grad",
        [back, silu, low, adapters, *back_more, *low_more, *adapters_more],
        [shape((rows, rank)), shape(up_adapter_out.shape)],
        scratch=small_scratch,
        limit=8,
    )
    extra = 2 * rank // pieces
    up_in_parts = call(
        lambda *refs: up_in_kernel(n, *refs),
        "up_in",
        [after(low_grad, *seen[3]), swap(low_grad, "sub"), normed_t, up_out_term, down_in_term],
        [shape((half // pieces + extra, rank))] * pieces,
        flops=4 * rows * half * rank,
    )
    up_in_blocks, _ = ring_all(up_in_parts, STREAMS)

    anywhere = pl.BlockSpec(memory_space=pl.ANY)
    (down_out_gradient,) = call(
        lambda *refs: down_out_place_kernel(n, *refs),
        "down_out_place",
        down_out_blocks,
        [shape((rank, local_width))],
        scratch=[pltpu.SemaphoreType.DMA((2 * pieces,))],
        specs=[anywhere] * (2 * pieces),
        out_specs=(anywhere,),
        limit=4,
    )
    up_in_gradient, up_out_gradient, down_in_gradient = call(
        lambda *refs: up_in_place_kernel(n, *refs),
        "up_in_place",
        up_in_blocks,
        [shape((local_width, rank)), shape(up_adapter_out.shape), shape(down_adapter_in.shape)],
        scratch=[pltpu.VMEM((2, 2 * rank, rank), BF16), pltpu.SemaphoreType.DMA((4 * pieces,))],
        specs=[anywhere] * (2 * pieces),
        out_specs=(anywhere, vmem, vmem),
        limit=4,
    )
    return up_in_gradient, up_out_gradient, down_in_gradient, down_out_gradient


def general_body(
    tokens,
    cotangent,
    rms_norm_gain,
    gate_codes,
    gate_block_scale,
    up_codes,
    up_block_scale,
    down_codes,
    down_block_scale,
    up_adapter_in,
    up_adapter_out,
    down_adapter_in,
    down_adapter_out,
    sequence_length_list,
    slot_sequence_index,
):
    rows = tokens.shape[0]
    local_width = tokens.shape[1]
    block = gate_block_scale.shape[0] and local_width // gate_codes.shape[0]
    blocks_here = gate_codes.shape[0]
    total_width = local_width * lax.axis_size("mp")
    own_squares = jnp.sum(jnp.square(tokens.astype(jnp.float32)), axis=-1, keepdims=True)
    squares = lax.psum(own_squares, "mp") / total_width
    inv_rms = lax.rsqrt(squares + EPS)
    local_normed_input = (
        tokens.astype(jnp.float32) * inv_rms * rms_norm_gain.astype(jnp.float32)[None, :]
    ).astype(jnp.bfloat16)
    seq_count = sequence_length_list.shape[1]
    longest = rows // seq_count
    total = rows * lax.axis_size("dp") * lax.axis_size("sub")
    ratios = longest / sequence_length_list[0].astype(jnp.float32)
    match = slot_sequence_index[:, None] == jnp.arange(seq_count, dtype=jnp.int32)[None, :]
    token_weight = jnp.sum(jnp.where(match, ratios[None, :], jnp.float32(0.0)), axis=-1)
    token_weight = token_weight * jnp.float32(1.0 / math.sqrt(total))
    local_output = (cotangent.astype(jnp.float32) * token_weight[:, None]).astype(jnp.bfloat16)
    partial_up = jnp.dot(local_normed_input, up_adapter_in, preferred_element_type=jnp.float32)
    partial_output = contract_dims(local_output, down_adapter_out, 1, 1)
    up_adapter_rank, output_adapter_rank = lax.psum((partial_up, partial_output), "mp")
    up_adapter_rank = up_adapter_rank.astype(jnp.bfloat16)
    output_adapter_rank = output_adapter_rank.astype(jnp.bfloat16)
    normed_blocks = local_normed_input.reshape(rows, blocks_here, block)
    out_blocks = local_output.reshape(rows, blocks_here, block)
    wide_gate = jnp.repeat(gate_block_scale.astype(jnp.float32), block, axis=1)[:, None, :]
    wide_up = jnp.repeat(up_block_scale.astype(jnp.float32), block, axis=1)[:, None, :]
    wide_down = jnp.repeat(down_block_scale.astype(jnp.float32), block, axis=0)
    dims_front = (((1, 2), (0, 1)), ((), ()))
    dims_back = (((1, 2), (1, 2)), ((), ()))
    quant_g = lax.all_gather(gate_codes, ("dp", "sub"), axis=1, tiled=True)
    quant_u = lax.all_gather(up_codes, ("dp", "sub"), axis=1, tiled=True)
    weight_g = (quant_g.astype(jnp.float32) * wide_gate).astype(jnp.bfloat16)
    weight_u = (quant_u.astype(jnp.float32) * wide_up).astype(jnp.bfloat16)
    gate_next = lax.dot_general(
        normed_blocks, weight_g, dims_front, preferred_element_type=jnp.float32
    )
    up_next = lax.dot_general(
        normed_blocks, weight_u, dims_front, preferred_element_type=jnp.float32
    )
    gate, base_up_projected = (
        lax.psum_scatter(gate_next, "mp", scatter_dimension=1, tiled=True),
        lax.psum_scatter(up_next, "mp", scatter_dimension=1, tiled=True),
    )
    up_projected = base_up_projected + ADAPTER_SCALE * jnp.dot(
        up_adapter_rank, up_adapter_out, preferred_element_type=jnp.float32
    )
    silu_gate = jax.nn.silu(gate)
    hidden_units = (silu_gate * up_projected).astype(jnp.bfloat16)
    partial_hidden = jnp.dot(hidden_units, down_adapter_in, preferred_element_type=jnp.float32)
    hidden_adapter_rank = lax.psum(partial_hidden, "mp").astype(jnp.bfloat16)
    weight_d = (
        lax.all_gather(down_codes, ("dp", "sub"), axis=0, tiled=True).astype(jnp.float32)
        * wide_down[:, :, None]
    ).astype(jnp.bfloat16)
    back_part = lax.dot_general(out_blocks, weight_d, dims_back, preferred_element_type=jnp.float32)
    base_backward = lax.psum_scatter(back_part, "mp", scatter_dimension=1, tiled=True)
    hidden_gradient = base_backward + ADAPTER_SCALE * contract_dims(
        output_adapter_rank, down_adapter_in, 1, 1
    )
    up_gradient = (hidden_gradient * silu_gate).astype(jnp.bfloat16)
    partial_gradient = contract_dims(up_gradient, up_adapter_out, 1, 1)
    up_adapter_rank_gradient = lax.psum(partial_gradient, "mp").astype(jnp.bfloat16)
    up_in_term = ADAPTER_SCALE * contract_dims(local_normed_input, up_adapter_rank_gradient, 0, 0)
    up_out_term = ADAPTER_SCALE * contract_dims(up_adapter_rank, up_gradient, 0, 0)
    down_in_term = ADAPTER_SCALE * contract_dims(hidden_units, output_adapter_rank, 0, 0)
    down_out_term = ADAPTER_SCALE * contract_dims(hidden_adapter_rank, local_output, 0, 0)
    sum_up_a, sum_up_b, sum_down_a, sum_down_b = lax.psum(
        (up_in_term, up_out_term, down_in_term, down_out_term), ("dp", "sub")
    )
    return (
        sum_up_a.astype(jnp.bfloat16),
        sum_up_b.astype(jnp.bfloat16),
        sum_down_a.astype(jnp.bfloat16),
        sum_down_b.astype(jnp.bfloat16),
    )


def body(tokens, cotangent, rms_norm_gain, gate_codes, *rest):
    whole_tiles = gate_codes.shape[1] % ROW_TILE == 0
    form = fast_body if whole_tiles else general_body
    return form(tokens, cotangent, rms_norm_gain, gate_codes, *rest)


def solution(mesh):
    placed = (
        P(("grp", "dp", "sub"), "mp"),
        P(("grp", "dp", "sub"), "mp"),
        P("mp"),
        P("mp", ("dp", "sub"), None),
        P("mp", None),
        P("mp", ("dp", "sub"), None),
        P("mp", None),
        P(("dp", "sub"), "mp", None),
        P(None, "mp"),
        P(("grp", "mp"), None),
        P("grp", "mp"),
        P(("grp", "mp"), None),
        P("grp", "mp"),
        P(("grp", "dp", "sub"), None),
        P(("grp", "dp", "sub")),
    )
    return jax.shard_map(
        body,
        mesh=mesh,
        in_specs=placed,
        out_specs=(P(("grp", "mp"), None), P("grp", "mp"), P(("grp", "mp"), None), P("grp", "mp")),
        check_vma=False,
    )
```

```python
import math

import jax
import jax.numpy as jnp
from jax import lax
from jax.experimental import pallas as pl
from jax.experimental.pallas import tpu as pltpu
from jax.sharding import PartitionSpec as P

ADAPTER_SCALE = 2.0
EPS = 1e-05
ROW_TILE = 16
LANES = 128
STREAMS = 2
MIB = 1024 * 1024

F32 = jnp.float32
BF16 = jnp.bfloat16


def contract_dims(left, right, left_dim, right_dim):
    return lax.dot_general(
        left, right, (((left_dim,), (right_dim,)), ((), ())), preferred_element_type=F32
    )


def dot(left, right):
    return jnp.dot(left, right, preferred_element_type=F32)


def ring_at(pos, n):
    if isinstance(pos, int):
        return 0 if pos == 0 else (2 * pos - 1 if 2 * pos <= n else 2 * (n - pos))
    return jnp.where(pos == 0, 0, jnp.where(2 * pos <= n, 2 * pos - 1, 2 * (n - pos)))


def ring_position():
    n = lax.axis_size("dp")
    place = lax.axis_index("dp")
    odd = lax.rem(place, 2) == 1
    return jnp.where(place == 0, 0, jnp.where(odd, (place + 1) // 2, n - place // 2))


def ring_step(x):
    n = lax.axis_size("dp")
    return lax.ppermute(x, "dp", [(ring_at(i, n), ring_at((i + 1) % n, n)) for i in range(n)])


def swap(x, axis):
    return lax.ppermute(x, axis, [(0, 1), (1, 0)])


def others(x, axis):
    n = lax.axis_size(axis)
    return [lax.ppermute(x, axis, [(i, (i + k) % n) for i in range(n)]) for k in range(1, n)]


def after(x, *done):
    return lax.optimization_barrier((x, *done))[0]


def call(kernel, name, args, out_shape, scratch=(), specs=None, limit=24, flops=0, out_specs=None):
    vmem = pl.BlockSpec(memory_space=pltpu.VMEM)
    moved = sum(a.size * a.dtype.itemsize for a in args) + sum(
        math.prod(s.shape) * s.dtype.itemsize for s in out_shape
    )
    return pl.pallas_call(
        kernel,
        out_shape=tuple(out_shape),
        in_specs=specs or [vmem] * len(args),
        out_specs=out_specs or tuple([vmem] * len(out_shape)),
        scratch_shapes=list(scratch),
        compiler_params=pltpu.CompilerParams(vmem_limit_bytes=limit * MIB),
        cost_estimate=pl.CostEstimate(flops=0, bytes_accessed=0, transcendentals=0),
        name=name,
    )(*args)


def shape(dims, dtype=BF16):
    return jax.ShapeDtypeStruct(tuple(dims), dtype)


def add_kernel(left, right, out_ref):
    out_ref[...] = (left[...].astype(F32) + right[...].astype(F32)).astype(BF16)


def add(left, right):
    return call(add_kernel, "add", [left, right], [shape(left.shape)], limit=4)[0]


def ring_all(parts, streams, last=()):
    n = lax.axis_size("dp")
    seen = []
    totals = list(parts[:streams])
    for k in range(1, n):
        seen.append([ring_step(t) for t in totals])
        totals = [add(t, p) for t, p in zip(seen[-1], parts[k * streams : (k + 1) * streams])]
    blocks = list(totals)
    for k in range(n - 1):
        if last and k == n - 2:
            totals = [after(t, *last) for t in totals]
        totals = [ring_step(t) for t in totals]
        seen.append(totals)
        blocks += totals
    return blocks + [swap(b, "sub") for b in blocks], seen


def scaled_halves(wide, low_ref, cols, scaled, product, send_ref, own_ref, copy):
    half = send_ref.shape[1]
    step = half // 4
    sub = lax.axis_index("sub")
    low_ref[:, cols] = jnp.zeros((wide.shape[0], LANES), F32)
    for n, (which, out_ref) in enumerate(((1 - sub, send_ref), (sub, own_ref))):

        @pl.loop(0, half // step)
        def _(j, n=n, which=which, out_ref=out_ref):
            first = pl.multiple_of(which * half + j * step, step)
            copy(n * (half // step) + j, first, step).wait()
            parts = []
            for i in range(step // LANES):
                tile = pl.ds(pl.multiple_of(first + i * LANES, LANES), LANES)
                parts.append(scaled(wide[:, tile].astype(F32), tile).astype(BF16))
            value = jnp.concatenate(parts, axis=1)
            out_ref[:, pl.ds(pl.multiple_of(j * step, step), step)] = value
            low_ref[:, cols] += product(value, pl.ds(first, step))


def column_copy(source, buffer, sems):
    def copy(k, first, step):
        at = pl.ds(first, step)
        return pltpu.make_async_copy(source.at[:, at], buffer.at[:, at], sems.at[k])

    return copy


def start_halves(source, buffer, sems):
    half = source.shape[1] // 2
    step = half // 4
    copy = column_copy(source, buffer, sems)
    sub = lax.axis_index("sub")
    for k in range(8):
        which = 1 - sub if k < 4 else sub
        copy(k, pl.multiple_of(which * half + k % 4 * step, step), step).start()
    return copy


def square_kernel(tokens, lengths, square_ref, buffer, sems):
    width = tokens.shape[1]
    step = width // sems.shape[0]
    copy = column_copy(tokens, buffer, sems)
    for k in range(width // step):
        copy(k, k * step, step).start()
    squares = jnp.zeros(square_ref.shape, F32)
    for k in range(width // step):
        copy(k, k * step, step).wait()
        for i in range(step // LANES):
            at = k * step + i * LANES
            squares = squares + jnp.square(buffer[:, at : at + LANES].astype(F32))
    square_ref[...] = jnp.broadcast_to(jnp.sum(squares, axis=1, keepdims=True), square_ref.shape)


def cotangent_kernel(
    total, cotangent, lengths, slots, adapter, send_ref, own_ref, low_ref, buffer, sems
):
    rows = cotangent.shape[0]
    copy = start_halves(cotangent, buffer, sems)
    index = jnp.broadcast_to(slots[...], (LANES, rows))
    weight = jnp.zeros((LANES, rows), F32)
    for s in range(lengths.shape[1]):
        length = jnp.full((LANES, rows), lengths[0, s], jnp.int32).astype(F32)
        weight = weight + jnp.where(index == s, (rows // lengths.shape[1]) / length, 0.0)
    row = (weight * F32(1.0 / math.sqrt(total))).T
    scaled_halves(
        buffer,
        low_ref,
        slice(None),
        lambda tile, cols: tile * row,
        lambda value, cols: contract_dims(value, adapter[:, cols], 1, 1),
        send_ref,
        own_ref,
        copy,
    )


def token_kernel(total_width, tokens, gain, adapter, low_out, squares, *refs):
    squares_more, (send_ref, own_ref, low_ref, buffer, sems) = refs[:-5], refs[-5:]
    copy = start_halves(tokens, buffer, sems)
    rank = adapter.shape[1]
    total = squares[...]
    for ref in squares_more:
        total = total + ref[...]
    row = lax.rsqrt(total / total_width + EPS)
    low_ref[:, rank:] = low_out[...]
    scaled_halves(
        buffer,
        low_ref,
        slice(0, rank),
        lambda tile, cols: tile * row * gain[:, cols].astype(F32),
        lambda value, cols: dot(value, adapter[cols, :]),
        send_ref,
        own_ref,
        copy,
    )


def transpose_kernel(own, got, out_ref):
    rows, step = own.shape[0], out_ref.shape[0]
    for i, ref in enumerate((own, got)):
        out_ref[:, i * rows : (i + 1) * rows] = ref[...].astype(F32).T.astype(BF16)


def widen(scale, wide):
    for g in range(scale.shape[0]):
        row = scale[g : g + 1, :].astype(F32)
        wide[g] = jnp.broadcast_to(row, (LANES, row.shape[1])).T


def place_shards(codes, got, first_got, moved, store):
    n = lax.axis_size("dp")
    sub, grp, place = (lax.axis_index(a) for a in ("sub", "grp", "dp"))
    pos = ring_position()
    blocks = codes.shape[0] // 2
    quarter = blocks // 2

    @pl.loop(0, blocks, unroll=4)
    def _(b):
        store(b, place * 2 + sub, codes[sub * blocks + b])
        store(b, place * 2 + 1 - sub, got[first_got + b])

    streams = len(moved) // (2 * (n - 1))
    size = quarter // streams
    for k in range(n - 1):
        there = ring_at(lax.rem(pos - k - 1 + n, n), n)
        for i in range(2 * streams):
            piece = moved[2 * streams * k + i]
            start = (grp if i % 2 == 0 else 1 - grp) * quarter + i // 2 * size

            @pl.loop(0, size, unroll=4)
            def _(b, piece=piece, start=start, there=there):
                store(start + b, there * 2 + sub, piece[b])
                store(start + b, there * 2 + 1 - sub, piece[size + b])


def front_kernel(first_got, own, got, scale, codes, codes_got, *refs):
    moved, (mine_ref, theirs_ref, wide, weight) = refs[:-4], refs[-4:]
    blocks, rows, units = codes.shape
    first = lax.axis_index("sub") * (blocks // 2)
    widen(scale, wide)

    def store(b, shard, piece):
        at = pl.ds(pl.multiple_of(shard * rows, ROW_TILE), rows)
        for g in range(units // LANES):
            cols = slice(g * LANES, (g + 1) * LANES)
            factor = wide[g * wide.shape[0] * LANES // units, pl.ds(first + b, 1), :]
            weight[b, at, cols] = (piece[:, cols].astype(F32) * factor).astype(BF16)

    place_shards(codes, codes_got, first_got, moved, store)
    matrix = weight[...].reshape(-1, units)
    mine_ref[...] = dot(own[...], matrix)
    theirs_ref[...] = dot(got[...], matrix).astype(BF16)


def back_kernel(first_got, own, got, scale, codes, codes_got, *refs):
    moved, (mine_ref, theirs_ref, wide, weight) = refs[:-4], refs[-4:]
    blocks, rows, block = codes.shape
    first = lax.axis_index("sub") * (blocks // 2)
    per_group = weight.shape[0] // wide.shape[0]
    widen(scale, wide)

    def store(b, shard, piece):
        at = pl.multiple_of(shard * rows, ROW_TILE)
        factor = wide[at // per_group, pl.ds(first + b, 1), :]
        cols = pl.ds(pl.multiple_of(b * block, block), block)
        weight[pl.ds(at, rows), cols] = (piece.astype(F32) * factor).astype(BF16)

    place_shards(codes, codes_got, first_got, moved, store)
    matrix = weight[...]
    mine_ref[...] = contract_dims(own[...], matrix, 1, 1)
    theirs_ref[...] = contract_dims(got[...], matrix, 1, 1).astype(BF16)


def place_own(scratch, own, more, axis):
    n = len(more) + 1
    size = own.shape[axis]
    for k, ref in enumerate((own, *more)):
        at = pl.ds(pl.multiple_of(lax.rem(lax.axis_index("mp") + n - k, n) * size, size), size)
        if axis == 0:
            scratch[at, :] = ref[...]
        else:
            scratch[:, at] = ref[...]


def own_units(full, ref, axis):
    size = ref.shape[axis]
    for i in range(full.shape[axis] // size):

        @pl.when(lax.axis_index("mp") == i)
        def _(i=i):
            ref[...] = lax.slice_in_dim(full, i * size, (i + 1) * size, axis=axis).astype(BF16)


def low_sums(low, low_more):
    total = low[...]
    for ref in low_more:
        total = total + ref[...]
    half = total.shape[1] // 2
    return total[:, :half].astype(BF16), total[:, half:].astype(BF16)


def gather_adapters(adapters, adapters_more, up_out_all, down_in_all):
    rank = up_out_all.shape[0]
    place_own(up_out_all, adapters.at[:rank], [r.at[:rank] for r in adapters_more], 1)
    place_own(down_in_all, adapters.at[rank:], [r.at[rank:] for r in adapters_more], 0)


def hidden_kernel(more, gate, up, low, adapters, *refs):
    gate_more, up_more, low_more, adapters_more = (refs[i * more : (i + 1) * more] for i in range(4))
    silu_ref, low_ref, down_in_term, up_out_all, down_in_all = refs[4 * more :]
    gather_adapters(adapters, adapters_more, up_out_all, down_in_all)
    low_up, low_out = low_sums(low, low_more)
    gate_sum, up_sum = gate[...], up[...]
    for ref in gate_more:
        gate_sum = gate_sum + ref[...].astype(F32)
    for ref in up_more:
        up_sum = up_sum + ref[...].astype(F32)
    up_sum = up_sum + ADAPTER_SCALE * dot(low_up, up_out_all[...])
    silu = gate_sum * jax.nn.sigmoid(gate_sum)
    silu_ref[...] = silu
    hidden = (silu * up_sum).astype(BF16)
    low_ref[...] = (ADAPTER_SCALE * dot(hidden, down_in_all[...])).astype(BF16)
    hidden_t = hidden.astype(F32).T.astype(BF16)
    own_units(ADAPTER_SCALE * dot(hidden_t, low_out), down_in_term, 0)


def up_grad_kernel(more, back, silu, low, adapters, *refs):
    back_more, low_more, adapters_more = (refs[i * more : (i + 1) * more] for i in range(3))
    low_ref, up_out_term, up_out_all, down_in_all = refs[3 * more :]
    gather_adapters(adapters, adapters_more, up_out_all, down_in_all)
    low_up, low_out = low_sums(low, low_more)
    total = back[...]
    for ref in back_more:
        total = total + ref[...].astype(F32)
    total = total + ADAPTER_SCALE * contract_dims(low_out, down_in_all[...], 1, 1)
    up_grad = (total * silu[...]).astype(BF16)
    low_ref[...] = (ADAPTER_SCALE * contract_dims(up_grad, up_out_all[...], 1, 1)).astype(BF16)
    low_up_t = low_up.astype(F32).T.astype(BF16)
    own_units(ADAPTER_SCALE * dot(low_up_t, up_grad), up_out_term, 1)


def down_out_kernel(n, low, low_got, grad, grad_got, *out_refs):
    pos = ring_position()
    streams = len(out_refs) // n
    low_t = jnp.concatenate([low[...], low_got[...]], axis=0).astype(F32).T.astype(BF16)
    rows = low.shape[0]
    for k, ref in enumerate(out_refs):
        size = ref.shape[1]
        block = lax.rem(pos - 1 - k // streams + 2 * n, n) * streams + k % streams
        at = pl.ds(pl.multiple_of(block * size, size), size)
        ref[...] = (
            dot(low_t[:, :rows], grad[:, at]) + dot(low_t[:, rows:], grad_got[:, at])
        ).astype(BF16)


def up_in_kernel(n, low, low_got, normed_t, up_out_term, down_in_term, *out_refs):
    pos = ring_position()
    streams = len(out_refs) // n
    size = normed_t.shape[0] // len(out_refs)
    extra = out_refs[0].shape[0] - size
    both = jnp.concatenate([low[...], low_got[...]], axis=0)
    for k, ref in enumerate(out_refs):
        block = lax.rem(pos - 1 - k // streams + 2 * n, n) * streams + k % streams
        at = pl.ds(pl.multiple_of(block * size, size), size)
        ref[pl.ds(0, size), :] = dot(normed_t[at, :], both).astype(BF16)
        per = up_out_term.shape[0] // extra
        index = pl.ds(pl.multiple_of(lax.rem(block, per) * extra, extra), extra)

        @pl.when(block < per)
        def _(ref=ref, index=index):
            ref[pl.ds(size, extra), :] = up_out_term[index, :]

        @pl.when(block >= per)
        def _(ref=ref, index=index):
            ref[pl.ds(size, extra), :] = down_in_term[index, :]


def copy_all(copies):
    for c in copies:
        c.start()
    for c in copies:
        c.wait()


def down_out_place_kernel(n, *refs):
    pieces, (out_ref, sems) = refs[:-2], refs[-2:]
    pos, sub = ring_position(), lax.axis_index("sub")
    per_core = len(pieces) // 2
    streams = per_core // n
    copies = []
    for i, piece in enumerate(pieces):
        half = sub if i < per_core else 1 - sub
        block = lax.rem(pos - i % per_core // streams + n, n) * streams + i % streams
        size = piece.shape[1]
        at = pl.ds(pl.multiple_of((half * per_core + block) * size, size), size)
        copies.append(pltpu.make_async_copy(piece, out_ref.at[:, at], sems.at[i]))
    copy_all(copies)


def up_in_place_kernel(n, *refs):
    pieces, (out_ref, up_out_ref, down_in_ref, small, sems) = refs[:-5], refs[-5:]
    pos, sub = ring_position(), lax.axis_index("sub")
    per_core = len(pieces) // 2
    streams = per_core // n
    size = out_ref.shape[0] // len(pieces)
    extra = pieces[0].shape[0] - size
    copies = []
    for i, piece in enumerate(pieces):
        half = sub if i < per_core else 1 - sub
        block = lax.rem(pos - i % per_core // streams + n, n) * streams + i % streams
        at = pl.ds(pl.multiple_of((half * per_core + block) * size, size), size)
        copies.append(
            pltpu.make_async_copy(piece.at[pl.ds(0, size), :], out_ref.at[at, :], sems.at[2 * i])
        )
        at = pl.ds(pl.multiple_of(block * extra, extra), extra)
        copies.append(
            pltpu.make_async_copy(
                piece.at[pl.ds(size, extra), :], small.at[i // per_core, at, :], sems.at[2 * i + 1]
            )
        )
    copy_all(copies)
    total = (small[0].astype(F32) + small[1].astype(F32)).astype(BF16)
    rows = up_out_ref.shape[0]
    up_out_ref[...] = total[:rows]
    down_in_ref[...] = total[rows:]


def half_kernel(*refs):
    sources, out_ref, sems = refs[:-2], refs[-2], refs[-1]
    other = 1 - lax.axis_index("sub")
    half = sources[0].shape[0] // 2
    copy_all(
        [
            pltpu.make_async_copy(
                ref.at[pl.ds(other * half, half)], out_ref.at[pl.ds(i * half, half)], sems.at[i]
            )
            for i, ref in enumerate(sources)
        ]
    )


def quarter_kernel(count, *refs):
    sources, got, out_refs, sems = refs[:count], refs[count], refs[count + 1 : -1], refs[-1]
    streams = len(out_refs) // count
    sub, grp = lax.axis_index("sub"), lax.axis_index("grp")
    half = sources[0].shape[0] // 2
    quarter = half // 2
    copies = []
    size = quarter // streams
    for i, out_ref in enumerate(out_refs):
        first = grp * quarter + i % streams * size
        own = sources[i // streams].at[pl.ds(sub * half + first, size)]
        theirs = got.at[pl.ds(i // streams * half + first, size)]
        for k, source in enumerate((own, theirs)):
            copies.append(
                pltpu.make_async_copy(source, out_ref.at[pl.ds(k * size, size)], sems.at[2 * i + k])
            )
    copy_all(copies)


def start_shards(codes, streams):
    blocks, rows, units = codes[0].shape
    count = len(codes)
    anywhere = pl.BlockSpec(memory_space=pl.ANY)
    (send,) = call(
        half_kernel,
        "halves",
        codes,
        [shape((count * blocks // 2, rows, units))],
        scratch=[pltpu.SemaphoreType.DMA((count,))],
        specs=[anywhere] * count,
        out_specs=(anywhere,),
        limit=4,
    )
    got = swap(send, "sub")
    moving = call(
        lambda *refs: quarter_kernel(count, *refs),
        "quarters",
        [*codes, got],
        [shape((blocks // 2 // streams, rows, units))] * (count * streams),
        scratch=[pltpu.SemaphoreType.DMA((2 * count * streams,))],
        specs=[anywhere] * (count + 1),
        out_specs=(anywhere,) * (count * streams),
        limit=4,
    )
    return list(moving), got


def fast_body(
    tokens,
    cotangent,
    rms_norm_gain,
    gate_codes,
    gate_block_scale,
    up_codes,
    up_block_scale,
    down_codes,
    down_block_scale,
    up_adapter_in,
    up_adapter_out,
    down_adapter_in,
    down_adapter_out,
    sequence_length_list,
    slot_sequence_index,
):
    rows, local_width = tokens.shape
    blocks, _, units = gate_codes.shape
    block = local_width // blocks
    half = local_width // 2
    rank = up_adapter_in.shape[1]
    total_width = local_width * lax.axis_size("mp")
    n = lax.axis_size("dp")
    more = lax.axis_size("mp") - 1

    (gate_moving, up_moving), front_got = start_shards([gate_codes, up_codes], 1)
    ring, crossed = [], []

    def step(moving, *done):
        ring.append(ring_step(after(moving, *done) if done else moving))
        if len(ring) > 2:
            crossed.append(swap(ring[-1], "grp"))

    step(gate_moving)
    step(up_moving)

    vmem = pl.BlockSpec(memory_space=pltpu.VMEM)
    smem = pl.BlockSpec(memory_space=pltpu.SMEM)
    hbm = pl.BlockSpec(memory_space=pltpu.HBM)
    buffers = [pltpu.VMEM((rows, local_width), BF16), pltpu.SemaphoreType.DMA((8,))]
    lengths = after(sequence_length_list, gate_moving, up_moving)
    (squares,) = call(
        square_kernel, "squares", [tokens, lengths], [shape((rows, LANES), F32)],
        scratch=buffers, specs=[hbm, smem], limit=16,
    )
    squares_more = others(squares, "mp")
    grad_send, grad, low_out = call(
        lambda *refs: cotangent_kernel(rows * n * lax.axis_size("sub"), *refs),
        "cotangent",
        [cotangent, after(lengths, squares), slot_sequence_index[None, :], down_adapter_out],
        [shape((rows, half))] * 2 + [shape((rows, rank), F32)],
        scratch=buffers,
        specs=[hbm, smem, vmem, vmem],
    )
    crossed += [swap(after(r, grad), "grp") for r in ring]
    step(ring[0], ring[1], grad)
    step(ring[1], ring[0], grad)
    down_turned = jnp.swapaxes(after(down_codes, ring[2]), 0, 1)
    down_moving, down_got = start_shards([down_turned], STREAMS)
    normed_send, normed, low = call(
        lambda *refs: token_kernel(total_width, *refs),
        "tokens",
        [tokens, rms_norm_gain[None, :], up_adapter_in, low_out, after(squares, *ring[2:4], *crossed[:2], *down_moving), *squares_more],
        [shape((rows, half))] * 2 + [shape((rows, 2 * rank), F32)],
        scratch=buffers,
        specs=[hbm] + [vmem] * (4 + more),
    )
    grad_got = swap(grad_send, "sub")
    normed_got = swap(normed_send, "sub")
    low_more = others(low, "mp")
    step(ring[2], ring[3], *crossed[:2])
    step(ring[3], ring[2], *crossed[:2])
    adapters = jnp.concatenate([up_adapter_out, down_adapter_in], axis=0)
    adapters_more = others(after(adapters, ring[4]), "mp")
    pinned = [*ring[4:6], *crossed[2:4], grad_got, normed_got]
    for moving in down_moving:
        step(moving, *pinned)
    for moving in ring[-STREAMS:]:
        step(moving, *low_more, *adapters_more)

    def product(kernel, name, own, got, scale, codes, codes_got, first_got, steps, weight_shape):
        groups = scale.shape[0]
        mine, theirs = call(
            lambda *refs: kernel(first_got, *refs),
            name,
            [own, got, scale, codes, codes_got, *[x for k in steps for x in (ring[k], crossed[k])]],
            [shape((rows, units), F32), shape((rows, units))],
            scratch=[pltpu.VMEM((groups, blocks, LANES), F32), pltpu.VMEM(weight_shape, BF16)],
            flops=4 * rows * half * units,
        )
        total = mine + swap(theirs, "sub").astype(F32)
        return total, others(total.astype(BF16), "mp"), mine

    front = (blocks // 2, block, units)
    first_down = ring[2 * (n - 1) : 2 * (n - 1) + STREAMS]
    half_blocks = blocks // 2
    gate, gate_more, gate_mine = product(
        front_kernel, "gate", normed, normed_got, after(gate_block_scale.T, *first_down), gate_codes, front_got, 0,
        range(0, 2 * (n - 1), 2), front,
    )
    up, up_more, up_mine = product(
        front_kernel, "up", normed, normed_got, after(up_block_scale.T, *first_down), up_codes, front_got, half_blocks,
        range(1, 2 * (n - 1), 2), front,
    )
    for _ in range(n - 3):
        for moving, other in zip(ring[-STREAMS:], crossed[-2 * STREAMS : -STREAMS]):
            step(moving, gate_mine, up_mine, other)
    small_scratch = [
        pltpu.VMEM((rank, units), BF16),
        pltpu.VMEM((units, rank), BF16),
    ]
    silu, low_hidden, down_in_term = call(
        lambda *refs: hidden_kernel(more, *refs),
        "hidden",
        [gate, up, low, after(adapters, *ring[-2 * STREAMS : -STREAMS]), *gate_more, *up_more, *low_more, *adapters_more],
        [shape((rows, units), F32), shape((rows, rank)), shape(down_adapter_in.shape)],
        scratch=small_scratch,
        limit=8,
    )
    pieces = STREAMS * n
    down_out_parts = call(
        lambda *refs: down_out_kernel(n, *refs),
        "down_out",
        [low_hidden, swap(low_hidden, "sub"), grad, grad_got],
        [shape((rank, half // pieces))] * pieces,
        flops=4 * rows * half * rank,
    )
    down_out_blocks, seen = ring_all(down_out_parts, STREAMS)
    (normed_t,) = call(
        transpose_kernel,
        "transpose",
        [normed, after(normed_got, low_hidden)],
        [shape((half, 2 * rows))],
        limit=32,
    )

    back, back_more, _ = product(
        back_kernel, "back", grad, grad_got, after(down_block_scale, normed_t, down_out_parts[0]), down_turned, down_got, 0,
        range(2 * (n - 1), (2 + STREAMS) * (n - 1)), (units, half),
    )
    low_grad, up_out_term = call(
        lambda *refs: up_grad_kernel(more, *refs),
        "up_grad",
        [back, silu, low, after(adapters, *seen[0]), *back_more, *low_more, *adapters_more],
        [shape((rows, rank)), shape(up_adapter_out.shape)],
        scratch=small_scratch,
        limit=8,
    )
    extra = 2 * rank // pieces
    up_in_parts = call(
        lambda *refs: up_in_kernel(n, *refs),
        "up_in",
        [after(low_grad, *seen[1]), swap(low_grad, "sub"), normed_t, up_out_term, down_in_term],
        [shape((half // pieces + extra, rank))] * pieces,
        flops=4 * rows * half * rank,
    )
    up_in_blocks, _ = ring_all(up_in_parts, STREAMS, down_out_blocks[-STREAMS:])

    anywhere = pl.BlockSpec(memory_space=pl.ANY)
    (down_out_gradient,) = call(
        lambda *refs: down_out_place_kernel(n, *refs),
        "down_out_place",
        down_out_blocks,
        [shape((rank, local_width))],
        scratch=[pltpu.SemaphoreType.DMA((2 * pieces,))],
        specs=[anywhere] * (2 * pieces),
        out_specs=(anywhere,),
        limit=4,
    )
    up_in_gradient, up_out_gradient, down_in_gradient = call(
        lambda *refs: up_in_place_kernel(n, *refs),
        "up_in_place",
        up_in_blocks,
        [shape((local_width, rank)), shape(up_adapter_out.shape), shape(down_adapter_in.shape)],
        scratch=[pltpu.VMEM((2, 2 * rank, rank), BF16), pltpu.SemaphoreType.DMA((4 * pieces,))],
        specs=[anywhere] * (2 * pieces),
        out_specs=(anywhere, vmem, vmem),
        limit=4,
    )
    return up_in_gradient, up_out_gradient, down_in_gradient, down_out_gradient


def general_body(
    tokens,
    cotangent,
    rms_norm_gain,
    gate_codes,
    gate_block_scale,
    up_codes,
    up_block_scale,
    down_codes,
    down_block_scale,
    up_adapter_in,
    up_adapter_out,
    down_adapter_in,
    down_adapter_out,
    sequence_length_list,
    slot_sequence_index,
):
    rows = tokens.shape[0]
    local_width = tokens.shape[1]
    block = gate_block_scale.shape[0] and local_width // gate_codes.shape[0]
    blocks_here = gate_codes.shape[0]
    total_width = local_width * lax.axis_size("mp")
    own_squares = jnp.sum(jnp.square(tokens.astype(jnp.float32)), axis=-1, keepdims=True)
    squares = lax.psum(own_squares, "mp") / total_width
    inv_rms = lax.rsqrt(squares + EPS)
    local_normed_input = (
        tokens.astype(jnp.float32) * inv_rms * rms_norm_gain.astype(jnp.float32)[None, :]
    ).astype(jnp.bfloat16)
    seq_count = sequence_length_list.shape[1]
    longest = rows // seq_count
    total = rows * lax.axis_size("dp") * lax.axis_size("sub")
    ratios = longest / sequence_length_list[0].astype(jnp.float32)
    match = slot_sequence_index[:, None] == jnp.arange(seq_count, dtype=jnp.int32)[None, :]
    token_weight = jnp.sum(jnp.where(match, ratios[None, :], jnp.float32(0.0)), axis=-1)
    token_weight = token_weight * jnp.float32(1.0 / math.sqrt(total))
    local_output = (cotangent.astype(jnp.float32) * token_weight[:, None]).astype(jnp.bfloat16)
    partial_up = jnp.dot(local_normed_input, up_adapter_in, preferred_element_type=jnp.float32)
    partial_output = contract_dims(local_output, down_adapter_out, 1, 1)
    up_adapter_rank, output_adapter_rank = lax.psum((partial_up, partial_output), "mp")
    up_adapter_rank = up_adapter_rank.astype(jnp.bfloat16)
    output_adapter_rank = output_adapter_rank.astype(jnp.bfloat16)
    normed_blocks = local_normed_input.reshape(rows, blocks_here, block)
    out_blocks = local_output.reshape(rows, blocks_here, block)
    wide_gate = jnp.repeat(gate_block_scale.astype(jnp.float32), block, axis=1)[:, None, :]
    wide_up = jnp.repeat(up_block_scale.astype(jnp.float32), block, axis=1)[:, None, :]
    wide_down = jnp.repeat(down_block_scale.astype(jnp.float32), block, axis=0)
    dims_front = (((1, 2), (0, 1)), ((), ()))
    dims_back = (((1, 2), (1, 2)), ((), ()))
    quant_g = lax.all_gather(gate_codes, ("dp", "sub"), axis=1, tiled=True)
    quant_u = lax.all_gather(up_codes, ("dp", "sub"), axis=1, tiled=True)
    weight_g = (quant_g.astype(jnp.float32) * wide_gate).astype(jnp.bfloat16)
    weight_u = (quant_u.astype(jnp.float32) * wide_up).astype(jnp.bfloat16)
    gate_next = lax.dot_general(
        normed_blocks, weight_g, dims_front, preferred_element_type=jnp.float32
    )
    up_next = lax.dot_general(
        normed_blocks, weight_u, dims_front, preferred_element_type=jnp.float32
    )
    gate, base_up_projected = (
        lax.psum_scatter(gate_next, "mp", scatter_dimension=1, tiled=True),
        lax.psum_scatter(up_next, "mp", scatter_dimension=1, tiled=True),
    )
    up_projected = base_up_projected + ADAPTER_SCALE * jnp.dot(
        up_adapter_rank, up_adapter_out, preferred_element_type=jnp.float32
    )
    silu_gate = jax.nn.silu(gate)
    hidden_units = (silu_gate * up_projected).astype(jnp.bfloat16)
    partial_hidden = jnp.dot(hidden_units, down_adapter_in, preferred_element_type=jnp.float32)
    hidden_adapter_rank = lax.psum(partial_hidden, "mp").astype(jnp.bfloat16)
    weight_d = (
        lax.all_gather(down_codes, ("dp", "sub"), axis=0, tiled=True).astype(jnp.float32)
        * wide_down[:, :, None]
    ).astype(jnp.bfloat16)
    back_part = lax.dot_general(out_blocks, weight_d, dims_back, preferred_element_type=jnp.float32)
    base_backward = lax.psum_scatter(back_part, "mp", scatter_dimension=1, tiled=True)
    hidden_gradient = base_backward + ADAPTER_SCALE * contract_dims(
        output_adapter_rank, down_adapter_in, 1, 1
    )
    up_gradient = (hidden_gradient * silu_gate).astype(jnp.bfloat16)
    partial_gradient = contract_dims(up_gradient, up_adapter_out, 1, 1)
    up_adapter_rank_gradient = lax.psum(partial_gradient, "mp").astype(jnp.bfloat16)
    up_in_term = ADAPTER_SCALE * contract_dims(local_normed_input, up_adapter_rank_gradient, 0, 0)
    up_out_term = ADAPTER_SCALE * contract_dims(up_adapter_rank, up_gradient, 0, 0)
    down_in_term = ADAPTER_SCALE * contract_dims(hidden_units, output_adapter_rank, 0, 0)
    down_out_term = ADAPTER_SCALE * contract_dims(hidden_adapter_rank, local_output, 0, 0)
    sum_up_a, sum_up_b, sum_down_a, sum_down_b = lax.psum(
        (up_in_term, up_out_term, down_in_term, down_out_term), ("dp", "sub")
    )
    return (
        sum_up_a.astype(jnp.bfloat16),
        sum_up_b.astype(jnp.bfloat16),
        sum_down_a.astype(jnp.bfloat16),
        sum_down_b.astype(jnp.bfloat16),
    )


def body(tokens, cotangent, rms_norm_gain, gate_codes, *rest):
    whole_tiles = gate_codes.shape[1] % ROW_TILE == 0
    form = fast_body if whole_tiles else general_body
    return form(tokens, cotangent, rms_norm_gain, gate_codes, *rest)


def solution(mesh):
    placed = (
        P(("grp", "dp", "sub"), "mp"),
        P(("grp", "dp", "sub"), "mp"),
        P("mp"),
        P("mp", ("dp", "sub"), None),
        P("mp", None),
        P("mp", ("dp", "sub"), None),
        P("mp", None),
        P(("dp", "sub"), "mp", None),
        P(None, "mp"),
        P(("grp", "mp"), None),
        P("grp", "mp"),
        P(("grp", "mp"), None),
        P("grp", "mp"),
        P(("grp", "dp", "sub"), None),
        P(("grp", "dp", "sub")),
    )
    return jax.shard_map(
        body,
        mesh=mesh,
        in_specs=placed,
        out_specs=(P(("grp", "mp"), None), P("grp", "mp"), P(("grp", "mp"), None), P("grp", "mp")),
        check_vma=False,
    )
```

```python
import math

import jax
import jax.numpy as jnp
from jax import lax
from jax.experimental import pallas as pl
from jax.experimental.pallas import tpu as pltpu
from jax.sharding import PartitionSpec as P

ADAPTER_SCALE = 2.0
EPS = 1e-05
ROW_TILE = 16
LANES = 128
STREAMS = 2
MIB = 1024 * 1024

F32 = jnp.float32
BF16 = jnp.bfloat16


def contract_dims(left, right, left_dim, right_dim):
    return lax.dot_general(
        left, right, (((left_dim,), (right_dim,)), ((), ())), preferred_element_type=F32
    )


def dot(left, right):
    return jnp.dot(left, right, preferred_element_type=F32)


def ring_at(pos, n):
    if isinstance(pos, int):
        return 0 if pos == 0 else (2 * pos - 1 if 2 * pos <= n else 2 * (n - pos))
    return jnp.where(pos == 0, 0, jnp.where(2 * pos <= n, 2 * pos - 1, 2 * (n - pos)))


def ring_position():
    n = lax.axis_size("dp")
    place = lax.axis_index("dp")
    odd = lax.rem(place, 2) == 1
    return jnp.where(place == 0, 0, jnp.where(odd, (place + 1) // 2, n - place // 2))


def ring_step(x):
    n = lax.axis_size("dp")
    return lax.ppermute(x, "dp", [(ring_at(i, n), ring_at((i + 1) % n, n)) for i in range(n)])


def swap(x, axis):
    return lax.ppermute(x, axis, [(0, 1), (1, 0)])


def others(x, axis):
    n = lax.axis_size(axis)
    return [lax.ppermute(x, axis, [(i, (i + k) % n) for i in range(n)]) for k in range(1, n)]


def after(x, *done):
    return lax.optimization_barrier((x, *done))[0]


def call(kernel, name, args, out_shape, scratch=(), specs=None, limit=24, flops=0, out_specs=None):
    vmem = pl.BlockSpec(memory_space=pltpu.VMEM)
    moved = sum(a.size * a.dtype.itemsize for a in args) + sum(
        math.prod(s.shape) * s.dtype.itemsize for s in out_shape
    )
    return pl.pallas_call(
        kernel,
        out_shape=tuple(out_shape),
        in_specs=specs or [vmem] * len(args),
        out_specs=out_specs or tuple([vmem] * len(out_shape)),
        scratch_shapes=list(scratch),
        compiler_params=pltpu.CompilerParams(vmem_limit_bytes=limit * MIB),
        cost_estimate=pl.CostEstimate(flops=0, bytes_accessed=0, transcendentals=0),
        name=name,
    )(*args)


def shape(dims, dtype=BF16):
    return jax.ShapeDtypeStruct(tuple(dims), dtype)


def add_kernel(left, right, out_ref):
    out_ref[...] = (left[...].astype(F32) + right[...].astype(F32)).astype(BF16)


def add(left, right):
    return call(add_kernel, "add", [left, right], [shape(left.shape)], limit=4)[0]


def ring_all(parts, streams):
    n = lax.axis_size("dp")
    seen = []
    totals = list(parts[:streams])
    for k in range(1, n):
        seen.append([ring_step(t) for t in totals])
        totals = [add(t, p) for t, p in zip(seen[-1], parts[k * streams : (k + 1) * streams])]
    blocks = list(totals)
    for _ in range(n - 1):
        totals = [ring_step(t) for t in totals]
        seen.append(totals)
        blocks += totals
    return blocks + [swap(b, "sub") for b in blocks], seen


def scaled_halves(wide, low_ref, cols, scaled, product, send_ref, own_ref, copy):
    half = send_ref.shape[1]
    step = half // 4
    sub = lax.axis_index("sub")
    low_ref[:, cols] = jnp.zeros((wide.shape[0], LANES), F32)
    for n, (which, out_ref) in enumerate(((1 - sub, send_ref), (sub, own_ref))):

        @pl.loop(0, half // step)
        def _(j, n=n, which=which, out_ref=out_ref):
            first = pl.multiple_of(which * half + j * step, step)
            copy(n * (half // step) + j, first, step).wait()
            parts = []
            for i in range(step // LANES):
                tile = pl.ds(pl.multiple_of(first + i * LANES, LANES), LANES)
                parts.append(scaled(wide[:, tile].astype(F32), tile).astype(BF16))
            value = jnp.concatenate(parts, axis=1)
            out_ref[:, pl.ds(pl.multiple_of(j * step, step), step)] = value
            low_ref[:, cols] += product(value, pl.ds(first, step))


def column_copy(source, buffer, sems):
    def copy(k, first, step):
        at = pl.ds(first, step)
        return pltpu.make_async_copy(source.at[:, at], buffer.at[:, at], sems.at[k])

    return copy


def start_halves(source, buffer, sems):
    half = source.shape[1] // 2
    step = half // 4
    copy = column_copy(source, buffer, sems)
    sub = lax.axis_index("sub")
    for k in range(8):
        which = 1 - sub if k < 4 else sub
        copy(k, pl.multiple_of(which * half + k % 4 * step, step), step).start()
    return copy


def square_kernel(tokens, lengths, square_ref, buffer, sems):
    width = tokens.shape[1]
    step = width // sems.shape[0]
    copy = column_copy(tokens, buffer, sems)
    for k in range(width // step):
        copy(k, k * step, step).start()
    squares = jnp.zeros(square_ref.shape, F32)
    for k in range(width // step):
        copy(k, k * step, step).wait()
        for i in range(step // LANES):
            at = k * step + i * LANES
            squares = squares + jnp.square(buffer[:, at : at + LANES].astype(F32))
    square_ref[...] = jnp.broadcast_to(jnp.sum(squares, axis=1, keepdims=True), square_ref.shape)


def cotangent_kernel(
    total, cotangent, lengths, slots, adapter, send_ref, own_ref, low_ref, buffer, sems
):
    rows = cotangent.shape[0]
    copy = start_halves(cotangent, buffer, sems)
    index = jnp.broadcast_to(slots[...], (LANES, rows))
    weight = jnp.zeros((LANES, rows), F32)
    for s in range(lengths.shape[1]):
        length = jnp.full((LANES, rows), lengths[0, s], jnp.int32).astype(F32)
        weight = weight + jnp.where(index == s, (rows // lengths.shape[1]) / length, 0.0)
    row = (weight * F32(1.0 / math.sqrt(total))).T
    scaled_halves(
        buffer,
        low_ref,
        slice(None),
        lambda tile, cols: tile * row,
        lambda value, cols: contract_dims(value, adapter[:, cols], 1, 1),
        send_ref,
        own_ref,
        copy,
    )


def token_kernel(total_width, tokens, gain, adapter, low_out, squares, *refs):
    squares_more, (send_ref, own_ref, low_ref, buffer, sems) = refs[:-5], refs[-5:]
    copy = start_halves(tokens, buffer, sems)
    rank = adapter.shape[1]
    total = squares[...]
    for ref in squares_more:
        total = total + ref[...]
    row = lax.rsqrt(total / total_width + EPS)
    low_ref[:, rank:] = low_out[...]
    scaled_halves(
        buffer,
        low_ref,
        slice(0, rank),
        lambda tile, cols: tile * row * gain[:, cols].astype(F32),
        lambda value, cols: dot(value, adapter[cols, :]),
        send_ref,
        own_ref,
        copy,
    )


def transpose_kernel(own, got, out_ref):
    rows, step = own.shape[0], out_ref.shape[0]
    for i, ref in enumerate((own, got)):
        out_ref[:, i * rows : (i + 1) * rows] = ref[...].astype(F32).T.astype(BF16)


def widen(scale, wide):
    for g in range(scale.shape[0]):
        row = scale[g : g + 1, :].astype(F32)
        wide[g] = jnp.broadcast_to(row, (LANES, row.shape[1])).T


def place_shards(codes, got, first_got, moved, store):
    n = lax.axis_size("dp")
    sub, grp, place = (lax.axis_index(a) for a in ("sub", "grp", "dp"))
    pos = ring_position()
    blocks = codes.shape[0] // 2
    quarter = blocks // 2

    @pl.loop(0, blocks, unroll=4)
    def _(b):
        store(b, place * 2 + sub, codes[sub * blocks + b])
        store(b, place * 2 + 1 - sub, got[first_got + b])

    streams = len(moved) // (2 * (n - 1))
    size = quarter // streams
    for k in range(n - 1):
        there = ring_at(lax.rem(pos - k - 1 + n, n), n)
        for i in range(2 * streams):
            piece = moved[2 * streams * k + i]
            start = (grp if i % 2 == 0 else 1 - grp) * quarter + i // 2 * size

            @pl.loop(0, size, unroll=4)
            def _(b, piece=piece, start=start, there=there):
                store(start + b, there * 2 + sub, piece[b])
                store(start + b, there * 2 + 1 - sub, piece[size + b])


def front_kernel(first_got, own, got, scale, codes, codes_got, *refs):
    moved, (mine_ref, theirs_ref, wide, weight) = refs[:-4], refs[-4:]
    blocks, rows, units = codes.shape
    first = lax.axis_index("sub") * (blocks // 2)
    widen(scale, wide)

    def store(b, shard, piece):
        at = pl.ds(pl.multiple_of(shard * rows, ROW_TILE), rows)
        for g in range(units // LANES):
            cols = slice(g * LANES, (g + 1) * LANES)
            factor = wide[g * wide.shape[0] * LANES // units, pl.ds(first + b, 1), :]
            weight[b, at, cols] = (piece[:, cols].astype(F32) * factor).astype(BF16)

    place_shards(codes, codes_got, first_got, moved, store)
    matrix = weight[...].reshape(-1, units)
    mine_ref[...] = dot(own[...], matrix)
    theirs_ref[...] = dot(got[...], matrix).astype(BF16)


def back_kernel(first_got, own, got, scale, codes, codes_got, *refs):
    moved, (mine_ref, theirs_ref, wide, weight) = refs[:-4], refs[-4:]
    blocks, rows, block = codes.shape
    first = lax.axis_index("sub") * (blocks // 2)
    per_group = weight.shape[0] // wide.shape[0]
    widen(scale, wide)

    def store(b, shard, piece):
        at = pl.multiple_of(shard * rows, ROW_TILE)
        factor = wide[at // per_group, pl.ds(first + b, 1), :]
        cols = pl.ds(pl.multiple_of(b * block, block), block)
        weight[pl.ds(at, rows), cols] = (piece.astype(F32) * factor).astype(BF16)

    place_shards(codes, codes_got, first_got, moved, store)
    matrix = weight[...]
    mine_ref[...] = contract_dims(own[...], matrix, 1, 1)
    theirs_ref[...] = contract_dims(got[...], matrix, 1, 1).astype(BF16)


def place_own(scratch, own, more, axis):
    n = len(more) + 1
    size = own.shape[axis]
    for k, ref in enumerate((own, *more)):
        at = pl.ds(pl.multiple_of(lax.rem(lax.axis_index("mp") + n - k, n) * size, size), size)
        if axis == 0:
            scratch[at, :] = ref[...]
        else:
            scratch[:, at] = ref[...]


def own_units(full, ref, axis):
    size = ref.shape[axis]
    for i in range(full.shape[axis] // size):

        @pl.when(lax.axis_index("mp") == i)
        def _(i=i):
            ref[...] = lax.slice_in_dim(full, i * size, (i + 1) * size, axis=axis).astype(BF16)


def low_sums(low, low_more):
    total = low[...]
    for ref in low_more:
        total = total + ref[...]
    half = total.shape[1] // 2
    return total[:, :half].astype(BF16), total[:, half:].astype(BF16)


def gather_adapters(adapters, adapters_more, up_out_all, down_in_all):
    rank = up_out_all.shape[0]
    place_own(up_out_all, adapters.at[:rank], [r.at[:rank] for r in adapters_more], 1)
    place_own(down_in_all, adapters.at[rank:], [r.at[rank:] for r in adapters_more], 0)


def hidden_kernel(more, gate, up, low, adapters, *refs):
    gate_more, up_more, low_more, adapters_more = (refs[i * more : (i + 1) * more] for i in range(4))
    silu_ref, low_ref, down_in_term, up_out_all, down_in_all = refs[4 * more :]
    gather_adapters(adapters, adapters_more, up_out_all, down_in_all)
    low_up, low_out = low_sums(low, low_more)
    gate_sum, up_sum = gate[...], up[...]
    for ref in gate_more:
        gate_sum = gate_sum + ref[...].astype(F32)
    for ref in up_more:
        up_sum = up_sum + ref[...].astype(F32)
    up_sum = up_sum + ADAPTER_SCALE * dot(low_up, up_out_all[...])
    silu = gate_sum * jax.nn.sigmoid(gate_sum)
    silu_ref[...] = silu
    hidden = (silu * up_sum).astype(BF16)
    low_ref[...] = (ADAPTER_SCALE * dot(hidden, down_in_all[...])).astype(BF16)
    hidden_t = hidden.astype(F32).T.astype(BF16)
    own_units(ADAPTER_SCALE * dot(hidden_t, low_out), down_in_term, 0)


def up_grad_kernel(more, back, silu, low, adapters, *refs):
    back_more, low_more, adapters_more = (refs[i * more : (i + 1) * more] for i in range(3))
    low_ref, up_out_term, up_out_all, down_in_all = refs[3 * more :]
    gather_adapters(adapters, adapters_more, up_out_all, down_in_all)
    low_up, low_out = low_sums(low, low_more)
    total = back[...]
    for ref in back_more:
        total = total + ref[...].astype(F32)
    total = total + ADAPTER_SCALE * contract_dims(low_out, down_in_all[...], 1, 1)
    up_grad = (total * silu[...]).astype(BF16)
    low_ref[...] = (ADAPTER_SCALE * contract_dims(up_grad, up_out_all[...], 1, 1)).astype(BF16)
    low_up_t = low_up.astype(F32).T.astype(BF16)
    own_units(ADAPTER_SCALE * dot(low_up_t, up_grad), up_out_term, 1)


def down_out_kernel(n, low, low_got, grad, grad_got, *out_refs):
    pos = ring_position()
    streams = len(out_refs) // n
    low_t = jnp.concatenate([low[...], low_got[...]], axis=0).astype(F32).T.astype(BF16)
    rows = low.shape[0]
    for k, ref in enumerate(out_refs):
        size = ref.shape[1]
        block = lax.rem(pos - 1 - k // streams + 2 * n, n) * streams + k % streams
        at = pl.ds(pl.multiple_of(block * size, size), size)
        ref[...] = (
            dot(low_t[:, :rows], grad[:, at]) + dot(low_t[:, rows:], grad_got[:, at])
        ).astype(BF16)


def up_in_kernel(n, low, low_got, normed_t, up_out_term, down_in_term, *out_refs):
    pos = ring_position()
    streams = len(out_refs) // n
    size = normed_t.shape[0] // len(out_refs)
    extra = out_refs[0].shape[0] - size
    both = jnp.concatenate([low[...], low_got[...]], axis=0)
    for k, ref in enumerate(out_refs):
        block = lax.rem(pos - 1 - k // streams + 2 * n, n) * streams + k % streams
        at = pl.ds(pl.multiple_of(block * size, size), size)
        ref[pl.ds(0, size), :] = dot(normed_t[at, :], both).astype(BF16)
        per = up_out_term.shape[0] // extra
        index = pl.ds(pl.multiple_of(lax.rem(block, per) * extra, extra), extra)

        @pl.when(block < per)
        def _(ref=ref, index=index):
            ref[pl.ds(size, extra), :] = up_out_term[index, :]

        @pl.when(block >= per)
        def _(ref=ref, index=index):
            ref[pl.ds(size, extra), :] = down_in_term[index, :]


def copy_all(copies):
    for c in copies:
        c.start()
    for c in copies:
        c.wait()


def place_kernel(n, *refs):
    pieces = refs[:-7]
    out_ref, up_out_ref, down_in_ref, wide_ref, small, sems, small_sems = refs[-7:]
    pos, sub = ring_position(), lax.axis_index("sub")
    count = len(pieces) // 2
    per_core = count // 2
    streams = per_core // n
    size = out_ref.shape[0] // count
    extra = pieces[count].shape[0] - size
    copies = []
    for i in range(count):
        half = sub if i < per_core else 1 - sub
        block = lax.rem(pos - i % per_core // streams + n, n) * streams + i % streams
        at = pl.ds(pl.multiple_of((half * per_core + block) * size, size), size)
        copies.append(pltpu.make_async_copy(pieces[i], wide_ref.at[:, at], sems.at[2 * i]))
        piece = pieces[count + i]
        copies.append(
            pltpu.make_async_copy(piece.at[pl.ds(0, size), :], out_ref.at[at, :], sems.at[2 * i + 1])
        )
        at = pl.ds(pl.multiple_of(block * extra, extra), extra)
        copies.append(
            pltpu.make_async_copy(
                piece.at[pl.ds(size, extra), :], small.at[i // per_core, at, :], small_sems.at[i]
            )
        )
    copy_all(copies)
    total = (small[0].astype(F32) + small[1].astype(F32)).astype(BF16)
    rows = up_out_ref.shape[0]
    up_out_ref[...] = total[:rows]
    down_in_ref[...] = total[rows:]


def half_kernel(*refs):
    sources, out_ref, sems = refs[:-2], refs[-2], refs[-1]
    other = 1 - lax.axis_index("sub")
    half = sources[0].shape[0] // 2
    copy_all(
        [
            pltpu.make_async_copy(
                ref.at[pl.ds(other * half, half)], out_ref.at[pl.ds(i * half, half)], sems.at[i]
            )
            for i, ref in enumerate(sources)
        ]
    )


def quarter_kernel(count, *refs):
    sources, got, out_refs, sems = refs[:count], refs[count], refs[count + 1 : -1], refs[-1]
    streams = len(out_refs) // count
    sub, grp = lax.axis_index("sub"), lax.axis_index("grp")
    half = sources[0].shape[0] // 2
    quarter = half // 2
    copies = []
    size = quarter // streams
    for i, out_ref in enumerate(out_refs):
        first = grp * quarter + i % streams * size
        own = sources[i // streams].at[pl.ds(sub * half + first, size)]
        theirs = got.at[pl.ds(i // streams * half + first, size)]
        for k, source in enumerate((own, theirs)):
            copies.append(
                pltpu.make_async_copy(source, out_ref.at[pl.ds(k * size, size)], sems.at[2 * i + k])
            )
    copy_all(copies)


def start_shards(codes, streams):
    blocks, rows, units = codes[0].shape
    count = len(codes)
    anywhere = pl.BlockSpec(memory_space=pl.ANY)
    (send,) = call(
        half_kernel,
        "halves",
        codes,
        [shape((count * blocks // 2, rows, units))],
        scratch=[pltpu.SemaphoreType.DMA((count,))],
        specs=[anywhere] * count,
        out_specs=(anywhere,),
        limit=4,
    )
    got = swap(send, "sub")
    moving = call(
        lambda *refs: quarter_kernel(count, *refs),
        "quarters",
        [*codes, got],
        [shape((blocks // 2 // streams, rows, units))] * (count * streams),
        scratch=[pltpu.SemaphoreType.DMA((2 * count * streams,))],
        specs=[anywhere] * (count + 1),
        out_specs=(anywhere,) * (count * streams),
        limit=4,
    )
    return list(moving), got


def fast_body(
    tokens,
    cotangent,
    rms_norm_gain,
    gate_codes,
    gate_block_scale,
    up_codes,
    up_block_scale,
    down_codes,
    down_block_scale,
    up_adapter_in,
    up_adapter_out,
    down_adapter_in,
    down_adapter_out,
    sequence_length_list,
    slot_sequence_index,
):
    rows, local_width = tokens.shape
    blocks, _, units = gate_codes.shape
    block = local_width // blocks
    half = local_width // 2
    rank = up_adapter_in.shape[1]
    total_width = local_width * lax.axis_size("mp")
    n = lax.axis_size("dp")
    more = lax.axis_size("mp") - 1

    (gate_moving, up_moving), front_got = start_shards([gate_codes, up_codes], 1)
    ring, crossed = [], []

    def step(moving, *done):
        ring.append(ring_step(after(moving, *done) if done else moving))
        if len(ring) > 2:
            crossed.append(swap(ring[-1], "grp"))

    step(gate_moving)
    step(up_moving)

    vmem = pl.BlockSpec(memory_space=pltpu.VMEM)
    smem = pl.BlockSpec(memory_space=pltpu.SMEM)
    hbm = pl.BlockSpec(memory_space=pltpu.HBM)
    buffers = [pltpu.VMEM((rows, local_width), BF16), pltpu.SemaphoreType.DMA((8,))]
    lengths = after(sequence_length_list, gate_moving, up_moving)
    (squares,) = call(
        square_kernel, "squares", [tokens, lengths], [shape((rows, LANES), F32)],
        scratch=buffers, specs=[hbm, smem], limit=16,
    )
    squares_more = others(squares, "mp")
    grad_send, grad, low_out = call(
        lambda *refs: cotangent_kernel(rows * n * lax.axis_size("sub"), *refs),
        "cotangent",
        [cotangent, after(lengths, squares), slot_sequence_index[None, :], down_adapter_out],
        [shape((rows, half))] * 2 + [shape((rows, rank), F32)],
        scratch=buffers,
        specs=[hbm, smem, vmem, vmem],
    )
    down_turned = jnp.swapaxes(after(down_codes, squares), 0, 1)
    down_moving, down_got = start_shards([down_turned], 1)
    crossed += [swap(after(r, grad), "grp") for r in ring]
    step(ring[0], ring[1], grad, *down_moving)
    step(ring[1], ring[0], grad, *down_moving)
    normed_send, normed, low = call(
        lambda *refs: token_kernel(total_width, *refs),
        "tokens",
        [tokens, rms_norm_gain[None, :], up_adapter_in, low_out, after(squares, *ring[2:4], *crossed[:2]), *squares_more],
        [shape((rows, half))] * 2 + [shape((rows, 2 * rank), F32)],
        scratch=buffers,
        specs=[hbm] + [vmem] * (4 + more),
    )
    grad_got = swap(grad_send, "sub")
    normed_got = swap(normed_send, "sub")
    low_more = others(low, "mp")
    step(ring[2], ring[3], *crossed[:2])
    step(ring[3], ring[2], *crossed[:2])
    adapters = jnp.concatenate([up_adapter_out, down_adapter_in], axis=0)
    adapters_more = others(after(adapters, ring[4]), "mp")
    step(down_moving[0], *ring[4:6], *crossed[2:4])
    step(ring[-1])

    def product(kernel, name, own, got, scale, codes, codes_got, first_got, steps, weight_shape):
        groups = scale.shape[0]
        mine, theirs = call(
            lambda *refs: kernel(first_got, *refs),
            name,
            [own, got, scale, codes, codes_got, *[x for k in steps for x in (ring[k], crossed[k])]],
            [shape((rows, units), F32), shape((rows, units))],
            scratch=[pltpu.VMEM((groups, blocks, LANES), F32), pltpu.VMEM(weight_shape, BF16)],
            flops=4 * rows * half * units,
        )
        total = mine + swap(theirs, "sub").astype(F32)
        return total, others(total.astype(BF16), "mp"), mine

    front = (blocks // 2, block, units)
    first_down = [ring[2 * (n - 1)], grad_got, *low_more, *adapters_more]
    half_blocks = blocks // 2
    gate, gate_more, gate_mine = product(
        front_kernel, "gate", normed, normed_got, after(gate_block_scale.T, *first_down), gate_codes, front_got, 0,
        range(0, 2 * (n - 1), 2), front,
    )
    up, up_more, up_mine = product(
        front_kernel, "up", normed, normed_got, after(up_block_scale.T, *first_down), up_codes, front_got, half_blocks,
        range(1, 2 * (n - 1), 2), front,
    )
    for _ in range(n - 3):
        step(ring[-1], gate_mine, up_mine, crossed[-2])
    small_scratch = [
        pltpu.VMEM((rank, units), BF16),
        pltpu.VMEM((units, rank), BF16),
    ]
    silu, low_hidden, down_in_term = call(
        lambda *refs: hidden_kernel(more, *refs),
        "hidden",
        [gate, up, low, after(adapters, ring[-2]), *gate_more, *up_more, *low_more, *adapters_more],
        [shape((rows, units), F32), shape((rows, rank)), shape(down_adapter_in.shape)],
        scratch=small_scratch,
        limit=8,
    )
    pieces = STREAMS * n
    down_out_parts = call(
        lambda *refs: down_out_kernel(n, *refs),
        "down_out",
        [low_hidden, swap(low_hidden, "sub"), grad, grad_got],
        [shape((rank, half // pieces))] * pieces,
        flops=4 * rows * half * rank,
    )
    down_out_blocks, seen = ring_all(down_out_parts, STREAMS)
    (normed_t,) = call(
        transpose_kernel,
        "transpose",
        [normed, after(normed_got, low_hidden)],
        [shape((half, 2 * rows))],
        limit=32,
    )

    back, back_more, _ = product(
        back_kernel, "back", grad, grad_got, after(down_block_scale, normed_t, *seen[0]), down_turned, down_got, 0,
        range(2 * (n - 1), 3 * (n - 1)), (units, half),
    )
    low_grad, up_out_term = call(
        lambda *refs: up_grad_kernel(more, *refs),
        "up_grad",
        [back, silu, low, adapters, *back_more, *low_more, *adapters_more],
        [shape((rows, rank)), shape(up_adapter_out.shape)],
        scratch=small_scratch,
        limit=8,
    )
    extra = 2 * rank // pieces
    up_in_parts = call(
        lambda *refs: up_in_kernel(n, *refs),
        "up_in",
        [after(low_grad, *seen[1]), swap(low_grad, "sub"), normed_t, up_out_term, down_in_term],
        [shape((half // pieces + extra, rank))] * pieces,
        flops=4 * rows * half * rank,
    )
    up_in_blocks, _ = ring_all(up_in_parts, STREAMS)

    anywhere = pl.BlockSpec(memory_space=pl.ANY)
    up_in_gradient, up_out_gradient, down_in_gradient, down_out_gradient = call(
        lambda *refs: place_kernel(n, *refs),
        "place",
        [*down_out_blocks, *up_in_blocks],
        [
            shape((local_width, rank)),
            shape(up_adapter_out.shape),
            shape(down_adapter_in.shape),
            shape((rank, local_width)),
        ],
        scratch=[
            pltpu.VMEM((2, 2 * rank, rank), BF16),
            pltpu.SemaphoreType.DMA((4 * pieces,)),
            pltpu.SemaphoreType.DMA((2 * pieces,)),
        ],
        specs=[anywhere] * (4 * pieces),
        out_specs=(anywhere, vmem, vmem, anywhere),
        limit=4,
    )
    return up_in_gradient, up_out_gradient, down_in_gradient, down_out_gradient


def general_body(
    tokens,
    cotangent,
    rms_norm_gain,
    gate_codes,
    gate_block_scale,
    up_codes,
    up_block_scale,
    down_codes,
    down_block_scale,
    up_adapter_in,
    up_adapter_out,
    down_adapter_in,
    down_adapter_out,
    sequence_length_list,
    slot_sequence_index,
):
    rows = tokens.shape[0]
    local_width = tokens.shape[1]
    block = gate_block_scale.shape[0] and local_width // gate_codes.shape[0]
    blocks_here = gate_codes.shape[0]
    total_width = local_width * lax.axis_size("mp")
    own_squares = jnp.sum(jnp.square(tokens.astype(jnp.float32)), axis=-1, keepdims=True)
    squares = lax.psum(own_squares, "mp") / total_width
    inv_rms = lax.rsqrt(squares + EPS)
    local_normed_input = (
        tokens.astype(jnp.float32) * inv_rms * rms_norm_gain.astype(jnp.float32)[None, :]
    ).astype(jnp.bfloat16)
    seq_count = sequence_length_list.shape[1]
    longest = rows // seq_count
    total = rows * lax.axis_size("dp") * lax.axis_size("sub")
    ratios = longest / sequence_length_list[0].astype(jnp.float32)
    match = slot_sequence_index[:, None] == jnp.arange(seq_count, dtype=jnp.int32)[None, :]
    token_weight = jnp.sum(jnp.where(match, ratios[None, :], jnp.float32(0.0)), axis=-1)
    token_weight = token_weight * jnp.float32(1.0 / math.sqrt(total))
    local_output = (cotangent.astype(jnp.float32) * token_weight[:, None]).astype(jnp.bfloat16)
    partial_up = jnp.dot(local_normed_input, up_adapter_in, preferred_element_type=jnp.float32)
    partial_output = contract_dims(local_output, down_adapter_out, 1, 1)
    up_adapter_rank, output_adapter_rank = lax.psum((partial_up, partial_output), "mp")
    up_adapter_rank = up_adapter_rank.astype(jnp.bfloat16)
    output_adapter_rank = output_adapter_rank.astype(jnp.bfloat16)
    normed_blocks = local_normed_input.reshape(rows, blocks_here, block)
    out_blocks = local_output.reshape(rows, blocks_here, block)
    wide_gate = jnp.repeat(gate_block_scale.astype(jnp.float32), block, axis=1)[:, None, :]
    wide_up = jnp.repeat(up_block_scale.astype(jnp.float32), block, axis=1)[:, None, :]
    wide_down = jnp.repeat(down_block_scale.astype(jnp.float32), block, axis=0)
    dims_front = (((1, 2), (0, 1)), ((), ()))
    dims_back = (((1, 2), (1, 2)), ((), ()))
    quant_g = lax.all_gather(gate_codes, ("dp", "sub"), axis=1, tiled=True)
    quant_u = lax.all_gather(up_codes, ("dp", "sub"), axis=1, tiled=True)
    weight_g = (quant_g.astype(jnp.float32) * wide_gate).astype(jnp.bfloat16)
    weight_u = (quant_u.astype(jnp.float32) * wide_up).astype(jnp.bfloat16)
    gate_next = lax.dot_general(
        normed_blocks, weight_g, dims_front, preferred_element_type=jnp.float32
    )
    up_next = lax.dot_general(
        normed_blocks, weight_u, dims_front, preferred_element_type=jnp.float32
    )
    gate, base_up_projected = (
        lax.psum_scatter(gate_next, "mp", scatter_dimension=1, tiled=True),
        lax.psum_scatter(up_next, "mp", scatter_dimension=1, tiled=True),
    )
    up_projected = base_up_projected + ADAPTER_SCALE * jnp.dot(
        up_adapter_rank, up_adapter_out, preferred_element_type=jnp.float32
    )
    silu_gate = jax.nn.silu(gate)
    hidden_units = (silu_gate * up_projected).astype(jnp.bfloat16)
    partial_hidden = jnp.dot(hidden_units, down_adapter_in, preferred_element_type=jnp.float32)
    hidden_adapter_rank = lax.psum(partial_hidden, "mp").astype(jnp.bfloat16)
    weight_d = (
        lax.all_gather(down_codes, ("dp", "sub"), axis=0, tiled=True).astype(jnp.float32)
        * wide_down[:, :, None]
    ).astype(jnp.bfloat16)
    back_part = lax.dot_general(out_blocks, weight_d, dims_back, preferred_element_type=jnp.float32)
    base_backward = lax.psum_scatter(back_part, "mp", scatter_dimension=1, tiled=True)
    hidden_gradient = base_backward + ADAPTER_SCALE * contract_dims(
        output_adapter_rank, down_adapter_in, 1, 1
    )
    up_gradient = (hidden_gradient * silu_gate).astype(jnp.bfloat16)
    partial_gradient = contract_dims(up_gradient, up_adapter_out, 1, 1)
    up_adapter_rank_gradient = lax.psum(partial_gradient, "mp").astype(jnp.bfloat16)
    up_in_term = ADAPTER_SCALE * contract_dims(local_normed_input, up_adapter_rank_gradient, 0, 0)
    up_out_term = ADAPTER_SCALE * contract_dims(up_adapter_rank, up_gradient, 0, 0)
    down_in_term = ADAPTER_SCALE * contract_dims(hidden_units, output_adapter_rank, 0, 0)
    down_out_term = ADAPTER_SCALE * contract_dims(hidden_adapter_rank, local_output, 0, 0)
    sum_up_a, sum_up_b, sum_down_a, sum_down_b = lax.psum(
        (up_in_term, up_out_term, down_in_term, down_out_term), ("dp", "sub")
    )
    return (
        sum_up_a.astype(jnp.bfloat16),
        sum_up_b.astype(jnp.bfloat16),
        sum_down_a.astype(jnp.bfloat16),
        sum_down_b.astype(jnp.bfloat16),
    )


def body(tokens, cotangent, rms_norm_gain, gate_codes, *rest):
    whole_tiles = gate_codes.shape[1] % ROW_TILE == 0
    form = fast_body if whole_tiles else general_body
    return form(tokens, cotangent, rms_norm_gain, gate_codes, *rest)


def solution(mesh):
    placed = (
        P(("grp", "dp", "sub"), "mp"),
        P(("grp", "dp", "sub"), "mp"),
        P("mp"),
        P("mp", ("dp", "sub"), None),
        P("mp", None),
        P("mp", ("dp", "sub"), None),
        P("mp", None),
        P(("dp", "sub"), "mp", None),
        P(None, "mp"),
        P(("grp", "mp"), None),
        P("grp", "mp"),
        P(("grp", "mp"), None),
        P("grp", "mp"),
        P(("grp", "dp", "sub"), None),
        P(("grp", "dp", "sub")),
    )
    return jax.shard_map(
        body,
        mesh=mesh,
        in_specs=placed,
        out_specs=(P(("grp", "mp"), None), P("grp", "mp"), P(("grp", "mp"), None), P("grp", "mp")),
        check_vma=False,
    )
```

```python
import math

import jax
import jax.numpy as jnp
from jax import lax
from jax.experimental import pallas as pl
from jax.experimental.pallas import tpu as pltpu
from jax.sharding import PartitionSpec as P

ADAPTER_SCALE = 2.0
EPS = 1e-05
ROW_TILE = 16
LANES = 128
STREAMS = 2
MIB = 1024 * 1024

F32 = jnp.float32
BF16 = jnp.bfloat16


def contract_dims(left, right, left_dim, right_dim):
    return lax.dot_general(
        left, right, (((left_dim,), (right_dim,)), ((), ())), preferred_element_type=F32
    )


def dot(left, right):
    return jnp.dot(left, right, preferred_element_type=F32)


def ring_at(pos, n):
    if isinstance(pos, int):
        return 0 if pos == 0 else (2 * pos - 1 if 2 * pos <= n else 2 * (n - pos))
    return jnp.where(pos == 0, 0, jnp.where(2 * pos <= n, 2 * pos - 1, 2 * (n - pos)))


def ring_position():
    n = lax.axis_size("dp")
    place = lax.axis_index("dp")
    odd = lax.rem(place, 2) == 1
    return jnp.where(place == 0, 0, jnp.where(odd, (place + 1) // 2, n - place // 2))


def ring_step(x):
    n = lax.axis_size("dp")
    return lax.ppermute(x, "dp", [(ring_at(i, n), ring_at((i + 1) % n, n)) for i in range(n)])


def swap(x, axis):
    return lax.ppermute(x, axis, [(0, 1), (1, 0)])


def others(x, axis):
    n = lax.axis_size(axis)
    return [lax.ppermute(x, axis, [(i, (i + k) % n) for i in range(n)]) for k in range(1, n)]


def after(x, *done):
    return lax.optimization_barrier((x, *done))[0]


def call(kernel, name, args, out_shape, scratch=(), specs=None, limit=24, flops=0, out_specs=None):
    vmem = pl.BlockSpec(memory_space=pltpu.VMEM)
    moved = sum(a.size * a.dtype.itemsize for a in args) + sum(
        math.prod(s.shape) * s.dtype.itemsize for s in out_shape
    )
    return pl.pallas_call(
        kernel,
        out_shape=tuple(out_shape),
        in_specs=specs or [vmem] * len(args),
        out_specs=out_specs or tuple([vmem] * len(out_shape)),
        scratch_shapes=list(scratch),
        compiler_params=pltpu.CompilerParams(vmem_limit_bytes=limit * MIB),
        cost_estimate=pl.CostEstimate(flops=0, bytes_accessed=0, transcendentals=0),
        name=name,
    )(*args)


def shape(dims, dtype=BF16):
    return jax.ShapeDtypeStruct(tuple(dims), dtype)


def add_kernel(left, right, out_ref):
    out_ref[...] = (left[...].astype(F32) + right[...].astype(F32)).astype(BF16)


def add(left, right):
    return call(add_kernel, "add", [left, right], [shape(left.shape)], limit=4)[0]


def ring_all(parts, streams, last=()):
    n = lax.axis_size("dp")
    seen = []
    totals = list(parts[:streams])
    for k in range(1, n):
        seen.append([ring_step(t) for t in totals])
        totals = [add(t, p) for t, p in zip(seen[-1], parts[k * streams : (k + 1) * streams])]
    blocks = list(totals)
    for k in range(n - 1):
        if last and k == n - 2:
            totals = [after(t, *last) for t in totals]
        totals = [ring_step(t) for t in totals]
        seen.append(totals)
        blocks += totals
    return blocks + [swap(b, "sub") for b in blocks], seen


def scaled_halves(wide, low_ref, cols, scaled, product, send_ref, own_ref, copy):
    half = send_ref.shape[1]
    step = half // 4
    sub = lax.axis_index("sub")
    low_ref[:, cols] = jnp.zeros((wide.shape[0], LANES), F32)
    for n, (which, out_ref) in enumerate(((1 - sub, send_ref), (sub, own_ref))):

        @pl.loop(0, half // step)
        def _(j, n=n, which=which, out_ref=out_ref):
            first = pl.multiple_of(which * half + j * step, step)
            copy(n * (half // step) + j, first, step).wait()
            parts = []
            for i in range(step // LANES):
                tile = pl.ds(pl.multiple_of(first + i * LANES, LANES), LANES)
                parts.append(scaled(wide[:, tile].astype(F32), tile).astype(BF16))
            value = jnp.concatenate(parts, axis=1)
            out_ref[:, pl.ds(pl.multiple_of(j * step, step), step)] = value
            low_ref[:, cols] += product(value, pl.ds(first, step))


def column_copy(source, buffer, sems):
    def copy(k, first, step):
        at = pl.ds(first, step)
        return pltpu.make_async_copy(source.at[:, at], buffer.at[:, at], sems.at[k])

    return copy


def start_halves(source, buffer, sems):
    half = source.shape[1] // 2
    step = half // 4
    copy = column_copy(source, buffer, sems)
    sub = lax.axis_index("sub")
    for k in range(8):
        which = 1 - sub if k < 4 else sub
        copy(k, pl.multiple_of(which * half + k % 4 * step, step), step).start()
    return copy


def square_kernel(tokens, lengths, square_ref, buffer, sems):
    width = tokens.shape[1]
    step = width // sems.shape[0]
    copy = column_copy(tokens, buffer, sems)
    for k in range(width // step):
        copy(k, k * step, step).start()
    squares = jnp.zeros(square_ref.shape, F32)
    for k in range(width // step):
        copy(k, k * step, step).wait()
        for i in range(step // LANES):
            at = k * step + i * LANES
            squares = squares + jnp.square(buffer[:, at : at + LANES].astype(F32))
    square_ref[...] = jnp.broadcast_to(jnp.sum(squares, axis=1, keepdims=True), square_ref.shape)


def cotangent_kernel(
    total, cotangent, lengths, slots, adapter, send_ref, own_ref, low_ref, buffer, sems
):
    rows = cotangent.shape[0]
    copy = start_halves(cotangent, buffer, sems)
    index = jnp.broadcast_to(slots[...], (LANES, rows))
    weight = jnp.zeros((LANES, rows), F32)
    for s in range(lengths.shape[1]):
        length = jnp.full((LANES, rows), lengths[0, s], jnp.int32).astype(F32)
        weight = weight + jnp.where(index == s, (rows // lengths.shape[1]) / length, 0.0)
    row = (weight * F32(1.0 / math.sqrt(total))).T
    scaled_halves(
        buffer,
        low_ref,
        slice(None),
        lambda tile, cols: tile * row,
        lambda value, cols: contract_dims(value, adapter[:, cols], 1, 1),
        send_ref,
        own_ref,
        copy,
    )


def token_kernel(total_width, tokens, gain, adapter, low_out, squares, *refs):
    squares_more, (send_ref, own_ref, low_ref, buffer, sems) = refs[:-5], refs[-5:]
    copy = start_halves(tokens, buffer, sems)
    rank = adapter.shape[1]
    total = squares[...]
    for ref in squares_more:
        total = total + ref[...]
    row = lax.rsqrt(total / total_width + EPS)
    low_ref[:, rank:] = low_out[...]
    scaled_halves(
        buffer,
        low_ref,
        slice(0, rank),
        lambda tile, cols: tile * row * gain[:, cols].astype(F32),
        lambda value, cols: dot(value, adapter[cols, :]),
        send_ref,
        own_ref,
        copy,
    )


def transpose_kernel(own, got, out_ref):
    rows, step = own.shape[0], out_ref.shape[0]
    for i, ref in enumerate((own, got)):
        out_ref[:, i * rows : (i + 1) * rows] = ref[...].astype(F32).T.astype(BF16)


def widen(scale, wide):
    for g in range(scale.shape[0]):
        row = scale[g : g + 1, :].astype(F32)
        wide[g] = jnp.broadcast_to(row, (LANES, row.shape[1])).T


def place_shards(codes, got, first_got, moved, store):
    n = lax.axis_size("dp")
    sub, grp, place = (lax.axis_index(a) for a in ("sub", "grp", "dp"))
    pos = ring_position()
    blocks = codes.shape[0] // 2
    quarter = blocks // 2

    @pl.loop(0, blocks, unroll=4)
    def _(b):
        store(b, place * 2 + sub, codes[sub * blocks + b])
        store(b, place * 2 + 1 - sub, got[first_got + b])

    streams = len(moved) // (2 * (n - 1))
    size = quarter // streams
    for k in range(n - 1):
        there = ring_at(lax.rem(pos - k - 1 + n, n), n)
        for i in range(2 * streams):
            piece = moved[2 * streams * k + i]
            start = (grp if i % 2 == 0 else 1 - grp) * quarter + i // 2 * size

            @pl.loop(0, size, unroll=4)
            def _(b, piece=piece, start=start, there=there):
                store(start + b, there * 2 + sub, piece[b])
                store(start + b, there * 2 + 1 - sub, piece[size + b])


def front_kernel(first_got, own, got, scale, codes, codes_got, *refs):
    moved, (mine_ref, theirs_ref, wide, weight) = refs[:-4], refs[-4:]
    blocks, rows, units = codes.shape
    first = lax.axis_index("sub") * (blocks // 2)
    widen(scale, wide)

    def store(b, shard, piece):
        at = pl.ds(pl.multiple_of(shard * rows, ROW_TILE), rows)
        for g in range(units // LANES):
            cols = slice(g * LANES, (g + 1) * LANES)
            factor = wide[g * wide.shape[0] * LANES // units, pl.ds(first + b, 1), :]
            weight[b, at, cols] = (piece[:, cols].astype(F32) * factor).astype(BF16)

    place_shards(codes, codes_got, first_got, moved, store)
    matrix = weight[...].reshape(-1, units)
    mine_ref[...] = dot(own[...], matrix)
    theirs_ref[...] = dot(got[...], matrix).astype(BF16)


def back_kernel(first_got, own, got, scale, codes, codes_got, *refs):
    moved, (mine_ref, theirs_ref, wide, weight) = refs[:-4], refs[-4:]
    blocks, rows, block = codes.shape
    first = lax.axis_index("sub") * (blocks // 2)
    per_group = weight.shape[0] // wide.shape[0]
    widen(scale, wide)

    def store(b, shard, piece):
        at = pl.multiple_of(shard * rows, ROW_TILE)
        factor = wide[at // per_group, pl.ds(first + b, 1), :]
        cols = pl.ds(pl.multiple_of(b * block, block), block)
        weight[pl.ds(at, rows), cols] = (piece.astype(F32) * factor).astype(BF16)

    place_shards(codes, codes_got, first_got, moved, store)
    matrix = weight[...]
    mine_ref[...] = contract_dims(own[...], matrix, 1, 1)
    theirs_ref[...] = contract_dims(got[...], matrix, 1, 1).astype(BF16)


def place_own(scratch, own, more, axis):
    n = len(more) + 1
    size = own.shape[axis]
    for k, ref in enumerate((own, *more)):
        at = pl.ds(pl.multiple_of(lax.rem(lax.axis_index("mp") + n - k, n) * size, size), size)
        if axis == 0:
            scratch[at, :] = ref[...]
        else:
            scratch[:, at] = ref[...]


def own_units(full, ref, axis):
    size = ref.shape[axis]
    for i in range(full.shape[axis] // size):

        @pl.when(lax.axis_index("mp") == i)
        def _(i=i):
            ref[...] = lax.slice_in_dim(full, i * size, (i + 1) * size, axis=axis).astype(BF16)


def low_sums(low, low_more):
    total = low[...]
    for ref in low_more:
        total = total + ref[:, ref.shape[1] - total.shape[1] :].astype(F32)
    half = total.shape[1] // 2
    return total[:, :half].astype(BF16), total[:, half:].astype(BF16)


def gather_adapters(adapters, adapters_more, up_out_all, down_in_all):
    rank = up_out_all.shape[0]
    place_own(up_out_all, adapters.at[:rank], [r.at[:rank] for r in adapters_more], 1)
    place_own(down_in_all, adapters.at[rank:], [r.at[rank:] for r in adapters_more], 0)


def hidden_kernel(more, gate, up, low, adapters, *refs):
    gate_more, up_more, adapters_more = (refs[i * more : (i + 1) * more] for i in range(3))
    silu_ref, low_ref, down_in_term, up_out_all, down_in_all = refs[3 * more :]
    gather_adapters(adapters, adapters_more, up_out_all, down_in_all)
    low_up, low_out = low_sums(low, gate_more)
    gate_sum, up_sum = gate[...], up[...]
    for ref in gate_more:
        gate_sum = gate_sum + ref[:, : gate_sum.shape[1]].astype(F32)
    for ref in up_more:
        up_sum = up_sum + ref[...].astype(F32)
    up_sum = up_sum + ADAPTER_SCALE * dot(low_up, up_out_all[...])
    silu = gate_sum * jax.nn.sigmoid(gate_sum)
    silu_ref[...] = silu
    hidden = (silu * up_sum).astype(BF16)
    low_ref[...] = (ADAPTER_SCALE * dot(hidden, down_in_all[...])).astype(BF16)
    hidden_t = hidden.astype(F32).T.astype(BF16)
    own_units(ADAPTER_SCALE * dot(hidden_t, low_out), down_in_term, 0)


def up_grad_kernel(more, back, silu, low, adapters, *refs):
    back_more, low_more, adapters_more = (refs[i * more : (i + 1) * more] for i in range(3))
    low_ref, up_out_term, up_out_all, down_in_all = refs[3 * more :]
    gather_adapters(adapters, adapters_more, up_out_all, down_in_all)
    low_up, low_out = low_sums(low, low_more)
    total = back[...]
    for ref in back_more:
        total = total + ref[...].astype(F32)
    total = total + ADAPTER_SCALE * contract_dims(low_out, down_in_all[...], 1, 1)
    up_grad = (total * silu[...]).astype(BF16)
    low_ref[...] = (ADAPTER_SCALE * contract_dims(up_grad, up_out_all[...], 1, 1)).astype(BF16)
    low_up_t = low_up.astype(F32).T.astype(BF16)
    own_units(ADAPTER_SCALE * dot(low_up_t, up_grad), up_out_term, 1)


def down_out_kernel(n, low, low_got, grad, grad_got, *out_refs):
    pos = ring_position()
    streams = len(out_refs) // n
    low_t = jnp.concatenate([low[...], low_got[...]], axis=0).astype(F32).T.astype(BF16)
    rows = low.shape[0]
    for k, ref in enumerate(out_refs):
        size = ref.shape[1]
        block = lax.rem(pos - 1 - k // streams + 2 * n, n) * streams + k % streams
        at = pl.ds(pl.multiple_of(block * size, size), size)
        ref[...] = (
            dot(low_t[:, :rows], grad[:, at]) + dot(low_t[:, rows:], grad_got[:, at])
        ).astype(BF16)


def up_in_kernel(n, low, low_got, normed_t, up_out_term, down_in_term, *out_refs):
    pos = ring_position()
    streams = len(out_refs) // n
    size = normed_t.shape[0] // len(out_refs)
    extra = out_refs[0].shape[0] - size
    both = jnp.concatenate([low[...], low_got[...]], axis=0)
    for k, ref in enumerate(out_refs):
        block = lax.rem(pos - 1 - k // streams + 2 * n, n) * streams + k % streams
        at = pl.ds(pl.multiple_of(block * size, size), size)
        ref[pl.ds(0, size), :] = dot(normed_t[at, :], both).astype(BF16)
        per = up_out_term.shape[0] // extra
        index = pl.ds(pl.multiple_of(lax.rem(block, per) * extra, extra), extra)

        @pl.when(block < per)
        def _(ref=ref, index=index):
            ref[pl.ds(size, extra), :] = up_out_term[index, :]

        @pl.when(block >= per)
        def _(ref=ref, index=index):
            ref[pl.ds(size, extra), :] = down_in_term[index, :]


def copy_all(copies):
    for c in copies:
        c.start()
    for c in copies:
        c.wait()


def place_kernel(n, *refs):
    pieces = refs[:-7]
    out_ref, up_out_ref, down_in_ref, wide_ref, small, sems, small_sems = refs[-7:]
    pos, sub = ring_position(), lax.axis_index("sub")
    count = len(pieces) // 2
    per_core = count // 2
    streams = per_core // n
    size = out_ref.shape[0] // count
    extra = pieces[count].shape[0] - size
    copies = []
    for i in range(count):
        half = sub if i < per_core else 1 - sub
        block = lax.rem(pos - i % per_core // streams + n, n) * streams + i % streams
        at = pl.ds(pl.multiple_of((half * per_core + block) * size, size), size)
        copies.append(pltpu.make_async_copy(pieces[i], wide_ref.at[:, at], sems.at[2 * i]))
        piece = pieces[count + i]
        copies.append(
            pltpu.make_async_copy(piece.at[pl.ds(0, size), :], out_ref.at[at, :], sems.at[2 * i + 1])
        )
        at = pl.ds(pl.multiple_of(block * extra, extra), extra)
        copies.append(
            pltpu.make_async_copy(
                piece.at[pl.ds(size, extra), :], small.at[i // per_core, at, :], small_sems.at[i]
            )
        )
    copy_all(copies)
    total = (small[0].astype(F32) + small[1].astype(F32)).astype(BF16)
    rows = up_out_ref.shape[0]
    up_out_ref[...] = total[:rows]
    down_in_ref[...] = total[rows:]


def half_kernel(*refs):
    sources, out_ref, sems = refs[:-2], refs[-2], refs[-1]
    other = 1 - lax.axis_index("sub")
    half = sources[0].shape[0] // 2
    copy_all(
        [
            pltpu.make_async_copy(
                ref.at[pl.ds(other * half, half)], out_ref.at[pl.ds(i * half, half)], sems.at[i]
            )
            for i, ref in enumerate(sources)
        ]
    )


def quarter_kernel(count, *refs):
    sources, got, out_refs, sems = refs[:count], refs[count], refs[count + 1 : -1], refs[-1]
    streams = len(out_refs) // count
    sub, grp = lax.axis_index("sub"), lax.axis_index("grp")
    half = sources[0].shape[0] // 2
    quarter = half // 2
    copies = []
    size = quarter // streams
    for i, out_ref in enumerate(out_refs):
        first = grp * quarter + i % streams * size
        own = sources[i // streams].at[pl.ds(sub * half + first, size)]
        theirs = got.at[pl.ds(i // streams * half + first, size)]
        for k, source in enumerate((own, theirs)):
            copies.append(
                pltpu.make_async_copy(source, out_ref.at[pl.ds(k * size, size)], sems.at[2 * i + k])
            )
    copy_all(copies)


def start_shards(codes, streams):
    blocks, rows, units = codes[0].shape
    count = len(codes)
    anywhere = pl.BlockSpec(memory_space=pl.ANY)
    (send,) = call(
        half_kernel,
        "halves",
        codes,
        [shape((count * blocks // 2, rows, units))],
        scratch=[pltpu.SemaphoreType.DMA((count,))],
        specs=[anywhere] * count,
        out_specs=(anywhere,),
        limit=4,
    )
    got = swap(send, "sub")
    moving = call(
        lambda *refs: quarter_kernel(count, *refs),
        "quarters",
        [*codes, got],
        [shape((blocks // 2 // streams, rows, units))] * (count * streams),
        scratch=[pltpu.SemaphoreType.DMA((2 * count * streams,))],
        specs=[anywhere] * (count + 1),
        out_specs=(anywhere,) * (count * streams),
        limit=4,
    )
    return list(moving), got


def fast_body(
    tokens,
    cotangent,
    rms_norm_gain,
    gate_codes,
    gate_block_scale,
    up_codes,
    up_block_scale,
    down_codes,
    down_block_scale,
    up_adapter_in,
    up_adapter_out,
    down_adapter_in,
    down_adapter_out,
    sequence_length_list,
    slot_sequence_index,
):
    rows, local_width = tokens.shape
    blocks, _, units = gate_codes.shape
    block = local_width // blocks
    half = local_width // 2
    rank = up_adapter_in.shape[1]
    total_width = local_width * lax.axis_size("mp")
    n = lax.axis_size("dp")
    more = lax.axis_size("mp") - 1

    (gate_moving, up_moving), front_got = start_shards([gate_codes, up_codes], 1)
    ring, crossed = [], []

    def step(moving, *done):
        ring.append(ring_step(after(moving, *done) if done else moving))

    def cross(k, *done):
        crossed.append(swap(after(ring[k], *done) if done else ring[k], "grp"))

    step(gate_moving)
    step(up_moving)

    vmem = pl.BlockSpec(memory_space=pltpu.VMEM)
    smem = pl.BlockSpec(memory_space=pltpu.SMEM)
    hbm = pl.BlockSpec(memory_space=pltpu.HBM)
    buffers = [pltpu.VMEM((rows, local_width), BF16), pltpu.SemaphoreType.DMA((8,))]
    lengths = after(sequence_length_list, gate_moving, up_moving)
    (squares,) = call(
        square_kernel, "squares", [tokens, lengths], [shape((rows, LANES), F32)],
        scratch=buffers, specs=[hbm, smem], limit=16,
    )
    squares_more = others(squares, "mp")
    grad_send, grad, low_out = call(
        lambda *refs: cotangent_kernel(rows * n * lax.axis_size("sub"), *refs),
        "cotangent",
        [cotangent, after(lengths, squares), slot_sequence_index[None, :], down_adapter_out],
        [shape((rows, half))] * 2 + [shape((rows, rank), F32)],
        scratch=buffers,
        specs=[hbm, smem, vmem, vmem],
    )
    cross(0, grad)
    cross(1, grad)
    step(ring[0], ring[1], grad)
    step(ring[1], ring[0], grad)
    adapters = jnp.concatenate([up_adapter_out, down_adapter_in], axis=0)
    adapters_more = others(after(adapters, *ring[:2]), "mp")
    normed_send, normed, low = call(
        lambda *refs: token_kernel(total_width, *refs),
        "tokens",
        [
            tokens,
            rms_norm_gain[None, :],
            up_adapter_in,
            low_out,
            after(squares, *ring[2:4], *crossed[:2], *adapters_more),
            *squares_more,
        ],
        [shape((rows, half))] * 2 + [shape((rows, 2 * rank), F32)],
        scratch=buffers,
        specs=[hbm] + [vmem] * (4 + more),
    )
    grad_got = swap(grad_send, "sub")
    normed_got = swap(normed_send, "sub")
    step(ring[2], ring[3], *crossed[:2])
    step(ring[3], ring[2], *crossed[:2])
    cross(2)
    cross(3)
    cross(4)
    cross(5)
    down_turned = jnp.swapaxes(after(down_codes, *ring[2:4]), 0, 1)
    down_moving, down_got = start_shards([down_turned], 1)
    step(down_moving[0], *ring[4:6], *crossed[2:4], grad_got, normed_got)
    cross(6)
    step(ring[6])
    cross(7)

    def product(kernel, name, own, got, scale, codes, codes_got, first_got, steps, weight_shape, beside=()):
        groups = scale.shape[0]
        mine, theirs = call(
            lambda *refs: kernel(first_got, *refs),
            name,
            [own, got, scale, codes, codes_got, *[x for k in steps for x in (ring[k], crossed[k])]],
            [shape((rows, units), F32), shape((rows, units))],
            scratch=[pltpu.VMEM((groups, blocks, LANES), F32), pltpu.VMEM(weight_shape, BF16)],
            flops=4 * rows * half * units,
        )
        total = mine + swap(theirs, "sub").astype(F32)
        send = jnp.concatenate([total.astype(BF16), *[b.astype(BF16) for b in beside]], axis=1)
        return total, others(send, "mp")

    front = (blocks // 2, block, units)
    first_down = [ring[2 * (n - 1)]]
    half_blocks = blocks // 2
    gate, gate_more = product(
        front_kernel, "gate", normed, normed_got, after(gate_block_scale.T, *first_down), gate_codes, front_got, 0,
        range(0, 2 * (n - 1), 2), front, [low],
    )
    up, up_more = product(
        front_kernel, "up", normed, normed_got, after(up_block_scale.T, *first_down), up_codes, front_got, half_blocks,
        range(1, 2 * (n - 1), 2), front,
    )
    small_scratch = [
        pltpu.VMEM((rank, units), BF16),
        pltpu.VMEM((units, rank), BF16),
    ]
    silu, low_hidden, down_in_term = call(
        lambda *refs: hidden_kernel(more, *refs),
        "hidden",
        [gate, up, low, adapters, *gate_more, *up_more, *adapters_more],
        [shape((rows, units), F32), shape((rows, rank)), shape(down_adapter_in.shape)],
        scratch=small_scratch,
        limit=8,
    )
    pieces = STREAMS * n
    for _ in range(n - 3):
        step(ring[-1], low_hidden)
        cross(-1)
    down_out_parts = call(
        lambda *refs: down_out_kernel(n, *refs),
        "down_out",
        [low_hidden, swap(low_hidden, "sub"), grad, grad_got],
        [shape((rank, half // pieces))] * pieces,
        flops=4 * rows * half * rank,
    )
    down_out_blocks, seen = ring_all(down_out_parts, STREAMS)
    (normed_t,) = call(
        transpose_kernel,
        "transpose",
        [normed, after(normed_got, low_hidden)],
        [shape((half, 2 * rows))],
        limit=32,
    )

    back, back_more = product(
        back_kernel, "back", grad, grad_got, after(down_block_scale, normed_t, *seen[0]), down_turned, down_got, 0,
        range(2 * (n - 1), 3 * (n - 1)), (units, half),
    )
    low_grad, up_out_term = call(
        lambda *refs: up_grad_kernel(more, *refs),
        "up_grad",
        [back, silu, low, adapters, *back_more, *gate_more, *adapters_more],
        [shape((rows, rank)), shape(up_adapter_out.shape)],
        scratch=small_scratch,
        limit=8,
    )
    extra = 2 * rank // pieces
    up_in_parts = call(
        lambda *refs: up_in_kernel(n, *refs),
        "up_in",
        [after(low_grad, *seen[1]), swap(low_grad, "sub"), normed_t, up_out_term, down_in_term],
        [shape((half // pieces + extra, rank))] * pieces,
        flops=4 * rows * half * rank,
    )
    up_in_blocks, _ = ring_all(up_in_parts, STREAMS, seen[-2])

    anywhere = pl.BlockSpec(memory_space=pl.ANY)
    up_in_gradient, up_out_gradient, down_in_gradient, down_out_gradient = call(
        lambda *refs: place_kernel(n, *refs),
        "place",
        [*down_out_blocks, *up_in_blocks],
        [
            shape((local_width, rank)),
            shape(up_adapter_out.shape),
            shape(down_adapter_in.shape),
            shape((rank, local_width)),
        ],
        scratch=[
            pltpu.VMEM((2, 2 * rank, rank), BF16),
            pltpu.SemaphoreType.DMA((4 * pieces,)),
            pltpu.SemaphoreType.DMA((2 * pieces,)),
        ],
        specs=[anywhere] * (4 * pieces),
        out_specs=(anywhere, vmem, vmem, anywhere),
        limit=4,
    )
    return up_in_gradient, up_out_gradient, down_in_gradient, down_out_gradient


def general_body(
    tokens,
    cotangent,
    rms_norm_gain,
    gate_codes,
    gate_block_scale,
    up_codes,
    up_block_scale,
    down_codes,
    down_block_scale,
    up_adapter_in,
    up_adapter_out,
    down_adapter_in,
    down_adapter_out,
    sequence_length_list,
    slot_sequence_index,
):
    rows = tokens.shape[0]
    local_width = tokens.shape[1]
    block = gate_block_scale.shape[0] and local_width // gate_codes.shape[0]
    blocks_here = gate_codes.shape[0]
    total_width = local_width * lax.axis_size("mp")
    own_squares = jnp.sum(jnp.square(tokens.astype(jnp.float32)), axis=-1, keepdims=True)
    squares = lax.psum(own_squares, "mp") / total_width
    inv_rms = lax.rsqrt(squares + EPS)
    local_normed_input = (
        tokens.astype(jnp.float32) * inv_rms * rms_norm_gain.astype(jnp.float32)[None, :]
    ).astype(jnp.bfloat16)
    seq_count = sequence_length_list.shape[1]
    longest = rows // seq_count
    total = rows * lax.axis_size("dp") * lax.axis_size("sub")
    ratios = longest / sequence_length_list[0].astype(jnp.float32)
    match = slot_sequence_index[:, None] == jnp.arange(seq_count, dtype=jnp.int32)[None, :]
    token_weight = jnp.sum(jnp.where(match, ratios[None, :], jnp.float32(0.0)), axis=-1)
    token_weight = token_weight * jnp.float32(1.0 / math.sqrt(total))
    local_output = (cotangent.astype(jnp.float32) * token_weight[:, None]).astype(jnp.bfloat16)
    partial_up = jnp.dot(local_normed_input, up_adapter_in, preferred_element_type=jnp.float32)
    partial_output = contract_dims(local_output, down_adapter_out, 1, 1)
    up_adapter_rank, output_adapter_rank = lax.psum((partial_up, partial_output), "mp")
    up_adapter_rank = up_adapter_rank.astype(jnp.bfloat16)
    output_adapter_rank = output_adapter_rank.astype(jnp.bfloat16)
    normed_blocks = local_normed_input.reshape(rows, blocks_here, block)
    out_blocks = local_output.reshape(rows, blocks_here, block)
    wide_gate = jnp.repeat(gate_block_scale.astype(jnp.float32), block, axis=1)[:, None, :]
    wide_up = jnp.repeat(up_block_scale.astype(jnp.float32), block, axis=1)[:, None, :]
    wide_down = jnp.repeat(down_block_scale.astype(jnp.float32), block, axis=0)
    dims_front = (((1, 2), (0, 1)), ((), ()))
    dims_back = (((1, 2), (1, 2)), ((), ()))
    quant_g = lax.all_gather(gate_codes, ("dp", "sub"), axis=1, tiled=True)
    quant_u = lax.all_gather(up_codes, ("dp", "sub"), axis=1, tiled=True)
    weight_g = (quant_g.astype(jnp.float32) * wide_gate).astype(jnp.bfloat16)
    weight_u = (quant_u.astype(jnp.float32) * wide_up).astype(jnp.bfloat16)
    gate_next = lax.dot_general(
        normed_blocks, weight_g, dims_front, preferred_element_type=jnp.float32
    )
    up_next = lax.dot_general(
        normed_blocks, weight_u, dims_front, preferred_element_type=jnp.float32
    )
    gate, base_up_projected = (
        lax.psum_scatter(gate_next, "mp", scatter_dimension=1, tiled=True),
        lax.psum_scatter(up_next, "mp", scatter_dimension=1, tiled=True),
    )
    up_projected = base_up_projected + ADAPTER_SCALE * jnp.dot(
        up_adapter_rank, up_adapter_out, preferred_element_type=jnp.float32
    )
    silu_gate = jax.nn.silu(gate)
    hidden_units = (silu_gate * up_projected).astype(jnp.bfloat16)
    partial_hidden = jnp.dot(hidden_units, down_adapter_in, preferred_element_type=jnp.float32)
    hidden_adapter_rank = lax.psum(partial_hidden, "mp").astype(jnp.bfloat16)
    weight_d = (
        lax.all_gather(down_codes, ("dp", "sub"), axis=0, tiled=True).astype(jnp.float32)
        * wide_down[:, :, None]
    ).astype(jnp.bfloat16)
    back_part = lax.dot_general(out_blocks, weight_d, dims_back, preferred_element_type=jnp.float32)
    base_backward = lax.psum_scatter(back_part, "mp", scatter_dimension=1, tiled=True)
    hidden_gradient = base_backward + ADAPTER_SCALE * contract_dims(
        output_adapter_rank, down_adapter_in, 1, 1
    )
    up_gradient = (hidden_gradient * silu_gate).astype(jnp.bfloat16)
    partial_gradient = contract_dims(up_gradient, up_adapter_out, 1, 1)
    up_adapter_rank_gradient = lax.psum(partial_gradient, "mp").astype(jnp.bfloat16)
    up_in_term = ADAPTER_SCALE * contract_dims(local_normed_input, up_adapter_rank_gradient, 0, 0)
    up_out_term = ADAPTER_SCALE * contract_dims(up_adapter_rank, up_gradient, 0, 0)
    down_in_term = ADAPTER_SCALE * contract_dims(hidden_units, output_adapter_rank, 0, 0)
    down_out_term = ADAPTER_SCALE * contract_dims(hidden_adapter_rank, local_output, 0, 0)
    sum_up_a, sum_up_b, sum_down_a, sum_down_b = lax.psum(
        (up_in_term, up_out_term, down_in_term, down_out_term), ("dp", "sub")
    )
    return (
        sum_up_a.astype(jnp.bfloat16),
        sum_up_b.astype(jnp.bfloat16),
        sum_down_a.astype(jnp.bfloat16),
        sum_down_b.astype(jnp.bfloat16),
    )


def body(tokens, cotangent, rms_norm_gain, gate_codes, *rest):
    whole_tiles = gate_codes.shape[1] % ROW_TILE == 0
    form = fast_body if whole_tiles else general_body
    return form(tokens, cotangent, rms_norm_gain, gate_codes, *rest)


def solution(mesh):
    placed = (
        P(("grp", "dp", "sub"), "mp"),
        P(("grp", "dp", "sub"), "mp"),
        P("mp"),
        P("mp", ("dp", "sub"), None),
        P("mp", None),
        P("mp", ("dp", "sub"), None),
        P("mp", None),
        P(("dp", "sub"), "mp", None),
        P(None, "mp"),
        P(("grp", "mp"), None),
        P("grp", "mp"),
        P(("grp", "mp"), None),
        P("grp", "mp"),
        P(("grp", "dp", "sub"), None),
        P(("grp", "dp", "sub")),
    )
    return jax.shard_map(
        body,
        mesh=mesh,
        in_specs=placed,
        out_specs=(P(("grp", "mp"), None), P("grp", "mp"), P(("grp", "mp"), None), P("grp", "mp")),
        check_vma=False,
    )
```

```python
import math

import jax
import jax.numpy as jnp
from jax import lax
from jax.experimental import pallas as pl
from jax.experimental.pallas import tpu as pltpu
from jax.sharding import PartitionSpec as P

ADAPTER_SCALE = 2.0
EPS = 1e-05
ROW_TILE = 16
LANES = 128
STREAMS = 2
MIB = 1024 * 1024

F32 = jnp.float32
BF16 = jnp.bfloat16


def contract_dims(left, right, left_dim, right_dim):
    return lax.dot_general(
        left, right, (((left_dim,), (right_dim,)), ((), ())), preferred_element_type=F32
    )


def dot(left, right):
    return jnp.dot(left, right, preferred_element_type=F32)


def ring_at(pos, n):
    if isinstance(pos, int):
        return 0 if pos == 0 else (2 * pos - 1 if 2 * pos <= n else 2 * (n - pos))
    return jnp.where(pos == 0, 0, jnp.where(2 * pos <= n, 2 * pos - 1, 2 * (n - pos)))


def ring_position():
    n = lax.axis_size("dp")
    place = lax.axis_index("dp")
    odd = lax.rem(place, 2) == 1
    return jnp.where(place == 0, 0, jnp.where(odd, (place + 1) // 2, n - place // 2))


def ring_step(x):
    n = lax.axis_size("dp")
    return lax.ppermute(x, "dp", [(ring_at(i, n), ring_at((i + 1) % n, n)) for i in range(n)])


def swap(x, axis):
    return lax.ppermute(x, axis, [(0, 1), (1, 0)])


def others(x, axis):
    n = lax.axis_size(axis)
    return [lax.ppermute(x, axis, [(i, (i + k) % n) for i in range(n)]) for k in range(1, n)]


def after(x, *done):
    return lax.optimization_barrier((x, *done))[0]


def call(kernel, name, args, out_shape, scratch=(), specs=None, limit=24, flops=0, out_specs=None):
    vmem = pl.BlockSpec(memory_space=pltpu.VMEM)
    moved = sum(a.size * a.dtype.itemsize for a in args) + sum(
        math.prod(s.shape) * s.dtype.itemsize for s in out_shape
    )
    return pl.pallas_call(
        kernel,
        out_shape=tuple(out_shape),
        in_specs=specs or [vmem] * len(args),
        out_specs=out_specs or tuple([vmem] * len(out_shape)),
        scratch_shapes=list(scratch),
        compiler_params=pltpu.CompilerParams(vmem_limit_bytes=limit * MIB),
        cost_estimate=pl.CostEstimate(flops=0, bytes_accessed=0, transcendentals=0),
        name=name,
    )(*args)


def shape(dims, dtype=BF16):
    return jax.ShapeDtypeStruct(tuple(dims), dtype)


def add_kernel(left, right, out_ref):
    out_ref[...] = (left[...].astype(F32) + right[...].astype(F32)).astype(BF16)


def add(left, right):
    return call(add_kernel, "add", [left, right], [shape(left.shape)], limit=4)[0]


def ring_all(parts, streams, last=()):
    n = lax.axis_size("dp")
    seen = []
    totals = list(parts[:streams])
    for k in range(1, n):
        seen.append([ring_step(t) for t in totals])
        totals = [add(t, p) for t, p in zip(seen[-1], parts[k * streams : (k + 1) * streams])]
    blocks = list(totals)
    for k in range(n - 1):
        if last and k == n - 2:
            totals = [after(t, *last) for t in totals]
        totals = [ring_step(t) for t in totals]
        seen.append(totals)
        blocks += totals
    return blocks + [swap(b, "sub") for b in blocks], seen


def scaled_halves(wide, low_ref, cols, scaled, product, send_ref, own_ref, copy):
    half = send_ref.shape[1]
    step = half // 4
    sub = lax.axis_index("sub")
    low_ref[:, cols] = jnp.zeros((wide.shape[0], LANES), F32)
    for n, (which, out_ref) in enumerate(((1 - sub, send_ref), (sub, own_ref))):

        @pl.loop(0, half // step)
        def _(j, n=n, which=which, out_ref=out_ref):
            first = pl.multiple_of(which * half + j * step, step)
            copy(n * (half // step) + j, first, step).wait()
            parts = []
            for i in range(step // LANES):
                tile = pl.ds(pl.multiple_of(first + i * LANES, LANES), LANES)
                parts.append(scaled(wide[:, tile].astype(F32), tile).astype(BF16))
            value = jnp.concatenate(parts, axis=1)
            out_ref[:, pl.ds(pl.multiple_of(j * step, step), step)] = value
            low_ref[:, cols] += product(value, pl.ds(first, step))


def column_copy(source, buffer, sems):
    def copy(k, first, step):
        at = pl.ds(first, step)
        return pltpu.make_async_copy(source.at[:, at], buffer.at[:, at], sems.at[k])

    return copy


def start_halves(source, buffer, sems):
    half = source.shape[1] // 2
    step = half // 4
    copy = column_copy(source, buffer, sems)
    sub = lax.axis_index("sub")
    for k in range(8):
        which = 1 - sub if k < 4 else sub
        copy(k, pl.multiple_of(which * half + k % 4 * step, step), step).start()
    return copy


def square_kernel(tokens, lengths, square_ref, buffer, sems):
    width = tokens.shape[1]
    step = width // sems.shape[0]
    copy = column_copy(tokens, buffer, sems)
    for k in range(width // step):
        copy(k, k * step, step).start()
    squares = jnp.zeros(square_ref.shape, F32)
    for k in range(width // step):
        copy(k, k * step, step).wait()
        for i in range(step // LANES):
            at = k * step + i * LANES
            squares = squares + jnp.square(buffer[:, at : at + LANES].astype(F32))
    square_ref[...] = jnp.broadcast_to(jnp.sum(squares, axis=1, keepdims=True), square_ref.shape)


def cotangent_kernel(
    total, cotangent, lengths, slots, adapter, send_ref, own_ref, low_ref, buffer, sems
):
    rows = cotangent.shape[0]
    copy = start_halves(cotangent, buffer, sems)
    index = jnp.broadcast_to(slots[...], (LANES, rows))
    weight = jnp.zeros((LANES, rows), F32)
    for s in range(lengths.shape[1]):
        length = jnp.full((LANES, rows), lengths[0, s], jnp.int32).astype(F32)
        weight = weight + jnp.where(index == s, (rows // lengths.shape[1]) / length, 0.0)
    row = (weight * F32(1.0 / math.sqrt(total))).T
    scaled_halves(
        buffer,
        low_ref,
        slice(None),
        lambda tile, cols: tile * row,
        lambda value, cols: contract_dims(value, adapter[:, cols], 1, 1),
        send_ref,
        own_ref,
        copy,
    )


def token_kernel(total_width, tokens, gain, adapter, low_out, squares, *refs):
    squares_more, (send_ref, own_ref, low_ref, buffer, sems) = refs[:-5], refs[-5:]
    copy = start_halves(tokens, buffer, sems)
    rank = adapter.shape[1]
    total = squares[...]
    for ref in squares_more:
        total = total + ref[...]
    row = lax.rsqrt(total / total_width + EPS)
    low_ref[:, rank:] = low_out[...]
    scaled_halves(
        buffer,
        low_ref,
        slice(0, rank),
        lambda tile, cols: tile * row * gain[:, cols].astype(F32),
        lambda value, cols: dot(value, adapter[cols, :]),
        send_ref,
        own_ref,
        copy,
    )


def transpose_kernel(own, got, out_ref):
    rows, step = own.shape[0], out_ref.shape[0]
    for i, ref in enumerate((own, got)):
        out_ref[:, i * rows : (i + 1) * rows] = ref[...].astype(F32).T.astype(BF16)


def widen(scale, wide):
    for g in range(scale.shape[0]):
        row = scale[g : g + 1, :].astype(F32)
        wide[g] = jnp.broadcast_to(row, (LANES, row.shape[1])).T


def place_shards(codes, got, first_got, moved, store):
    n = lax.axis_size("dp")
    sub, grp, place = (lax.axis_index(a) for a in ("sub", "grp", "dp"))
    pos = ring_position()
    blocks = codes.shape[0] // 2
    quarter = blocks // 2

    @pl.loop(0, blocks, unroll=4)
    def _(b):
        store(b, place * 2 + sub, codes[sub * blocks + b])
        store(b, place * 2 + 1 - sub, got[first_got + b])

    streams = len(moved) // (2 * (n - 1))
    size = quarter // streams
    for k in range(n - 1):
        there = ring_at(lax.rem(pos - k - 1 + n, n), n)
        for i in range(2 * streams):
            piece = moved[2 * streams * k + i]
            start = (grp if i % 2 == 0 else 1 - grp) * quarter + i // 2 * size

            @pl.loop(0, size, unroll=4)
            def _(b, piece=piece, start=start, there=there):
                store(start + b, there * 2 + sub, piece[b])
                store(start + b, there * 2 + 1 - sub, piece[size + b])


def front_kernel(first_got, term, own, got, scale, codes, codes_got, *refs):
    moved, (mine_ref, theirs_ref, wide, weight) = term.split(refs)
    blocks, rows, units = codes.shape
    first = lax.axis_index("sub") * (blocks // 2)
    widen(scale, wide)

    def store(b, shard, piece):
        at = pl.ds(pl.multiple_of(shard * rows, ROW_TILE), rows)
        for g in range(units // LANES):
            cols = slice(g * LANES, (g + 1) * LANES)
            factor = wide[g * wide.shape[0] * LANES // units, pl.ds(first + b, 1), :]
            weight[b, at, cols] = (piece[:, cols].astype(F32) * factor).astype(BF16)

    place_shards(codes, codes_got, first_got, moved, store)
    matrix = weight[...].reshape(-1, units)
    mine_ref[...] = term.added(dot(own[...], matrix))
    theirs_ref[...] = dot(got[...], matrix).astype(BF16)


def back_kernel(first_got, term, own, got, scale, codes, codes_got, *refs):
    moved, (mine_ref, theirs_ref, wide, weight) = term.split(refs)
    blocks, rows, block = codes.shape
    first = lax.axis_index("sub") * (blocks // 2)
    per_group = weight.shape[0] // wide.shape[0]
    widen(scale, wide)

    def store(b, shard, piece):
        at = pl.multiple_of(shard * rows, ROW_TILE)
        factor = wide[at // per_group, pl.ds(first + b, 1), :]
        cols = pl.ds(pl.multiple_of(b * block, block), block)
        weight[pl.ds(at, rows), cols] = (piece.astype(F32) * factor).astype(BF16)

    place_shards(codes, codes_got, first_got, moved, store)
    matrix = weight[...]
    mine_ref[...] = term.added(contract_dims(own[...], matrix, 1, 1))
    theirs_ref[...] = contract_dims(got[...], matrix, 1, 1).astype(BF16)


def place_own(scratch, own, more, axis):
    n = len(more) + 1
    size = own.shape[axis]
    for k, ref in enumerate((own, *more)):
        at = pl.ds(pl.multiple_of(lax.rem(lax.axis_index("mp") + n - k, n) * size, size), size)
        if axis == 0:
            scratch[at, :] = ref[...]
        else:
            scratch[:, at] = ref[...]


def own_units(full, ref, axis):
    size = ref.shape[axis]
    for i in range(full.shape[axis] // size):

        @pl.when(lax.axis_index("mp") == i)
        def _(i=i):
            ref[...] = lax.slice_in_dim(full, i * size, (i + 1) * size, axis=axis).astype(BF16)


class NoTerm:
    arrays = ()

    def split(self, refs):
        return refs[:-4], refs[-4:]

    def added(self, product):
        return product


class UpTerm:
    def __init__(self, low, adapters, more):
        self.arrays = (low, adapters, *more)

    def split(self, refs):
        count = len(self.arrays)
        self.refs, self.all = refs[:count], refs[-1]
        return refs[count:-5], refs[-5:-1]

    def added(self, product):
        low, adapters, *more = self.refs
        rank = self.all.shape[0]
        place_own(self.all, adapters.at[:rank], [r.at[:rank] for r in more], 1)
        return product + ADAPTER_SCALE * dot(low[:, :rank].astype(BF16), self.all[...])


class DownTerm(UpTerm):
    def added(self, product):
        low, adapters, *more = self.refs
        rank = self.all.shape[1]
        place_own(self.all, adapters.at[rank:], [r.at[rank:] for r in more], 0)
        return product + ADAPTER_SCALE * contract_dims(
            low[:, rank:].astype(BF16), self.all[...], 1, 1
        )


def hidden_kernel(more, gate, up, adapters, *refs):
    gate_more, up_more, adapters_more = (refs[i * more : (i + 1) * more] for i in range(3))
    silu_ref, hidden_ref, low_ref, down_in_all = refs[3 * more :]
    rank = low_ref.shape[1]
    place_own(down_in_all, adapters.at[rank:], [r.at[rank:] for r in adapters_more], 0)
    gate_sum, up_sum = gate[...], up[...]
    for ref in gate_more:
        gate_sum = gate_sum + ref[...].astype(F32)
    for ref in up_more:
        up_sum = up_sum + ref[...].astype(F32)
    silu = gate_sum * jax.nn.sigmoid(gate_sum)
    silu_ref[...] = silu
    hidden = (silu * up_sum).astype(BF16)
    hidden_ref[...] = hidden
    low_ref[...] = (ADAPTER_SCALE * dot(hidden, down_in_all[...])).astype(BF16)


def up_grad_kernel(more, back, silu, adapters, *refs):
    back_more, adapters_more = (refs[i * more : (i + 1) * more] for i in range(2))
    up_grad_ref, low_ref, up_out_all = refs[2 * more :]
    rank = low_ref.shape[1]
    place_own(up_out_all, adapters.at[:rank], [r.at[:rank] for r in adapters_more], 1)
    total = back[...]
    for ref in back_more:
        total = total + ref[...].astype(F32)
    up_grad = (total * silu[...]).astype(BF16)
    up_grad_ref[...] = up_grad
    low_ref[...] = (ADAPTER_SCALE * contract_dims(up_grad, up_out_all[...], 1, 1)).astype(BF16)


def small_kernel(more, hidden, up_grad, low, *refs):
    low_more, (up_out_term, down_in_term) = refs[:more], refs[more:]
    total = low[...]
    for ref in low_more:
        total = total + ref[...]
    rank = total.shape[1] // 2
    low_up, low_out = total[:, :rank].astype(BF16), total[:, rank:].astype(BF16)
    low_up_t = low_up.astype(F32).T.astype(BF16)
    own_units(ADAPTER_SCALE * dot(low_up_t, up_grad[...]), up_out_term, 1)
    hidden_t = hidden[...].astype(F32).T.astype(BF16)
    own_units(ADAPTER_SCALE * dot(hidden_t, low_out), down_in_term, 0)


def down_out_kernel(n, low, low_got, grad, grad_got, *out_refs):
    pos = ring_position()
    streams = len(out_refs) // n
    low_t = jnp.concatenate([low[...], low_got[...]], axis=0).astype(F32).T.astype(BF16)
    rows = low.shape[0]
    for k, ref in enumerate(out_refs):
        size = ref.shape[1]
        block = lax.rem(pos - 1 - k // streams + 2 * n, n) * streams + k % streams
        at = pl.ds(pl.multiple_of(block * size, size), size)
        ref[...] = (
            dot(low_t[:, :rows], grad[:, at]) + dot(low_t[:, rows:], grad_got[:, at])
        ).astype(BF16)


def up_in_kernel(n, low, low_got, normed_t, up_out_term, down_in_term, *out_refs):
    pos = ring_position()
    streams = len(out_refs) // n
    size = normed_t.shape[0] // len(out_refs)
    extra = out_refs[0].shape[0] - size
    both = jnp.concatenate([low[...], low_got[...]], axis=0)
    for k, ref in enumerate(out_refs):
        block = lax.rem(pos - 1 - k // streams + 2 * n, n) * streams + k % streams
        at = pl.ds(pl.multiple_of(block * size, size), size)
        ref[pl.ds(0, size), :] = dot(normed_t[at, :], both).astype(BF16)
        per = up_out_term.shape[0] // extra
        index = pl.ds(pl.multiple_of(lax.rem(block, per) * extra, extra), extra)

        @pl.when(block < per)
        def _(ref=ref, index=index):
            ref[pl.ds(size, extra), :] = up_out_term[index, :]

        @pl.when(block >= per)
        def _(ref=ref, index=index):
            ref[pl.ds(size, extra), :] = down_in_term[index, :]


def copy_all(copies):
    for c in copies:
        c.start()
    for c in copies:
        c.wait()


def place_kernel(n, *refs):
    pieces = refs[:-7]
    out_ref, up_out_ref, down_in_ref, wide_ref, small, sems, small_sems = refs[-7:]
    pos, sub = ring_position(), lax.axis_index("sub")
    count = len(pieces) // 2
    per_core = count // 2
    streams = per_core // n
    size = out_ref.shape[0] // count
    extra = pieces[count].shape[0] - size
    copies = []
    for i in range(count):
        half = sub if i < per_core else 1 - sub
        block = lax.rem(pos - i % per_core // streams + n, n) * streams + i % streams
        at = pl.ds(pl.multiple_of((half * per_core + block) * size, size), size)
        copies.append(pltpu.make_async_copy(pieces[i], wide_ref.at[:, at], sems.at[2 * i]))
        piece = pieces[count + i]
        copies.append(
            pltpu.make_async_copy(piece.at[pl.ds(0, size), :], out_ref.at[at, :], sems.at[2 * i + 1])
        )
        at = pl.ds(pl.multiple_of(block * extra, extra), extra)
        copies.append(
            pltpu.make_async_copy(
                piece.at[pl.ds(size, extra), :], small.at[i // per_core, at, :], small_sems.at[i]
            )
        )
    copy_all(copies)
    total = (small[0].astype(F32) + small[1].astype(F32)).astype(BF16)
    rows = up_out_ref.shape[0]
    up_out_ref[...] = total[:rows]
    down_in_ref[...] = total[rows:]


def half_kernel(*refs):
    sources, out_ref, sems = refs[:-2], refs[-2], refs[-1]
    other = 1 - lax.axis_index("sub")
    half = sources[0].shape[0] // 2
    copy_all(
        [
            pltpu.make_async_copy(
                ref.at[pl.ds(other * half, half)], out_ref.at[pl.ds(i * half, half)], sems.at[i]
            )
            for i, ref in enumerate(sources)
        ]
    )


def quarter_kernel(count, *refs):
    sources, got, out_refs, sems = refs[:count], refs[count], refs[count + 1 : -1], refs[-1]
    streams = len(out_refs) // count
    sub, grp = lax.axis_index("sub"), lax.axis_index("grp")
    half = sources[0].shape[0] // 2
    quarter = half // 2
    copies = []
    size = quarter // streams
    for i, out_ref in enumerate(out_refs):
        first = grp * quarter + i % streams * size
        own = sources[i // streams].at[pl.ds(sub * half + first, size)]
        theirs = got.at[pl.ds(i // streams * half + first, size)]
        for k, source in enumerate((own, theirs)):
            copies.append(
                pltpu.make_async_copy(source, out_ref.at[pl.ds(k * size, size)], sems.at[2 * i + k])
            )
    copy_all(copies)


def start_shards(codes, streams):
    blocks, rows, units = codes[0].shape
    count = len(codes)
    anywhere = pl.BlockSpec(memory_space=pl.ANY)
    (send,) = call(
        half_kernel,
        "halves",
        codes,
        [shape((count * blocks // 2, rows, units))],
        scratch=[pltpu.SemaphoreType.DMA((count,))],
        specs=[anywhere] * count,
        out_specs=(anywhere,),
        limit=4,
    )
    got = swap(send, "sub")
    moving = call(
        lambda *refs: quarter_kernel(count, *refs),
        "quarters",
        [*codes, got],
        [shape((blocks // 2 // streams, rows, units))] * (count * streams),
        scratch=[pltpu.SemaphoreType.DMA((2 * count * streams,))],
        specs=[anywhere] * (count + 1),
        out_specs=(anywhere,) * (count * streams),
        limit=4,
    )
    return list(moving), got


def fast_body(
    tokens,
    cotangent,
    rms_norm_gain,
    gate_codes,
    gate_block_scale,
    up_codes,
    up_block_scale,
    down_codes,
    down_block_scale,
    up_adapter_in,
    up_adapter_out,
    down_adapter_in,
    down_adapter_out,
    sequence_length_list,
    slot_sequence_index,
):
    rows, local_width = tokens.shape
    blocks, _, units = gate_codes.shape
    block = local_width // blocks
    half = local_width // 2
    rank = up_adapter_in.shape[1]
    total_width = local_width * lax.axis_size("mp")
    n = lax.axis_size("dp")
    more = lax.axis_size("mp") - 1

    (gate_moving, up_moving), front_got = start_shards([gate_codes, up_codes], 1)
    ring, crossed = [], []

    def step(moving, *done):
        ring.append(ring_step(after(moving, *done) if done else moving))

    def cross(k, *done):
        crossed.append(swap(after(ring[k], *done) if done else ring[k], "grp"))

    step(gate_moving)
    step(up_moving)

    vmem = pl.BlockSpec(memory_space=pltpu.VMEM)
    smem = pl.BlockSpec(memory_space=pltpu.SMEM)
    hbm = pl.BlockSpec(memory_space=pltpu.HBM)
    buffers = [pltpu.VMEM((rows, local_width), BF16), pltpu.SemaphoreType.DMA((8,))]
    lengths = after(sequence_length_list, gate_moving, up_moving)
    (squares,) = call(
        square_kernel, "squares", [tokens, lengths], [shape((rows, LANES), F32)],
        scratch=buffers, specs=[hbm, smem], limit=16,
    )
    squares_more = others(squares, "mp")
    grad_send, grad, low_out = call(
        lambda *refs: cotangent_kernel(rows * n * lax.axis_size("sub"), *refs),
        "cotangent",
        [cotangent, after(lengths, squares), slot_sequence_index[None, :], down_adapter_out],
        [shape((rows, half))] * 2 + [shape((rows, rank), F32)],
        scratch=buffers,
        specs=[hbm, smem, vmem, vmem],
    )
    cross(0, grad)
    cross(1, grad)
    step(ring[0], ring[1], grad)
    step(ring[1], ring[0], grad)
    adapters = jnp.concatenate([up_adapter_out, down_adapter_in], axis=0)
    adapters_more = others(after(adapters, *ring[:2]), "mp")
    normed_send, normed, low = call(
        lambda *refs: token_kernel(total_width, *refs),
        "tokens",
        [
            tokens,
            rms_norm_gain[None, :],
            up_adapter_in,
            low_out,
            after(squares, *ring[2:4], *crossed[:2], *adapters_more),
            *squares_more,
        ],
        [shape((rows, half))] * 2 + [shape((rows, 2 * rank), F32)],
        scratch=buffers,
        specs=[hbm] + [vmem] * (4 + more),
    )
    grad_got = swap(grad_send, "sub")
    normed_got = swap(normed_send, "sub")
    step(ring[2], ring[3], *crossed[:2])
    step(ring[3], ring[2], *crossed[:2])
    cross(2, normed)
    cross(3, normed)
    cross(4)
    cross(5)
    down_turned = jnp.swapaxes(after(down_codes, *ring[2:4]), 0, 1)
    down_moving, down_got = start_shards([down_turned], 1)
    step(down_moving[0], *ring[4:6], *crossed[2:4], grad_got, normed_got)
    cross(6)
    step(ring[6])
    cross(7)

    def product(kernel, name, own, got, scale, codes, codes_got, first_got, steps, weight_shape, term, extra=()):
        groups = scale.shape[0]
        mine, theirs = call(
            lambda *refs: kernel(first_got, term, *refs),
            name,
            [own, got, scale, codes, codes_got, *term.arrays, *[x for k in steps for x in (ring[k], crossed[k])]],
            [shape((rows, units), F32), shape((rows, units))],
            scratch=[pltpu.VMEM((groups, blocks, LANES), F32), pltpu.VMEM(weight_shape, BF16), *extra],
            flops=4 * rows * half * units,
        )
        total = mine + swap(theirs, "sub").astype(F32)
        return total, others(total.astype(BF16), "mp")

    front = (blocks // 2, block, units)
    first_down = [ring[2 * (n - 1)]]
    half_blocks = blocks // 2
    gate, gate_more = product(
        front_kernel, "gate", normed, normed_got, after(gate_block_scale.T, *first_down), gate_codes, front_got, 0,
        range(0, 2 * (n - 1), 2), front, NoTerm(),
    )
    up, up_more = product(
        front_kernel, "up", normed, normed_got, after(up_block_scale.T, *first_down), up_codes, front_got, half_blocks,
        range(1, 2 * (n - 1), 2), front, UpTerm(low, adapters, adapters_more),
        [pltpu.VMEM((rank, units), BF16)],
    )
    silu, hidden, low_hidden = call(
        lambda *refs: hidden_kernel(more, *refs),
        "hidden",
        [gate, up, adapters, *gate_more, *up_more, *adapters_more],
        [shape((rows, units), F32), shape((rows, units)), shape((rows, rank))],
        scratch=[pltpu.VMEM((units, rank), BF16)],
        limit=8,
    )
    low_hidden_got = swap(low_hidden, "sub")
    pieces = STREAMS * n
    down_out_parts = call(
        lambda *refs: down_out_kernel(n, *refs),
        "down_out",
        [low_hidden, low_hidden_got, grad, grad_got],
        [shape((rank, half // pieces))] * pieces,
        flops=4 * rows * half * rank,
    )
    for _ in range(n - 3):
        step(ring[-1], down_out_parts[0])
    down_out_blocks, seen = ring_all(down_out_parts, STREAMS)
    for k in range(3 * (n - 1) - (n - 3), 3 * (n - 1)):
        cross(k, *seen[0])
    (normed_t,) = call(
        transpose_kernel,
        "transpose",
        [normed, after(normed_got, low_hidden)],
        [shape((half, 2 * rows))],
        limit=32,
    )

    back, back_more = product(
        back_kernel, "back", grad, grad_got, after(down_block_scale, normed_t, *seen[0]), down_turned, down_got, 0,
        range(2 * (n - 1), 3 * (n - 1)), (units, half), DownTerm(low, adapters, adapters_more),
        [pltpu.VMEM((units, rank), BF16)],
    )
    up_grad, low_grad = call(
        lambda *refs: up_grad_kernel(more, *refs),
        "up_grad",
        [back, silu, adapters, *back_more, *adapters_more],
        [shape((rows, units)), shape((rows, rank))],
        scratch=[pltpu.VMEM((rank, units), BF16)],
        limit=8,
    )
    low_more = others(after(low, *seen[0]), "mp")
    up_out_term, down_in_term = call(
        lambda *refs: small_kernel(more, *refs),
        "small",
        [hidden, up_grad, low, *low_more],
        [shape(up_adapter_out.shape), shape(down_adapter_in.shape)],
        limit=8,
    )
    extra = 2 * rank // pieces
    up_in_parts = call(
        lambda *refs: up_in_kernel(n, *refs),
        "up_in",
        [after(low_grad, *seen[1]), swap(low_grad, "sub"), normed_t, up_out_term, down_in_term],
        [shape((half // pieces + extra, rank))] * pieces,
        flops=4 * rows * half * rank,
    )
    up_in_blocks, _ = ring_all(up_in_parts, STREAMS, down_out_blocks[-STREAMS:])

    anywhere = pl.BlockSpec(memory_space=pl.ANY)
    up_in_gradient, up_out_gradient, down_in_gradient, down_out_gradient = call(
        lambda *refs: place_kernel(n, *refs),
        "place",
        [*down_out_blocks, *up_in_blocks],
        [
            shape((local_width, rank)),
            shape(up_adapter_out.shape),
            shape(down_adapter_in.shape),
            shape((rank, local_width)),
        ],
        scratch=[
            pltpu.VMEM((2, 2 * rank, rank), BF16),
            pltpu.SemaphoreType.DMA((4 * pieces,)),
            pltpu.SemaphoreType.DMA((2 * pieces,)),
        ],
        specs=[anywhere] * (4 * pieces),
        out_specs=(anywhere, vmem, vmem, anywhere),
        limit=4,
    )
    return up_in_gradient, up_out_gradient, down_in_gradient, down_out_gradient


def general_body(
    tokens,
    cotangent,
    rms_norm_gain,
    gate_codes,
    gate_block_scale,
    up_codes,
    up_block_scale,
    down_codes,
    down_block_scale,
    up_adapter_in,
    up_adapter_out,
    down_adapter_in,
    down_adapter_out,
    sequence_length_list,
    slot_sequence_index,
):
    rows = tokens.shape[0]
    local_width = tokens.shape[1]
    block = gate_block_scale.shape[0] and local_width // gate_codes.shape[0]
    blocks_here = gate_codes.shape[0]
    total_width = local_width * lax.axis_size("mp")
    own_squares = jnp.sum(jnp.square(tokens.astype(jnp.float32)), axis=-1, keepdims=True)
    squares = lax.psum(own_squares, "mp") / total_width
    inv_rms = lax.rsqrt(squares + EPS)
    local_normed_input = (
        tokens.astype(jnp.float32) * inv_rms * rms_norm_gain.astype(jnp.float32)[None, :]
    ).astype(jnp.bfloat16)
    seq_count = sequence_length_list.shape[1]
    longest = rows // seq_count
    total = rows * lax.axis_size("dp") * lax.axis_size("sub")
    ratios = longest / sequence_length_list[0].astype(jnp.float32)
    match = slot_sequence_index[:, None] == jnp.arange(seq_count, dtype=jnp.int32)[None, :]
    token_weight = jnp.sum(jnp.where(match, ratios[None, :], jnp.float32(0.0)), axis=-1)
    token_weight = token_weight * jnp.float32(1.0 / math.sqrt(total))
    local_output = (cotangent.astype(jnp.float32) * token_weight[:, None]).astype(jnp.bfloat16)
    partial_up = jnp.dot(local_normed_input, up_adapter_in, preferred_element_type=jnp.float32)
    partial_output = contract_dims(local_output, down_adapter_out, 1, 1)
    up_adapter_rank, output_adapter_rank = lax.psum((partial_up, partial_output), "mp")
    up_adapter_rank = up_adapter_rank.astype(jnp.bfloat16)
    output_adapter_rank = output_adapter_rank.astype(jnp.bfloat16)
    normed_blocks = local_normed_input.reshape(rows, blocks_here, block)
    out_blocks = local_output.reshape(rows, blocks_here, block)
    wide_gate = jnp.repeat(gate_block_scale.astype(jnp.float32), block, axis=1)[:, None, :]
    wide_up = jnp.repeat(up_block_scale.astype(jnp.float32), block, axis=1)[:, None, :]
    wide_down = jnp.repeat(down_block_scale.astype(jnp.float32), block, axis=0)
    dims_front = (((1, 2), (0, 1)), ((), ()))
    dims_back = (((1, 2), (1, 2)), ((), ()))
    quant_g = lax.all_gather(gate_codes, ("dp", "sub"), axis=1, tiled=True)
    quant_u = lax.all_gather(up_codes, ("dp", "sub"), axis=1, tiled=True)
    weight_g = (quant_g.astype(jnp.float32) * wide_gate).astype(jnp.bfloat16)
    weight_u = (quant_u.astype(jnp.float32) * wide_up).astype(jnp.bfloat16)
    gate_next = lax.dot_general(
        normed_blocks, weight_g, dims_front, preferred_element_type=jnp.float32
    )
    up_next = lax.dot_general(
        normed_blocks, weight_u, dims_front, preferred_element_type=jnp.float32
    )
    gate, base_up_projected = (
        lax.psum_scatter(gate_next, "mp", scatter_dimension=1, tiled=True),
        lax.psum_scatter(up_next, "mp", scatter_dimension=1, tiled=True),
    )
    up_projected = base_up_projected + ADAPTER_SCALE * jnp.dot(
        up_adapter_rank, up_adapter_out, preferred_element_type=jnp.float32
    )
    silu_gate = jax.nn.silu(gate)
    hidden_units = (silu_gate * up_projected).astype(jnp.bfloat16)
    partial_hidden = jnp.dot(hidden_units, down_adapter_in, preferred_element_type=jnp.float32)
    hidden_adapter_rank = lax.psum(partial_hidden, "mp").astype(jnp.bfloat16)
    weight_d = (
        lax.all_gather(down_codes, ("dp", "sub"), axis=0, tiled=True).astype(jnp.float32)
        * wide_down[:, :, None]
    ).astype(jnp.bfloat16)
    back_part = lax.dot_general(out_blocks, weight_d, dims_back, preferred_element_type=jnp.float32)
    base_backward = lax.psum_scatter(back_part, "mp", scatter_dimension=1, tiled=True)
    hidden_gradient = base_backward + ADAPTER_SCALE * contract_dims(
        output_adapter_rank, down_adapter_in, 1, 1
    )
    up_gradient = (hidden_gradient * silu_gate).astype(jnp.bfloat16)
    partial_gradient = contract_dims(up_gradient, up_adapter_out, 1, 1)
    up_adapter_rank_gradient = lax.psum(partial_gradient, "mp").astype(jnp.bfloat16)
    up_in_term = ADAPTER_SCALE * contract_dims(local_normed_input, up_adapter_rank_gradient, 0, 0)
    up_out_term = ADAPTER_SCALE * contract_dims(up_adapter_rank, up_gradient, 0, 0)
    down_in_term = ADAPTER_SCALE * contract_dims(hidden_units, output_adapter_rank, 0, 0)
    down_out_term = ADAPTER_SCALE * contract_dims(hidden_adapter_rank, local_output, 0, 0)
    sum_up_a, sum_up_b, sum_down_a, sum_down_b = lax.psum(
        (up_in_term, up_out_term, down_in_term, down_out_term), ("dp", "sub")
    )
    return (
        sum_up_a.astype(jnp.bfloat16),
        sum_up_b.astype(jnp.bfloat16),
        sum_down_a.astype(jnp.bfloat16),
        sum_down_b.astype(jnp.bfloat16),
    )


def body(tokens, cotangent, rms_norm_gain, gate_codes, *rest):
    whole_tiles = gate_codes.shape[1] % ROW_TILE == 0
    form = fast_body if whole_tiles else general_body
    return form(tokens, cotangent, rms_norm_gain, gate_codes, *rest)


def solution(mesh):
    placed = (
        P(("grp", "dp", "sub"), "mp"),
        P(("grp", "dp", "sub"), "mp"),
        P("mp"),
        P("mp", ("dp", "sub"), None),
        P("mp", None),
        P("mp", ("dp", "sub"), None),
        P("mp", None),
        P(("dp", "sub"), "mp", None),
        P(None, "mp"),
        P(("grp", "mp"), None),
        P("grp", "mp"),
        P(("grp", "mp"), None),
        P("grp", "mp"),
        P(("grp", "dp", "sub"), None),
        P(("grp", "dp", "sub")),
    )
    return jax.shard_map(
        body,
        mesh=mesh,
        in_specs=placed,
        out_specs=(P(("grp", "mp"), None), P("grp", "mp"), P(("grp", "mp"), None), P("grp", "mp")),
        check_vma=False,
    )
```

```python
import math

import jax
import jax.numpy as jnp
from jax import lax
from jax.experimental import pallas as pl
from jax.experimental.pallas import tpu as pltpu
from jax.sharding import PartitionSpec as P

ADAPTER_SCALE = 2.0
EPS = 1e-05
ROW_TILE = 16
LANES = 128
STREAMS = 2
WIDE_STREAMS = 2
TALL_STREAMS = 2
MIB = 1024 * 1024

F32 = jnp.float32
BF16 = jnp.bfloat16


def contract_dims(left, right, left_dim, right_dim):
    return lax.dot_general(
        left, right, (((left_dim,), (right_dim,)), ((), ())), preferred_element_type=F32
    )


def dot(left, right):
    return jnp.dot(left, right, preferred_element_type=F32)


def ring_at(pos, n):
    if isinstance(pos, int):
        return 0 if pos == 0 else (2 * pos - 1 if 2 * pos <= n else 2 * (n - pos))
    return jnp.where(pos == 0, 0, jnp.where(2 * pos <= n, 2 * pos - 1, 2 * (n - pos)))


def ring_position():
    n = lax.axis_size("dp")
    place = lax.axis_index("dp")
    odd = lax.rem(place, 2) == 1
    return jnp.where(place == 0, 0, jnp.where(odd, (place + 1) // 2, n - place // 2))


def ring_step(x):
    n = lax.axis_size("dp")
    return lax.ppermute(x, "dp", [(ring_at(i, n), ring_at((i + 1) % n, n)) for i in range(n)])


def swap(x, axis):
    return lax.ppermute(x, axis, [(0, 1), (1, 0)])


def others(x, axis):
    n = lax.axis_size(axis)
    return [lax.ppermute(x, axis, [(i, (i + k) % n) for i in range(n)]) for k in range(1, n)]


def after(x, *done):
    return lax.optimization_barrier((x, *done))[0]


def call(kernel, name, args, out_shape, scratch=(), specs=None, limit=24, flops=0, out_specs=None):
    vmem = pl.BlockSpec(memory_space=pltpu.VMEM)
    moved = sum(a.size * a.dtype.itemsize for a in args) + sum(
        math.prod(s.shape) * s.dtype.itemsize for s in out_shape
    )
    return pl.pallas_call(
        kernel,
        out_shape=tuple(out_shape),
        in_specs=specs or [vmem] * len(args),
        out_specs=out_specs or tuple([vmem] * len(out_shape)),
        scratch_shapes=list(scratch),
        compiler_params=pltpu.CompilerParams(vmem_limit_bytes=limit * MIB),
        cost_estimate=pl.CostEstimate(flops=0, bytes_accessed=0, transcendentals=0),
        name=name,
    )(*args)


def shape(dims, dtype=BF16):
    return jax.ShapeDtypeStruct(tuple(dims), dtype)


def add_kernel(left, right, out_ref):
    out_ref[...] = (left[...].astype(F32) + right[...].astype(F32)).astype(BF16)


def add(left, right):
    return call(add_kernel, "add", [left, right], [shape(left.shape)], limit=4)[0]


def ring_all(parts, streams, last=()):
    n = lax.axis_size("dp")
    seen = []
    totals = list(parts[:streams])
    for k in range(1, n):
        seen.append([ring_step(t) for t in totals])
        totals = [add(t, p) for t, p in zip(seen[-1], parts[k * streams : (k + 1) * streams])]
    blocks = list(totals)
    for k in range(n - 1):
        if last and k == n - 2:
            totals = [after(t, *last) for t in totals]
        totals = [ring_step(t) for t in totals]
        seen.append(totals)
        blocks += totals
    return blocks + [swap(b, "sub") for b in blocks], seen


def scaled_halves(wide, low_ref, cols, scaled, product, send_ref, own_ref, copy):
    half = send_ref.shape[1]
    step = half // 4
    sub = lax.axis_index("sub")
    low_ref[:, cols] = jnp.zeros((wide.shape[0], LANES), F32)
    for n, (which, out_ref) in enumerate(((1 - sub, send_ref), (sub, own_ref))):

        @pl.loop(0, half // step)
        def _(j, n=n, which=which, out_ref=out_ref):
            first = pl.multiple_of(which * half + j * step, step)
            copy(n * (half // step) + j, first, step).wait()
            parts = []
            for i in range(step // LANES):
                tile = pl.ds(pl.multiple_of(first + i * LANES, LANES), LANES)
                parts.append(scaled(wide[:, tile].astype(F32), tile).astype(BF16))
            value = jnp.concatenate(parts, axis=1)
            out_ref[:, pl.ds(pl.multiple_of(j * step, step), step)] = value
            low_ref[:, cols] += product(value, pl.ds(first, step))


def column_copy(source, buffer, sems):
    def copy(k, first, step):
        at = pl.ds(first, step)
        return pltpu.make_async_copy(source.at[:, at], buffer.at[:, at], sems.at[k])

    return copy


def start_halves(source, buffer, sems):
    half = source.shape[1] // 2
    step = half // 4
    copy = column_copy(source, buffer, sems)
    sub = lax.axis_index("sub")
    for k in range(8):
        which = 1 - sub if k < 4 else sub
        copy(k, pl.multiple_of(which * half + k % 4 * step, step), step).start()
    return copy


def square_kernel(tokens, lengths, square_ref, buffer, sems):
    width = tokens.shape[1]
    step = width // sems.shape[0]
    copy = column_copy(tokens, buffer, sems)
    for k in range(width // step):
        copy(k, k * step, step).start()
    squares = jnp.zeros(square_ref.shape, F32)
    for k in range(width // step):
        copy(k, k * step, step).wait()
        for i in range(step // LANES):
            at = k * step + i * LANES
            squares = squares + jnp.square(buffer[:, at : at + LANES].astype(F32))
    square_ref[...] = jnp.broadcast_to(jnp.sum(squares, axis=1, keepdims=True), square_ref.shape)


def cotangent_kernel(
    total, cotangent, lengths, slots, adapter, send_ref, own_ref, low_ref, buffer, sems
):
    rows = cotangent.shape[0]
    copy = start_halves(cotangent, buffer, sems)
    index = jnp.broadcast_to(slots[...], (LANES, rows))
    weight = jnp.zeros((LANES, rows), F32)
    for s in range(lengths.shape[1]):
        length = jnp.full((LANES, rows), lengths[0, s], jnp.int32).astype(F32)
        weight = weight + jnp.where(index == s, (rows // lengths.shape[1]) / length, 0.0)
    row = (weight * F32(1.0 / math.sqrt(total))).T
    scaled_halves(
        buffer,
        low_ref,
        slice(None),
        lambda tile, cols: tile * row,
        lambda value, cols: contract_dims(value, adapter[:, cols], 1, 1),
        send_ref,
        own_ref,
        copy,
    )


def token_kernel(total_width, tokens, gain, adapter, low_out, squares, *refs):
    squares_more, (send_ref, own_ref, low_ref, buffer, sems) = refs[:-5], refs[-5:]
    copy = start_halves(tokens, buffer, sems)
    rank = adapter.shape[1]
    total = squares[...]
    for ref in squares_more:
        total = total + ref[...]
    row = lax.rsqrt(total / total_width + EPS)
    low_ref[:, rank:] = low_out[...]
    scaled_halves(
        buffer,
        low_ref,
        slice(0, rank),
        lambda tile, cols: tile * row * gain[:, cols].astype(F32),
        lambda value, cols: dot(value, adapter[cols, :]),
        send_ref,
        own_ref,
        copy,
    )


def transpose_kernel(own, got, out_ref):
    rows, step = own.shape[0], out_ref.shape[0]
    for i, ref in enumerate((own, got)):
        out_ref[:, i * rows : (i + 1) * rows] = ref[...].astype(F32).T.astype(BF16)


def widen(scale, wide):
    for g in range(scale.shape[0]):
        row = scale[g : g + 1, :].astype(F32)
        wide[g] = jnp.broadcast_to(row, (LANES, row.shape[1])).T


def place_shards(codes, got, first_got, moved, store):
    n = lax.axis_size("dp")
    sub, grp, place = (lax.axis_index(a) for a in ("sub", "grp", "dp"))
    pos = ring_position()
    blocks = codes.shape[0] // 2
    quarter = blocks // 2

    @pl.loop(0, blocks, unroll=4)
    def _(b):
        store(b, place * 2 + sub, codes[sub * blocks + b])
        store(b, place * 2 + 1 - sub, got[first_got + b])

    streams = len(moved) // (2 * (n - 1))
    size = quarter // streams
    for k in range(n - 1):
        there = ring_at(lax.rem(pos - k - 1 + n, n), n)
        for i in range(2 * streams):
            piece = moved[2 * streams * k + i]
            start = (grp if i % 2 == 0 else 1 - grp) * quarter + i // 2 * size

            @pl.loop(0, size, unroll=4)
            def _(b, piece=piece, start=start, there=there):
                store(start + b, there * 2 + sub, piece[b])
                store(start + b, there * 2 + 1 - sub, piece[size + b])


def front_kernel(first_got, term, own, got, scale, codes, codes_got, *refs):
    moved, (mine_ref, theirs_ref, wide, weight) = term.split(refs)
    blocks, rows, units = codes.shape
    first = lax.axis_index("sub") * (blocks // 2)
    widen(scale, wide)

    def store(b, shard, piece):
        at = pl.ds(pl.multiple_of(shard * rows, ROW_TILE), rows)
        for g in range(units // LANES):
            cols = slice(g * LANES, (g + 1) * LANES)
            factor = wide[g * wide.shape[0] * LANES // units, pl.ds(first + b, 1), :]
            weight[b, at, cols] = (piece[:, cols].astype(F32) * factor).astype(BF16)

    place_shards(codes, codes_got, first_got, moved, store)
    matrix = weight[...].reshape(-1, units)
    mine_ref[...] = term.added(dot(own[...], matrix))
    theirs_ref[...] = dot(got[...], matrix).astype(BF16)


def back_kernel(first_got, term, own, got, scale, codes, codes_got, *refs):
    moved, (mine_ref, theirs_ref, wide, weight) = term.split(refs)
    blocks, rows, block = codes.shape
    first = lax.axis_index("sub") * (blocks // 2)
    per_group = weight.shape[0] // wide.shape[0]
    widen(scale, wide)

    def store(b, shard, piece):
        at = pl.multiple_of(shard * rows, ROW_TILE)
        factor = wide[at // per_group, pl.ds(first + b, 1), :]
        cols = pl.ds(pl.multiple_of(b * block, block), block)
        weight[pl.ds(at, rows), cols] = (piece.astype(F32) * factor).astype(BF16)

    place_shards(codes, codes_got, first_got, moved, store)
    matrix = weight[...]
    mine_ref[...] = term.added(contract_dims(own[...], matrix, 1, 1))
    theirs_ref[...] = contract_dims(got[...], matrix, 1, 1).astype(BF16)


def place_own(scratch, own, more, axis):
    n = len(more) + 1
    size = own.shape[axis]
    for k, ref in enumerate((own, *more)):
        at = pl.ds(pl.multiple_of(lax.rem(lax.axis_index("mp") + n - k, n) * size, size), size)
        if axis == 0:
            scratch[at, :] = ref[...]
        else:
            scratch[:, at] = ref[...]


def own_units(full, ref, axis):
    size = ref.shape[axis]
    for i in range(full.shape[axis] // size):

        @pl.when(lax.axis_index("mp") == i)
        def _(i=i):
            ref[...] = lax.slice_in_dim(full, i * size, (i + 1) * size, axis=axis).astype(BF16)


class NoTerm:
    arrays = ()

    def split(self, refs):
        return refs[:-4], refs[-4:]

    def added(self, product):
        return product


class UpTerm:
    def __init__(self, low, adapters, more):
        self.arrays = (low, adapters, *more)

    def split(self, refs):
        count = len(self.arrays)
        self.refs, self.all = refs[:count], refs[-1]
        return refs[count:-5], refs[-5:-1]

    def added(self, product):
        low, adapters, *more = self.refs
        rank = self.all.shape[0]
        place_own(self.all, adapters.at[:rank], [r.at[:rank] for r in more], 1)
        return product + ADAPTER_SCALE * dot(low[:, :rank].astype(BF16), self.all[...])


class DownTerm(UpTerm):
    def added(self, product):
        low, adapters, *more = self.refs
        rank = self.all.shape[1]
        place_own(self.all, adapters.at[rank:], [r.at[rank:] for r in more], 0)
        return product + ADAPTER_SCALE * contract_dims(
            low[:, rank:].astype(BF16), self.all[...], 1, 1
        )


def hidden_kernel(more, gate, up, adapters, *refs):
    gate_more, up_more, adapters_more = (refs[i * more : (i + 1) * more] for i in range(3))
    silu_ref, hidden_ref, low_ref, down_in_all = refs[3 * more :]
    rank = low_ref.shape[1]
    place_own(down_in_all, adapters.at[rank:], [r.at[rank:] for r in adapters_more], 0)
    gate_sum, up_sum = gate[...], up[...]
    for ref in gate_more:
        gate_sum = gate_sum + ref[...].astype(F32)
    for ref in up_more:
        up_sum = up_sum + ref[...].astype(F32)
    silu = gate_sum * jax.nn.sigmoid(gate_sum)
    silu_ref[...] = silu
    hidden = (silu * up_sum).astype(BF16)
    hidden_ref[...] = hidden
    low_ref[...] = (ADAPTER_SCALE * dot(hidden, down_in_all[...])).astype(BF16)


def up_grad_kernel(more, back, silu, adapters, *refs):
    back_more, adapters_more = (refs[i * more : (i + 1) * more] for i in range(2))
    up_grad_ref, low_ref, up_out_all = refs[2 * more :]
    rank = low_ref.shape[1]
    place_own(up_out_all, adapters.at[:rank], [r.at[:rank] for r in adapters_more], 1)
    total = back[...]
    for ref in back_more:
        total = total + ref[...].astype(F32)
    up_grad = (total * silu[...]).astype(BF16)
    up_grad_ref[...] = up_grad
    low_ref[...] = (ADAPTER_SCALE * contract_dims(up_grad, up_out_all[...], 1, 1)).astype(BF16)


def small_kernel(more, hidden, up_grad, low, *refs):
    low_more, (up_out_term, down_in_term) = refs[:more], refs[more:]
    total = low[...]
    for ref in low_more:
        total = total + ref[...]
    rank = total.shape[1] // 2
    low_up, low_out = total[:, :rank].astype(BF16), total[:, rank:].astype(BF16)
    low_up_t = low_up.astype(F32).T.astype(BF16)
    own_units(ADAPTER_SCALE * dot(low_up_t, up_grad[...]), up_out_term, 1)
    hidden_t = hidden[...].astype(F32).T.astype(BF16)
    own_units(ADAPTER_SCALE * dot(hidden_t, low_out), down_in_term, 0)


def down_out_kernel(n, low, low_got, grad, grad_got, *out_refs):
    pos = ring_position()
    streams = len(out_refs) // n
    low_t = jnp.concatenate([low[...], low_got[...]], axis=0).astype(F32).T.astype(BF16)
    rows = low.shape[0]
    for k, ref in enumerate(out_refs):
        size = ref.shape[1]
        block = lax.rem(pos - 1 - k // streams + 2 * n, n) * streams + k % streams
        at = pl.ds(pl.multiple_of(block * size, size), size)
        ref[...] = (
            dot(low_t[:, :rows], grad[:, at]) + dot(low_t[:, rows:], grad_got[:, at])
        ).astype(BF16)


def up_in_kernel(n, low, low_got, normed_t, up_out_term, down_in_term, *out_refs):
    pos = ring_position()
    streams = len(out_refs) // n
    size = normed_t.shape[0] // len(out_refs)
    extra = out_refs[0].shape[0] - size
    both = jnp.concatenate([low[...], low_got[...]], axis=0)
    for k, ref in enumerate(out_refs):
        block = lax.rem(pos - 1 - k // streams + 2 * n, n) * streams + k % streams
        at = pl.ds(pl.multiple_of(block * size, size), size)
        ref[pl.ds(0, size), :] = dot(normed_t[at, :], both).astype(BF16)
        per = up_out_term.shape[0] // extra
        index = pl.ds(pl.multiple_of(lax.rem(block, per) * extra, extra), extra)

        @pl.when(block < per)
        def _(ref=ref, index=index):
            ref[pl.ds(size, extra), :] = up_out_term[index, :]

        @pl.when(block >= per)
        def _(ref=ref, index=index):
            ref[pl.ds(size, extra), :] = down_in_term[index, :]


def copy_all(copies):
    for c in copies:
        c.start()
    for c in copies:
        c.wait()


def place_of(i, count, n, pos, sub, size):
    per_core = count // 2
    streams = per_core // n
    half = sub if i < per_core else 1 - sub
    block = lax.rem(pos - i % per_core // streams + n, n) * streams + i % streams
    return pl.ds(pl.multiple_of((half * per_core + block) * size, size), size)


def place_kernel(n, wide_count, *refs):
    pieces = refs[:-7]
    out_ref, up_out_ref, down_in_ref, wide_ref, small, sems, small_sems = refs[-7:]
    pos, sub = ring_position(), lax.axis_index("sub")
    wide, tall = pieces[:wide_count], pieces[wide_count:]
    copies = []
    for i, piece in enumerate(wide):
        at = place_of(i, len(wide), n, pos, sub, piece.shape[1])
        copies.append(pltpu.make_async_copy(piece, wide_ref.at[:, at], sems.at[i]))
    size = out_ref.shape[0] // len(tall)
    extra = tall[0].shape[0] - size
    for i, piece in enumerate(tall):
        at = place_of(i, len(tall), n, pos, sub, size)
        copies.append(
            pltpu.make_async_copy(
                piece.at[pl.ds(0, size), :], out_ref.at[at, :], sems.at[len(wide) + i]
            )
        )
        half = i // (len(tall) // 2)
        at = place_of(i % (len(tall) // 2), len(tall), n, pos, 0, extra)
        copies.append(
            pltpu.make_async_copy(
                piece.at[pl.ds(size, extra), :], small.at[half, at, :], small_sems.at[i]
            )
        )
    copy_all(copies)
    total = (small[0].astype(F32) + small[1].astype(F32)).astype(BF16)
    rows = up_out_ref.shape[0]
    up_out_ref[...] = total[:rows]
    down_in_ref[...] = total[rows:]


def half_kernel(*refs):
    sources, out_ref, sems = refs[:-2], refs[-2], refs[-1]
    other = 1 - lax.axis_index("sub")
    half = sources[0].shape[0] // 2
    copy_all(
        [
            pltpu.make_async_copy(
                ref.at[pl.ds(other * half, half)], out_ref.at[pl.ds(i * half, half)], sems.at[i]
            )
            for i, ref in enumerate(sources)
        ]
    )


def quarter_kernel(count, *refs):
    sources, got, out_refs, sems = refs[:count], refs[count], refs[count + 1 : -1], refs[-1]
    streams = len(out_refs) // count
    sub, grp = lax.axis_index("sub"), lax.axis_index("grp")
    half = sources[0].shape[0] // 2
    quarter = half // 2
    copies = []
    size = quarter // streams
    for i, out_ref in enumerate(out_refs):
        first = grp * quarter + i % streams * size
        own = sources[i // streams].at[pl.ds(sub * half + first, size)]
        theirs = got.at[pl.ds(i // streams * half + first, size)]
        for k, source in enumerate((own, theirs)):
            copies.append(
                pltpu.make_async_copy(source, out_ref.at[pl.ds(k * size, size)], sems.at[2 * i + k])
            )
    copy_all(copies)


def start_shards(codes, streams):
    blocks, rows, units = codes[0].shape
    count = len(codes)
    anywhere = pl.BlockSpec(memory_space=pl.ANY)
    (send,) = call(
        half_kernel,
        "halves",
        codes,
        [shape((count * blocks // 2, rows, units))],
        scratch=[pltpu.SemaphoreType.DMA((count,))],
        specs=[anywhere] * count,
        out_specs=(anywhere,),
        limit=4,
    )
    got = swap(send, "sub")
    moving = call(
        lambda *refs: quarter_kernel(count, *refs),
        "quarters",
        [*codes, got],
        [shape((blocks // 2 // streams, rows, units))] * (count * streams),
        scratch=[pltpu.SemaphoreType.DMA((2 * count * streams,))],
        specs=[anywhere] * (count + 1),
        out_specs=(anywhere,) * (count * streams),
        limit=4,
    )
    return list(moving), got


def fast_body(
    tokens,
    cotangent,
    rms_norm_gain,
    gate_codes,
    gate_block_scale,
    up_codes,
    up_block_scale,
    down_codes,
    down_block_scale,
    up_adapter_in,
    up_adapter_out,
    down_adapter_in,
    down_adapter_out,
    sequence_length_list,
    slot_sequence_index,
):
    rows, local_width = tokens.shape
    blocks, _, units = gate_codes.shape
    block = local_width // blocks
    half = local_width // 2
    rank = up_adapter_in.shape[1]
    total_width = local_width * lax.axis_size("mp")
    n = lax.axis_size("dp")
    more = lax.axis_size("mp") - 1

    (gate_moving, up_moving), front_got = start_shards([gate_codes, up_codes], 1)
    ring, crossed = [], []

    def step(moving, *done):
        ring.append(ring_step(after(moving, *done) if done else moving))

    def cross(k, *done):
        crossed.append(swap(after(ring[k], *done) if done else ring[k], "grp"))

    step(gate_moving)
    step(up_moving)

    vmem = pl.BlockSpec(memory_space=pltpu.VMEM)
    smem = pl.BlockSpec(memory_space=pltpu.SMEM)
    hbm = pl.BlockSpec(memory_space=pltpu.HBM)
    buffers = [pltpu.VMEM((rows, local_width), BF16), pltpu.SemaphoreType.DMA((8,))]
    lengths = after(sequence_length_list, gate_moving, up_moving)
    (squares,) = call(
        square_kernel, "squares", [tokens, lengths], [shape((rows, LANES), F32)],
        scratch=buffers, specs=[hbm, smem], limit=16,
    )
    squares_more = others(squares, "mp")
    grad_send, grad, low_out = call(
        lambda *refs: cotangent_kernel(rows * n * lax.axis_size("sub"), *refs),
        "cotangent",
        [cotangent, after(lengths, squares), slot_sequence_index[None, :], down_adapter_out],
        [shape((rows, half))] * 2 + [shape((rows, rank), F32)],
        scratch=buffers,
        specs=[hbm, smem, vmem, vmem],
    )
    cross(0, grad)
    cross(1, grad)
    step(ring[0], ring[1], grad)
    step(ring[1], ring[0], grad)
    adapters = jnp.concatenate([up_adapter_out, down_adapter_in], axis=0)
    adapters_more = others(after(adapters, *ring[:2]), "mp")
    normed_send, normed, low = call(
        lambda *refs: token_kernel(total_width, *refs),
        "tokens",
        [
            tokens,
            rms_norm_gain[None, :],
            up_adapter_in,
            low_out,
            after(squares, *ring[2:4], *crossed[:2], *adapters_more),
            *squares_more,
        ],
        [shape((rows, half))] * 2 + [shape((rows, 2 * rank), F32)],
        scratch=buffers,
        specs=[hbm] + [vmem] * (4 + more),
    )
    grad_got = swap(grad_send, "sub")
    normed_got = swap(normed_send, "sub")
    step(ring[2], ring[3], *crossed[:2])
    step(ring[3], ring[2], *crossed[:2])
    cross(2)
    cross(3)
    cross(4)
    cross(5)
    down_turned = jnp.swapaxes(after(down_codes, ring[4]), 0, 1)
    down_moving, down_got = start_shards([down_turned], STREAMS)
    front_steps = 2 * (n - 1)
    for moving in down_moving:
        step(moving, *ring[4:6], *crossed[2:4], grad_got, normed_got)
    for k in range(STREAMS):
        cross(front_steps + k)
    for k in range(STREAMS):
        step(ring[front_steps + k])
        cross(-1)

    def product(kernel, name, own, got, scale, codes, codes_got, first_got, steps, weight_shape, term, extra=()):
        groups = scale.shape[0]
        mine, theirs = call(
            lambda *refs: kernel(first_got, term, *refs),
            name,
            [own, got, scale, codes, codes_got, *term.arrays, *[x for k in steps for x in (ring[k], crossed[k])]],
            [shape((rows, units), F32), shape((rows, units))],
            scratch=[pltpu.VMEM((groups, blocks, LANES), F32), pltpu.VMEM(weight_shape, BF16), *extra],
            flops=4 * rows * half * units,
        )
        total = mine + swap(theirs, "sub").astype(F32)
        return total, others(total.astype(BF16), "mp"), mine

    front = (blocks // 2, block, units)
    first_down = [*ring[front_steps : front_steps + STREAMS]]
    half_blocks = blocks // 2
    gate, gate_more, gate_mine = product(
        front_kernel, "gate", normed, normed_got, after(gate_block_scale.T, *first_down), gate_codes, front_got, 0,
        range(0, 2 * (n - 1), 2), front, NoTerm(),
    )
    up, up_more, up_mine = product(
        front_kernel, "up", normed, normed_got, after(up_block_scale.T, *first_down), up_codes, front_got, half_blocks,
        range(1, 2 * (n - 1), 2), front, UpTerm(low, adapters, adapters_more),
        [pltpu.VMEM((rank, units), BF16)],
    )
    for k in range(STREAMS):
        before = front_steps + STREAMS + k
        step(ring[before], gate_mine, up_mine, crossed[before - STREAMS])
        cross(-1)
    silu, hidden, low_hidden = call(
        lambda *refs: hidden_kernel(more, *refs),
        "hidden",
        [gate, up, adapters, *gate_more, *up_more, *adapters_more],
        [shape((rows, units), F32), shape((rows, units)), shape((rows, rank))],
        scratch=[pltpu.VMEM((units, rank), BF16)],
        limit=8,
    )
    low_hidden_got = swap(low_hidden, "sub")
    down_out_parts = call(
        lambda *refs: down_out_kernel(n, *refs),
        "down_out",
        [low_hidden, low_hidden_got, grad, grad_got],
        [shape((rank, half // (WIDE_STREAMS * n)))] * (WIDE_STREAMS * n),
        flops=4 * rows * half * rank,
    )
    down_out_blocks, seen = ring_all(down_out_parts, WIDE_STREAMS)
    (normed_t,) = call(
        transpose_kernel,
        "transpose",
        [normed, after(normed_got, low_hidden)],
        [shape((half, 2 * rows))],
        limit=32,
    )

    back, back_more, _ = product(
        back_kernel, "back", grad, grad_got, after(down_block_scale, normed_t, down_out_parts[0]), down_turned, down_got, 0,
        range(front_steps, (2 + STREAMS) * (n - 1)), (units, half), DownTerm(low, adapters, adapters_more),
        [pltpu.VMEM((units, rank), BF16)],
    )
    up_grad, low_grad = call(
        lambda *refs: up_grad_kernel(more, *refs),
        "up_grad",
        [back, silu, adapters, *back_more, *adapters_more],
        [shape((rows, units)), shape((rows, rank))],
        scratch=[pltpu.VMEM((rank, units), BF16)],
        limit=8,
    )
    low_more = others(after(low, *seen[0]), "mp")
    up_out_term, down_in_term = call(
        lambda *refs: small_kernel(more, *refs),
        "small",
        [hidden, up_grad, low, *low_more],
        [shape(up_adapter_out.shape), shape(down_adapter_in.shape)],
        limit=8,
    )
    extra = 2 * rank // (TALL_STREAMS * n)
    up_in_parts = call(
        lambda *refs: up_in_kernel(n, *refs),
        "up_in",
        [after(low_grad, *seen[2]), swap(low_grad, "sub"), normed_t, up_out_term, down_in_term],
        [shape((half // (TALL_STREAMS * n) + extra, rank))] * (TALL_STREAMS * n),
        flops=4 * rows * half * rank,
    )
    up_in_blocks, _ = ring_all(up_in_parts, TALL_STREAMS, ())

    anywhere = pl.BlockSpec(memory_space=pl.ANY)
    up_in_gradient, up_out_gradient, down_in_gradient, down_out_gradient = call(
        lambda *refs: place_kernel(n, len(down_out_blocks), *refs),
        "place",
        [*down_out_blocks, *up_in_blocks],
        [
            shape((local_width, rank)),
            shape(up_adapter_out.shape),
            shape(down_adapter_in.shape),
            shape((rank, local_width)),
        ],
        scratch=[
            pltpu.VMEM((2, 2 * rank, rank), BF16),
            pltpu.SemaphoreType.DMA((2 * n * (WIDE_STREAMS + TALL_STREAMS),)),
            pltpu.SemaphoreType.DMA((2 * n * TALL_STREAMS,)),
        ],
        specs=[anywhere] * (2 * n * (WIDE_STREAMS + TALL_STREAMS)),
        out_specs=(anywhere, vmem, vmem, anywhere),
        limit=4,
    )
    return up_in_gradient, up_out_gradient, down_in_gradient, down_out_gradient


def general_body(
    tokens,
    cotangent,
    rms_norm_gain,
    gate_codes,
    gate_block_scale,
    up_codes,
    up_block_scale,
    down_codes,
    down_block_scale,
    up_adapter_in,
    up_adapter_out,
    down_adapter_in,
    down_adapter_out,
    sequence_length_list,
    slot_sequence_index,
):
    rows = tokens.shape[0]
    local_width = tokens.shape[1]
    block = gate_block_scale.shape[0] and local_width // gate_codes.shape[0]
    blocks_here = gate_codes.shape[0]
    total_width = local_width * lax.axis_size("mp")
    own_squares = jnp.sum(jnp.square(tokens.astype(jnp.float32)), axis=-1, keepdims=True)
    squares = lax.psum(own_squares, "mp") / total_width
    inv_rms = lax.rsqrt(squares + EPS)
    local_normed_input = (
        tokens.astype(jnp.float32) * inv_rms * rms_norm_gain.astype(jnp.float32)[None, :]
    ).astype(jnp.bfloat16)
    seq_count = sequence_length_list.shape[1]
    longest = rows // seq_count
    total = rows * lax.axis_size("dp") * lax.axis_size("sub")
    ratios = longest / sequence_length_list[0].astype(jnp.float32)
    match = slot_sequence_index[:, None] == jnp.arange(seq_count, dtype=jnp.int32)[None, :]
    token_weight = jnp.sum(jnp.where(match, ratios[None, :], jnp.float32(0.0)), axis=-1)
    token_weight = token_weight * jnp.float32(1.0 / math.sqrt(total))
    local_output = (cotangent.astype(jnp.float32) * token_weight[:, None]).astype(jnp.bfloat16)
    partial_up = jnp.dot(local_normed_input, up_adapter_in, preferred_element_type=jnp.float32)
    partial_output = contract_dims(local_output, down_adapter_out, 1, 1)
    up_adapter_rank, output_adapter_rank = lax.psum((partial_up, partial_output), "mp")
    up_adapter_rank = up_adapter_rank.astype(jnp.bfloat16)
    output_adapter_rank = output_adapter_rank.astype(jnp.bfloat16)
    normed_blocks = local_normed_input.reshape(rows, blocks_here, block)
    out_blocks = local_output.reshape(rows, blocks_here, block)
    wide_gate = jnp.repeat(gate_block_scale.astype(jnp.float32), block, axis=1)[:, None, :]
    wide_up = jnp.repeat(up_block_scale.astype(jnp.float32), block, axis=1)[:, None, :]
    wide_down = jnp.repeat(down_block_scale.astype(jnp.float32), block, axis=0)
    dims_front = (((1, 2), (0, 1)), ((), ()))
    dims_back = (((1, 2), (1, 2)), ((), ()))
    quant_g = lax.all_gather(gate_codes, ("dp", "sub"), axis=1, tiled=True)
    quant_u = lax.all_gather(up_codes, ("dp", "sub"), axis=1, tiled=True)
    weight_g = (quant_g.astype(jnp.float32) * wide_gate).astype(jnp.bfloat16)
    weight_u = (quant_u.astype(jnp.float32) * wide_up).astype(jnp.bfloat16)
    gate_next = lax.dot_general(
        normed_blocks, weight_g, dims_front, preferred_element_type=jnp.float32
    )
    up_next = lax.dot_general(
        normed_blocks, weight_u, dims_front, preferred_element_type=jnp.float32
    )
    gate, base_up_projected = (
        lax.psum_scatter(gate_next, "mp", scatter_dimension=1, tiled=True),
        lax.psum_scatter(up_next, "mp", scatter_dimension=1, tiled=True),
    )
    up_projected = base_up_projected + ADAPTER_SCALE * jnp.dot(
        up_adapter_rank, up_adapter_out, preferred_element_type=jnp.float32
    )
    silu_gate = jax.nn.silu(gate)
    hidden_units = (silu_gate * up_projected).astype(jnp.bfloat16)
    partial_hidden = jnp.dot(hidden_units, down_adapter_in, preferred_element_type=jnp.float32)
    hidden_adapter_rank = lax.psum(partial_hidden, "mp").astype(jnp.bfloat16)
    weight_d = (
        lax.all_gather(down_codes, ("dp", "sub"), axis=0, tiled=True).astype(jnp.float32)
        * wide_down[:, :, None]
    ).astype(jnp.bfloat16)
    back_part = lax.dot_general(out_blocks, weight_d, dims_back, preferred_element_type=jnp.float32)
    base_backward = lax.psum_scatter(back_part, "mp", scatter_dimension=1, tiled=True)
    hidden_gradient = base_backward + ADAPTER_SCALE * contract_dims(
        output_adapter_rank, down_adapter_in, 1, 1
    )
    up_gradient = (hidden_gradient * silu_gate).astype(jnp.bfloat16)
    partial_gradient = contract_dims(up_gradient, up_adapter_out, 1, 1)
    up_adapter_rank_gradient = lax.psum(partial_gradient, "mp").astype(jnp.bfloat16)
    up_in_term = ADAPTER_SCALE * contract_dims(local_normed_input, up_adapter_rank_gradient, 0, 0)
    up_out_term = ADAPTER_SCALE * contract_dims(up_adapter_rank, up_gradient, 0, 0)
    down_in_term = ADAPTER_SCALE * contract_dims(hidden_units, output_adapter_rank, 0, 0)
    down_out_term = ADAPTER_SCALE * contract_dims(hidden_adapter_rank, local_output, 0, 0)
    sum_up_a, sum_up_b, sum_down_a, sum_down_b = lax.psum(
        (up_in_term, up_out_term, down_in_term, down_out_term), ("dp", "sub")
    )
    return (
        sum_up_a.astype(jnp.bfloat16),
        sum_up_b.astype(jnp.bfloat16),
        sum_down_a.astype(jnp.bfloat16),
        sum_down_b.astype(jnp.bfloat16),
    )


def body(tokens, cotangent, rms_norm_gain, gate_codes, *rest):
    whole_tiles = gate_codes.shape[1] % ROW_TILE == 0
    form = fast_body if whole_tiles else general_body
    return form(tokens, cotangent, rms_norm_gain, gate_codes, *rest)


def solution(mesh):
    placed = (
        P(("grp", "dp", "sub"), "mp"),
        P(("grp", "dp", "sub"), "mp"),
        P("mp"),
        P("mp", ("dp", "sub"), None),
        P("mp", None),
        P("mp", ("dp", "sub"), None),
        P("mp", None),
        P(("dp", "sub"), "mp", None),
        P(None, "mp"),
        P(("grp", "mp"), None),
        P("grp", "mp"),
        P(("grp", "mp"), None),
        P("grp", "mp"),
        P(("grp", "dp", "sub"), None),
        P(("grp", "dp", "sub")),
    )
    return jax.shard_map(
        body,
        mesh=mesh,
        in_specs=placed,
        out_specs=(P(("grp", "mp"), None), P("grp", "mp"), P(("grp", "mp"), None), P("grp", "mp")),
        check_vma=False,
    )
```

```python
import math

import jax
import jax.numpy as jnp
from jax import lax
from jax.experimental import pallas as pl
from jax.experimental.pallas import tpu as pltpu
from jax.sharding import PartitionSpec as P

ADAPTER_SCALE = 2.0
EPS = 1e-05
ROW_TILE = 16
LANES = 128
STREAMS = 2
WIDE_STREAMS = 2
TALL_STREAMS = 2
MIB = 1024 * 1024

F32 = jnp.float32
BF16 = jnp.bfloat16


def contract_dims(left, right, left_dim, right_dim):
    return lax.dot_general(
        left, right, (((left_dim,), (right_dim,)), ((), ())), preferred_element_type=F32
    )


def dot(left, right):
    return jnp.dot(left, right, preferred_element_type=F32)


def ring_at(pos, n):
    if isinstance(pos, int):
        return 0 if pos == 0 else (2 * pos - 1 if 2 * pos <= n else 2 * (n - pos))
    return jnp.where(pos == 0, 0, jnp.where(2 * pos <= n, 2 * pos - 1, 2 * (n - pos)))


def ring_position():
    n = lax.axis_size("dp")
    place = lax.axis_index("dp")
    odd = lax.rem(place, 2) == 1
    return jnp.where(place == 0, 0, jnp.where(odd, (place + 1) // 2, n - place // 2))


def ring_step(x):
    n = lax.axis_size("dp")
    return lax.ppermute(x, "dp", [(ring_at(i, n), ring_at((i + 1) % n, n)) for i in range(n)])


def swap(x, axis):
    return lax.ppermute(x, axis, [(0, 1), (1, 0)])


def others(x, axis):
    n = lax.axis_size(axis)
    return [lax.ppermute(x, axis, [(i, (i + k) % n) for i in range(n)]) for k in range(1, n)]


def after(x, *done):
    return lax.optimization_barrier((x, *done))[0]


def call(kernel, name, args, out_shape, scratch=(), specs=None, limit=24, flops=0, out_specs=None):
    vmem = pl.BlockSpec(memory_space=pltpu.VMEM)
    moved = sum(a.size * a.dtype.itemsize for a in args) + sum(
        math.prod(s.shape) * s.dtype.itemsize for s in out_shape
    )
    return pl.pallas_call(
        kernel,
        out_shape=tuple(out_shape),
        in_specs=specs or [vmem] * len(args),
        out_specs=out_specs or tuple([vmem] * len(out_shape)),
        scratch_shapes=list(scratch),
        compiler_params=pltpu.CompilerParams(vmem_limit_bytes=limit * MIB),
        cost_estimate=pl.CostEstimate(flops=0, bytes_accessed=0, transcendentals=0),
        name=name,
    )(*args)


def shape(dims, dtype=BF16):
    return jax.ShapeDtypeStruct(tuple(dims), dtype)


def add_kernel(left, right, out_ref):
    out_ref[...] = (left[...].astype(F32) + right[...].astype(F32)).astype(BF16)


def add(left, right):
    return call(add_kernel, "add", [left, right], [shape(left.shape)], limit=4)[0]


def ring_all(parts, streams, last=()):
    n = lax.axis_size("dp")
    seen = []
    totals = list(parts[:streams])
    for k in range(1, n):
        seen.append([ring_step(t) for t in totals])
        totals = [add(t, p) for t, p in zip(seen[-1], parts[k * streams : (k + 1) * streams])]
    blocks = list(totals)
    for k in range(n - 1):
        if last and k == n - 2:
            totals = [after(t, *last) for t in totals]
        totals = [ring_step(t) for t in totals]
        seen.append(totals)
        blocks += totals
    return blocks + [swap(b, "sub") for b in blocks], seen


def scaled_halves(wide, low_ref, cols, scaled, product, send_ref, own_ref, copy):
    half = send_ref.shape[1]
    step = half // 4
    sub = lax.axis_index("sub")
    low_ref[:, cols] = jnp.zeros((wide.shape[0], LANES), F32)
    for n, (which, out_ref) in enumerate(((1 - sub, send_ref), (sub, own_ref))):

        @pl.loop(0, half // step)
        def _(j, n=n, which=which, out_ref=out_ref):
            first = pl.multiple_of(which * half + j * step, step)
            copy(n * (half // step) + j, first, step).wait()
            parts = []
            for i in range(step // LANES):
                tile = pl.ds(pl.multiple_of(first + i * LANES, LANES), LANES)
                parts.append(scaled(wide[:, tile].astype(F32), tile).astype(BF16))
            value = jnp.concatenate(parts, axis=1)
            out_ref[:, pl.ds(pl.multiple_of(j * step, step), step)] = value
            low_ref[:, cols] += product(value, pl.ds(first, step))


def column_copy(source, buffer, sems):
    def copy(k, first, step):
        at = pl.ds(first, step)
        return pltpu.make_async_copy(source.at[:, at], buffer.at[:, at], sems.at[k])

    return copy


def start_halves(source, buffer, sems):
    half = source.shape[1] // 2
    step = half // 4
    copy = column_copy(source, buffer, sems)
    sub = lax.axis_index("sub")
    for k in range(8):
        which = 1 - sub if k < 4 else sub
        copy(k, pl.multiple_of(which * half + k % 4 * step, step), step).start()
    return copy


def square_kernel(tokens, lengths, square_ref, buffer, sems):
    width = tokens.shape[1]
    step = width // sems.shape[0]
    copy = column_copy(tokens, buffer, sems)
    for k in range(width // step):
        copy(k, k * step, step).start()
    squares = jnp.zeros(square_ref.shape, F32)
    for k in range(width // step):
        copy(k, k * step, step).wait()
        for i in range(step // LANES):
            at = k * step + i * LANES
            squares = squares + jnp.square(buffer[:, at : at + LANES].astype(F32))
    square_ref[...] = jnp.broadcast_to(jnp.sum(squares, axis=1, keepdims=True), square_ref.shape)


def cotangent_kernel(
    total, cotangent, lengths, slots, adapter, send_ref, own_ref, low_ref, buffer, sems
):
    rows = cotangent.shape[0]
    copy = start_halves(cotangent, buffer, sems)
    index = jnp.broadcast_to(slots[...], (LANES, rows))
    weight = jnp.zeros((LANES, rows), F32)
    for s in range(lengths.shape[1]):
        length = jnp.full((LANES, rows), lengths[0, s], jnp.int32).astype(F32)
        weight = weight + jnp.where(index == s, (rows // lengths.shape[1]) / length, 0.0)
    row = (weight * F32(1.0 / math.sqrt(total))).T
    scaled_halves(
        buffer,
        low_ref,
        slice(None),
        lambda tile, cols: tile * row,
        lambda value, cols: contract_dims(value, adapter[:, cols], 1, 1),
        send_ref,
        own_ref,
        copy,
    )


def token_kernel(total_width, tokens, gain, adapter, low_out, squares, *refs):
    squares_more, (send_ref, own_ref, low_ref, buffer, sems) = refs[:-5], refs[-5:]
    copy = start_halves(tokens, buffer, sems)
    rank = adapter.shape[1]
    total = squares[...]
    for ref in squares_more:
        total = total + ref[...]
    row = lax.rsqrt(total / total_width + EPS)
    low_ref[:, rank:] = low_out[...]
    scaled_halves(
        buffer,
        low_ref,
        slice(0, rank),
        lambda tile, cols: tile * row * gain[:, cols].astype(F32),
        lambda value, cols: dot(value, adapter[cols, :]),
        send_ref,
        own_ref,
        copy,
    )


def transpose_kernel(own, got, out_ref):
    rows, step = own.shape[0], out_ref.shape[0]
    for i, ref in enumerate((own, got)):
        out_ref[:, i * rows : (i + 1) * rows] = ref[...].astype(F32).T.astype(BF16)


def widen(scale, wide):
    for g in range(scale.shape[0]):
        row = scale[g : g + 1, :].astype(F32)
        wide[g] = jnp.broadcast_to(row, (LANES, row.shape[1])).T


def place_shards(codes, got, first_got, moved, store):
    n = lax.axis_size("dp")
    sub, grp, place = (lax.axis_index(a) for a in ("sub", "grp", "dp"))
    pos = ring_position()
    blocks = codes.shape[0] // 2
    quarter = blocks // 2

    @pl.loop(0, blocks, unroll=4)
    def _(b):
        store(b, place * 2 + sub, codes[sub * blocks + b])
        store(b, place * 2 + 1 - sub, got[first_got + b])

    streams = len(moved) // (2 * (n - 1))
    size = quarter // streams
    for k in range(n - 1):
        there = ring_at(lax.rem(pos - k - 1 + n, n), n)
        for i in range(2 * streams):
            piece = moved[2 * streams * k + i]
            start = (grp if i % 2 == 0 else 1 - grp) * quarter + i // 2 * size

            @pl.loop(0, size, unroll=4)
            def _(b, piece=piece, start=start, there=there):
                store(start + b, there * 2 + sub, piece[b])
                store(start + b, there * 2 + 1 - sub, piece[size + b])


def front_kernel(first_got, term, own, got, scale, codes, codes_got, *refs):
    moved, (mine_ref, theirs_ref, wide, weight) = term.split(refs)
    blocks, rows, units = codes.shape
    first = lax.axis_index("sub") * (blocks // 2)
    widen(scale, wide)

    def store(b, shard, piece):
        at = pl.ds(pl.multiple_of(shard * rows, ROW_TILE), rows)
        for g in range(units // LANES):
            cols = slice(g * LANES, (g + 1) * LANES)
            factor = wide[g * wide.shape[0] * LANES // units, pl.ds(first + b, 1), :]
            weight[b, at, cols] = (piece[:, cols].astype(F32) * factor).astype(BF16)

    place_shards(codes, codes_got, first_got, moved, store)
    matrix = weight[...].reshape(-1, units)
    mine_ref[...] = term.added(dot(own[...], matrix))
    theirs_ref[...] = dot(got[...], matrix).astype(BF16)


def back_kernel(first_got, term, own, got, scale, codes, codes_got, *refs):
    moved, (mine_ref, theirs_ref, wide, weight) = term.split(refs)
    blocks, rows, block = codes.shape
    first = lax.axis_index("sub") * (blocks // 2)
    per_group = weight.shape[0] // wide.shape[0]
    widen(scale, wide)

    def store(b, shard, piece):
        at = pl.multiple_of(shard * rows, ROW_TILE)
        factor = wide[at // per_group, pl.ds(first + b, 1), :]
        cols = pl.ds(pl.multiple_of(b * block, block), block)
        weight[pl.ds(at, rows), cols] = (piece.astype(F32) * factor).astype(BF16)

    place_shards(codes, codes_got, first_got, moved, store)
    matrix = weight[...]
    mine_ref[...] = term.added(contract_dims(own[...], matrix, 1, 1))
    theirs_ref[...] = contract_dims(got[...], matrix, 1, 1).astype(BF16)


def place_own(scratch, own, more, axis):
    n = len(more) + 1
    size = own.shape[axis]
    for k, ref in enumerate((own, *more)):
        at = pl.ds(pl.multiple_of(lax.rem(lax.axis_index("mp") + n - k, n) * size, size), size)
        if axis == 0:
            scratch[at, :] = ref[...]
        else:
            scratch[:, at] = ref[...]


def own_units(full, ref, axis):
    size = ref.shape[axis]
    for i in range(full.shape[axis] // size):

        @pl.when(lax.axis_index("mp") == i)
        def _(i=i):
            ref[...] = lax.slice_in_dim(full, i * size, (i + 1) * size, axis=axis).astype(BF16)


class NoTerm:
    arrays = ()

    def split(self, refs):
        return refs[:-4], refs[-4:]

    def added(self, product):
        return product


class UpTerm:
    def __init__(self, low, adapters, more):
        self.arrays = (low, adapters, *more)

    def split(self, refs):
        count = len(self.arrays)
        self.refs, self.all = refs[:count], refs[-1]
        return refs[count:-5], refs[-5:-1]

    def added(self, product):
        low, adapters, *more = self.refs
        rank = self.all.shape[0]
        place_own(self.all, adapters.at[:rank], [r.at[:rank] for r in more], 1)
        return product + ADAPTER_SCALE * dot(low[:, :rank].astype(BF16), self.all[...])


class DownTerm(UpTerm):
    def added(self, product):
        low, adapters, *more = self.refs
        rank = self.all.shape[1]
        place_own(self.all, adapters.at[rank:], [r.at[rank:] for r in more], 0)
        return product + ADAPTER_SCALE * contract_dims(
            low[:, rank:].astype(BF16), self.all[...], 1, 1
        )


def hidden_kernel(more, gate, up, adapters, *refs):
    gate_more, up_more, adapters_more = (refs[i * more : (i + 1) * more] for i in range(3))
    silu_ref, hidden_ref, low_ref, down_in_all = refs[3 * more :]
    rank = low_ref.shape[1]
    place_own(down_in_all, adapters.at[rank:], [r.at[rank:] for r in adapters_more], 0)
    gate_sum, up_sum = gate[...], up[...]
    for ref in gate_more:
        gate_sum = gate_sum + ref[...].astype(F32)
    for ref in up_more:
        up_sum = up_sum + ref[...].astype(F32)
    silu = gate_sum * jax.nn.sigmoid(gate_sum)
    silu_ref[...] = silu
    hidden = (silu * up_sum).astype(BF16)
    hidden_ref[...] = hidden
    low_ref[...] = (ADAPTER_SCALE * dot(hidden, down_in_all[...])).astype(BF16)


def up_grad_kernel(more, back, silu, adapters, *refs):
    back_more, adapters_more = (refs[i * more : (i + 1) * more] for i in range(2))
    up_grad_ref, low_ref, up_out_all = refs[2 * more :]
    rank = low_ref.shape[1]
    place_own(up_out_all, adapters.at[:rank], [r.at[:rank] for r in adapters_more], 1)
    total = back[...]
    for ref in back_more:
        total = total + ref[...].astype(F32)
    up_grad = (total * silu[...]).astype(BF16)
    up_grad_ref[...] = up_grad
    low_ref[...] = (ADAPTER_SCALE * contract_dims(up_grad, up_out_all[...], 1, 1)).astype(BF16)


def small_kernel(more, hidden, up_grad, low, *refs):
    low_more, (up_out_term, down_in_term) = refs[:more], refs[more:]
    total = low[...]
    for ref in low_more:
        total = total + ref[...]
    rank = total.shape[1] // 2
    low_up, low_out = total[:, :rank].astype(BF16), total[:, rank:].astype(BF16)
    low_up_t = low_up.astype(F32).T.astype(BF16)
    own_units(ADAPTER_SCALE * dot(low_up_t, up_grad[...]), up_out_term, 1)
    hidden_t = hidden[...].astype(F32).T.astype(BF16)
    own_units(ADAPTER_SCALE * dot(hidden_t, low_out), down_in_term, 0)


def down_out_kernel(n, low, low_got, grad, grad_got, *out_refs):
    pos = ring_position()
    streams = len(out_refs) // n
    low_t = jnp.concatenate([low[...], low_got[...]], axis=0).astype(F32).T.astype(BF16)
    rows = low.shape[0]
    for k, ref in enumerate(out_refs):
        size = ref.shape[1]
        block = lax.rem(pos - 1 - k // streams + 2 * n, n) * streams + k % streams
        at = pl.ds(pl.multiple_of(block * size, size), size)
        ref[...] = (
            dot(low_t[:, :rows], grad[:, at]) + dot(low_t[:, rows:], grad_got[:, at])
        ).astype(BF16)


def up_in_kernel(n, low, low_got, normed_t, up_out_term, down_in_term, *out_refs):
    pos = ring_position()
    streams = len(out_refs) // n
    size = normed_t.shape[0] // len(out_refs)
    extra = out_refs[0].shape[0] - size
    both = jnp.concatenate([low[...], low_got[...]], axis=0)
    for k, ref in enumerate(out_refs):
        block = lax.rem(pos - 1 - k // streams + 2 * n, n) * streams + k % streams
        at = pl.ds(pl.multiple_of(block * size, size), size)
        ref[pl.ds(0, size), :] = dot(normed_t[at, :], both).astype(BF16)
        per = up_out_term.shape[0] // extra
        index = pl.ds(pl.multiple_of(lax.rem(block, per) * extra, extra), extra)

        @pl.when(block < per)
        def _(ref=ref, index=index):
            ref[pl.ds(size, extra), :] = up_out_term[index, :]

        @pl.when(block >= per)
        def _(ref=ref, index=index):
            ref[pl.ds(size, extra), :] = down_in_term[index, :]


def copy_all(copies):
    for c in copies:
        c.start()
    for c in copies:
        c.wait()


def place_of(i, count, n, pos, sub, size):
    per_core = count // 2
    streams = per_core // n
    half = sub if i < per_core else 1 - sub
    block = lax.rem(pos - i % per_core // streams + n, n) * streams + i % streams
    return pl.ds(pl.multiple_of((half * per_core + block) * size, size), size)


def place_kernel(n, wide_count, *refs):
    pieces = refs[:-7]
    out_ref, up_out_ref, down_in_ref, wide_ref, small, sems, small_sems = refs[-7:]
    pos, sub = ring_position(), lax.axis_index("sub")
    wide, tall = pieces[:wide_count], pieces[wide_count:]
    copies = []
    for i, piece in enumerate(wide):
        at = place_of(i, len(wide), n, pos, sub, piece.shape[1])
        copies.append(pltpu.make_async_copy(piece, wide_ref.at[:, at], sems.at[i]))
    size = out_ref.shape[0] // len(tall)
    extra = tall[0].shape[0] - size
    for i, piece in enumerate(tall):
        at = place_of(i, len(tall), n, pos, sub, size)
        copies.append(
            pltpu.make_async_copy(
                piece.at[pl.ds(0, size), :], out_ref.at[at, :], sems.at[len(wide) + i]
            )
        )
        half = i // (len(tall) // 2)
        at = place_of(i % (len(tall) // 2), len(tall), n, pos, 0, extra)
        copies.append(
            pltpu.make_async_copy(
                piece.at[pl.ds(size, extra), :], small.at[half, at, :], small_sems.at[i]
            )
        )
    copy_all(copies)
    total = (small[0].astype(F32) + small[1].astype(F32)).astype(BF16)
    rows = up_out_ref.shape[0]
    up_out_ref[...] = total[:rows]
    down_in_ref[...] = total[rows:]


def half_kernel(*refs):
    sources, out_ref, sems = refs[:-2], refs[-2], refs[-1]
    other = 1 - lax.axis_index("sub")
    half = sources[0].shape[0] // 2
    copy_all(
        [
            pltpu.make_async_copy(
                ref.at[pl.ds(other * half, half)], out_ref.at[pl.ds(i * half, half)], sems.at[i]
            )
            for i, ref in enumerate(sources)
        ]
    )


def quarter_kernel(count, *refs):
    sources, got, out_refs, sems = refs[:count], refs[count], refs[count + 1 : -1], refs[-1]
    streams = len(out_refs) // count
    sub, grp = lax.axis_index("sub"), lax.axis_index("grp")
    half = sources[0].shape[0] // 2
    quarter = half // 2
    copies = []
    size = quarter // streams
    for i, out_ref in enumerate(out_refs):
        first = grp * quarter + i % streams * size
        own = sources[i // streams].at[pl.ds(sub * half + first, size)]
        theirs = got.at[pl.ds(i // streams * half + first, size)]
        for k, source in enumerate((own, theirs)):
            copies.append(
                pltpu.make_async_copy(source, out_ref.at[pl.ds(k * size, size)], sems.at[2 * i + k])
            )
    copy_all(copies)


def start_shards(codes, streams):
    blocks, rows, units = codes[0].shape
    count = len(codes)
    anywhere = pl.BlockSpec(memory_space=pl.ANY)
    (send,) = call(
        half_kernel,
        "halves",
        codes,
        [shape((count * blocks // 2, rows, units))],
        scratch=[pltpu.SemaphoreType.DMA((count,))],
        specs=[anywhere] * count,
        out_specs=(anywhere,),
        limit=4,
    )
    got = swap(send, "sub")
    moving = call(
        lambda *refs: quarter_kernel(count, *refs),
        "quarters",
        [*codes, got],
        [shape((blocks // 2 // streams, rows, units))] * (count * streams),
        scratch=[pltpu.SemaphoreType.DMA((2 * count * streams,))],
        specs=[anywhere] * (count + 1),
        out_specs=(anywhere,) * (count * streams),
        limit=4,
    )
    return list(moving), got


def fast_body(
    tokens,
    cotangent,
    rms_norm_gain,
    gate_codes,
    gate_block_scale,
    up_codes,
    up_block_scale,
    down_codes,
    down_block_scale,
    up_adapter_in,
    up_adapter_out,
    down_adapter_in,
    down_adapter_out,
    sequence_length_list,
    slot_sequence_index,
):
    rows, local_width = tokens.shape
    blocks, _, units = gate_codes.shape
    block = local_width // blocks
    half = local_width // 2
    rank = up_adapter_in.shape[1]
    total_width = local_width * lax.axis_size("mp")
    n = lax.axis_size("dp")
    more = lax.axis_size("mp") - 1

    (gate_moving, up_moving), front_got = start_shards([gate_codes, up_codes], 1)
    ring, crossed = [], []

    def step(moving, *done):
        ring.append(ring_step(after(moving, *done) if done else moving))

    def cross(k, *done):
        crossed.append(swap(after(ring[k], *done) if done else ring[k], "grp"))

    step(gate_moving)
    step(up_moving)

    vmem = pl.BlockSpec(memory_space=pltpu.VMEM)
    smem = pl.BlockSpec(memory_space=pltpu.SMEM)
    hbm = pl.BlockSpec(memory_space=pltpu.HBM)
    buffers = [pltpu.VMEM((rows, local_width), BF16), pltpu.SemaphoreType.DMA((8,))]
    lengths = after(sequence_length_list, gate_moving, up_moving)
    (squares,) = call(
        square_kernel, "squares", [tokens, lengths], [shape((rows, LANES), F32)],
        scratch=buffers, specs=[hbm, smem], limit=16,
    )
    squares_more = others(squares, "mp")
    grad_send, grad, low_out = call(
        lambda *refs: cotangent_kernel(rows * n * lax.axis_size("sub"), *refs),
        "cotangent",
        [cotangent, after(lengths, squares), slot_sequence_index[None, :], down_adapter_out],
        [shape((rows, half))] * 2 + [shape((rows, rank), F32)],
        scratch=buffers,
        specs=[hbm, smem, vmem, vmem],
    )
    cross(0, grad)
    cross(1, grad)
    step(ring[0], grad)
    step(ring[1], ring[0], grad)
    adapters = jnp.concatenate([up_adapter_out, down_adapter_in], axis=0)
    adapters_more = others(after(adapters, *ring[:2]), "mp")
    normed_send, normed, low = call(
        lambda *refs: token_kernel(total_width, *refs),
        "tokens",
        [
            tokens,
            rms_norm_gain[None, :],
            up_adapter_in,
            low_out,
            after(squares, *ring[2:4], *crossed[:2], *adapters_more),
            *squares_more,
        ],
        [shape((rows, half))] * 2 + [shape((rows, 2 * rank), F32)],
        scratch=buffers,
        specs=[hbm] + [vmem] * (4 + more),
    )
    grad_got = swap(grad_send, "sub")
    normed_got = swap(normed_send, "sub")
    step(ring[2], ring[3], *crossed[:2])
    step(ring[3], ring[2], *crossed[:2])
    cross(2)
    cross(3)
    cross(4)
    cross(5)
    down_turned = jnp.swapaxes(after(down_codes, ring[4]), 0, 1)
    down_moving, down_got = start_shards([down_turned], STREAMS)
    front_steps = 2 * (n - 1)
    for moving in down_moving:
        step(moving, *ring[4:6], *crossed[2:4], grad_got, normed_got)
    for k in range(STREAMS):
        cross(front_steps + k)
    for k in range(STREAMS):
        step(ring[front_steps + k])
        cross(-1)

    def product(kernel, name, own, got, scale, codes, codes_got, first_got, steps, weight_shape, term, extra=()):
        groups = scale.shape[0]
        mine, theirs = call(
            lambda *refs: kernel(first_got, term, *refs),
            name,
            [own, got, scale, codes, codes_got, *term.arrays, *[x for k in steps for x in (ring[k], crossed[k])]],
            [shape((rows, units), F32), shape((rows, units))],
            scratch=[pltpu.VMEM((groups, blocks, LANES), F32), pltpu.VMEM(weight_shape, BF16), *extra],
            flops=4 * rows * half * units,
        )
        total = mine + swap(theirs, "sub").astype(F32)
        return total, others(total.astype(BF16), "mp"), mine

    front = (blocks // 2, block, units)
    first_down = [*ring[front_steps : front_steps + STREAMS]]
    half_blocks = blocks // 2
    gate, gate_more, gate_mine = product(
        front_kernel, "gate", normed, normed_got, after(gate_block_scale.T, *first_down), gate_codes, front_got, 0,
        range(0, 2 * (n - 1), 2), front, NoTerm(),
    )
    up, up_more, up_mine = product(
        front_kernel, "up", normed, normed_got, after(up_block_scale.T, *first_down), up_codes, front_got, half_blocks,
        range(1, 2 * (n - 1), 2), front, UpTerm(low, adapters, adapters_more),
        [pltpu.VMEM((rank, units), BF16)],
    )
    for k in range(STREAMS):
        before = front_steps + STREAMS + k
        step(ring[before], gate_mine, up_mine, crossed[before - STREAMS])
        cross(-1)
    silu, hidden, low_hidden = call(
        lambda *refs: hidden_kernel(more, *refs),
        "hidden",
        [gate, up, adapters, *gate_more, *up_more, *adapters_more],
        [shape((rows, units), F32), shape((rows, units)), shape((rows, rank))],
        scratch=[pltpu.VMEM((units, rank), BF16)],
        limit=8,
    )
    low_hidden_got = swap(low_hidden, "sub")
    down_out_parts = call(
        lambda *refs: down_out_kernel(n, *refs),
        "down_out",
        [low_hidden, low_hidden_got, grad, grad_got],
        [shape((rank, half // (WIDE_STREAMS * n)))] * (WIDE_STREAMS * n),
        flops=4 * rows * half * rank,
    )
    down_out_blocks, seen = ring_all(down_out_parts, WIDE_STREAMS)
    (normed_t,) = call(
        transpose_kernel,
        "transpose",
        [normed, after(normed_got, low_hidden)],
        [shape((half, 2 * rows))],
        limit=32,
    )

    back, back_more, _ = product(
        back_kernel, "back", grad, grad_got, after(down_block_scale, normed_t, down_out_parts[0]), down_turned, down_got, 0,
        range(front_steps, (2 + STREAMS) * (n - 1)), (units, half), DownTerm(low, adapters, adapters_more),
        [pltpu.VMEM((units, rank), BF16)],
    )
    up_grad, low_grad = call(
        lambda *refs: up_grad_kernel(more, *refs),
        "up_grad",
        [back, silu, adapters, *back_more, *adapters_more],
        [shape((rows, units)), shape((rows, rank))],
        scratch=[pltpu.VMEM((rank, units), BF16)],
        limit=8,
    )
    low_more = others(after(low, *seen[0]), "mp")
    up_out_term, down_in_term = call(
        lambda *refs: small_kernel(more, *refs),
        "small",
        [hidden, up_grad, low, *low_more],
        [shape(up_adapter_out.shape), shape(down_adapter_in.shape)],
        limit=8,
    )
    extra = 2 * rank // (TALL_STREAMS * n)
    up_in_parts = call(
        lambda *refs: up_in_kernel(n, *refs),
        "up_in",
        [after(low_grad, *seen[2]), swap(low_grad, "sub"), normed_t, up_out_term, down_in_term],
        [shape((half // (TALL_STREAMS * n) + extra, rank))] * (TALL_STREAMS * n),
        flops=4 * rows * half * rank,
    )
    up_in_blocks, _ = ring_all(up_in_parts, TALL_STREAMS, down_out_blocks[-WIDE_STREAMS:])

    anywhere = pl.BlockSpec(memory_space=pl.ANY)
    up_in_gradient, up_out_gradient, down_in_gradient, down_out_gradient = call(
        lambda *refs: place_kernel(n, len(down_out_blocks), *refs),
        "place",
        [*down_out_blocks, *up_in_blocks],
        [
            shape((local_width, rank)),
            shape(up_adapter_out.shape),
            shape(down_adapter_in.shape),
            shape((rank, local_width)),
        ],
        scratch=[
            pltpu.VMEM((2, 2 * rank, rank), BF16),
            pltpu.SemaphoreType.DMA((2 * n * (WIDE_STREAMS + TALL_STREAMS),)),
            pltpu.SemaphoreType.DMA((2 * n * TALL_STREAMS,)),
        ],
        specs=[anywhere] * (2 * n * (WIDE_STREAMS + TALL_STREAMS)),
        out_specs=(anywhere, vmem, vmem, anywhere),
        limit=4,
    )
    return up_in_gradient, up_out_gradient, down_in_gradient, down_out_gradient


def general_body(
    tokens,
    cotangent,
    rms_norm_gain,
    gate_codes,
    gate_block_scale,
    up_codes,
    up_block_scale,
    down_codes,
    down_block_scale,
    up_adapter_in,
    up_adapter_out,
    down_adapter_in,
    down_adapter_out,
    sequence_length_list,
    slot_sequence_index,
):
    rows = tokens.shape[0]
    local_width = tokens.shape[1]
    block = gate_block_scale.shape[0] and local_width // gate_codes.shape[0]
    blocks_here = gate_codes.shape[0]
    total_width = local_width * lax.axis_size("mp")
    own_squares = jnp.sum(jnp.square(tokens.astype(jnp.float32)), axis=-1, keepdims=True)
    squares = lax.psum(own_squares, "mp") / total_width
    inv_rms = lax.rsqrt(squares + EPS)
    local_normed_input = (
        tokens.astype(jnp.float32) * inv_rms * rms_norm_gain.astype(jnp.float32)[None, :]
    ).astype(jnp.bfloat16)
    seq_count = sequence_length_list.shape[1]
    longest = rows // seq_count
    total = rows * lax.axis_size("dp") * lax.axis_size("sub")
    ratios = longest / sequence_length_list[0].astype(jnp.float32)
    match = slot_sequence_index[:, None] == jnp.arange(seq_count, dtype=jnp.int32)[None, :]
    token_weight = jnp.sum(jnp.where(match, ratios[None, :], jnp.float32(0.0)), axis=-1)
    token_weight = token_weight * jnp.float32(1.0 / math.sqrt(total))
    local_output = (cotangent.astype(jnp.float32) * token_weight[:, None]).astype(jnp.bfloat16)
    partial_up = jnp.dot(local_normed_input, up_adapter_in, preferred_element_type=jnp.float32)
    partial_output = contract_dims(local_output, down_adapter_out, 1, 1)
    up_adapter_rank, output_adapter_rank = lax.psum((partial_up, partial_output), "mp")
    up_adapter_rank = up_adapter_rank.astype(jnp.bfloat16)
    output_adapter_rank = output_adapter_rank.astype(jnp.bfloat16)
    normed_blocks = local_normed_input.reshape(rows, blocks_here, block)
    out_blocks = local_output.reshape(rows, blocks_here, block)
    wide_gate = jnp.repeat(gate_block_scale.astype(jnp.float32), block, axis=1)[:, None, :]
    wide_up = jnp.repeat(up_block_scale.astype(jnp.float32), block, axis=1)[:, None, :]
    wide_down = jnp.repeat(down_block_scale.astype(jnp.float32), block, axis=0)
    dims_front = (((1, 2), (0, 1)), ((), ()))
    dims_back = (((1, 2), (1, 2)), ((), ()))
    quant_g = lax.all_gather(gate_codes, ("dp", "sub"), axis=1, tiled=True)
    quant_u = lax.all_gather(up_codes, ("dp", "sub"), axis=1, tiled=True)
    weight_g = (quant_g.astype(jnp.float32) * wide_gate).astype(jnp.bfloat16)
    weight_u = (quant_u.astype(jnp.float32) * wide_up).astype(jnp.bfloat16)
    gate_next = lax.dot_general(
        normed_blocks, weight_g, dims_front, preferred_element_type=jnp.float32
    )
    up_next = lax.dot_general(
        normed_blocks, weight_u, dims_front, preferred_element_type=jnp.float32
    )
    gate, base_up_projected = (
        lax.psum_scatter(gate_next, "mp", scatter_dimension=1, tiled=True),
        lax.psum_scatter(up_next, "mp", scatter_dimension=1, tiled=True),
    )
    up_projected = base_up_projected + ADAPTER_SCALE * jnp.dot(
        up_adapter_rank, up_adapter_out, preferred_element_type=jnp.float32
    )
    silu_gate = jax.nn.silu(gate)
    hidden_units = (silu_gate * up_projected).astype(jnp.bfloat16)
    partial_hidden = jnp.dot(hidden_units, down_adapter_in, preferred_element_type=jnp.float32)
    hidden_adapter_rank = lax.psum(partial_hidden, "mp").astype(jnp.bfloat16)
    weight_d = (
        lax.all_gather(down_codes, ("dp", "sub"), axis=0, tiled=True).astype(jnp.float32)
        * wide_down[:, :, None]
    ).astype(jnp.bfloat16)
    back_part = lax.dot_general(out_blocks, weight_d, dims_back, preferred_element_type=jnp.float32)
    base_backward = lax.psum_scatter(back_part, "mp", scatter_dimension=1, tiled=True)
    hidden_gradient = base_backward + ADAPTER_SCALE * contract_dims(
        output_adapter_rank, down_adapter_in, 1, 1
    )
    up_gradient = (hidden_gradient * silu_gate).astype(jnp.bfloat16)
    partial_gradient = contract_dims(up_gradient, up_adapter_out, 1, 1)
    up_adapter_rank_gradient = lax.psum(partial_gradient, "mp").astype(jnp.bfloat16)
    up_in_term = ADAPTER_SCALE * contract_dims(local_normed_input, up_adapter_rank_gradient, 0, 0)
    up_out_term = ADAPTER_SCALE * contract_dims(up_adapter_rank, up_gradient, 0, 0)
    down_in_term = ADAPTER_SCALE * contract_dims(hidden_units, output_adapter_rank, 0, 0)
    down_out_term = ADAPTER_SCALE * contract_dims(hidden_adapter_rank, local_output, 0, 0)
    sum_up_a, sum_up_b, sum_down_a, sum_down_b = lax.psum(
        (up_in_term, up_out_term, down_in_term, down_out_term), ("dp", "sub")
    )
    return (
        sum_up_a.astype(jnp.bfloat16),
        sum_up_b.astype(jnp.bfloat16),
        sum_down_a.astype(jnp.bfloat16),
        sum_down_b.astype(jnp.bfloat16),
    )


def body(tokens, cotangent, rms_norm_gain, gate_codes, *rest):
    whole_tiles = gate_codes.shape[1] % ROW_TILE == 0
    ring_of_four = lax.axis_size("dp") == 4
    pairs = lax.axis_size("grp") == 2 and lax.axis_size("sub") == 2
    form = fast_body if whole_tiles and ring_of_four and pairs else general_body
    return form(tokens, cotangent, rms_norm_gain, gate_codes, *rest)


def solution(mesh):
    placed = (
        P(("grp", "dp", "sub"), "mp"),
        P(("grp", "dp", "sub"), "mp"),
        P("mp"),
        P("mp", ("dp", "sub"), None),
        P("mp", None),
        P("mp", ("dp", "sub"), None),
        P("mp", None),
        P(("dp", "sub"), "mp", None),
        P(None, "mp"),
        P(("grp", "mp"), None),
        P("grp", "mp"),
        P(("grp", "mp"), None),
        P("grp", "mp"),
        P(("grp", "dp", "sub"), None),
        P(("grp", "dp", "sub")),
    )
    return jax.shard_map(
        body,
        mesh=mesh,
        in_specs=placed,
        out_specs=(P(("grp", "mp"), None), P("grp", "mp"), P(("grp", "mp"), None), P("grp", "mp")),
        check_vma=False,
    )
```

```python
import math

import jax
import jax.numpy as jnp
from jax import lax
from jax.experimental import pallas as pl
from jax.experimental.pallas import tpu as pltpu
from jax.sharding import PartitionSpec as P

ADAPTER_SCALE = 2.0
EPS = 1e-05
ROW_TILE = 16
LANES = 128
STREAMS = 2
WIDE_STREAMS = 2
TALL_STREAMS = 2
MIB = 1024 * 1024

F32 = jnp.float32
BF16 = jnp.bfloat16


def contract_dims(left, right, left_dim, right_dim):
    return lax.dot_general(
        left, right, (((left_dim,), (right_dim,)), ((), ())), preferred_element_type=F32
    )


def dot(left, right):
    return jnp.dot(left, right, preferred_element_type=F32)


def ring_at(pos, n):
    if isinstance(pos, int):
        return 0 if pos == 0 else (2 * pos - 1 if 2 * pos <= n else 2 * (n - pos))
    return jnp.where(pos == 0, 0, jnp.where(2 * pos <= n, 2 * pos - 1, 2 * (n - pos)))


def ring_position():
    n = lax.axis_size("dp")
    place = lax.axis_index("dp")
    odd = lax.rem(place, 2) == 1
    return jnp.where(place == 0, 0, jnp.where(odd, (place + 1) // 2, n - place // 2))


def ring_step(x):
    n = lax.axis_size("dp")
    return lax.ppermute(x, "dp", [(ring_at(i, n), ring_at((i + 1) % n, n)) for i in range(n)])


def swap(x, axis):
    return lax.ppermute(x, axis, [(0, 1), (1, 0)])


def others(x, axis):
    n = lax.axis_size(axis)
    return [lax.ppermute(x, axis, [(i, (i + k) % n) for i in range(n)]) for k in range(1, n)]


def after(x, *done):
    return lax.optimization_barrier((x, *done))[0]


def call(kernel, name, args, out_shape, scratch=(), specs=None, limit=24, flops=0, out_specs=None):
    vmem = pl.BlockSpec(memory_space=pltpu.VMEM)
    moved = sum(a.size * a.dtype.itemsize for a in args) + sum(
        math.prod(s.shape) * s.dtype.itemsize for s in out_shape
    )
    return pl.pallas_call(
        kernel,
        out_shape=tuple(out_shape),
        in_specs=specs or [vmem] * len(args),
        out_specs=out_specs or tuple([vmem] * len(out_shape)),
        scratch_shapes=list(scratch),
        compiler_params=pltpu.CompilerParams(vmem_limit_bytes=limit * MIB),
        cost_estimate=pl.CostEstimate(flops=0, bytes_accessed=0, transcendentals=0),
        name=name,
    )(*args)


def shape(dims, dtype=BF16):
    return jax.ShapeDtypeStruct(tuple(dims), dtype)


def add_kernel(left, right, out_ref):
    out_ref[...] = (left[...].astype(F32) + right[...].astype(F32)).astype(BF16)


def add(left, right):
    return call(add_kernel, "add", [left, right], [shape(left.shape)], limit=4)[0]


def ring_all(parts, streams, last=()):
    n = lax.axis_size("dp")
    seen = []
    totals = list(parts[:streams])
    for k in range(1, n):
        seen.append([ring_step(t) for t in totals])
        totals = [add(t, p) for t, p in zip(seen[-1], parts[k * streams : (k + 1) * streams])]
    blocks = list(totals)
    for k in range(n - 1):
        if last and k == n - 2:
            totals = [after(t, *last) for t in totals]
        totals = [ring_step(t) for t in totals]
        seen.append(totals)
        blocks += totals
    return blocks + [swap(b, "sub") for b in blocks], seen


def scaled_halves(wide, low_ref, cols, scaled, product, send_ref, own_ref, copy):
    half = send_ref.shape[1]
    step = half // 4
    sub = lax.axis_index("sub")
    low_ref[:, cols] = jnp.zeros((wide.shape[0], LANES), F32)
    for n, (which, out_ref) in enumerate(((1 - sub, send_ref), (sub, own_ref))):

        @pl.loop(0, half // step)
        def _(j, n=n, which=which, out_ref=out_ref):
            first = pl.multiple_of(which * half + j * step, step)
            copy(n * (half // step) + j, first, step).wait()
            parts = []
            for i in range(step // LANES):
                tile = pl.ds(pl.multiple_of(first + i * LANES, LANES), LANES)
                parts.append(scaled(wide[:, tile].astype(F32), tile).astype(BF16))
            value = jnp.concatenate(parts, axis=1)
            out_ref[:, pl.ds(pl.multiple_of(j * step, step), step)] = value
            low_ref[:, cols] += product(value, pl.ds(first, step))


def column_copy(source, buffer, sems):
    def copy(k, first, step):
        at = pl.ds(first, step)
        return pltpu.make_async_copy(source.at[:, at], buffer.at[:, at], sems.at[k])

    return copy


def start_halves(source, buffer, sems):
    half = source.shape[1] // 2
    step = half // 4
    copy = column_copy(source, buffer, sems)
    sub = lax.axis_index("sub")
    for k in range(8):
        which = 1 - sub if k < 4 else sub
        copy(k, pl.multiple_of(which * half + k % 4 * step, step), step).start()
    return copy


def square_kernel(tokens, lengths, square_ref, buffer, sems):
    width = tokens.shape[1]
    step = width // sems.shape[0]
    copy = column_copy(tokens, buffer, sems)
    for k in range(width // step):
        copy(k, k * step, step).start()
    squares = jnp.zeros(square_ref.shape, F32)
    for k in range(width // step):
        copy(k, k * step, step).wait()
        for i in range(step // LANES):
            at = k * step + i * LANES
            squares = squares + jnp.square(buffer[:, at : at + LANES].astype(F32))
    square_ref[...] = jnp.broadcast_to(jnp.sum(squares, axis=1, keepdims=True), square_ref.shape)


def cotangent_kernel(
    total, cotangent, lengths, slots, adapter, send_ref, own_ref, low_ref, buffer, sems
):
    rows = cotangent.shape[0]
    copy = start_halves(cotangent, buffer, sems)
    index = jnp.broadcast_to(slots[...], (LANES, rows))
    weight = jnp.zeros((LANES, rows), F32)
    for s in range(lengths.shape[1]):
        length = jnp.full((LANES, rows), lengths[0, s], jnp.int32).astype(F32)
        weight = weight + jnp.where(index == s, (rows // lengths.shape[1]) / length, 0.0)
    row = (weight * F32(1.0 / math.sqrt(total))).T
    scaled_halves(
        buffer,
        low_ref,
        slice(None),
        lambda tile, cols: tile * row,
        lambda value, cols: contract_dims(value, adapter[:, cols], 1, 1),
        send_ref,
        own_ref,
        copy,
    )


def token_kernel(total_width, tokens, gain, adapter, low_out, squares, *refs):
    squares_more, (send_ref, own_ref, low_ref, buffer, sems) = refs[:-5], refs[-5:]
    copy = start_halves(tokens, buffer, sems)
    rank = adapter.shape[1]
    total = squares[...]
    for ref in squares_more:
        total = total + ref[...]
    row = lax.rsqrt(total / total_width + EPS)
    low_ref[:, rank:] = low_out[...]
    scaled_halves(
        buffer,
        low_ref,
        slice(0, rank),
        lambda tile, cols: tile * row * gain[:, cols].astype(F32),
        lambda value, cols: dot(value, adapter[cols, :]),
        send_ref,
        own_ref,
        copy,
    )


def both_kernel(own, got, out_ref):
    rows = own.shape[0]
    out_ref[:rows, :] = own[...]
    out_ref[rows:, :] = got[...]


def widen(scale, wide):
    for g in range(scale.shape[0]):
        row = scale[g : g + 1, :].astype(F32)
        wide[g] = jnp.broadcast_to(row, (LANES, row.shape[1])).T


def place_shards(codes, got, first_got, moved, store):
    n = lax.axis_size("dp")
    sub, grp, place = (lax.axis_index(a) for a in ("sub", "grp", "dp"))
    pos = ring_position()
    blocks = codes.shape[0] // 2
    quarter = blocks // 2

    @pl.loop(0, blocks, unroll=4)
    def _(b):
        store(b, place * 2 + sub, codes[sub * blocks + b])
        store(b, place * 2 + 1 - sub, got[first_got + b])

    streams = len(moved) // (2 * (n - 1))
    size = quarter // streams
    for k in range(n - 1):
        there = ring_at(lax.rem(pos - k - 1 + n, n), n)
        for i in range(2 * streams):
            piece = moved[2 * streams * k + i]
            start = (grp if i % 2 == 0 else 1 - grp) * quarter + i // 2 * size

            @pl.loop(0, size, unroll=4)
            def _(b, piece=piece, start=start, there=there):
                store(start + b, there * 2 + sub, piece[b])
                store(start + b, there * 2 + 1 - sub, piece[size + b])


def front_kernel(first_got, term, own, got, scale, codes, codes_got, *refs):
    moved, (mine_ref, theirs_ref, wide, weight) = term.split(refs)
    blocks, rows, units = codes.shape
    first = lax.axis_index("sub") * (blocks // 2)
    widen(scale, wide)

    def store(b, shard, piece):
        at = pl.ds(pl.multiple_of(shard * rows, ROW_TILE), rows)
        for g in range(units // LANES):
            cols = slice(g * LANES, (g + 1) * LANES)
            factor = wide[g * wide.shape[0] * LANES // units, pl.ds(first + b, 1), :]
            weight[b, at, cols] = (piece[:, cols].astype(F32) * factor).astype(BF16)

    place_shards(codes, codes_got, first_got, moved, store)
    matrix = weight[...].reshape(-1, units)
    mine_ref[...] = term.added(dot(own[...], matrix))
    theirs_ref[...] = dot(got[...], matrix).astype(BF16)


def back_kernel(first_got, term, own, got, scale, codes, codes_got, *refs):
    moved, (mine_ref, theirs_ref, wide, weight) = term.split(refs)
    blocks, rows, block = codes.shape
    first = lax.axis_index("sub") * (blocks // 2)
    per_group = weight.shape[0] // wide.shape[0]
    widen(scale, wide)

    def store(b, shard, piece):
        at = pl.multiple_of(shard * rows, ROW_TILE)
        factor = wide[at // per_group, pl.ds(first + b, 1), :]
        cols = pl.ds(pl.multiple_of(b * block, block), block)
        weight[pl.ds(at, rows), cols] = (piece.astype(F32) * factor).astype(BF16)

    place_shards(codes, codes_got, first_got, moved, store)
    matrix = weight[...]
    mine_ref[...] = term.added(contract_dims(own[...], matrix, 1, 1))
    theirs_ref[...] = contract_dims(got[...], matrix, 1, 1).astype(BF16)


def place_own(scratch, own, more, axis):
    n = len(more) + 1
    size = own.shape[axis]
    for k, ref in enumerate((own, *more)):
        at = pl.ds(pl.multiple_of(lax.rem(lax.axis_index("mp") + n - k, n) * size, size), size)
        if axis == 0:
            scratch[at, :] = ref[...]
        else:
            scratch[:, at] = ref[...]


def own_units(full, ref, axis):
    size = ref.shape[axis]
    for i in range(full.shape[axis] // size):

        @pl.when(lax.axis_index("mp") == i)
        def _(i=i):
            ref[...] = lax.slice_in_dim(full, i * size, (i + 1) * size, axis=axis).astype(BF16)


class NoTerm:
    arrays = ()

    def split(self, refs):
        return refs[:-4], refs[-4:]

    def added(self, product):
        return product


class UpTerm:
    def __init__(self, low, adapters, more):
        self.arrays = (low, adapters, *more)

    def split(self, refs):
        count = len(self.arrays)
        self.refs, self.all = refs[:count], refs[-1]
        return refs[count:-5], refs[-5:-1]

    def added(self, product):
        low, adapters, *more = self.refs
        rank = self.all.shape[0]
        place_own(self.all, adapters.at[:rank], [r.at[:rank] for r in more], 1)
        return product + ADAPTER_SCALE * dot(low[:, :rank].astype(BF16), self.all[...])


class DownTerm(UpTerm):
    def added(self, product):
        low, adapters, *more = self.refs
        rank = self.all.shape[1]
        place_own(self.all, adapters.at[rank:], [r.at[rank:] for r in more], 0)
        return product + ADAPTER_SCALE * contract_dims(
            low[:, rank:].astype(BF16), self.all[...], 1, 1
        )


def hidden_kernel(more, gate, up, adapters, *refs):
    gate_more, up_more, adapters_more = (refs[i * more : (i + 1) * more] for i in range(3))
    silu_ref, hidden_ref, low_ref, down_in_all = refs[3 * more :]
    rank = low_ref.shape[1]
    place_own(down_in_all, adapters.at[rank:], [r.at[rank:] for r in adapters_more], 0)
    gate_sum, up_sum = gate[...], up[...]
    for ref in gate_more:
        gate_sum = gate_sum + ref[...].astype(F32)
    for ref in up_more:
        up_sum = up_sum + ref[...].astype(F32)
    silu = gate_sum * jax.nn.sigmoid(gate_sum)
    silu_ref[...] = silu
    hidden = (silu * up_sum).astype(BF16)
    hidden_ref[...] = hidden
    low_ref[...] = (ADAPTER_SCALE * dot(hidden, down_in_all[...])).astype(BF16)


def up_grad_kernel(more, back, silu, adapters, *refs):
    back_more, adapters_more = (refs[i * more : (i + 1) * more] for i in range(2))
    up_grad_ref, low_ref, up_out_all = refs[2 * more :]
    rank = low_ref.shape[1]
    place_own(up_out_all, adapters.at[:rank], [r.at[:rank] for r in adapters_more], 1)
    total = back[...]
    for ref in back_more:
        total = total + ref[...].astype(F32)
    up_grad = (total * silu[...]).astype(BF16)
    up_grad_ref[...] = up_grad
    low_ref[...] = (ADAPTER_SCALE * contract_dims(up_grad, up_out_all[...], 1, 1)).astype(BF16)


def small_kernel(more, hidden, up_grad, low, *refs):
    low_more, (up_out_term, down_in_term) = refs[:more], refs[more:]
    total = low[...]
    for ref in low_more:
        total = total + ref[...]
    rank = total.shape[1] // 2
    low_up, low_out = total[:, :rank].astype(BF16), total[:, rank:].astype(BF16)
    low_up_t = low_up.astype(F32).T.astype(BF16)
    own_units(ADAPTER_SCALE * dot(low_up_t, up_grad[...]), up_out_term, 1)
    hidden_t = hidden[...].astype(F32).T.astype(BF16)
    own_units(ADAPTER_SCALE * dot(hidden_t, low_out), down_in_term, 0)


def down_out_kernel(n, low, low_got, grad, grad_got, *out_refs):
    pos = ring_position()
    streams = len(out_refs) // n
    low_t = jnp.concatenate([low[...], low_got[...]], axis=0).astype(F32).T.astype(BF16)
    rows = low.shape[0]
    for k, ref in enumerate(out_refs):
        size = ref.shape[1]
        block = lax.rem(pos - 1 - k // streams + 2 * n, n) * streams + k % streams
        at = pl.ds(pl.multiple_of(block * size, size), size)
        ref[...] = (
            dot(low_t[:, :rows], grad[:, at]) + dot(low_t[:, rows:], grad_got[:, at])
        ).astype(BF16)


def up_in_kernel(n, low, low_got, normed_both, up_out_term, down_in_term, *out_refs):
    pos = ring_position()
    streams = len(out_refs) // n
    size = normed_both.shape[1] // len(out_refs)
    extra = out_refs[0].shape[0] - size
    low_t = jnp.concatenate([low[...], low_got[...]], axis=0).astype(F32).T.astype(BF16)
    for k, ref in enumerate(out_refs):
        block = lax.rem(pos - 1 - k // streams + 2 * n, n) * streams + k % streams
        at = pl.ds(pl.multiple_of(block * size, size), size)
        ref[pl.ds(0, size), :] = dot(low_t, normed_both[:, at]).T.astype(BF16)
        per = up_out_term.shape[0] // extra
        index = pl.ds(pl.multiple_of(lax.rem(block, per) * extra, extra), extra)

        @pl.when(block < per)
        def _(ref=ref, index=index):
            ref[pl.ds(size, extra), :] = up_out_term[index, :]

        @pl.when(block >= per)
        def _(ref=ref, index=index):
            ref[pl.ds(size, extra), :] = down_in_term[index, :]


def copy_all(copies):
    for c in copies:
        c.start()
    for c in copies:
        c.wait()


def place_of(i, count, n, pos, sub, size):
    per_core = count // 2
    streams = per_core // n
    half = sub if i < per_core else 1 - sub
    block = lax.rem(pos - i % per_core // streams + n, n) * streams + i % streams
    return pl.ds(pl.multiple_of((half * per_core + block) * size, size), size)


def place_kernel(n, wide_count, *refs):
    pieces = refs[:-7]
    out_ref, up_out_ref, down_in_ref, wide_ref, small, sems, small_sems = refs[-7:]
    pos, sub = ring_position(), lax.axis_index("sub")
    wide, tall = pieces[:wide_count], pieces[wide_count:]
    copies = []
    for i, piece in enumerate(wide):
        at = place_of(i, len(wide), n, pos, sub, piece.shape[1])
        copies.append(pltpu.make_async_copy(piece, wide_ref.at[:, at], sems.at[i]))
    size = out_ref.shape[0] // len(tall)
    extra = tall[0].shape[0] - size
    for i, piece in enumerate(tall):
        at = place_of(i, len(tall), n, pos, sub, size)
        copies.append(
            pltpu.make_async_copy(
                piece.at[pl.ds(0, size), :], out_ref.at[at, :], sems.at[len(wide) + i]
            )
        )
        half = i // (len(tall) // 2)
        at = place_of(i % (len(tall) // 2), len(tall), n, pos, 0, extra)
        copies.append(
            pltpu.make_async_copy(
                piece.at[pl.ds(size, extra), :], small.at[half, at, :], small_sems.at[i]
            )
        )
    copy_all(copies)
    total = (small[0].astype(F32) + small[1].astype(F32)).astype(BF16)
    rows = up_out_ref.shape[0]
    up_out_ref[...] = total[:rows]
    down_in_ref[...] = total[rows:]


def half_kernel(*refs):
    sources, out_ref, sems = refs[:-2], refs[-2], refs[-1]
    other = 1 - lax.axis_index("sub")
    half = sources[0].shape[0] // 2
    copy_all(
        [
            pltpu.make_async_copy(
                ref.at[pl.ds(other * half, half)], out_ref.at[pl.ds(i * half, half)], sems.at[i]
            )
            for i, ref in enumerate(sources)
        ]
    )


def quarter_kernel(count, *refs):
    sources, got, out_refs, sems = refs[:count], refs[count], refs[count + 1 : -1], refs[-1]
    streams = len(out_refs) // count
    sub, grp = lax.axis_index("sub"), lax.axis_index("grp")
    half = sources[0].shape[0] // 2
    quarter = half // 2
    copies = []
    size = quarter // streams
    for i, out_ref in enumerate(out_refs):
        first = grp * quarter + i % streams * size
        own = sources[i // streams].at[pl.ds(sub * half + first, size)]
        theirs = got.at[pl.ds(i // streams * half + first, size)]
        for k, source in enumerate((own, theirs)):
            copies.append(
                pltpu.make_async_copy(source, out_ref.at[pl.ds(k * size, size)], sems.at[2 * i + k])
            )
    copy_all(copies)


def start_shards(codes, streams):
    blocks, rows, units = codes[0].shape
    count = len(codes)
    anywhere = pl.BlockSpec(memory_space=pl.ANY)
    (send,) = call(
        half_kernel,
        "halves",
        codes,
        [shape((count * blocks // 2, rows, units))],
        scratch=[pltpu.SemaphoreType.DMA((count,))],
        specs=[anywhere] * count,
        out_specs=(anywhere,),
        limit=4,
    )
    got = swap(send, "sub")
    moving = call(
        lambda *refs: quarter_kernel(count, *refs),
        "quarters",
        [*codes, got],
        [shape((blocks // 2 // streams, rows, units))] * (count * streams),
        scratch=[pltpu.SemaphoreType.DMA((2 * count * streams,))],
        specs=[anywhere] * (count + 1),
        out_specs=(anywhere,) * (count * streams),
        limit=4,
    )
    return list(moving), got


def fast_body(
    tokens,
    cotangent,
    rms_norm_gain,
    gate_codes,
    gate_block_scale,
    up_codes,
    up_block_scale,
    down_codes,
    down_block_scale,
    up_adapter_in,
    up_adapter_out,
    down_adapter_in,
    down_adapter_out,
    sequence_length_list,
    slot_sequence_index,
):
    rows, local_width = tokens.shape
    blocks, _, units = gate_codes.shape
    block = local_width // blocks
    half = local_width // 2
    rank = up_adapter_in.shape[1]
    total_width = local_width * lax.axis_size("mp")
    n = lax.axis_size("dp")
    more = lax.axis_size("mp") - 1

    (gate_moving, up_moving), front_got = start_shards([gate_codes, up_codes], 1)
    ring, crossed = [], []

    def step(moving, *done):
        ring.append(ring_step(after(moving, *done) if done else moving))

    def cross(k, *done):
        crossed.append(swap(after(ring[k], *done) if done else ring[k], "grp"))

    step(gate_moving)
    step(up_moving)

    vmem = pl.BlockSpec(memory_space=pltpu.VMEM)
    smem = pl.BlockSpec(memory_space=pltpu.SMEM)
    hbm = pl.BlockSpec(memory_space=pltpu.HBM)
    buffers = [pltpu.VMEM((rows, local_width), BF16), pltpu.SemaphoreType.DMA((8,))]
    lengths = after(sequence_length_list, gate_moving, up_moving)
    (squares,) = call(
        square_kernel, "squares", [tokens, lengths], [shape((rows, LANES), F32)],
        scratch=buffers, specs=[hbm, smem], limit=16,
    )
    squares_more = others(squares, "mp")
    grad_send, grad, low_out = call(
        lambda *refs: cotangent_kernel(rows * n * lax.axis_size("sub"), *refs),
        "cotangent",
        [cotangent, after(lengths, squares), slot_sequence_index[None, :], down_adapter_out],
        [shape((rows, half))] * 2 + [shape((rows, rank), F32)],
        scratch=buffers,
        specs=[hbm, smem, vmem, vmem],
    )
    cross(0, grad)
    cross(1, grad)
    step(ring[0], grad)
    step(ring[1], ring[0], grad)
    adapters = jnp.concatenate([up_adapter_out, down_adapter_in], axis=0)
    adapters_more = others(after(adapters, *ring[:2]), "mp")
    normed_send, normed, low = call(
        lambda *refs: token_kernel(total_width, *refs),
        "tokens",
        [
            tokens,
            rms_norm_gain[None, :],
            up_adapter_in,
            low_out,
            after(squares, *ring[2:4], *crossed[:2], *adapters_more),
            *squares_more,
        ],
        [shape((rows, half))] * 2 + [shape((rows, 2 * rank), F32)],
        scratch=buffers,
        specs=[hbm] + [vmem] * (4 + more),
    )
    grad_got = swap(grad_send, "sub")
    normed_got = swap(normed_send, "sub")
    step(ring[2], ring[3], *crossed[:2])
    step(ring[3], ring[2], *crossed[:2])
    cross(2)
    cross(3)
    cross(4)
    cross(5)
    down_turned = jnp.swapaxes(after(down_codes, ring[4]), 0, 1)
    down_moving, down_got = start_shards([down_turned], STREAMS)
    front_steps = 2 * (n - 1)
    for moving in down_moving:
        step(moving, *ring[4:6], *crossed[2:4], grad_got, normed_got)
    for k in range(STREAMS):
        cross(front_steps + k)
    for k in range(STREAMS):
        step(ring[front_steps + k])
        cross(-1)

    def product(kernel, name, own, got, scale, codes, codes_got, first_got, steps, weight_shape, term, extra=()):
        groups = scale.shape[0]
        mine, theirs = call(
            lambda *refs: kernel(first_got, term, *refs),
            name,
            [own, got, scale, codes, codes_got, *term.arrays, *[x for k in steps for x in (ring[k], crossed[k])]],
            [shape((rows, units), F32), shape((rows, units))],
            scratch=[pltpu.VMEM((groups, blocks, LANES), F32), pltpu.VMEM(weight_shape, BF16), *extra],
            flops=4 * rows * half * units,
        )
        total = mine + swap(theirs, "sub").astype(F32)
        return total, others(total.astype(BF16), "mp"), mine

    front = (blocks // 2, block, units)
    first_down = [*ring[front_steps : front_steps + STREAMS]]
    half_blocks = blocks // 2
    gate, gate_more, gate_mine = product(
        front_kernel, "gate", normed, normed_got, after(gate_block_scale.T, *first_down), gate_codes, front_got, 0,
        range(0, 2 * (n - 1), 2), front, NoTerm(),
    )
    up, up_more, up_mine = product(
        front_kernel, "up", normed, normed_got, after(up_block_scale.T, *first_down), up_codes, front_got, half_blocks,
        range(1, 2 * (n - 1), 2), front, UpTerm(low, adapters, adapters_more),
        [pltpu.VMEM((rank, units), BF16)],
    )
    for k in range(STREAMS):
        before = front_steps + STREAMS + k
        step(ring[before], gate_mine, up_mine, crossed[before - STREAMS])
        cross(-1)
    silu, hidden, low_hidden = call(
        lambda *refs: hidden_kernel(more, *refs),
        "hidden",
        [gate, up, adapters, *gate_more, *up_more, *adapters_more],
        [shape((rows, units), F32), shape((rows, units)), shape((rows, rank))],
        scratch=[pltpu.VMEM((units, rank), BF16)],
        limit=8,
    )
    low_hidden_got = swap(low_hidden, "sub")
    down_out_parts = call(
        lambda *refs: down_out_kernel(n, *refs),
        "down_out",
        [low_hidden, low_hidden_got, grad, grad_got],
        [shape((rank, half // (WIDE_STREAMS * n)))] * (WIDE_STREAMS * n),
        flops=4 * rows * half * rank,
    )
    down_out_blocks, seen = ring_all(down_out_parts, WIDE_STREAMS)
    (normed_both,) = call(
        both_kernel,
        "both",
        [normed, after(normed_got, low_hidden)],
        [shape((2 * rows, half))],
        limit=32,
    )

    back, back_more, _ = product(
        back_kernel, "back", grad, grad_got, after(down_block_scale, normed_both, down_out_parts[0]), down_turned, down_got, 0,
        range(front_steps, (2 + STREAMS) * (n - 1)), (units, half), DownTerm(low, adapters, adapters_more),
        [pltpu.VMEM((units, rank), BF16)],
    )
    up_grad, low_grad = call(
        lambda *refs: up_grad_kernel(more, *refs),
        "up_grad",
        [back, silu, adapters, *back_more, *adapters_more],
        [shape((rows, units)), shape((rows, rank))],
        scratch=[pltpu.VMEM((rank, units), BF16)],
        limit=8,
    )
    low_more = others(after(low, *seen[0]), "mp")
    up_out_term, down_in_term = call(
        lambda *refs: small_kernel(more, *refs),
        "small",
        [hidden, up_grad, low, *low_more],
        [shape(up_adapter_out.shape), shape(down_adapter_in.shape)],
        limit=8,
    )
    extra = 2 * rank // (TALL_STREAMS * n)
    up_in_parts = call(
        lambda *refs: up_in_kernel(n, *refs),
        "up_in",
        [after(low_grad, *seen[2]), swap(low_grad, "sub"), normed_both, up_out_term, down_in_term],
        [shape((half // (TALL_STREAMS * n) + extra, rank))] * (TALL_STREAMS * n),
        flops=4 * rows * half * rank,
    )
    up_in_blocks, _ = ring_all(up_in_parts, TALL_STREAMS, down_out_blocks[-WIDE_STREAMS:])

    anywhere = pl.BlockSpec(memory_space=pl.ANY)
    up_in_gradient, up_out_gradient, down_in_gradient, down_out_gradient = call(
        lambda *refs: place_kernel(n, len(down_out_blocks), *refs),
        "place",
        [*down_out_blocks, *up_in_blocks],
        [
            shape((local_width, rank)),
            shape(up_adapter_out.shape),
            shape(down_adapter_in.shape),
            shape((rank, local_width)),
        ],
        scratch=[
            pltpu.VMEM((2, 2 * rank, rank), BF16),
            pltpu.SemaphoreType.DMA((2 * n * (WIDE_STREAMS + TALL_STREAMS),)),
            pltpu.SemaphoreType.DMA((2 * n * TALL_STREAMS,)),
        ],
        specs=[anywhere] * (2 * n * (WIDE_STREAMS + TALL_STREAMS)),
        out_specs=(anywhere, vmem, vmem, anywhere),
        limit=4,
    )
    return up_in_gradient, up_out_gradient, down_in_gradient, down_out_gradient


def general_body(
    tokens,
    cotangent,
    rms_norm_gain,
    gate_codes,
    gate_block_scale,
    up_codes,
    up_block_scale,
    down_codes,
    down_block_scale,
    up_adapter_in,
    up_adapter_out,
    down_adapter_in,
    down_adapter_out,
    sequence_length_list,
    slot_sequence_index,
):
    rows = tokens.shape[0]
    local_width = tokens.shape[1]
    block = gate_block_scale.shape[0] and local_width // gate_codes.shape[0]
    blocks_here = gate_codes.shape[0]
    total_width = local_width * lax.axis_size("mp")
    own_squares = jnp.sum(jnp.square(tokens.astype(jnp.float32)), axis=-1, keepdims=True)
    squares = lax.psum(own_squares, "mp") / total_width
    inv_rms = lax.rsqrt(squares + EPS)
    local_normed_input = (
        tokens.astype(jnp.float32) * inv_rms * rms_norm_gain.astype(jnp.float32)[None, :]
    ).astype(jnp.bfloat16)
    seq_count = sequence_length_list.shape[1]
    longest = rows // seq_count
    total = rows * lax.axis_size("dp") * lax.axis_size("sub")
    ratios = longest / sequence_length_list[0].astype(jnp.float32)
    match = slot_sequence_index[:, None] == jnp.arange(seq_count, dtype=jnp.int32)[None, :]
    token_weight = jnp.sum(jnp.where(match, ratios[None, :], jnp.float32(0.0)), axis=-1)
    token_weight = token_weight * jnp.float32(1.0 / math.sqrt(total))
    local_output = (cotangent.astype(jnp.float32) * token_weight[:, None]).astype(jnp.bfloat16)
    partial_up = jnp.dot(local_normed_input, up_adapter_in, preferred_element_type=jnp.float32)
    partial_output = contract_dims(local_output, down_adapter_out, 1, 1)
    up_adapter_rank, output_adapter_rank = lax.psum((partial_up, partial_output), "mp")
    up_adapter_rank = up_adapter_rank.astype(jnp.bfloat16)
    output_adapter_rank = output_adapter_rank.astype(jnp.bfloat16)
    normed_blocks = local_normed_input.reshape(rows, blocks_here, block)
    out_blocks = local_output.reshape(rows, blocks_here, block)
    wide_gate = jnp.repeat(gate_block_scale.astype(jnp.float32), block, axis=1)[:, None, :]
    wide_up = jnp.repeat(up_block_scale.astype(jnp.float32), block, axis=1)[:, None, :]
    wide_down = jnp.repeat(down_block_scale.astype(jnp.float32), block, axis=0)
    dims_front = (((1, 2), (0, 1)), ((), ()))
    dims_back = (((1, 2), (1, 2)), ((), ()))
    quant_g = lax.all_gather(gate_codes, ("dp", "sub"), axis=1, tiled=True)
    quant_u = lax.all_gather(up_codes, ("dp", "sub"), axis=1, tiled=True)
    weight_g = (quant_g.astype(jnp.float32) * wide_gate).astype(jnp.bfloat16)
    weight_u = (quant_u.astype(jnp.float32) * wide_up).astype(jnp.bfloat16)
    gate_next = lax.dot_general(
        normed_blocks, weight_g, dims_front, preferred_element_type=jnp.float32
    )
    up_next = lax.dot_general(
        normed_blocks, weight_u, dims_front, preferred_element_type=jnp.float32
    )
    gate, base_up_projected = (
        lax.psum_scatter(gate_next, "mp", scatter_dimension=1, tiled=True),
        lax.psum_scatter(up_next, "mp", scatter_dimension=1, tiled=True),
    )
    up_projected = base_up_projected + ADAPTER_SCALE * jnp.dot(
        up_adapter_rank, up_adapter_out, preferred_element_type=jnp.float32
    )
    silu_gate = jax.nn.silu(gate)
    hidden_units = (silu_gate * up_projected).astype(jnp.bfloat16)
    partial_hidden = jnp.dot(hidden_units, down_adapter_in, preferred_element_type=jnp.float32)
    hidden_adapter_rank = lax.psum(partial_hidden, "mp").astype(jnp.bfloat16)
    weight_d = (
        lax.all_gather(down_codes, ("dp", "sub"), axis=0, tiled=True).astype(jnp.float32)
        * wide_down[:, :, None]
    ).astype(jnp.bfloat16)
    back_part = lax.dot_general(out_blocks, weight_d, dims_back, preferred_element_type=jnp.float32)
    base_backward = lax.psum_scatter(back_part, "mp", scatter_dimension=1, tiled=True)
    hidden_gradient = base_backward + ADAPTER_SCALE * contract_dims(
        output_adapter_rank, down_adapter_in, 1, 1
    )
    up_gradient = (hidden_gradient * silu_gate).astype(jnp.bfloat16)
    partial_gradient = contract_dims(up_gradient, up_adapter_out, 1, 1)
    up_adapter_rank_gradient = lax.psum(partial_gradient, "mp").astype(jnp.bfloat16)
    up_in_term = ADAPTER_SCALE * contract_dims(local_normed_input, up_adapter_rank_gradient, 0, 0)
    up_out_term = ADAPTER_SCALE * contract_dims(up_adapter_rank, up_gradient, 0, 0)
    down_in_term = ADAPTER_SCALE * contract_dims(hidden_units, output_adapter_rank, 0, 0)
    down_out_term = ADAPTER_SCALE * contract_dims(hidden_adapter_rank, local_output, 0, 0)
    sum_up_a, sum_up_b, sum_down_a, sum_down_b = lax.psum(
        (up_in_term, up_out_term, down_in_term, down_out_term), ("dp", "sub")
    )
    return (
        sum_up_a.astype(jnp.bfloat16),
        sum_up_b.astype(jnp.bfloat16),
        sum_down_a.astype(jnp.bfloat16),
        sum_down_b.astype(jnp.bfloat16),
    )


def body(tokens, cotangent, rms_norm_gain, gate_codes, *rest):
    whole_tiles = gate_codes.shape[1] % ROW_TILE == 0
    ring_of_four = lax.axis_size("dp") == 4
    pairs = lax.axis_size("grp") == 2 and lax.axis_size("sub") == 2
    form = fast_body if whole_tiles and ring_of_four and pairs else general_body
    return form(tokens, cotangent, rms_norm_gain, gate_codes, *rest)


def solution(mesh):
    placed = (
        P(("grp", "dp", "sub"), "mp"),
        P(("grp", "dp", "sub"), "mp"),
        P("mp"),
        P("mp", ("dp", "sub"), None),
        P("mp", None),
        P("mp", ("dp", "sub"), None),
        P("mp", None),
        P(("dp", "sub"), "mp", None),
        P(None, "mp"),
        P(("grp", "mp"), None),
        P("grp", "mp"),
        P(("grp", "mp"), None),
        P("grp", "mp"),
        P(("grp", "dp", "sub"), None),
        P(("grp", "dp", "sub")),
    )
    return jax.shard_map(
        body,
        mesh=mesh,
        in_specs=placed,
        out_specs=(P(("grp", "mp"), None), P("grp", "mp"), P(("grp", "mp"), None), P("grp", "mp")),
        check_vma=False,
    )
```
